32 devices in a mesh: items: 4 (over y, core), blk: 2 (over x), heads: 4 (over z).
Axes of the slice: x: 2, y: 2, z: 4, core: 2. Of those that a mesh axis runs over, the one named last changes fastest.
Arguments:
- inputs: bfloat16 [2048, 32, 768], P('blk', 'items'), may hold values from -6 to 6
- padding: int32 [2048, 32], P('blk', 'items'), may hold values from 0 to 1, as said below
- language: int32 [32], P('items'), may hold values from 0 to 31
- lang_table: bfloat16 [32, 768], replicated, may hold values from -3 to 3
- latents: bfloat16 [256, 1280], P('blk'), may hold values from -6 to 6
- in_gain: float32 [768], replicated, may hold values from 0.5 to 1.5
- in_bias: float32 [768], replicated, may hold values from -2 to 2
- lat_gain: float32 [1280], replicated, may hold values from 0.5 to 1.5
- lat_bias: float32 [1280], replicated, may hold values from -2 to 2
- mid_gain: float32 [1280], replicated, may hold values from 0.5 to 1.5
- mid_bias: float32 [1280], replicated, may hold values from -2 to 2
- w_query: bfloat16 [1280, 1280], P(None, 'heads'), may hold values from -0.15625 to 0.15625
- w_key: bfloat16 [768, 1280], P(None, 'heads'), may hold values from -0.21875 to 0.21875
- w_value: bfloat16 [768, 1280], P(None, 'heads'), may hold values from -0.21875 to 0.21875
- w_out: bfloat16 [1280, 1280], P('heads'), may hold values from -4 to 4
- w_up: bfloat16 [1280, 1280], P(None, 'heads'), may hold values from -0.15625 to 0.15625
- b_up: float32 [1280], P('heads'), may hold values from -3 to 3
- w_down: bfloat16 [1280, 1280], P('heads'), may hold values from -0.15625 to 0.15625
- b_down: float32 [1280], replicated, may hold values from -3 to 3
- cotangent: bfloat16 [32, 256, 1280], P('items', 'blk'), may hold values from -6 to 6
Outputs:
- mixed_latents: bfloat16 [32, 256, 1280], P('items', 'blk')
- grad_inputs: bfloat16 [2048, 32, 768], P('blk', 'items', 'heads')
- grad_latents: float32 [256, 1280], P('blk')
- grad_lang_table: float32 [32, 768], P(None, 'heads')
- grad_in_gain: float32 [768], P('heads')
- grad_in_bias: float32 [768], P('heads')
- grad_lat_gain: float32 [1280], replicated
- grad_lat_bias: float32 [1280], replicated
- grad_mid_gain: float32 [1280], replicated
- grad_mid_bias: float32 [1280], replicated
- grad_w_query: float32 [1280, 1280], P(None, 'heads')
- grad_w_key: float32 [768, 1280], P(None, 'heads')
- grad_w_value: float32 [768, 1280], P(None, 'heads')
- grad_w_out: float32 [1280, 1280], P('heads')
- grad_w_up: float32 [1280, 1280], P(None, 'heads')
- grad_b_up: float32 [1280], P('heads')
- grad_w_down: float32 [1280, 1280], P('heads')
- grad_b_down: float32 [1280], replicated
The draws below stay inside these ranges and needn't reach their ends.
Inputs may be any that keep to these rules, and one draw needn't show every extreme that they name: `padding`: each sequence's live bytes are a prefix of 256 to 2048 bytes; in each run of sequences k * 8 to (k + 1) * 8 - 1, one sequence drawn from the seed is live in full.
All inputs are finite; a program needn't handle non-finite values.
Results may differ from the reference program's by a relative error of at most 0.02.
Values may be sent and summed in bfloat16 or wider, within the bound.
A program may use at most 320 MiB of HBM per device.

```python
from functools import partial
import jax
import jax.numpy as jnp
from jax import lax

DIN = 768
DL = 1280
NLAT = 256
HEADS = 8
SEQ_LEN = 2048
SEQ_DEV = 8
NLANG = 32
SEQS = 32


def draw_padding(key, part):
    key = jax.random.fold_in(key, 11)
    len_key, pick_key = jax.random.split(key)
    lengths = jax.random.randint(len_key, (SEQS,), SEQ_LEN // 8, SEQ_LEN + 1)
    groups = SEQS // SEQ_DEV
    chosen = jax.random.randint(pick_key, (groups,), 0, SEQ_DEV) + jnp.arange(groups) * SEQ_DEV
    lengths = lengths.at[chosen].set(SEQ_LEN)
    positions = jnp.arange(SEQ_LEN)[:, None]
    return (positions < lengths[None, :]).astype(jnp.int32)


def place_ends(entries, own_key, least, largest):
    shape = entries.shape
    spot = [jax.random.randint(jax.random.fold_in(own_key, axis), (), 0, shape[axis]) for axis in range(len(shape))]
    entries = entries.at[tuple(spot)].set(least)
    longest = shape.index(max(shape))
    spot[longest] = (spot[longest] + 1) % shape[longest]
    return entries.at[tuple(spot)].set(largest)


def block_levels(key, dims, cuts, least, top_value):
    factor_of = 1.0
    for dim, blocks in cuts:
        draws = jax.random.uniform(jax.random.fold_in(jax.random.fold_in(key, 6), dim), (blocks,), jnp.float32, least / len(cuts), top_value / len(cuts))
        factor_of = factor_of * jnp.repeat(jnp.exp(draws), dims[dim] // blocks).reshape((-1,) + (1,) * (len(dims) - 1 - dim))
    return factor_of


def scatter_about(own_key, shape, scale, bound, cuts=(), kind=jnp.bfloat16):
    loudness = block_levels(own_key, shape, cuts, -0.22, 0.18) if cuts else 1.0
    array = jax.random.normal(own_key, shape, jnp.float32) * scale * loudness
    return jnp.minimum(jnp.maximum(array, -bound), bound).astype(kind)


def setup_inputs(seed: int = 0) -> dict:
    seeds = jax.random.split(jax.random.key(seed), 21)
    return {
        "inputs": scatter_about(seeds[0], (SEQ_LEN, SEQS, DIN), 1.0, 6.0, ((0, 2), (1, 4))),
        "padding": draw_padding(jax.random.fold_in(seeds[20], 71), 0),
        "language": place_ends(jax.random.randint(seeds[2], (SEQS,), 0, NLANG), jax.random.fold_in(seeds[2], 1), 0, NLANG - 1).astype(jnp.int32),
        "lang_table": scatter_about(seeds[3], (NLANG, DIN), 0.5, 3.0),
        "latents": scatter_about(seeds[4], (NLAT, DL), 1.0, 6.0, ((0, 2),)),
        "in_gain": jnp.clip(1.0 + 0.1 * jax.random.normal(seeds[5], (DIN,), jnp.float32), 0.5, 1.5),
        "in_bias": scatter_about(seeds[6], (DIN,), 0.3, 2.0, (), jnp.float32),
        "lat_gain": jnp.clip(1.0 + 0.1 * jax.random.normal(seeds[7], (DL,), jnp.float32), 0.5, 1.5),
        "lat_bias": scatter_about(seeds[8], (DL,), 0.3, 2.0, (), jnp.float32),
        "mid_gain": jnp.clip(1.0 + 0.1 * jax.random.normal(seeds[9], (DL,), jnp.float32), 0.5, 1.5),
        "mid_bias": scatter_about(seeds[10], (DL,), 0.3, 2.0, (), jnp.float32),
        "w_query": scatter_about(seeds[11], (DL, DL), DL ** -0.5, 0.15625, ((1, 4),)),
        "w_key": scatter_about(seeds[12], (DIN, DL), DIN ** -0.5, 0.21875, ((1, 4),)),
        "w_value": scatter_about(seeds[13], (DIN, DL), DIN ** -0.5, 0.21875, ((1, 4),)),
        "w_out": scatter_about(seeds[14], (DL, DL), (max(DL * 4 // SEQ_LEN, 1)) ** -0.5, 4.0, ((0, 4),)),
        "w_up": scatter_about(seeds[15], (DL, DL), DL ** -0.5, 0.15625, ((1, 4),)),
        "b_up": scatter_about(seeds[16], (DL,), 0.5, 3.0, ((0, 4),), jnp.float32),
        "w_down": scatter_about(seeds[17], (DL, DL), DL ** -0.5, 0.15625, ((0, 4),)),
        "b_down": scatter_about(seeds[18], (DL,), 0.5, 3.0, (), jnp.float32),
        "cotangent": scatter_about(seeds[19], (SEQS, NLAT, DL), 1.0, 6.0, ((0, 4), (1, 2))),
    }


EPS = 1e-05
MASKED = -1e+30
HIGH = lax.Precision.HIGHEST

@jax.custom_vjp
def low(v):
    return lax.optimization_barrier(v.astype(jnp.bfloat16)).astype(jnp.float32)

@jax.custom_vjp
def low_back(v):
    return v

def low_keep(v):
    return (low(v), None)

def low_pass(kept, grad):
    return (grad,)

def back_keep(v):
    return (v, None)

def back_low(kept, grad):
    return (low(grad),)
low.defvjp(low_keep, low_pass)
low_back.defvjp(back_keep, back_low)

def norm_rows(values, gain, bias):
    average = lax.optimization_barrier(jnp.mean(values, axis=-1, keepdims=True))
    centred = values - average
    spread = lax.optimization_barrier(jnp.mean(centred * centred, axis=-1, keepdims=True))
    return centred * lax.rsqrt(spread + EPS) * gain + bias

def forward(padding, language, inputs, lang_table, latents, in_gain, in_bias, lat_gain, lat_bias, mid_gain, mid_bias, w_query, w_key, w_value, w_out, w_up, b_up, w_down, b_down):
    head_dim = DL // HEADS
    factor = head_dim ** (-0.5)
    lat_norm = low(norm_rows(latents, lat_gain, lat_bias))
    queries = low(low_back(jnp.dot(lat_norm, w_query, precision=HIGH))).reshape(NLAT, HEADS, head_dim)
    pair_count = SEQS // 2
    byte_groups = inputs.reshape(SEQ_LEN, pair_count, 2, DIN).transpose(1, 0, 2, 3)
    live_groups = padding.reshape(SEQ_LEN, pair_count, 2).transpose(1, 0, 2)
    lang_groups = language.reshape(pair_count, 2)
    lang_index = jnp.arange(NLANG, dtype=jnp.int32)

    def group_step(carried, pieces):
        byte_block, live_block, lang_block = pieces
        onehot = (lang_block[:, None] == lang_index[None, :]).astype(jnp.float32)
        embedded = jnp.dot(onehot, lang_table, precision=HIGH)
        x_norm = low(norm_rows(byte_block + embedded[None], in_gain, in_bias))
        key_heads = low(low_back(jnp.einsum('tgi,ic->tgc', x_norm, w_key, precision=HIGH)))
        key_heads = key_heads.reshape(SEQ_LEN, 2, HEADS, head_dim)
        value_heads = low(low_back(jnp.einsum('tgi,ic->tgc', x_norm, w_value, precision=HIGH)))
        value_heads = value_heads.reshape(SEQ_LEN, 2, HEADS, head_dim)
        scores = low_back(jnp.einsum('rhd,tghd->grht', queries, key_heads, precision=HIGH) * factor)
        scores = jnp.where(jnp.transpose(live_block)[:, None, None, :] > 0, scores, MASKED)
        weights = low(jax.nn.softmax(scores, axis=-1))
        attended = jnp.einsum('grht,tghd->grhd', weights, value_heads, precision=HIGH).reshape(2, NLAT, DL)
        attended = low(low_back(attended))
        branch = low_back(jnp.einsum('grc,cd->grd', attended, w_out, precision=HIGH))
        middle = latents[None] + branch
        mid_norm = low(norm_rows(middle, mid_gain, mid_bias))
        hidden = low_back(jnp.einsum('grc,cd->grd', mid_norm, w_up, precision=HIGH) + b_up)
        active = low(jax.nn.gelu(hidden))
        result = middle + jnp.einsum('grc,cd->grd', active, w_down, precision=HIGH) + b_down
        return (carried, result)
    start_carry = jnp.zeros((), jnp.float32)
    finished, stacked = lax.scan(jax.checkpoint(group_step), start_carry, (byte_groups, live_groups, lang_groups))
    return stacked.reshape(SEQS, NLAT, DL)

def reference(inputs, padding, language, lang_table, latents, in_gain, in_bias, lat_gain, lat_bias, mid_gain, mid_bias, w_query, w_key, w_value, w_out, w_up, b_up, w_down, b_down, cotangent):
    floats = tuple((array_in.astype(jnp.float32) for array_in in (inputs, lang_table, latents, in_gain, in_bias, lat_gain, lat_bias, mid_gain, mid_bias, w_query, w_key, w_value, w_out, w_up, b_up, w_down, b_down)))
    mixed, pullback = jax.vjp(partial(forward, padding, language), *floats)
    grads = pullback(cotangent.astype(jnp.float32))
    return (mixed.astype(jnp.bfloat16), grads[0].astype(jnp.bfloat16), grads[2], grads[1], grads[3], grads[4], grads[5], grads[6], grads[7], grads[8], grads[9], grads[10], grads[11], grads[12], grads[13], grads[14], grads[15], grads[16])
```

```python
import functools

import jax
import jax.numpy as jnp
from jax import lax
from jax.experimental import pallas as pl
from jax.experimental.pallas import tpu as pltpu
from jax.sharding import PartitionSpec as P

HEADS = 8
EPS = 1e-05
MASKED = -1e30
LOG2E = 1.4426950408889634
F32 = jnp.float32
BF16 = jnp.bfloat16
NT = (((1,), (1,)), ((), ()))
VMEM_LIMIT = 60 * 1024 * 1024


def dot(a, b):
    return jnp.dot(a, b, preferred_element_type=F32)


def dot_nt(a, b):
    return lax.dot_general(a, b, NT, preferred_element_type=F32)


def norm_keep(values, gain, bias):
    average = jnp.mean(values, axis=-1, keepdims=True)
    centred = values - average
    inverse = lax.rsqrt(jnp.mean(centred * centred, axis=-1, keepdims=True) + EPS)
    normed = centred * inverse
    return (normed * gain + bias, normed, inverse)


def norm_back(grad_norm, normed, inverse, gain):
    scaled = grad_norm * gain
    first = jnp.mean(scaled, axis=-1, keepdims=True)
    second = jnp.mean(scaled * normed, axis=-1, keepdims=True)
    return (scaled - first - normed * second) * inverse


def norm_columns(x, emb):
    shifted = x.astype(F32) + emb
    centred = shifted - jnp.mean(shifted, axis=0, keepdims=True)
    inverse = lax.rsqrt(jnp.mean(centred * centred, axis=0, keepdims=True) + EPS)
    return centred * inverse, inverse


def head_rows(h, per_shard, head_dim):
    key = (h // per_shard) * 2 * per_shard + lax.rem(h, per_shard)
    key_at = pl.multiple_of(key * head_dim, head_dim)
    return pl.ds(key_at, head_dim), pl.ds(pl.multiple_of(key_at + per_shard * head_dim, head_dim), head_dim)


def forward_kernel(per_shard, x_ref, emb_ref, gain_ref, bias_ref, w_ref, q_ref, mask_ref, kv_ref, o_ref, lse_ref, xn_ref, stat_ref):
    heads, rows, head_dim = q_ref.shape
    length = x_ref.shape[1]
    piece = min(256, length)

    def norm_step(i, _):
        at = pl.ds(pl.multiple_of(i * piece, piece), piece)
        normed, _unused = norm_columns(x_ref[:, at], emb_ref[...])
        xn_ref[:, at] = (normed * gain_ref[...] + bias_ref[...]).astype(BF16)
        return 0

    lax.fori_loop(0, length // piece, norm_step, 0)
    block = 512 if w_ref.shape[0] % 512 == 0 else 160

    def pair_step(i, _):
        at = pl.ds(pl.multiple_of(i * block, block), block)
        kv_ref[at] = dot(w_ref[at], xn_ref[...]).astype(BF16)
        return 0

    lax.fori_loop(0, w_ref.shape[0] // block, pair_step, 0)
    factor = LOG2E * head_dim ** (-0.5)
    lane = lax.broadcasted_iota(jnp.int32, (rows, 128), 1)
    stat_ref[...] = jnp.zeros_like(stat_ref)

    def head_step(h, _):
        at_key, at_value = head_rows(h, per_shard, head_dim)
        scores = dot(q_ref[h], kv_ref[at_key]) * factor + mask_ref[...]
        top = jnp.max(scores, axis=1, keepdims=True)
        weights = jnp.exp2(scores - top)
        total = jnp.sum(weights, axis=1, keepdims=True)
        out = dot_nt(kv_ref[at_value], weights.astype(BF16))
        stat_ref[...] = jnp.where(lane == h, top + jnp.log2(total), stat_ref[...])
        inverse = jnp.transpose(jnp.broadcast_to(1.0 / total, (rows, 128)))[:1]
        o_ref[pl.ds(pl.multiple_of(h * head_dim, head_dim), head_dim)] = (out * inverse).astype(BF16)
        return 0

    lax.fori_loop(0, heads, head_step, 0)
    lse_ref[...] = jnp.transpose(stat_ref[...])[:heads]


def forward_call(x_cols, emb, gain, bias, w_rows, q, mask, per_shard):
    seqs, width, length = x_cols.shape
    heads, rows, head_dim = q.shape
    pair_rows = w_rows.shape[0]
    whole = pl.BlockSpec(memory_space=pltpu.VMEM)

    def per_seq(*dims):
        return pl.BlockSpec((None,) + dims, lambda s: (s, 0, 0))

    return pl.pallas_call(
        functools.partial(forward_kernel, per_shard),
        grid=(seqs,),
        in_specs=[per_seq(width, length), per_seq(width, 1), whole, whole, whole, whole, per_seq(1, length)],
        out_specs=[per_seq(pair_rows, length), per_seq(heads * head_dim, rows), per_seq(heads, rows)],
        out_shape=[
            jax.ShapeDtypeStruct((seqs, pair_rows, length), BF16),
            jax.ShapeDtypeStruct((seqs, heads * head_dim, rows), BF16),
            jax.ShapeDtypeStruct((seqs, heads, rows), F32),
        ],
        scratch_shapes=[pltpu.VMEM((width, length), BF16), pltpu.VMEM((rows, 128), F32)],
        compiler_params=pltpu.CompilerParams(vmem_limit_bytes=VMEM_LIMIT),
        name="attend",
    )(x_cols, emb, gain, bias, w_rows, q, mask)


def backward_kernel(per_shard, x_ref, emb_ref, gain_ref, bias_ref, w_ref, q_ref, qt_ref, do_ref, dot_ref, lse_ref, delta_ref, mask_ref, kv_ref,
                    g_ref, dw_ref, dq_ref, dgain_ref, dbias_ref, demb_ref, xn_ref, dkv_ref):
    heads, rows, head_dim = q_ref.shape
    width, length = x_ref.shape
    piece = min(256, length)

    @pl.when(pl.program_id(0) == 0)
    def _():
        dw_ref[...] = jnp.zeros_like(dw_ref)
        dq_ref[...] = jnp.zeros_like(dq_ref)
        dgain_ref[...] = jnp.zeros_like(dgain_ref)
        dbias_ref[...] = jnp.zeros_like(dbias_ref)

    def norm_step(i, _):
        at = pl.ds(pl.multiple_of(i * piece, piece), piece)
        normed, _unused = norm_columns(x_ref[:, at], emb_ref[...])
        xn_ref[:, at] = (normed * gain_ref[...] + bias_ref[...]).astype(BF16)
        return 0

    lax.fori_loop(0, length // piece, norm_step, 0)
    scale = head_dim ** (-0.5)
    factor = LOG2E * scale

    def head_step(h, _):
        at_key, at_value = head_rows(h, per_shard, head_dim)
        keys = kv_ref[at_key]
        weights = jnp.exp2(dot(q_ref[h], keys) * factor + mask_ref[...] - lse_ref[h])
        dkv_ref[at_value] = dot(dot_ref[h], weights.astype(BF16)).astype(BF16)
        grad = dot(do_ref[h], kv_ref[at_value]) - delta_ref[h]
        grad = (weights * grad).astype(BF16)
        dkv_ref[at_key] = (dot(qt_ref[h], grad) * scale).astype(BF16)
        dq_ref[h] += dot_nt(keys, grad) * scale
        return 0

    lax.fori_loop(0, heads, head_step, 0)
    block = 512 if dw_ref.shape[0] % 512 == 0 else 160

    def weight_step(i, _):
        at = pl.ds(pl.multiple_of(i * block, block), block)
        dw_ref[at] += dot_nt(dkv_ref[at], xn_ref[...])
        return 0

    lax.fori_loop(0, dw_ref.shape[0] // block, weight_step, 0)

    def byte_step(i, carry):
        at = pl.ds(pl.multiple_of(i * piece, piece), piece)
        grad = dot(w_ref[...], dkv_ref[:, at])
        normed, inverse = norm_columns(x_ref[:, at], emb_ref[...])
        dbias_ref[...] += jnp.sum(grad, axis=1, keepdims=True)
        dgain_ref[...] += jnp.sum(grad * normed, axis=1, keepdims=True)
        scaled = grad * gain_ref[...]
        first = jnp.mean(scaled, axis=0, keepdims=True)
        second = jnp.mean(scaled * normed, axis=0, keepdims=True)
        shifted = (scaled - first - normed * second) * inverse
        g_ref[:, at] = shifted.astype(BF16)
        return carry + jnp.sum(shifted, axis=1, keepdims=True)

    demb_ref[...] = lax.fori_loop(0, length // piece, byte_step, jnp.zeros((width, 1), F32))


def backward_call(x_cols, emb, gain, bias, w, q, qt, grad_out, grad_out_t, lse, delta, mask, pairs, per_shard):
    seqs, width, length = x_cols.shape
    heads, rows, head_dim = q.shape
    pair_rows = w.shape[1]
    whole = pl.BlockSpec(memory_space=pltpu.VMEM)

    def per_seq(*dims):
        return pl.BlockSpec((None,) + dims, lambda s: (s,) + (0,) * len(dims))

    return pl.pallas_call(
        functools.partial(backward_kernel, per_shard),
        grid=(seqs,),
        in_specs=[
            per_seq(width, length), per_seq(width, 1), whole, whole, whole, whole, whole,
            per_seq(heads, rows, head_dim), per_seq(heads, head_dim, rows),
            per_seq(heads, rows, 1), per_seq(heads, rows, 1), per_seq(1, length), per_seq(pair_rows, length),
        ],
        out_specs=[per_seq(width, length), whole, whole, whole, whole, per_seq(width, 1)],
        out_shape=[
            jax.ShapeDtypeStruct((seqs, width, length), BF16),
            jax.ShapeDtypeStruct((pair_rows, width), F32),
            jax.ShapeDtypeStruct((heads, head_dim, rows), F32),
            jax.ShapeDtypeStruct((width, 1), F32),
            jax.ShapeDtypeStruct((width, 1), F32),
            jax.ShapeDtypeStruct((seqs, width, 1), F32),
        ],
        scratch_shapes=[pltpu.VMEM((width, length), BF16), pltpu.VMEM((pair_rows, length), BF16)],
        compiler_params=pltpu.CompilerParams(vmem_limit_bytes=VMEM_LIMIT),
        name="attend_back",
    )(x_cols, emb, gain, bias, w, q, qt, grad_out, grad_out_t, lse, delta, mask, pairs)


REST = ("items", "blk")
ALL = ("heads", "items", "blk")


def gather_rows(shard):
    count = lax.axis_size("items") * lax.axis_size("blk")
    me = lax.axis_index("items") * lax.axis_size("blk") + lax.axis_index("blk")
    share = shard.shape[0] // count
    part = lax.dynamic_slice_in_dim(shard, me * share, share, 0)
    return lax.all_gather(part, ALL, axis=0, tiled=True)


def scatter_rows(whole):
    part = lax.psum_scatter(whole.astype(BF16), ALL, scatter_dimension=0, tiled=True)
    return lax.all_gather(part, REST, axis=0, tiled=True)


def on_device(inputs, padding, language, lang_table, latents, in_gain, in_bias, lat_gain, lat_bias, mid_gain, mid_bias,
              w_query, w_key, w_value, w_out, w_up, b_up, w_down, b_down, cotangent):
    length, local_seqs, width = inputs.shape
    local_rows, width_lat = latents.shape
    cols = w_query.shape[1]
    head_dim = width_lat // HEADS
    per_shard = cols // head_dim
    shards = lax.axis_size("heads")
    blocks = lax.axis_size("blk")
    rows = local_rows * blocks
    seqs = local_seqs // shards
    me = lax.axis_index("heads")
    first = me * seqs

    pair_shard = jnp.concatenate([w_key.T, w_value.T], axis=0)
    pair_rows = gather_rows(pair_shard)
    latent_shard = jnp.concatenate([w_out, w_up.T, w_down], axis=0)
    lat_all = gather_rows(latent_shard).reshape(shards, 3, cols, width_lat)
    out_all, up_all, down_all = (lat_all[:, i].reshape(width_lat, width_lat) for i in range(3))

    all_latents = lax.all_gather(latents, "blk", axis=0, tiled=True).astype(F32)
    lat_out, _, _ = norm_keep(all_latents, lat_gain, lat_bias)
    lat_low = lat_out.astype(BF16)
    query_part = dot(lat_low, w_query).astype(BF16)
    queries = lax.all_gather(query_part, "heads", axis=1, tiled=True)
    q = queries.reshape(rows, HEADS, head_dim).transpose(1, 0, 2)

    own = lax.dynamic_slice_in_dim(inputs, first, seqs, 1)
    x_cols = jnp.transpose(own, (1, 2, 0))
    live = jnp.transpose(lax.dynamic_slice_in_dim(padding, first, seqs, 1))
    mask = jnp.where(live > 0, 0.0, MASKED).astype(F32)[:, None, :]
    own_lang = lax.dynamic_slice_in_dim(language, first, seqs, 0)
    onehot = (own_lang[:, None] == jnp.arange(lang_table.shape[0], dtype=jnp.int32)[None, :]).astype(F32)
    emb = jnp.dot(onehot, lang_table.astype(F32), precision=lax.Precision.HIGHEST)[:, :, None]
    gain_col, bias_col = in_gain[:, None], in_bias[:, None]

    pairs, o_cols, lse = forward_call(x_cols, emb, gain_col, bias_col, pair_rows, q, mask, per_shard)

    parts = o_cols.reshape(seqs, width_lat, blocks, local_rows).transpose(2, 0, 3, 1)
    parts = lax.all_to_all(parts, "blk", 0, 0, tiled=True).astype(F32)
    lse_parts = lse.reshape(seqs, HEADS, blocks, local_rows).transpose(2, 0, 3, 1)
    lse_parts = lax.all_to_all(lse_parts, "blk", 0, 0, tiled=True)
    top = jnp.max(lse_parts, axis=0)
    shares = jnp.exp2(lse_parts - top)
    total = jnp.sum(shares, axis=0)
    own_lse = top + jnp.log2(total)
    shares = shares / total
    attended = jnp.sum(parts.reshape(blocks, seqs, local_rows, HEADS, head_dim) * shares[..., None], axis=0)
    att_low = attended.reshape(seqs * local_rows, width_lat).astype(BF16)

    cot = lax.dynamic_slice_in_dim(cotangent, first, seqs, 0).reshape(seqs * local_rows, width_lat)
    lat_f32 = latents.astype(F32)
    middle = (lat_f32[None] + dot(att_low, out_all).reshape(seqs, local_rows, width_lat)).reshape(seqs * local_rows, width_lat)
    mid_out, mid_normed, mid_inverse = norm_keep(middle, mid_gain, mid_bias)
    mid_low = mid_out.astype(BF16)
    b_up_all = lax.all_gather(b_up, "heads", axis=0, tiled=True)
    hidden = dot_nt(mid_low, up_all) + b_up_all
    active, gelu_back = jax.vjp(jax.nn.gelu, hidden)
    active_low = active.astype(BF16)
    own_mixed = (middle + dot(active_low, down_all) + b_down).astype(BF16).reshape(seqs, local_rows, width_lat)
    mixed_latents = lax.all_gather(own_mixed, "heads", axis=0, tiled=True)

    grad_b_down = jnp.sum(cot.astype(F32), axis=0)
    grad_w_down = dot(active_low.T, cot)
    grad_active = dot_nt(cot, down_all)
    grad_hidden = gelu_back(grad_active)[0].astype(BF16)
    grad_b_up = jnp.sum(grad_hidden.astype(F32), axis=0)
    grad_w_up = dot(grad_hidden.T, mid_low)
    grad_mid_norm = dot(grad_hidden, up_all)
    grad_mid_gain = jnp.sum(grad_mid_norm * mid_normed, axis=0)
    grad_mid_bias = jnp.sum(grad_mid_norm, axis=0)
    grad_middle = cot.astype(F32) + norm_back(grad_mid_norm, mid_normed, mid_inverse, mid_gain)
    grad_branch = grad_middle.astype(BF16)
    grad_w_out = dot(att_low.T, grad_branch)
    grad_att = dot_nt(grad_branch, out_all).astype(BF16).reshape(seqs, local_rows, width_lat)
    grad_att_heads = grad_att.reshape(seqs, local_rows, HEADS, head_dim)
    delta = jnp.sum(grad_att_heads.astype(F32) * attended, axis=-1)
    lat_sum = jnp.sum(grad_middle.reshape(seqs, local_rows, width_lat), axis=0)

    all_grad_att = lax.all_gather(grad_att, "blk", axis=1, tiled=True).reshape(seqs, rows, HEADS, head_dim)
    stats = lax.all_gather(jnp.concatenate([own_lse, delta], axis=-1), "blk", axis=1, tiled=True)
    stats = jnp.transpose(stats, (0, 2, 1))[..., None]
    g_cols, dw_pair, dq, dgain, dbias, demb = backward_call(
        x_cols, emb, gain_col, bias_col, pair_rows.T, q, q.transpose(0, 2, 1),
        all_grad_att.transpose(0, 2, 1, 3), all_grad_att.transpose(0, 2, 3, 1),
        stats[:, :HEADS], stats[:, HEADS:], mask, pairs, per_shard)

    send = g_cols.reshape(seqs, shards, width // shards, length).transpose(1, 0, 2, 3)
    got = lax.all_to_all(send, "heads", 0, 0, tiled=True)
    grad_inputs = got.reshape(local_seqs, width // shards, length).transpose(2, 0, 1)

    grad_rows = jnp.stack([grad_w_out, grad_w_up, grad_w_down], axis=0).reshape(3, shards, cols, width_lat)
    lat_total = scatter_rows(grad_rows.transpose(1, 0, 2, 3).reshape(-1, width_lat)).astype(F32)
    pair_total = scatter_rows(dw_pair).astype(F32)

    dq_part = lax.psum_scatter(dq.reshape(width_lat, rows).astype(BF16), "heads", scatter_dimension=0, tiled=True)
    query_low = lax.psum(dq_part, REST)
    grad_w_query = dot(lat_low.T, query_low.T)
    lat_mine = lax.dynamic_slice_in_dim(query_low, lax.axis_index("blk") * local_rows, local_rows, 1)
    grad_lat_part = dot(lat_mine.T, w_query.T)
    grad_lat_norm = lax.psum(grad_lat_part.astype(BF16), "heads").astype(F32)
    lat_sum = lax.psum(lat_sum.astype(BF16), ("heads", "items")).astype(F32)
    _, own_normed, own_inverse = norm_keep(lat_f32, lat_gain, lat_bias)
    grad_latents = lat_sum + norm_back(grad_lat_norm, own_normed, own_inverse, lat_gain)
    lat_small = jnp.concatenate([jnp.sum(grad_lat_norm * own_normed, axis=0), jnp.sum(grad_lat_norm, axis=0)])
    lat_small = lax.psum(lat_small, "blk")

    table = jnp.dot(onehot.T, demb[:, :, 0], precision=lax.Precision.HIGHEST)
    small = jnp.concatenate([table.reshape(-1), dgain[:, 0], dbias[:, 0], grad_mid_gain, grad_mid_bias, grad_b_up, grad_b_down])
    small = lax.psum(small, ALL)
    sizes = [table.size, width, width, width_lat, width_lat, width_lat, width_lat]
    ends = [sum(sizes[:i]) for i in range(len(sizes) + 1)]
    table, dgain, dbias, dmid_gain, dmid_bias, db_up, db_down = (small[ends[i]:ends[i + 1]] for i in range(7))
    share = width // shards
    table = lax.dynamic_slice_in_dim(table.reshape(-1, width), me * share, share, 1)
    return (
        mixed_latents,
        grad_inputs,
        grad_latents,
        table,
        lax.dynamic_slice_in_dim(dgain, me * share, share, 0),
        lax.dynamic_slice_in_dim(dbias, me * share, share, 0),
        lat_small[:width_lat],
        lat_small[width_lat:],
        dmid_gain,
        dmid_bias,
        grad_w_query,
        pair_total[:cols].T,
        pair_total[cols:].T,
        lat_total[:cols],
        lat_total[cols:2 * cols].T,
        lax.dynamic_slice_in_dim(db_up, me * cols, cols, 0),
        lat_total[2 * cols:],
        db_down,
    )


def solution(mesh):
    placed = (
        P("blk", "items", None), P("blk", "items"), P("items"), P(), P("blk", None), P(), P(), P(), P(), P(), P(),
        P(None, "heads"), P(None, "heads"), P(None, "heads"), P("heads", None), P(None, "heads"), P("heads"),
        P("heads", None), P(), P("items", "blk", None),
    )
    out = (
        P("items", "blk", None), P("blk", "items", "heads"), P("blk", None), P(None, "heads"), P("heads"), P("heads"),
        P(), P(), P(), P(), P(None, "heads"), P(None, "heads"), P(None, "heads"), P("heads", None), P(None, "heads"),
        P("heads"), P("heads", None), P(),
    )
    return jax.shard_map(on_device, mesh=mesh, in_specs=placed, out_specs=out, check_vma=False)
```

```python
import functools

import jax
import jax.numpy as jnp
from jax import lax
from jax.experimental import pallas as pl
from jax.experimental.pallas import tpu as pltpu
from jax.sharding import PartitionSpec as P

HEADS = 8
EPS = 1e-05
MASKED = -1e30
LOG2E = 1.4426950408889634
F32 = jnp.float32
BF16 = jnp.bfloat16
NT = (((1,), (1,)), ((), ()))
VMEM_LIMIT = 60 * 1024 * 1024


def dot(a, b):
    return jnp.dot(a, b, preferred_element_type=F32)


def dot_nt(a, b):
    return lax.dot_general(a, b, NT, preferred_element_type=F32)


def norm_keep(values, gain, bias):
    average = jnp.mean(values, axis=-1, keepdims=True)
    centred = values - average
    inverse = lax.rsqrt(jnp.mean(centred * centred, axis=-1, keepdims=True) + EPS)
    normed = centred * inverse
    return (normed * gain + bias, normed, inverse)


def norm_back(grad_norm, normed, inverse, gain):
    scaled = grad_norm * gain
    first = jnp.mean(scaled, axis=-1, keepdims=True)
    second = jnp.mean(scaled * normed, axis=-1, keepdims=True)
    return (scaled - first - normed * second) * inverse


def norm_columns(x, emb):
    shifted = x.astype(F32) + emb
    centred = shifted - jnp.mean(shifted, axis=0, keepdims=True)
    inverse = lax.rsqrt(jnp.mean(centred * centred, axis=0, keepdims=True) + EPS)
    return centred * inverse, inverse


def head_rows(h, per_shard, head_dim):
    key = (h // per_shard) * 2 * per_shard + lax.rem(h, per_shard)
    key_at = pl.multiple_of(key * head_dim, head_dim)
    return pl.ds(key_at, head_dim), pl.ds(pl.multiple_of(key_at + per_shard * head_dim, head_dim), head_dim)


def forward_kernel(per_shard, x_ref, emb_ref, gain_ref, bias_ref, w_ref, q_ref, mask_ref, kv_ref, o_ref, lse_ref, xn_ref, stat_ref):
    heads, rows, head_dim = q_ref.shape
    length = x_ref.shape[1]
    piece = min(256, length)

    def norm_step(i, _):
        at = pl.ds(pl.multiple_of(i * piece, piece), piece)
        normed, _unused = norm_columns(x_ref[:, at], emb_ref[...])
        xn_ref[:, at] = (normed * gain_ref[...] + bias_ref[...]).astype(BF16)
        return 0

    lax.fori_loop(0, length // piece, norm_step, 0)
    block = 512 if w_ref.shape[0] % 512 == 0 else 160

    def pair_step(i, _):
        at = pl.ds(pl.multiple_of(i * block, block), block)
        kv_ref[at] = dot(w_ref[at], xn_ref[...]).astype(BF16)
        return 0

    lax.fori_loop(0, w_ref.shape[0] // block, pair_step, 0)
    factor = LOG2E * head_dim ** (-0.5)
    lane = lax.broadcasted_iota(jnp.int32, (rows, 128), 1)
    stat_ref[...] = jnp.zeros_like(stat_ref)

    def head_step(h, _):
        at_key, at_value = head_rows(h, per_shard, head_dim)
        scores = dot(q_ref[h], kv_ref[at_key]) * factor + mask_ref[...]
        top = jnp.max(scores, axis=1, keepdims=True)
        weights = jnp.exp2(scores - top)
        total = jnp.sum(weights, axis=1, keepdims=True)
        out = dot_nt(kv_ref[at_value], weights.astype(BF16))
        stat_ref[...] = jnp.where(lane == h, top + jnp.log2(total), stat_ref[...])
        inverse = jnp.transpose(jnp.broadcast_to(1.0 / total, (rows, 128)))[:1]
        o_ref[pl.ds(pl.multiple_of(h * head_dim, head_dim), head_dim)] = (out * inverse).astype(BF16)
        return 0

    lax.fori_loop(0, heads, head_step, 0)
    lse_ref[...] = jnp.transpose(stat_ref[...])[:heads]


def forward_call(x_cols, emb, gain, bias, w_rows, q, mask, per_shard):
    seqs, width, length = x_cols.shape
    heads, rows, head_dim = q.shape
    pair_rows = w_rows.shape[0]
    whole = pl.BlockSpec(memory_space=pltpu.VMEM)

    def per_seq(*dims):
        return pl.BlockSpec((None,) + dims, lambda s: (s, 0, 0))

    return pl.pallas_call(
        functools.partial(forward_kernel, per_shard),
        grid=(seqs,),
        in_specs=[per_seq(width, length), per_seq(width, 1), whole, whole, whole, whole, per_seq(1, length)],
        out_specs=[per_seq(pair_rows, length), per_seq(heads * head_dim, rows), per_seq(heads, rows)],
        out_shape=[
            jax.ShapeDtypeStruct((seqs, pair_rows, length), BF16),
            jax.ShapeDtypeStruct((seqs, heads * head_dim, rows), BF16),
            jax.ShapeDtypeStruct((seqs, heads, rows), F32),
        ],
        scratch_shapes=[pltpu.VMEM((width, length), BF16), pltpu.VMEM((rows, 128), F32)],
        compiler_params=pltpu.CompilerParams(vmem_limit_bytes=VMEM_LIMIT),
        name="attend",
    )(x_cols, emb, gain, bias, w_rows, q, mask)


def backward_kernel(per_shard, x_ref, emb_ref, gain_ref, bias_ref, w_ref, q_ref, qt_ref, do_ref, dot_ref, lse_ref, delta_ref, mask_ref, kv_ref,
                    g_ref, dw_ref, dq_ref, dgain_ref, dbias_ref, demb_ref, xn_ref, dkv_ref):
    heads, rows, head_dim = q_ref.shape
    width, length = x_ref.shape
    piece = min(256, length)

    @pl.when(pl.program_id(0) == 0)
    def _():
        dw_ref[...] = jnp.zeros_like(dw_ref)
        dq_ref[...] = jnp.zeros_like(dq_ref)
        dgain_ref[...] = jnp.zeros_like(dgain_ref)
        dbias_ref[...] = jnp.zeros_like(dbias_ref)

    def norm_step(i, _):
        at = pl.ds(pl.multiple_of(i * piece, piece), piece)
        normed, _unused = norm_columns(x_ref[:, at], emb_ref[...])
        xn_ref[:, at] = (normed * gain_ref[...] + bias_ref[...]).astype(BF16)
        return 0

    lax.fori_loop(0, length // piece, norm_step, 0)
    scale = head_dim ** (-0.5)
    factor = LOG2E * scale

    def head_step(h, _):
        at_key, at_value = head_rows(h, per_shard, head_dim)
        keys = kv_ref[at_key]
        weights = jnp.exp2(dot(q_ref[h], keys) * factor + mask_ref[...] - lse_ref[h])
        dkv_ref[at_value] = dot(dot_ref[h], weights.astype(BF16)).astype(BF16)
        grad = dot(do_ref[h], kv_ref[at_value]) - delta_ref[h]
        grad = (weights * grad).astype(BF16)
        dkv_ref[at_key] = (dot(qt_ref[h], grad) * scale).astype(BF16)
        dq_ref[h] += dot_nt(keys, grad) * scale
        return 0

    lax.fori_loop(0, heads, head_step, 0)
    block = 512 if dw_ref.shape[0] % 512 == 0 else 160

    def weight_step(i, _):
        at = pl.ds(pl.multiple_of(i * block, block), block)
        dw_ref[at] += dot_nt(dkv_ref[at], xn_ref[...])
        return 0

    lax.fori_loop(0, dw_ref.shape[0] // block, weight_step, 0)

    def byte_step(i, carry):
        at = pl.ds(pl.multiple_of(i * piece, piece), piece)
        grad = dot(w_ref[...], dkv_ref[:, at])
        normed, inverse = norm_columns(x_ref[:, at], emb_ref[...])
        dbias_ref[...] += jnp.sum(grad, axis=1, keepdims=True)
        dgain_ref[...] += jnp.sum(grad * normed, axis=1, keepdims=True)
        scaled = grad * gain_ref[...]
        first = jnp.mean(scaled, axis=0, keepdims=True)
        second = jnp.mean(scaled * normed, axis=0, keepdims=True)
        shifted = (scaled - first - normed * second) * inverse
        g_ref[:, at] = shifted.astype(BF16)
        return carry + jnp.sum(shifted, axis=1, keepdims=True)

    demb_ref[...] = lax.fori_loop(0, length // piece, byte_step, jnp.zeros((width, 1), F32))


def backward_call(x_cols, emb, gain, bias, w, q, qt, grad_out, grad_out_t, lse, delta, mask, pairs, per_shard):
    seqs, width, length = x_cols.shape
    heads, rows, head_dim = q.shape
    pair_rows = w.shape[1]
    whole = pl.BlockSpec(memory_space=pltpu.VMEM)

    def per_seq(*dims):
        return pl.BlockSpec((None,) + dims, lambda s: (s,) + (0,) * len(dims))

    return pl.pallas_call(
        functools.partial(backward_kernel, per_shard),
        grid=(seqs,),
        in_specs=[
            per_seq(width, length), per_seq(width, 1), whole, whole, whole, whole, whole,
            per_seq(heads, rows, head_dim), per_seq(heads, head_dim, rows),
            per_seq(heads, rows, 1), per_seq(heads, rows, 1), per_seq(1, length), per_seq(pair_rows, length),
        ],
        out_specs=[per_seq(width, length), whole, whole, whole, whole, per_seq(width, 1)],
        out_shape=[
            jax.ShapeDtypeStruct((seqs, width, length), BF16),
            jax.ShapeDtypeStruct((pair_rows, width), F32),
            jax.ShapeDtypeStruct((heads, head_dim, rows), F32),
            jax.ShapeDtypeStruct((width, 1), F32),
            jax.ShapeDtypeStruct((width, 1), F32),
            jax.ShapeDtypeStruct((seqs, width, 1), F32),
        ],
        scratch_shapes=[pltpu.VMEM((width, length), BF16), pltpu.VMEM((pair_rows, length), BF16)],
        compiler_params=pltpu.CompilerParams(vmem_limit_bytes=VMEM_LIMIT),
        name="attend_back",
    )(x_cols, emb, gain, bias, w, q, qt, grad_out, grad_out_t, lse, delta, mask, pairs)


def mesh_at(di=None, db=None, dh=None, core=None):
    items, blk, heads = lax.axis_index("items"), lax.axis_index("blk"), lax.axis_index("heads")
    return (items if di is None else di, blk if db is None else db, heads if dh is None else dh)


def places():
    items, blk, heads = lax.axis_index("items"), lax.axis_index("blk"), lax.axis_index("heads")
    core = lax.rem(items, 2)
    return items, blk, heads, items // 2, core


def send(src, dst, sems, recvs, target):
    copy = pltpu.make_async_remote_copy(
        src_ref=src, dst_ref=dst, send_sem=sems, recv_sem=recvs, device_id=target, device_id_type=pl.DeviceIdType.MESH)
    copy.start()
    return copy


def greet(targets):
    barrier = pltpu.get_barrier_semaphore()
    for target in targets:
        pl.semaphore_signal(barrier, inc=1, device_id=target, device_id_type=pl.DeviceIdType.MESH)
    pl.semaphore_wait(barrier, len(targets))


def first_kernel(x_ref, emb_ref, gain_ref, bias_ref, mask_ref, lat_ref, lgain_ref, lbias_ref, wq_ref, pair_shard, lat_shard, bup_ref,
                 pair_ref, all_ref, kv_ref, att_ref, lse_ref, qt_ref, latn_ref, bup_all,
                 xn_ref, q_ref, o_tmp, o_own, o_send, o_got, stat_ref, stat_send, stat_own, stat_got,
                 pair_ss, pair_rs, lat_ss, lat_rs, q_ss, q_rs, misc_ss, misc_rs, o_ss, o_rs, own_sem):
    items, blk, me, hi, core = places()
    shards = lax.axis_size("heads")
    seqs, width, length = x_ref.shape
    rows = qt_ref.shape[1]
    local_rows = rows // 2
    heads, _, head_dim = q_ref.shape
    cols = heads * head_dim // shards
    per_shard = heads // shards
    sibling = items + 1 - 2 * core
    other = 1 - blk
    to_sib, to_x, to_y = mesh_at(di=sibling), mesh_at(db=other), mesh_at(di=(1 - hi) * 2 + core)
    z_of = [lax.rem(me + d, shards) for d in range(shards)]
    z_back = [lax.rem(me + shards - d, shards) for d in range(shards)]
    greet([to_sib, to_y] + [mesh_at(dh=z_of[d]) for d in range(1, shards)] + [mesh_at(db=other, dh=z_of[d]) for d in range(shards)])

    share = cols // 4
    chip = hi * 2 + blk
    chip_x, chip_y, chip_xy = hi * 2 + other, (1 - hi) * 2 + blk, (1 - hi) * 2 + other

    def region(ref, shard, chip_at, lanes_of):
        half = ref.shape[2] // 2
        return ref.at[:, pl.ds(pl.multiple_of(shard * cols + chip_at * share, 16), share), pl.ds(pl.multiple_of(lanes_of * half, 128), half)]

    def lane_half(ref, shard, lanes_of):
        half = ref.shape[2] // 2
        return ref.at[:, pl.ds(pl.multiple_of(shard * cols, 16), cols), pl.ds(pl.multiple_of(lanes_of * half, 128), half)]

    pending = []
    kinds = {"pair": (pair_shard, pair_ref, pair_ss, pair_rs), "lat": (lat_shard, all_ref, lat_ss, lat_rs)}

    def recv(kind, d, stage, where):
        _, dst, ss, rs = kinds[kind]
        pltpu.make_async_remote_copy(src_ref=where, dst_ref=where, send_sem=ss.at[d, stage], recv_sem=rs.at[d, stage],
                                     device_id=to_sib, device_id_type=pl.DeviceIdType.MESH).wait_recv()

    def out_z(kind, d):
        src, dst, ss, rs = kinds[kind]
        pending.append(send(region(src, 0, chip, core), region(dst, me, chip, core), ss.at[d, 0], rs.at[d, 0], mesh_at(dh=z_back[d])))

    def after_z(kind, d):
        _, dst, ss, rs = kinds[kind]
        mine = region(dst, z_of[d], chip, core)
        recv(kind, d, 0, mine)
        pending.append(send(mine, mine, ss.at[d, 1], rs.at[d, 1], to_x))
        pending.append(send(mine, mine, ss.at[d, 2], rs.at[d, 2], to_y))

    def after_x(kind, d):
        _, dst, ss, rs = kinds[kind]
        got = region(dst, z_of[d], chip_x, core)
        recv(kind, d, 1, got)
        pending.append(send(got, got, ss.at[d, 3], rs.at[d, 3], to_y))

    def after_y(kind, d):
        _, dst, ss, rs = kinds[kind]
        recv(kind, d, 2, region(dst, z_of[d], chip_y, core))
        recv(kind, d, 3, region(dst, z_of[d], chip_xy, core))
        half = lane_half(dst, z_of[d], core)
        pending.append(send(half, half, ss.at[d, 4], rs.at[d, 4], to_sib))

    def after_sib(kind, d):
        _, dst, ss, rs = kinds[kind]
        recv(kind, d, 4, lane_half(dst, z_of[d], 1 - core))

    for d in range(1, shards):
        out_z("pair", d)
    for d in range(1, shards):
        out_z("lat", d)
    own_pair = pltpu.make_async_copy(pair_shard, pair_ref.at[:, pl.ds(pl.multiple_of(me * cols, 16), cols)], own_sem.at[0])
    own_lat = pltpu.make_async_copy(lat_shard, all_ref.at[:, pl.ds(pl.multiple_of(me * cols, 16), cols)], own_sem.at[1])
    own_pair.start()
    own_lat.start()
    my_rows = pl.ds(pl.multiple_of(blk * local_rows, 128), local_rows)
    other_rows = pl.ds(pl.multiple_of(other * local_rows, 128), local_rows)

    lat_out, _, _ = norm_keep(lat_ref[...].astype(F32), lgain_ref[...], lbias_ref[...])
    lat_low = lat_out.astype(BF16)
    latn_ref[my_rows] = lat_low
    my_cols = pl.ds(pl.multiple_of(me * cols, 16), cols)
    qt_ref[my_cols, my_rows] = dot_nt(wq_ref[...], lat_low).astype(BF16)
    bup_all[me] = bup_ref[...]
    my_q = qt_ref.at[my_cols, my_rows]
    for d in range(1, shards):
        pending.append(send(my_q, my_q, q_ss.at[0, d], q_rs.at[0, d], mesh_at(dh=z_back[d])))
    for d in range(shards):
        pending.append(send(my_q, my_q, q_ss.at[1, d], q_rs.at[1, d], mesh_at(db=other, dh=z_back[d])))
    for d in range(1, shards):
        pending.append(send(bup_ref, bup_all.at[me], misc_ss.at[d], misc_rs.at[d], mesh_at(dh=z_back[d])))
    pending.append(send(latn_ref.at[my_rows], latn_ref.at[my_rows], misc_ss.at[0], misc_rs.at[0], to_x))

    def wait_plain(where, ss, rs):
        pltpu.make_async_remote_copy(src_ref=where, dst_ref=where, send_sem=ss, recv_sem=rs,
                                     device_id=to_sib, device_id_type=pl.DeviceIdType.MESH).wait_recv()

    piece = min(256, length)

    def norm_bytes(s):
        def norm_step(i, _):
            at = pl.ds(pl.multiple_of(i * piece, piece), piece)
            normed, _unused = norm_columns(x_ref[s, :, at], emb_ref[s])
            xn_ref[s, :, at] = (normed * gain_ref[...] + bias_ref[...]).astype(BF16)
            return 0
        lax.fori_loop(0, length // piece, norm_step, 0)

    def project(d):
        at = pl.ds(pl.multiple_of(z_of[d] * cols, 16), cols)

        def step(i, _):
            s, part = i // 2, lax.rem(i, 2)
            kv_ref[s, part, at] = dot(pair_ref[part, at], xn_ref[s]).astype(BF16)
            return 0
        lax.fori_loop(0, 2 * seqs, step, 0)

    factor = LOG2E * head_dim ** (-0.5)
    lane = lax.broadcasted_iota(jnp.int32, (rows, 128), 1)
    stat_ref[...] = jnp.zeros_like(stat_ref)

    def turn_queries(d):
        for j in range(per_shard):
            h = z_of[d] * per_shard + j
            q_ref[h] = jnp.transpose(qt_ref[pl.ds(pl.multiple_of(h * head_dim, 16), head_dim)])

    def attend(d, s):
        def head_step(j, _):
            h = z_of[d] * per_shard + j
            at = pl.ds(pl.multiple_of(h * head_dim, 16), head_dim)
            scores = dot(q_ref[h], kv_ref[s, 0, at]) * factor + mask_ref[s]
            top = jnp.max(scores, axis=1, keepdims=True)
            weights = jnp.exp2(scores - top)
            total = jnp.sum(weights, axis=1, keepdims=True)
            out = dot_nt(kv_ref[s, 1, at], weights.astype(BF16))
            stat_ref[s] = jnp.where(lane == h, top + jnp.log2(total), stat_ref[s])
            inverse = jnp.transpose(jnp.broadcast_to(1.0 / total, (rows, 128)))[:1]
            o_tmp[...] = out * inverse
            o_own[s, at] = o_tmp[:, my_rows]
            o_send[s, at] = o_tmp[:, other_rows].astype(BF16)
            return 0
        lax.fori_loop(0, per_shard, head_step, 0)
        part = pl.ds(pl.multiple_of(z_of[d] * cols, 16), cols)
        pending.append(send(o_send.at[s, part], o_got.at[s, part], o_ss.at[d, s], o_rs.at[d, s], to_x))

    norm_bytes(0)
    after_z("pair", 1)
    for s in range(1, seqs):
        norm_bytes(s)
    after_z("pair", 2)
    after_x("pair", 1)
    own_pair.wait()
    project(0)
    after_z("pair", 3)
    after_x("pair", 2)
    after_y("pair", 1)
    for d in range(1, shards):
        there = z_of[d]
        wait_plain(qt_ref.at[pl.ds(pl.multiple_of(there * cols, 16), cols), my_rows], q_ss.at[0, d], q_rs.at[0, d])
    for d in range(shards):
        there = z_of[d]
        wait_plain(qt_ref.at[pl.ds(pl.multiple_of(there * cols, 16), cols), other_rows], q_ss.at[1, d], q_rs.at[1, d])
    turn_queries(0)
    attend(0, 0)
    after_x("pair", 3)
    after_y("pair", 2)
    after_z("lat", 1)
    for s in range(1, seqs):
        attend(0, s)
    after_sib("pair", 1)
    project(1)
    after_y("pair", 3)
    after_x("lat", 1)
    after_z("lat", 2)
    turn_queries(1)
    for s in range(seqs):
        attend(1, s)
    after_x("lat", 2)
    after_y("lat", 1)
    after_z("lat", 3)
    after_sib("pair", 2)
    project(2)
    after_x("lat", 3)
    after_y("lat", 2)
    turn_queries(2)
    for s in range(seqs):
        attend(2, s)
    after_sib("pair", 3)
    project(3)
    turn_queries(3)
    for s in range(seqs):
        attend(3, s)

    for s in range(seqs):
        at = pl.ds(s * heads, heads)
        stats = jnp.transpose(stat_ref[s])[:heads]
        stat_send[...] = stats
        stat_own[at] = stat_send[:, my_rows]
        stat_got[0, at] = stat_send[:, other_rows]
    pending.append(send(stat_got.at[0], stat_got.at[1], o_ss.at[shards, 0], o_rs.at[shards, 0], to_x))
    after_y("lat", 3)
    wait_plain(stat_got.at[1], o_ss.at[shards, 0], o_rs.at[shards, 0])
    own_lse, got_lse = stat_own[...], stat_got[1]
    top = jnp.maximum(own_lse, got_lse)
    own_share, got_share = jnp.exp2(own_lse - top), jnp.exp2(got_lse - top)
    total = own_share + got_share
    lse = top + jnp.log2(total)
    own_share, got_share = own_share / total, got_share / total
    for s in range(seqs):
        lse_ref[s] = lse[s * heads:(s + 1) * heads]
        for d in range(shards):
            part = pl.ds(pl.multiple_of(z_of[d] * cols, 16), cols)
            wait_plain(o_got.at[s, part], o_ss.at[d, s], o_rs.at[d, s])
    for s in range(seqs):
        for h in range(heads):
            at = slice(h * head_dim, (h + 1) * head_dim)
            n = s * heads + h
            att_ref[s, at] = o_own[s, at] * own_share[n:n + 1] + o_got[s, at].astype(F32) * got_share[n:n + 1]
    for d in range(1, shards):
        wait_plain(bup_all.at[z_of[d]], misc_ss.at[d], misc_rs.at[d])
    wait_plain(latn_ref.at[other_rows], misc_ss.at[0], misc_rs.at[0])
    for d in range(1, shards):
        after_sib("lat", d)
    own_lat.wait()
    for copy in pending:
        copy.wait_send()


def first_call(x_cols, emb, gain, bias, mask, latents, lat_gain, lat_bias, wq_rows, pair_shard, lat_shard, b_up, rows):
    seqs, width, length = x_cols.shape
    local_rows, width_lat = latents.shape
    shards = lax.axis_size("heads")
    heads = HEADS
    head_dim = width_lat // heads
    whole = pl.BlockSpec(memory_space=pltpu.VMEM)
    hbm = pl.BlockSpec(memory_space=pl.ANY)
    out = jax.ShapeDtypeStruct
    sem = pltpu.SemaphoreType.DMA
    return pl.pallas_call(
        first_kernel,
        in_specs=[whole] * 9 + [whole, hbm, whole],
        out_specs=[whole, hbm] + [whole] * 6,
        out_shape=[
            out((2, width_lat, width), BF16),
            out((3, width_lat, width_lat), BF16),
            out((seqs, 2, width_lat, length), BF16),
            out((seqs, width_lat, local_rows), F32),
            out((seqs, heads, local_rows), F32),
            out((width_lat, rows), BF16),
            out((rows, width_lat), BF16),
            out((shards,) + b_up.shape, F32),
        ],
        scratch_shapes=[
            pltpu.VMEM((seqs, width, length), BF16),
            pltpu.VMEM((heads, rows, head_dim), BF16),
            pltpu.VMEM((head_dim, rows), F32),
            pltpu.VMEM((seqs, width_lat, local_rows), F32),
            pltpu.VMEM((seqs, width_lat, local_rows), BF16),
            pltpu.VMEM((seqs, width_lat, local_rows), BF16),
            pltpu.VMEM((seqs, rows, 128), F32),
            pltpu.VMEM((heads, rows), F32),
            pltpu.VMEM((seqs * heads, local_rows), F32),
            pltpu.VMEM((2, seqs * heads, local_rows), F32),
            sem((shards, 5)), sem((shards, 5)), sem((shards, 5)), sem((shards, 5)),
            sem((2, shards)), sem((2, shards)), sem((shards,)), sem((shards,)),
            sem((shards + 1, seqs)), sem((shards + 1, seqs)), sem((2,)),
        ],
        compiler_params=pltpu.CompilerParams(vmem_limit_bytes=VMEM_LIMIT, collective_id=1, has_side_effects=True),
        name="first",
    )(x_cols, emb, gain, bias, mask, latents, lat_gain, lat_bias, wq_rows, pair_shard, lat_shard, b_up)


REST = ("items", "blk")
ALL = ("heads", "items", "blk")


def gather_rows(shard):
    count = lax.axis_size("items") * lax.axis_size("blk")
    me = lax.axis_index("items") * lax.axis_size("blk") + lax.axis_index("blk")
    share = shard.shape[0] // count
    part = lax.dynamic_slice_in_dim(shard, me * share, share, 0)
    return lax.all_gather(part, ALL, axis=0, tiled=True)


def scatter_rows(whole):
    part = lax.psum_scatter(whole.astype(BF16), ALL, scatter_dimension=0, tiled=True)
    return lax.all_gather(part, REST, axis=0, tiled=True)


def general_device(inputs, padding, language, lang_table, latents, in_gain, in_bias, lat_gain, lat_bias, mid_gain, mid_bias,
              w_query, w_key, w_value, w_out, w_up, b_up, w_down, b_down, cotangent):
    length, local_seqs, width = inputs.shape
    local_rows, width_lat = latents.shape
    cols = w_query.shape[1]
    head_dim = width_lat // HEADS
    per_shard = cols // head_dim
    shards = lax.axis_size("heads")
    blocks = lax.axis_size("blk")
    rows = local_rows * blocks
    seqs = local_seqs // shards
    me = lax.axis_index("heads")
    first = me * seqs

    pair_shard = jnp.concatenate([w_key.T, w_value.T], axis=0)
    pair_rows = gather_rows(pair_shard)
    latent_shard = jnp.concatenate([w_out, w_up.T, w_down], axis=0)
    lat_all = gather_rows(latent_shard).reshape(shards, 3, cols, width_lat)
    out_all, up_all, down_all = (lat_all[:, i].reshape(width_lat, width_lat) for i in range(3))

    all_latents = lax.all_gather(latents, "blk", axis=0, tiled=True).astype(F32)
    lat_out, _, _ = norm_keep(all_latents, lat_gain, lat_bias)
    lat_low = lat_out.astype(BF16)
    query_part = dot(lat_low, w_query).astype(BF16)
    queries = lax.all_gather(query_part, "heads", axis=1, tiled=True)
    q = queries.reshape(rows, HEADS, head_dim).transpose(1, 0, 2)

    own = lax.dynamic_slice_in_dim(inputs, first, seqs, 1)
    x_cols = jnp.transpose(own, (1, 2, 0))
    live = jnp.transpose(lax.dynamic_slice_in_dim(padding, first, seqs, 1))
    mask = jnp.where(live > 0, 0.0, MASKED).astype(F32)[:, None, :]
    own_lang = lax.dynamic_slice_in_dim(language, first, seqs, 0)
    onehot = (own_lang[:, None] == jnp.arange(lang_table.shape[0], dtype=jnp.int32)[None, :]).astype(F32)
    emb = jnp.dot(onehot, lang_table.astype(F32), precision=lax.Precision.HIGHEST)[:, :, None]
    gain_col, bias_col = in_gain[:, None], in_bias[:, None]

    pairs, o_cols, lse = forward_call(x_cols, emb, gain_col, bias_col, pair_rows, q, mask, per_shard)

    parts = o_cols.reshape(seqs, width_lat, blocks, local_rows).transpose(2, 0, 3, 1)
    parts = lax.all_to_all(parts, "blk", 0, 0, tiled=True).astype(F32)
    lse_parts = lse.reshape(seqs, HEADS, blocks, local_rows).transpose(2, 0, 3, 1)
    lse_parts = lax.all_to_all(lse_parts, "blk", 0, 0, tiled=True)
    top = jnp.max(lse_parts, axis=0)
    shares = jnp.exp2(lse_parts - top)
    total = jnp.sum(shares, axis=0)
    own_lse = top + jnp.log2(total)
    shares = shares / total
    attended = jnp.sum(parts.reshape(blocks, seqs, local_rows, HEADS, head_dim) * shares[..., None], axis=0)
    att_low = attended.reshape(seqs * local_rows, width_lat).astype(BF16)

    cot = lax.dynamic_slice_in_dim(cotangent, first, seqs, 0).reshape(seqs * local_rows, width_lat)
    lat_f32 = latents.astype(F32)
    middle = (lat_f32[None] + dot(att_low, out_all).reshape(seqs, local_rows, width_lat)).reshape(seqs * local_rows, width_lat)
    mid_out, mid_normed, mid_inverse = norm_keep(middle, mid_gain, mid_bias)
    mid_low = mid_out.astype(BF16)
    b_up_all = lax.all_gather(b_up, "heads", axis=0, tiled=True)
    hidden = dot_nt(mid_low, up_all) + b_up_all
    active, gelu_back = jax.vjp(jax.nn.gelu, hidden)
    active_low = active.astype(BF16)
    own_mixed = (middle + dot(active_low, down_all) + b_down).astype(BF16).reshape(seqs, local_rows, width_lat)
    mixed_latents = lax.all_gather(own_mixed, "heads", axis=0, tiled=True)

    grad_b_down = jnp.sum(cot.astype(F32), axis=0)
    grad_w_down = dot(active_low.T, cot)
    grad_active = dot_nt(cot, down_all)
    grad_hidden = gelu_back(grad_active)[0].astype(BF16)
    grad_b_up = jnp.sum(grad_hidden.astype(F32), axis=0)
    grad_w_up = dot(grad_hidden.T, mid_low)
    grad_mid_norm = dot(grad_hidden, up_all)
    grad_mid_gain = jnp.sum(grad_mid_norm * mid_normed, axis=0)
    grad_mid_bias = jnp.sum(grad_mid_norm, axis=0)
    grad_middle = cot.astype(F32) + norm_back(grad_mid_norm, mid_normed, mid_inverse, mid_gain)
    grad_branch = grad_middle.astype(BF16)
    grad_w_out = dot(att_low.T, grad_branch)
    grad_att = dot_nt(grad_branch, out_all).astype(BF16).reshape(seqs, local_rows, width_lat)
    grad_att_heads = grad_att.reshape(seqs, local_rows, HEADS, head_dim)
    delta = jnp.sum(grad_att_heads.astype(F32) * attended, axis=-1)
    lat_sum = jnp.sum(grad_middle.reshape(seqs, local_rows, width_lat), axis=0)

    all_grad_att = lax.all_gather(grad_att, "blk", axis=1, tiled=True).reshape(seqs, rows, HEADS, head_dim)
    stats = lax.all_gather(jnp.concatenate([own_lse, delta], axis=-1), "blk", axis=1, tiled=True)
    stats = jnp.transpose(stats, (0, 2, 1))[..., None]
    g_cols, dw_pair, dq, dgain, dbias, demb = backward_call(
        x_cols, emb, gain_col, bias_col, pair_rows.T, q, q.transpose(0, 2, 1),
        all_grad_att.transpose(0, 2, 1, 3), all_grad_att.transpose(0, 2, 3, 1),
        stats[:, :HEADS], stats[:, HEADS:], mask, pairs, per_shard)

    send = g_cols.reshape(seqs, shards, width // shards, length).transpose(1, 0, 2, 3)
    got = lax.all_to_all(send, "heads", 0, 0, tiled=True)
    grad_inputs = got.reshape(local_seqs, width // shards, length).transpose(2, 0, 1)

    grad_rows = jnp.stack([grad_w_out, grad_w_up, grad_w_down], axis=0).reshape(3, shards, cols, width_lat)
    lat_total = scatter_rows(grad_rows.transpose(1, 0, 2, 3).reshape(-1, width_lat)).astype(F32)
    pair_total = scatter_rows(dw_pair).astype(F32)

    dq_part = lax.psum_scatter(dq.reshape(width_lat, rows).astype(BF16), "heads", scatter_dimension=0, tiled=True)
    query_low = lax.psum(dq_part, REST)
    grad_w_query = dot(lat_low.T, query_low.T)
    lat_mine = lax.dynamic_slice_in_dim(query_low, lax.axis_index("blk") * local_rows, local_rows, 1)
    grad_lat_part = dot(lat_mine.T, w_query.T)
    grad_lat_norm = lax.psum(grad_lat_part.astype(BF16), "heads").astype(F32)
    lat_sum = lax.psum(lat_sum.astype(BF16), ("heads", "items")).astype(F32)
    _, own_normed, own_inverse = norm_keep(lat_f32, lat_gain, lat_bias)
    grad_latents = lat_sum + norm_back(grad_lat_norm, own_normed, own_inverse, lat_gain)
    lat_small = jnp.concatenate([jnp.sum(grad_lat_norm * own_normed, axis=0), jnp.sum(grad_lat_norm, axis=0)])
    lat_small = lax.psum(lat_small, "blk")

    table = jnp.dot(onehot.T, demb[:, :, 0], precision=lax.Precision.HIGHEST)
    small = jnp.concatenate([table.reshape(-1), dgain[:, 0], dbias[:, 0], grad_mid_gain, grad_mid_bias, grad_b_up, grad_b_down])
    small = lax.psum(small, ALL)
    sizes = [table.size, width, width, width_lat, width_lat, width_lat, width_lat]
    ends = [sum(sizes[:i]) for i in range(len(sizes) + 1)]
    table, dgain, dbias, dmid_gain, dmid_bias, db_up, db_down = (small[ends[i]:ends[i + 1]] for i in range(7))
    share = width // shards
    table = lax.dynamic_slice_in_dim(table.reshape(-1, width), me * share, share, 1)
    return (
        mixed_latents,
        grad_inputs,
        grad_latents,
        table,
        lax.dynamic_slice_in_dim(dgain, me * share, share, 0),
        lax.dynamic_slice_in_dim(dbias, me * share, share, 0),
        lat_small[:width_lat],
        lat_small[width_lat:],
        dmid_gain,
        dmid_bias,
        grad_w_query,
        pair_total[:cols].T,
        pair_total[cols:].T,
        lat_total[:cols],
        lat_total[cols:2 * cols].T,
        lax.dynamic_slice_in_dim(db_up, me * cols, cols, 0),
        lat_total[2 * cols:],
        db_down,
    )


def fast_device(inputs, padding, language, lang_table, latents, in_gain, in_bias, lat_gain, lat_bias, mid_gain, mid_bias,
              w_query, w_key, w_value, w_out, w_up, b_up, w_down, b_down, cotangent):
    length, local_seqs, width = inputs.shape
    local_rows, width_lat = latents.shape
    cols = w_query.shape[1]
    head_dim = width_lat // HEADS
    per_shard = cols // head_dim
    shards = lax.axis_size("heads")
    blocks = lax.axis_size("blk")
    rows = local_rows * blocks
    seqs = local_seqs // shards
    me = lax.axis_index("heads")
    first = me * seqs

    own = lax.dynamic_slice_in_dim(inputs, first, seqs, 1)
    x_cols = jnp.transpose(own, (1, 2, 0))
    live = jnp.transpose(lax.dynamic_slice_in_dim(padding, first, seqs, 1))
    mask = jnp.where(live > 0, 0.0, MASKED).astype(F32)[:, None, :]
    own_lang = lax.dynamic_slice_in_dim(language, first, seqs, 0)
    onehot = (own_lang[:, None] == jnp.arange(lang_table.shape[0], dtype=jnp.int32)[None, :]).astype(F32)
    emb = jnp.dot(onehot, lang_table.astype(F32), precision=lax.Precision.HIGHEST)[:, :, None]
    gain_col, bias_col = in_gain[:, None], in_bias[:, None]

    b_up_tile = jnp.pad(b_up[None, :], ((0, 7), (0, -cols % 128)))
    pair_all, lat_all, pairs, att_cols, lse_cols, queries_t, lat_low, b_up_tiles = first_call(
        x_cols, emb, gain_col, bias_col, mask, latents, lat_gain[None], lat_bias[None], w_query.T,
        jnp.stack([w_key.T, w_value.T]), jnp.stack([w_out, w_up.T, w_down]), b_up_tile, rows)
    out_all, up_all, down_all = lat_all[0], lat_all[1], lat_all[2]
    b_up_all = b_up_tiles[:, 0, :cols].reshape(-1)
    pair_rows = jnp.transpose(pair_all.reshape(2, shards, cols, width), (1, 0, 2, 3)).reshape(-1, width)
    pairs = jnp.transpose(pairs.reshape(seqs, 2, shards, cols, length), (0, 2, 1, 3, 4)).reshape(seqs, -1, length)
    qt = queries_t.reshape(HEADS, head_dim, rows)
    q = qt.transpose(0, 2, 1)
    attended = jnp.transpose(att_cols, (0, 2, 1)).reshape(seqs, local_rows, HEADS, head_dim)
    own_lse = jnp.transpose(lse_cols, (0, 2, 1))
    att_low = attended.reshape(seqs * local_rows, width_lat).astype(BF16)

    cot = lax.dynamic_slice_in_dim(cotangent, first, seqs, 0).reshape(seqs * local_rows, width_lat)
    lat_f32 = latents.astype(F32)
    middle = (lat_f32[None] + dot(att_low, out_all).reshape(seqs, local_rows, width_lat)).reshape(seqs * local_rows, width_lat)
    mid_out, mid_normed, mid_inverse = norm_keep(middle, mid_gain, mid_bias)
    mid_low = mid_out.astype(BF16)
    hidden = dot_nt(mid_low, up_all) + b_up_all
    active, gelu_back = jax.vjp(jax.nn.gelu, hidden)
    active_low = active.astype(BF16)
    own_mixed = (middle + dot(active_low, down_all) + b_down).astype(BF16).reshape(seqs, local_rows, width_lat)
    mixed_latents = lax.all_gather(own_mixed, "heads", axis=0, tiled=True)

    grad_b_down = jnp.sum(cot.astype(F32), axis=0)
    grad_w_down = dot(active_low.T, cot)
    grad_active = dot_nt(cot, down_all)
    grad_hidden = gelu_back(grad_active)[0].astype(BF16)
    grad_b_up = jnp.sum(grad_hidden.astype(F32), axis=0)
    grad_w_up = dot(grad_hidden.T, mid_low)
    grad_mid_norm = dot(grad_hidden, up_all)
    grad_mid_gain = jnp.sum(grad_mid_norm * mid_normed, axis=0)
    grad_mid_bias = jnp.sum(grad_mid_norm, axis=0)
    grad_middle = cot.astype(F32) + norm_back(grad_mid_norm, mid_normed, mid_inverse, mid_gain)
    grad_branch = grad_middle.astype(BF16)
    grad_w_out = dot(att_low.T, grad_branch)
    grad_att = dot_nt(grad_branch, out_all).astype(BF16).reshape(seqs, local_rows, width_lat)
    grad_att_heads = grad_att.reshape(seqs, local_rows, HEADS, head_dim)
    delta = jnp.sum(grad_att_heads.astype(F32) * attended, axis=-1)
    lat_sum = jnp.sum(grad_middle.reshape(seqs, local_rows, width_lat), axis=0)

    all_grad_att = lax.all_gather(grad_att, "blk", axis=1, tiled=True).reshape(seqs, rows, HEADS, head_dim)
    stats = lax.all_gather(jnp.concatenate([own_lse, delta], axis=-1), "blk", axis=1, tiled=True)
    stats = jnp.transpose(stats, (0, 2, 1))[..., None]
    g_cols, dw_pair, dq, dgain, dbias, demb = backward_call(
        x_cols, emb, gain_col, bias_col, pair_rows.T, q, qt,
        all_grad_att.transpose(0, 2, 1, 3), all_grad_att.transpose(0, 2, 3, 1),
        stats[:, :HEADS], stats[:, HEADS:], mask, pairs, per_shard)

    send = g_cols.reshape(seqs, shards, width // shards, length).transpose(1, 0, 2, 3)
    got = lax.all_to_all(send, "heads", 0, 0, tiled=True)
    grad_inputs = got.reshape(local_seqs, width // shards, length).transpose(2, 0, 1)

    grad_rows = jnp.stack([grad_w_out, grad_w_up, grad_w_down], axis=0).reshape(3, shards, cols, width_lat)
    lat_total = scatter_rows(grad_rows.transpose(1, 0, 2, 3).reshape(-1, width_lat)).astype(F32)
    pair_total = scatter_rows(dw_pair).astype(F32)

    dq_part = lax.psum_scatter(dq.reshape(width_lat, rows).astype(BF16), "heads", scatter_dimension=0, tiled=True)
    query_low = lax.psum(dq_part, REST)
    grad_w_query = dot(lat_low.T, query_low.T)
    lat_mine = lax.dynamic_slice_in_dim(query_low, lax.axis_index("blk") * local_rows, local_rows, 1)
    grad_lat_part = dot(lat_mine.T, w_query.T)
    grad_lat_norm = lax.psum(grad_lat_part.astype(BF16), "heads").astype(F32)
    lat_sum = lax.psum(lat_sum.astype(BF16), ("heads", "items")).astype(F32)
    _, own_normed, own_inverse = norm_keep(lat_f32, lat_gain, lat_bias)
    grad_latents = lat_sum + norm_back(grad_lat_norm, own_normed, own_inverse, lat_gain)
    lat_small = jnp.concatenate([jnp.sum(grad_lat_norm * own_normed, axis=0), jnp.sum(grad_lat_norm, axis=0)])
    lat_small = lax.psum(lat_small, "blk")

    table = jnp.dot(onehot.T, demb[:, :, 0], precision=lax.Precision.HIGHEST)
    small = jnp.concatenate([table.reshape(-1), dgain[:, 0], dbias[:, 0], grad_mid_gain, grad_mid_bias, grad_b_up, grad_b_down])
    small = lax.psum(small, ALL)
    sizes = [table.size, width, width, width_lat, width_lat, width_lat, width_lat]
    ends = [sum(sizes[:i]) for i in range(len(sizes) + 1)]
    table, dgain, dbias, dmid_gain, dmid_bias, db_up, db_down = (small[ends[i]:ends[i + 1]] for i in range(7))
    share = width // shards
    table = lax.dynamic_slice_in_dim(table.reshape(-1, width), me * share, share, 1)
    return (
        mixed_latents,
        grad_inputs,
        grad_latents,
        table,
        lax.dynamic_slice_in_dim(dgain, me * share, share, 0),
        lax.dynamic_slice_in_dim(dbias, me * share, share, 0),
        lat_small[:width_lat],
        lat_small[width_lat:],
        dmid_gain,
        dmid_bias,
        grad_w_query,
        pair_total[:cols].T,
        pair_total[cols:].T,
        lat_total[:cols],
        lat_total[cols:2 * cols].T,
        lax.dynamic_slice_in_dim(db_up, me * cols, cols, 0),
        lat_total[2 * cols:],
        db_down,
    )


def solution(mesh):
    placed = (
        P("blk", "items", None), P("blk", "items"), P("items"), P(), P("blk", None), P(), P(), P(), P(), P(), P(),
        P(None, "heads"), P(None, "heads"), P(None, "heads"), P("heads", None), P(None, "heads"), P("heads"),
        P("heads", None), P(), P("items", "blk", None),
    )
    out = (
        P("items", "blk", None), P("blk", "items", "heads"), P("blk", None), P(None, "heads"), P("heads"), P("heads"),
        P(), P(), P(), P(), P(None, "heads"), P(None, "heads"), P(None, "heads"), P("heads", None), P(None, "heads"),
        P("heads"), P("heads", None), P(),
    )
    fits = mesh.shape["blk"] == 2 and mesh.shape["items"] == 4 and mesh.shape["heads"] == 4
    return jax.shard_map(fast_device if fits else general_device, mesh=mesh, in_specs=placed, out_specs=out, check_vma=False)
```

```python
import functools

import jax
import jax.numpy as jnp
from jax import lax
from jax.experimental import pallas as pl
from jax.experimental.pallas import tpu as pltpu
from jax.sharding import PartitionSpec as P

HEADS = 8
EPS = 1e-05
MASKED = -1e30
LOG2E = 1.4426950408889634
F32 = jnp.float32
BF16 = jnp.bfloat16
NT = (((1,), (1,)), ((), ()))
VMEM_LIMIT = 60 * 1024 * 1024


def dot(a, b):
    return jnp.dot(a, b, preferred_element_type=F32)


def dot_nt(a, b):
    return lax.dot_general(a, b, NT, preferred_element_type=F32)


def norm_keep(values, gain, bias):
    average = jnp.mean(values, axis=-1, keepdims=True)
    centred = values - average
    inverse = lax.rsqrt(jnp.mean(centred * centred, axis=-1, keepdims=True) + EPS)
    normed = centred * inverse
    return (normed * gain + bias, normed, inverse)


def norm_back(grad_norm, normed, inverse, gain):
    scaled = grad_norm * gain
    first = jnp.mean(scaled, axis=-1, keepdims=True)
    second = jnp.mean(scaled * normed, axis=-1, keepdims=True)
    return (scaled - first - normed * second) * inverse


def norm_columns(x, emb):
    shifted = x.astype(F32) + emb
    centred = shifted - jnp.mean(shifted, axis=0, keepdims=True)
    inverse = lax.rsqrt(jnp.mean(centred * centred, axis=0, keepdims=True) + EPS)
    return centred * inverse, inverse


def head_rows(h, per_shard, head_dim):
    key = (h // per_shard) * 2 * per_shard + lax.rem(h, per_shard)
    key_at = pl.multiple_of(key * head_dim, head_dim)
    return pl.ds(key_at, head_dim), pl.ds(pl.multiple_of(key_at + per_shard * head_dim, head_dim), head_dim)


def forward_kernel(per_shard, x_ref, emb_ref, gain_ref, bias_ref, w_ref, q_ref, mask_ref, kv_ref, o_ref, lse_ref, xn_ref, stat_ref):
    heads, rows, head_dim = q_ref.shape
    length = x_ref.shape[1]
    piece = min(256, length)

    def norm_step(i, _):
        at = pl.ds(pl.multiple_of(i * piece, piece), piece)
        normed, _unused = norm_columns(x_ref[:, at], emb_ref[...])
        xn_ref[:, at] = (normed * gain_ref[...] + bias_ref[...]).astype(BF16)
        return 0

    lax.fori_loop(0, length // piece, norm_step, 0)
    block = 512 if w_ref.shape[0] % 512 == 0 else 160

    def pair_step(i, _):
        at = pl.ds(pl.multiple_of(i * block, block), block)
        kv_ref[at] = dot(w_ref[at], xn_ref[...]).astype(BF16)
        return 0

    lax.fori_loop(0, w_ref.shape[0] // block, pair_step, 0)
    factor = LOG2E * head_dim ** (-0.5)
    lane = lax.broadcasted_iota(jnp.int32, (rows, 128), 1)
    stat_ref[...] = jnp.zeros_like(stat_ref)

    def head_step(h, _):
        at_key, at_value = head_rows(h, per_shard, head_dim)
        scores = dot(q_ref[h], kv_ref[at_key]) * factor + mask_ref[...]
        top = jnp.max(scores, axis=1, keepdims=True)
        weights = jnp.exp2(scores - top)
        total = jnp.sum(weights, axis=1, keepdims=True)
        out = dot_nt(kv_ref[at_value], weights.astype(BF16))
        stat_ref[...] = jnp.where(lane == h, top + jnp.log2(total), stat_ref[...])
        inverse = jnp.transpose(jnp.broadcast_to(1.0 / total, (rows, 128)))[:1]
        o_ref[pl.ds(pl.multiple_of(h * head_dim, head_dim), head_dim)] = (out * inverse).astype(BF16)
        return 0

    lax.fori_loop(0, heads, head_step, 0)
    lse_ref[...] = jnp.transpose(stat_ref[...])[:heads]


def forward_call(x_cols, emb, gain, bias, w_rows, q, mask, per_shard):
    seqs, width, length = x_cols.shape
    heads, rows, head_dim = q.shape
    pair_rows = w_rows.shape[0]
    whole = pl.BlockSpec(memory_space=pltpu.VMEM)

    def per_seq(*dims):
        return pl.BlockSpec((None,) + dims, lambda s: (s, 0, 0))

    return pl.pallas_call(
        functools.partial(forward_kernel, per_shard),
        grid=(seqs,),
        in_specs=[per_seq(width, length), per_seq(width, 1), whole, whole, whole, whole, per_seq(1, length)],
        out_specs=[per_seq(pair_rows, length), per_seq(heads * head_dim, rows), per_seq(heads, rows)],
        out_shape=[
            jax.ShapeDtypeStruct((seqs, pair_rows, length), BF16),
            jax.ShapeDtypeStruct((seqs, heads * head_dim, rows), BF16),
            jax.ShapeDtypeStruct((seqs, heads, rows), F32),
        ],
        scratch_shapes=[pltpu.VMEM((width, length), BF16), pltpu.VMEM((rows, 128), F32)],
        compiler_params=pltpu.CompilerParams(vmem_limit_bytes=VMEM_LIMIT),
        name="attend",
    )(x_cols, emb, gain, bias, w_rows, q, mask)


def backward_kernel(per_shard, x_ref, emb_ref, gain_ref, bias_ref, w_ref, q_ref, qt_ref, do_ref, dot_ref, lse_ref, delta_ref, mask_ref, kv_ref,
                    g_ref, dw_ref, dq_ref, dgain_ref, dbias_ref, demb_ref, xn_ref, dkv_ref):
    heads, rows, head_dim = q_ref.shape
    width, length = x_ref.shape
    piece = min(256, length)

    @pl.when(pl.program_id(0) == 0)
    def _():
        dw_ref[...] = jnp.zeros_like(dw_ref)
        dq_ref[...] = jnp.zeros_like(dq_ref)
        dgain_ref[...] = jnp.zeros_like(dgain_ref)
        dbias_ref[...] = jnp.zeros_like(dbias_ref)

    def norm_step(i, _):
        at = pl.ds(pl.multiple_of(i * piece, piece), piece)
        normed, _unused = norm_columns(x_ref[:, at], emb_ref[...])
        xn_ref[:, at] = (normed * gain_ref[...] + bias_ref[...]).astype(BF16)
        return 0

    lax.fori_loop(0, length // piece, norm_step, 0)
    scale = head_dim ** (-0.5)
    factor = LOG2E * scale

    def head_step(h, _):
        at_key, at_value = head_rows(h, per_shard, head_dim)
        keys = kv_ref[at_key]
        weights = jnp.exp2(dot(q_ref[h], keys) * factor + mask_ref[...] - lse_ref[h])
        dkv_ref[at_value] = dot(dot_ref[h], weights.astype(BF16)).astype(BF16)
        grad = dot(do_ref[h], kv_ref[at_value]) - delta_ref[h]
        grad = (weights * grad).astype(BF16)
        dkv_ref[at_key] = (dot(qt_ref[h], grad) * scale).astype(BF16)
        dq_ref[h] += dot_nt(keys, grad) * scale
        return 0

    lax.fori_loop(0, heads, head_step, 0)
    block = 512 if dw_ref.shape[0] % 512 == 0 else 160

    def weight_step(i, _):
        at = pl.ds(pl.multiple_of(i * block, block), block)
        dw_ref[at] += dot_nt(dkv_ref[at], xn_ref[...])
        return 0

    lax.fori_loop(0, dw_ref.shape[0] // block, weight_step, 0)

    def byte_step(i, carry):
        at = pl.ds(pl.multiple_of(i * piece, piece), piece)
        grad = dot(w_ref[...], dkv_ref[:, at])
        normed, inverse = norm_columns(x_ref[:, at], emb_ref[...])
        dbias_ref[...] += jnp.sum(grad, axis=1, keepdims=True)
        dgain_ref[...] += jnp.sum(grad * normed, axis=1, keepdims=True)
        scaled = grad * gain_ref[...]
        first = jnp.mean(scaled, axis=0, keepdims=True)
        second = jnp.mean(scaled * normed, axis=0, keepdims=True)
        shifted = (scaled - first - normed * second) * inverse
        g_ref[:, at] = shifted.astype(BF16)
        return carry + jnp.sum(shifted, axis=1, keepdims=True)

    demb_ref[...] = lax.fori_loop(0, length // piece, byte_step, jnp.zeros((width, 1), F32))


def backward_call(x_cols, emb, gain, bias, w, q, qt, grad_out, grad_out_t, lse, delta, mask, pairs, per_shard):
    seqs, width, length = x_cols.shape
    heads, rows, head_dim = q.shape
    pair_rows = w.shape[1]
    whole = pl.BlockSpec(memory_space=pltpu.VMEM)

    def per_seq(*dims):
        return pl.BlockSpec((None,) + dims, lambda s: (s,) + (0,) * len(dims))

    return pl.pallas_call(
        functools.partial(backward_kernel, per_shard),
        grid=(seqs,),
        in_specs=[
            per_seq(width, length), per_seq(width, 1), whole, whole, whole, whole, whole,
            per_seq(heads, rows, head_dim), per_seq(heads, head_dim, rows),
            per_seq(heads, rows, 1), per_seq(heads, rows, 1), per_seq(1, length), per_seq(pair_rows, length),
        ],
        out_specs=[per_seq(width, length), whole, whole, whole, whole, per_seq(width, 1)],
        out_shape=[
            jax.ShapeDtypeStruct((seqs, width, length), BF16),
            jax.ShapeDtypeStruct((pair_rows, width), F32),
            jax.ShapeDtypeStruct((heads, head_dim, rows), F32),
            jax.ShapeDtypeStruct((width, 1), F32),
            jax.ShapeDtypeStruct((width, 1), F32),
            jax.ShapeDtypeStruct((seqs, width, 1), F32),
        ],
        scratch_shapes=[pltpu.VMEM((width, length), BF16), pltpu.VMEM((pair_rows, length), BF16)],
        compiler_params=pltpu.CompilerParams(vmem_limit_bytes=VMEM_LIMIT),
        name="attend_back",
    )(x_cols, emb, gain, bias, w, q, qt, grad_out, grad_out_t, lse, delta, mask, pairs)


def mesh_at(di=None, db=None, dh=None, core=None):
    items, blk, heads = lax.axis_index("items"), lax.axis_index("blk"), lax.axis_index("heads")
    return (items if di is None else di, blk if db is None else db, heads if dh is None else dh)


def places():
    items, blk, heads = lax.axis_index("items"), lax.axis_index("blk"), lax.axis_index("heads")
    core = lax.rem(items, 2)
    return items, blk, heads, items // 2, core


def send(src, dst, sems, recvs, target):
    copy = pltpu.make_async_remote_copy(
        src_ref=src, dst_ref=dst, send_sem=sems, recv_sem=recvs, device_id=target, device_id_type=pl.DeviceIdType.MESH)
    copy.start()
    return copy


def greet(targets):
    barrier = pltpu.get_barrier_semaphore()
    for target in targets:
        pl.semaphore_signal(barrier, inc=1, device_id=target, device_id_type=pl.DeviceIdType.MESH)
    pl.semaphore_wait(barrier, len(targets))


def first_kernel(x_ref, rows_ref, mask_ref, lat_ref, lgain_ref, lbias_ref, wq_ref, pair_shard, lat_shard, bup_ref,
                 wcols_ref, all_ref, kv_out, xn_out, att_ref, lse_ref, qt_ref, latn_ref, bup_all,
                 xn_ref, pair_ref, kv_ref, cols_ref, q_ref, o_tmp, o_own, o_send, o_got, stat_ref, stat_send, stat_own, stat_got,
                 pair_ss, pair_rs, lat_ss, lat_rs, q_ss, q_rs, misc_ss, misc_rs, o_ss, o_rs, own_sem, xn_sem, kv_sem):
    items, blk, me, hi, core = places()
    shards = lax.axis_size("heads")
    seqs, width, length = x_ref.shape
    rows = qt_ref.shape[3]
    local_rows = rows // 2
    heads, _, head_dim = q_ref.shape
    cols = heads * head_dim // shards
    per_shard = heads // shards
    sibling = items + 1 - 2 * core
    other = 1 - blk
    to_sib, to_x, to_y = mesh_at(di=sibling), mesh_at(db=other), mesh_at(di=(1 - hi) * 2 + core)
    z_of = [lax.rem(me + d, shards) for d in range(shards)]
    z_back = [lax.rem(me + shards - d, shards) for d in range(shards)]
    greet([to_sib, to_x, to_y] + [mesh_at(dh=z_of[d]) for d in range(1, shards)])

    share = cols // 4
    chip = hi * 2 + blk
    chip_x, chip_y, chip_xy = hi * 2 + other, (1 - hi) * 2 + blk, (1 - hi) * 2 + other

    def region(ref, shard, chip_at, lanes_of):
        half = ref.shape[2] // 2
        return ref.at[:, pl.ds(pl.multiple_of(shard * cols + chip_at * share, 16), share), pl.ds(pl.multiple_of(lanes_of * half, 128), half)]

    def lane_half(ref, shard, lanes_of):
        half = ref.shape[2] // 2
        return ref.at[:, pl.ds(pl.multiple_of(shard * cols, 16), cols), pl.ds(pl.multiple_of(lanes_of * half, 128), half)]

    pending = []
    local = []
    kinds = {"pair": (pair_shard, pair_ref, pair_ss, pair_rs), "lat": (lat_shard, all_ref, lat_ss, lat_rs)}

    def recv(kind, d, stage, where):
        _, dst, ss, rs = kinds[kind]
        pltpu.make_async_remote_copy(src_ref=where, dst_ref=where, send_sem=ss.at[d, stage], recv_sem=rs.at[d, stage],
                                     device_id=to_sib, device_id_type=pl.DeviceIdType.MESH).wait_recv()

    def out_z(kind, d):
        src, dst, ss, rs = kinds[kind]
        pending.append(send(region(src, 0, chip, core), region(dst, me, chip, core), ss.at[d, 0], rs.at[d, 0], mesh_at(dh=z_back[d])))

    def after_z(kind, d):
        _, dst, ss, rs = kinds[kind]
        mine = region(dst, z_of[d], chip, core)
        recv(kind, d, 0, mine)
        pending.append(send(mine, mine, ss.at[d, 1], rs.at[d, 1], to_x))
        pending.append(send(mine, mine, ss.at[d, 2], rs.at[d, 2], to_y))

    def after_x(kind, d):
        _, dst, ss, rs = kinds[kind]
        got = region(dst, z_of[d], chip_x, core)
        recv(kind, d, 1, got)
        pending.append(send(got, got, ss.at[d, 3], rs.at[d, 3], to_y))

    def after_y(kind, d):
        _, dst, ss, rs = kinds[kind]
        recv(kind, d, 2, region(dst, z_of[d], chip_y, core))
        recv(kind, d, 3, region(dst, z_of[d], chip_xy, core))
        half = lane_half(dst, z_of[d], core)
        pending.append(send(half, half, ss.at[d, 4], rs.at[d, 4], to_sib))

    def after_sib(kind, d):
        _, dst, ss, rs = kinds[kind]
        recv(kind, d, 4, lane_half(dst, z_of[d], 1 - core))

    for d in range(1, shards):
        out_z("pair", d)
    own_pair = pltpu.make_async_copy(pair_shard, pair_ref.at[:, pl.ds(pl.multiple_of(me * cols, 16), cols)], own_sem.at[0])
    own_lat = pltpu.make_async_copy(lat_shard, all_ref.at[:, pl.ds(pl.multiple_of(me * cols, 16), cols)], own_sem.at[1])
    own_pair.start()
    own_lat.start()
    my_rows = pl.ds(pl.multiple_of(blk * local_rows, 128), local_rows)
    other_rows = pl.ds(pl.multiple_of(other * local_rows, 128), local_rows)

    lat_out, _, _ = norm_keep(lat_ref[...].astype(F32), lgain_ref[...], lbias_ref[...])
    lat_low = lat_out.astype(BF16)
    latn_ref[...] = lat_low
    at_head = pl.ds(pl.multiple_of(core * head_dim, 16), head_dim)
    qt_ref[core, me, :, my_rows] = dot_nt(wq_ref[at_head], lat_low).astype(BF16)
    bup_all[me] = bup_ref[...]
    for d in range(1, shards):
        my_q = qt_ref.at[core, me, :, my_rows]
        pending.append(send(my_q, my_q, q_ss.at[0, d], q_rs.at[0, d], mesh_at(dh=z_back[d])))
    for d in range(1, shards):
        pending.append(send(bup_ref, bup_all.at[me], misc_ss.at[d], misc_rs.at[d], mesh_at(dh=z_back[d])))
    cols_ref[...] = jnp.transpose(rows_ref[...])

    def queries_z():
        for d in range(1, shards):
            wait_plain(qt_ref.at[core, z_of[d], :, my_rows], q_ss.at[0, d], q_rs.at[0, d])
        part = qt_ref.at[core, :, :, my_rows]
        pending.append(send(part, part, q_ss.at[1, 0], q_rs.at[1, 0], to_x))

    def queries_x():
        wait_plain(qt_ref.at[core, :, :, other_rows], q_ss.at[1, 0], q_rs.at[1, 0])
        pending.append(send(qt_ref.at[core], qt_ref.at[core], q_ss.at[1, 1], q_rs.at[1, 1], to_sib))

    def queries_sib():
        wait_plain(qt_ref.at[1 - core], q_ss.at[1, 1], q_rs.at[1, 1])

    def wait_plain(where, ss, rs):
        pltpu.make_async_remote_copy(src_ref=where, dst_ref=where, send_sem=ss, recv_sem=rs,
                                     device_id=to_sib, device_id_type=pl.DeviceIdType.MESH).wait_recv()

    piece = min(256, length)

    def norm_bytes(s):
        def norm_step(i, _):
            at = pl.ds(pl.multiple_of(i * piece, piece), piece)
            normed, _unused = norm_columns(x_ref[s, :, at], cols_ref[:, 2 + s:3 + s])
            xn_ref[s, :, at] = (normed * cols_ref[:, 0:1] + cols_ref[:, 1:2]).astype(BF16)
            return 0
        lax.fori_loop(0, length // piece, norm_step, 0)
        copy = pltpu.make_async_copy(xn_ref.at[s], xn_out.at[s], xn_sem.at[s])
        copy.start()
        local.append(copy)

    def project(d):
        at = pl.ds(pl.multiple_of(z_of[d] * cols, 16), cols)

        def step(i, _):
            s, part = i // 2, lax.rem(i, 2)
            kv_ref[s, part, at] = dot(pair_ref[part, at], xn_ref[s]).astype(BF16)
            return 0
        lax.fori_loop(0, 2 * seqs, step, 0)
        copy = pltpu.make_async_copy(kv_ref.at[:, :, at], kv_out.at[:, :, at], kv_sem.at[d])
        copy.start()
        local.append(copy)

    factor = LOG2E * head_dim ** (-0.5)
    lane = lax.broadcasted_iota(jnp.int32, (rows, 128), 1)
    stat_ref[...] = jnp.zeros_like(stat_ref)

    def turn_queries(d):
        for j in range(per_shard):
            h = z_of[d] * per_shard + j
            q_ref[h] = jnp.transpose(qt_ref[j, z_of[d]])

    def attend(d, s):
        def head_step(j, _):
            h = z_of[d] * per_shard + j
            at = pl.ds(pl.multiple_of(h * head_dim, 16), head_dim)
            scores = dot(q_ref[h], kv_ref[s, 0, at]) * factor + mask_ref[s]
            top = jnp.max(scores, axis=1, keepdims=True)
            weights = jnp.exp2(scores - top)
            total = jnp.sum(weights, axis=1, keepdims=True)
            out = dot_nt(kv_ref[s, 1, at], weights.astype(BF16))
            stat_ref[s] = jnp.where(lane == h, top + jnp.log2(total), stat_ref[s])
            inverse = jnp.transpose(jnp.broadcast_to(1.0 / total, (rows, 128)))[:1]
            o_tmp[...] = out * inverse
            o_own[s, at] = o_tmp[:, my_rows]
            o_send[s, at] = o_tmp[:, other_rows].astype(BF16)
            return 0
        lax.fori_loop(0, per_shard, head_step, 0)
        part = pl.ds(pl.multiple_of(z_of[d] * cols, 16), cols)
        pending.append(send(o_send.at[s, part], o_got.at[s, part], o_ss.at[d, s], o_rs.at[d, s], to_x))

    norm_bytes(0)
    after_z("pair", 1)
    queries_z()
    for s in range(1, seqs):
        norm_bytes(s)
    after_z("pair", 2)
    after_x("pair", 1)
    after_z("pair", 3)
    for d in range(1, shards):
        out_z("lat", d)
    own_pair.wait()
    project(0)
    queries_x()
    after_x("pair", 2)
    after_y("pair", 1)
    after_x("pair", 3)
    queries_sib()
    turn_queries(0)
    attend(0, 0)
    after_y("pair", 2)
    after_y("pair", 3)
    after_z("lat", 1)
    for s in range(1, seqs):
        attend(0, s)
    after_z("lat", 2)
    after_x("lat", 1)
    after_sib("pair", 1)
    project(1)
    turn_queries(1)
    after_z("lat", 3)
    attend(1, 0)
    after_x("lat", 2)
    for s in range(1, seqs):
        attend(1, s)
    after_x("lat", 3)
    after_y("lat", 1)
    after_sib("pair", 2)
    project(2)
    turn_queries(2)
    for s in range(seqs):
        attend(2, s)
    after_y("lat", 2)
    after_sib("pair", 3)
    project(3)
    turn_queries(3)
    for s in range(seqs):
        attend(3, s)

    for s in range(seqs):
        at = pl.ds(s * heads, heads)
        stats = jnp.transpose(stat_ref[s])[:heads]
        stat_send[...] = stats
        stat_own[at] = stat_send[:, my_rows]
        stat_got[0, at] = stat_send[:, other_rows]
    pending.append(send(stat_got.at[0], stat_got.at[1], o_ss.at[shards, 0], o_rs.at[shards, 0], to_x))
    block = 256
    for part in range(2):
        for i in range(pair_ref.shape[1] // block):
            wcols_ref[part, :, i * block:(i + 1) * block] = jnp.transpose(pair_ref[part, i * block:(i + 1) * block])
    after_y("lat", 3)
    wait_plain(stat_got.at[1], o_ss.at[shards, 0], o_rs.at[shards, 0])
    own_lse, got_lse = stat_own[...], stat_got[1]
    top = jnp.maximum(own_lse, got_lse)
    own_share, got_share = jnp.exp2(own_lse - top), jnp.exp2(got_lse - top)
    total = own_share + got_share
    lse = top + jnp.log2(total)
    own_share, got_share = own_share / total, got_share / total
    for s in range(seqs):
        lse_ref[s] = lse[s * heads:(s + 1) * heads]
        for d in range(shards):
            part = pl.ds(pl.multiple_of(z_of[d] * cols, 16), cols)
            wait_plain(o_got.at[s, part], o_ss.at[d, s], o_rs.at[d, s])
    for s in range(seqs):
        for h in range(heads):
            at = slice(h * head_dim, (h + 1) * head_dim)
            n = s * heads + h
            att_ref[s, at] = o_own[s, at] * own_share[n:n + 1] + o_got[s, at].astype(F32) * got_share[n:n + 1]
    for d in range(1, shards):
        wait_plain(bup_all.at[z_of[d]], misc_ss.at[d], misc_rs.at[d])
    for d in range(1, shards):
        after_sib("lat", d)
    own_lat.wait()
    for copy in local:
        copy.wait()
    for copy in pending:
        copy.wait_send()


def first_call(x_cols, rows_in, mask, latents, lat_gain, lat_bias, wq_rows, pair_shard, lat_shard, b_up, rows):
    seqs, width, length = x_cols.shape
    local_rows, width_lat = latents.shape
    shards = lax.axis_size("heads")
    heads = HEADS
    head_dim = width_lat // heads
    whole = pl.BlockSpec(memory_space=pltpu.VMEM)
    hbm = pl.BlockSpec(memory_space=pl.ANY)
    out = jax.ShapeDtypeStruct
    sem = pltpu.SemaphoreType.DMA
    return pl.pallas_call(
        first_kernel,
        in_specs=[whole] * 10,
        out_specs=[whole, hbm, hbm, hbm] + [whole] * 5,
        out_shape=[
            out((2, width, width_lat), BF16),
            out((3, width_lat, width_lat), BF16),
            out((seqs, 2, width_lat, length), BF16),
            out((seqs, width, length), BF16),
            out((seqs, width_lat, local_rows), F32),
            out((seqs, heads, local_rows), F32),
            out((heads // shards, shards, head_dim, rows), BF16),
            out((local_rows, width_lat), BF16),
            out((shards,) + b_up.shape, F32),
        ],
        scratch_shapes=[
            pltpu.VMEM((seqs, width, length), BF16),
            pltpu.VMEM((2, width_lat, width), BF16),
            pltpu.VMEM((seqs, 2, width_lat, length), BF16),
            pltpu.VMEM((width, rows_in.shape[0]), F32),
            pltpu.VMEM((heads, rows, head_dim), BF16),
            pltpu.VMEM((head_dim, rows), F32),
            pltpu.VMEM((seqs, width_lat, local_rows), F32),
            pltpu.VMEM((seqs, width_lat, local_rows), BF16),
            pltpu.VMEM((seqs, width_lat, local_rows), BF16),
            pltpu.VMEM((seqs, rows, 128), F32),
            pltpu.VMEM((heads, rows), F32),
            pltpu.VMEM((seqs * heads, local_rows), F32),
            pltpu.VMEM((2, seqs * heads, local_rows), F32),
            sem((shards, 5)), sem((shards, 5)), sem((shards, 5)), sem((shards, 5)),
            sem((2, shards)), sem((2, shards)), sem((shards,)), sem((shards,)),
            sem((shards + 1, seqs)), sem((shards + 1, seqs)), sem((2,)), sem((seqs,)), sem((shards,)),
        ],
        compiler_params=pltpu.CompilerParams(vmem_limit_bytes=VMEM_LIMIT, collective_id=1, has_side_effects=True),
        name="first",
    )(x_cols, rows_in, mask, latents, lat_gain, lat_bias, wq_rows, pair_shard, lat_shard, b_up)


class Reduce:
    def __init__(self, src, half, got_sib, got_chip, got_z, out, ss, rs, pending):
        self.src, self.half, self.got_sib, self.got_chip, self.got_z, self.out = src, half, got_sib, got_chip, got_z, out
        self.ss, self.rs, self.pending = ss, rs, pending
        items, blk, self.me, hi, self.core = places()
        self.shards = lax.axis_size("heads")
        other = 1 - blk
        self.chip = hi * 2 + blk
        self.peers = [(hi * 2 + other, mesh_at(db=other)), ((1 - hi) * 2 + blk, mesh_at(di=(1 - hi) * 2 + self.core)),
                      ((1 - hi) * 2 + other, mesh_at(di=(1 - hi) * 2 + self.core, db=other))]
        self.to_sib = mesh_at(di=items + 1 - 2 * self.core)
        self.n, _, self.cols, self.width = half.shape
        self.share = self.cols // 4
        self.z_of = [lax.rem(self.me + d, self.shards) for d in range(self.shards)]
        self.z_back = [lax.rem(self.me + self.shards - d, self.shards) for d in range(self.shards)]

    def rows(self, chip):
        return pl.ds(pl.multiple_of(chip * self.share, 16), self.share)

    def lanes(self, core):
        return pl.ds(pl.multiple_of(core * self.width, 128), self.width)

    def go(self, src, dst, i, target):
        self.pending.append(send(src, dst, self.ss.at[i], self.rs.at[i], target))

    def arrived(self, where, i):
        pltpu.make_async_remote_copy(src_ref=where, dst_ref=where, send_sem=self.ss.at[i], recv_sem=self.rs.at[i],
                                     device_id=self.to_sib, device_id_type=pl.DeviceIdType.MESH).wait_recv()

    def start(self):
        self.go(self.src.at[:, :, :, self.lanes(1 - self.core)], self.got_sib, 0, self.to_sib)

    def join_sib(self):
        self.arrived(self.got_sib, 0)

        def step(i, _):
            n, h = i // self.shards, lax.rem(i, self.shards)
            own = self.src[n, h, :, self.lanes(self.core)]
            self.half[n, h] = (own.astype(F32) + self.got_sib[n, h].astype(F32)).astype(self.half.dtype)
            return 0
        lax.fori_loop(0, self.n * self.shards, step, 0)
        self.send_chips()

    def send_chips(self):
        for j, (chip, target) in enumerate(self.peers):
            self.go(self.half.at[:, :, self.rows(chip)], self.got_chip.at[j], 1 + j, target)

    def join_chips(self):
        for j in range(3):
            self.arrived(self.got_chip.at[j], 1 + j)
        mine = self.rows(self.chip)

        def step(i, _):
            n, h = i // self.shards, lax.rem(i, self.shards)
            total = self.half[n, h, mine].astype(F32)
            for j in range(3):
                total += self.got_chip[j, n, h].astype(F32)
            self.half[n, h, mine] = total.astype(self.half.dtype)
            return 0
        lax.fori_loop(0, self.n * self.shards, step, 0)
        for d in range(1, self.shards):
            self.go(self.half.at[:, self.z_back[d], mine], self.got_z.at[d - 1], 3 + d, mesh_at(dh=self.z_back[d]))

    def join_z(self):
        for d in range(1, self.shards):
            self.arrived(self.got_z.at[d - 1], 3 + d)
        mine = self.rows(self.chip)
        for n in range(self.n):
            total = self.half[n, self.me, mine].astype(F32)
            for d in range(1, self.shards):
                total += self.got_z[d - 1, n].astype(F32)
            self.out[n, mine, self.lanes(self.core)] = total.astype(self.out.dtype)
        region = self.out.at[:, mine, self.lanes(self.core)]
        for j, (_, target) in enumerate(self.peers):
            self.go(region, region, 7 + j, target)

    def share_chips(self):
        for j, (chip, _) in enumerate(self.peers):
            self.arrived(self.out.at[:, self.rows(chip), self.lanes(self.core)], 7 + j)
        half = self.out.at[:, :, self.lanes(self.core)]
        self.go(half, half, 10, self.to_sib)

    def finish(self):
        self.arrived(self.out.at[:, :, self.lanes(1 - self.core)], 10)


def second_kernel(x_hbm, rows_ref, mask_ref, w_ref, qt_ref, kv_hbm, xn_hbm, do_in, stat_in, mixed_in, lat_in, grads_hbm, vec_in, lang_in, latsum_in,
                  g_out, mixed_out, dq_out, dw_out, dlat_out, latn_out, small_out, lats_out,
                  x_ref, xn_ref, cols_ref, kv_ref, dkv_ref, q_ref, do_ref, stat_ref, stat_cols, dq_ref, dw_ref,
                  g_half, g_chip, g_z, w_half, w_sib, w_z, q_half, q_sib, q_chip, q_z, s_half, s_sib, s_chip, s_z,
                  small_ref, demb_ref, s_ref, l_sib, l_half, l_y, l_sum, l_z,
                  g_ss, g_rs, w_ss, w_rs, q_ss, q_rs, s_ss, s_rs, l_ss, l_rs, do_ss, do_rs, misc_ss, misc_rs, mix_ss, mix_rs, a_ss, a_rs, load_sem, kv_sem):
    items, blk, me, hi, core = places()
    shards = lax.axis_size("heads")
    seqs, width, length = x_ref.shape
    heads, rows, head_dim = q_ref.shape
    local_rows = rows // 2
    per_shard = heads // shards
    cols = per_shard * head_dim
    stat_rows = stat_in.shape[0]
    other = 1 - blk
    to_x, to_sib = mesh_at(db=other), mesh_at(di=items + 1 - 2 * core)
    to_y = mesh_at(di=(1 - hi) * 2 + core)
    to_xy = mesh_at(di=(1 - hi) * 2 + core, db=other)
    z_of = [lax.rem(me + d, shards) for d in range(shards)]
    z_back = [lax.rem(me + shards - d, shards) for d in range(shards)]
    my_rows = pl.ds(pl.multiple_of(blk * local_rows, 128), local_rows)
    other_rows = pl.ds(pl.multiple_of(other * local_rows, 128), local_rows)
    pending = []
    dot_ref = w_sib.at[:, :, :, pl.ds(0, rows)]
    grads = Reduce(None, g_half, None, g_chip, g_z, dlat_out, g_ss, g_rs, pending)
    narrow = w_half.shape[3]
    w_chip = g_chip.at[:, pl.ds(0, 2), :, :, pl.ds(0, narrow)]
    pair = Reduce(dw_ref, w_half, w_sib, w_chip, w_z, dw_out, w_ss, w_rs, pending)
    query = Reduce(dq_ref, q_half, q_sib, q_chip, q_z, dq_out, q_ss, q_rs, pending)
    small = Reduce(s_ref, s_half, s_sib, s_chip, s_z, small_out, s_ss, s_rs, pending)
    greet([to_sib, to_x, to_y, to_xy] + [mesh_at(dh=z_of[d]) for d in range(1, shards)])

    def arrived(where, ss, rs):
        pltpu.make_async_remote_copy(src_ref=where, dst_ref=where, send_sem=ss, recv_sem=rs,
                                     device_id=to_sib, device_id_type=pl.DeviceIdType.MESH).wait_recv()

    pending.append(send(stat_in, stat_ref.at[pl.ds(0, stat_rows), my_rows], misc_ss.at[0], misc_rs.at[0], to_x))
    for s in range(seqs):
        pending.append(send(do_in.at[s], dot_ref.at[s, :, :, my_rows], do_ss.at[s], do_rs.at[s], to_x))
    pending.append(send(lat_in, latn_out.at[my_rows], misc_ss.at[1], misc_rs.at[1], to_x))
    wide = l_half.shape[1]
    my_lanes = pl.ds(pl.multiple_of(core * wide, 128), wide)
    his_lanes = pl.ds(pl.multiple_of((1 - core) * wide, 128), wide)
    pending.append(send(latsum_in.at[:, his_lanes], l_sib, l_ss.at[0], l_rs.at[0], to_sib))
    mine = pl.ds(me * seqs, seqs)
    for d in range(1, shards):
        pending.append(send(mixed_in, mixed_out.at[mine], mix_ss.at[d], mix_rs.at[d], mesh_at(dh=z_back[d])))
    loads = [
        pltpu.make_async_copy(xn_hbm, xn_ref, load_sem.at[0]),
        pltpu.make_async_copy(x_hbm, x_ref, load_sem.at[1]),
        pltpu.make_async_copy(grads_hbm, g_half, load_sem.at[2]),
        pltpu.make_async_copy(mixed_in, mixed_out.at[mine], load_sem.at[3]),
        pltpu.make_async_copy(lat_in, latn_out.at[my_rows], load_sem.at[4]),
    ]
    own_do = pltpu.make_async_copy(do_in, dot_ref.at[:, :, :, my_rows], load_sem.at[5])

    def load_pair(n, start):
        s, h = n // heads, lax.rem(n, heads)
        slot = lax.rem(n, 2)
        copy = pltpu.make_async_copy(kv_hbm.at[s, :, pl.ds(pl.multiple_of(h * head_dim, 16), head_dim)], kv_ref.at[slot], kv_sem.at[slot])
        copy.start() if start else copy.wait()

    load_pair(0, True)
    for copy in loads:
        copy.start()
    own_do.start()
    stat_ref[:stat_rows, my_rows] = stat_in[...]
    stat_ref[stat_rows:] = jnp.zeros((128 - stat_rows, rows), F32)
    for h in range(heads):
        q_ref[h] = jnp.transpose(qt_ref[h % per_shard, h // per_shard])
    dq_ref[...] = jnp.zeros_like(dq_ref)
    small_ref[...] = jnp.zeros_like(small_ref)
    arrived(stat_ref.at[pl.ds(0, stat_rows), other_rows], misc_ss.at[0], misc_rs.at[0])
    stat_cols[...] = jnp.transpose(stat_ref[...])
    own_do.wait()
    scale = head_dim ** (-0.5)
    factor = LOG2E * scale
    lane = lax.broadcasted_iota(jnp.int32, (rows, 128), 1)
    cols_ref[...] = jnp.transpose(rows_ref[...])
    gain = cols_ref[:, 0:1]

    def head_steps(s):
        arrived(dot_ref.at[s, :, :, other_rows], do_ss.at[s], do_rs.at[s])
        for h in range(heads):
            inner = h % per_shard * head_dim
            do_ref[h] = jnp.transpose(dot_ref[s, h // per_shard, inner:inner + head_dim])

        def head_step(h, _):
            n = s * heads + h
            slot = lax.rem(n, 2)
            load_pair(n, False)

            @pl.when(n + 1 < seqs * heads)
            def _():
                load_pair(n + 1, True)

            at = pl.ds(pl.multiple_of(h * head_dim, 16), head_dim)
            lse = jnp.sum(jnp.where(lane == s * 2 * heads + h, stat_cols[...], 0.0), axis=1, keepdims=True)
            delta = jnp.sum(jnp.where(lane == s * 2 * heads + heads + h, stat_cols[...], 0.0), axis=1, keepdims=True)
            keys = kv_ref[slot, 0]
            weights = jnp.exp2(dot(q_ref[h], keys) * factor + mask_ref[s] - lse)
            part = pl.ds(pl.multiple_of(lax.rem(h, per_shard) * head_dim, 16), head_dim)
            dkv_ref[s, 1, at] = dot(dot_ref[s, h // per_shard, part], weights.astype(BF16)).astype(BF16)
            grad = dot(do_ref[h], kv_ref[slot, 1]) - delta
            grad = (weights * grad).astype(BF16)
            dkv_ref[s, 0, at] = (dot(qt_ref[lax.rem(h, per_shard), h // per_shard], grad) * scale).astype(BF16)
            dq_ref[0, h // per_shard, part] += dot_nt(keys, grad) * scale
            return 0

        lax.fori_loop(0, heads, head_step, 0)

    piece = min(256, length)

    def byte_steps(s):
        def byte_step(i, carry):
            at = pl.ds(pl.multiple_of(i * piece, piece), piece)
            grad = dot(w_ref[0], dkv_ref[s, 0, :, at]) + dot(w_ref[1], dkv_ref[s, 1, :, at])
            normed, inverse = norm_columns(x_ref[s, :, at], cols_ref[:, 2 + s:3 + s])
            small_ref[:, 0:1] += jnp.sum(grad * normed, axis=1, keepdims=True)
            small_ref[:, 1:2] += jnp.sum(grad, axis=1, keepdims=True)
            scaled = grad * gain
            first = jnp.mean(scaled, axis=0, keepdims=True)
            second = jnp.mean(scaled * normed, axis=0, keepdims=True)
            shifted = (scaled - first - normed * second) * inverse
            x_ref[s, :, at] = shifted.astype(BF16)
            return carry + jnp.sum(shifted, axis=1, keepdims=True)

        demb_ref[:, s:s + 1] = lax.fori_loop(0, length // piece, byte_step, jnp.zeros((width, 1), F32))
        share = width // shards
        for d in range(1, shards):
            there = pl.ds(pl.multiple_of(z_back[d] * share, 16), share)
            pending.append(send(x_ref.at[s, there], g_out.at[me * seqs + s], a_ss.at[s, d], a_rs.at[s, d], mesh_at(dh=z_back[d])))
        own = pltpu.make_async_copy(x_ref.at[s, pl.ds(pl.multiple_of(me * share, 16), share)], g_out.at[me * seqs + s], load_sem.at[6 + s])
        own.start()
        loads.append(own)

    def latents_sib():
        arrived(l_sib, l_ss.at[0], l_rs.at[0])
        l_half[...] = latsum_in[:, my_lanes] + l_sib[...]
        pending.append(send(l_half, l_y, l_ss.at[1], l_rs.at[1], to_y))

    lat_share = local_rows // shards

    def latents_y():
        arrived(l_y, l_ss.at[1], l_rs.at[1])
        l_sum[...] = l_half[...] + l_y[...]
        for d in range(1, shards):
            there = pl.ds(pl.multiple_of(z_back[d] * lat_share, 8), lat_share)
            pending.append(send(l_sum.at[there], l_z.at[d - 1], l_ss.at[1 + d], l_rs.at[1 + d], mesh_at(dh=z_back[d])))

    def latents_z():
        total = l_sum[pl.ds(pl.multiple_of(me * lat_share, 8), lat_share)]
        for d in range(1, shards):
            arrived(l_z.at[d - 1], l_ss.at[1 + d], l_rs.at[1 + d])
            total += l_z[d - 1]
        lats_out[:, my_lanes] = total
        half = lats_out.at[:, my_lanes]
        pending.append(send(half, half, l_ss.at[5], l_rs.at[5], to_sib))

    def small_start():
        wide_lane = lax.broadcasted_iota(jnp.int32, (width, 128), 1)
        block = jnp.where(wide_lane == 32, small_ref[:, 0:1], 0.0) + jnp.where(wide_lane == 33, small_ref[:, 1:2], 0.0)
        for s in range(seqs):
            block += demb_ref[:, s:s + 1] * lang_in[s:s + 1]
        share = width // shards
        for h in range(shards):
            s_ref[0, h, :, :128] = block[h * share:(h + 1) * share]
            s_ref[0, h, :, 128:] = jnp.zeros((share, 128), F32)
            s_ref[0, h, :vec_in.shape[0], 128:] = vec_in[...]
        small.start()

    def weight_steps(part):
        def weight_step(h, _):
            at = pl.ds(pl.multiple_of(h * cols, 16), cols)
            total = dot_nt(dkv_ref[0, part, at], xn_ref[0])
            for s in range(1, seqs):
                total += dot_nt(dkv_ref[s, part, at], xn_ref[s])
            dw_ref[part, h] = total.astype(BF16)
            return 0
        lax.fori_loop(0, shards, weight_step, 0)

    head_steps(0)
    loads[2].wait()
    grads.send_chips()
    latents_sib()
    loads[1].wait()
    byte_steps(0)
    latents_y()
    for s in range(1, seqs):
        head_steps(s)
    query.start()
    for s in range(1, seqs):
        byte_steps(s)
    small_start()
    grads.join_chips()
    query.join_sib()
    loads[0].wait()
    weight_steps(0)
    query.join_chips()
    small.join_sib()
    weight_steps(1)
    pair.start()
    query.join_z()
    small.join_chips()
    grads.join_z()
    latents_z()
    pair.join_sib()
    query.share_chips()
    small.join_z()
    grads.share_chips()
    pair.join_chips()
    query.finish()
    small.share_chips()
    pair.join_z()
    pair.share_chips()
    grads.finish()
    small.finish()
    arrived(lats_out.at[:, his_lanes], l_ss.at[5], l_rs.at[5])
    arrived(latn_out.at[other_rows], misc_ss.at[1], misc_rs.at[1])
    for d in range(1, shards):
        there = pl.ds(z_of[d] * seqs, seqs)
        arrived(mixed_out.at[there], mix_ss.at[d], mix_rs.at[d])
        for s in range(seqs):
            arrived(g_out.at[z_of[d] * seqs + s], a_ss.at[s, d], a_rs.at[s, d])
    for own in loads[3:]:
        own.wait()
    pair.finish()
    for copy in pending:
        copy.wait_send()


def second_call(x_cols, rows_in, mask, w_cols, qt, pairs, xn, grad_out, stats, mixed, lat_low, grads, vectors, lang_rows, lat_sum):
    seqs, width, length = x_cols.shape
    rows, width_lat = qt.shape[3], pairs.shape[2]
    local_rows = lat_low.shape[0]
    shards = lax.axis_size("heads")
    heads = HEADS
    head_dim = width_lat // heads
    cols = width_lat // shards
    share = cols // 4
    whole = pl.BlockSpec(memory_space=pltpu.VMEM)
    hbm = pl.BlockSpec(memory_space=pl.ANY)
    out = jax.ShapeDtypeStruct
    vmem = pltpu.VMEM
    sem = pltpu.SemaphoreType.DMA

    assert seqs == 2

    def reduce_buffers(n, lanes, kind, cols=cols):
        half, share = lanes // 2, cols // 4
        return [vmem((n, shards, cols, half), kind), vmem((n, shards, cols, half), kind), vmem((3, n, shards, share, half), kind),
                vmem((shards - 1, n, share, half), kind)]

    return pl.pallas_call(
        second_kernel,
        in_specs=[hbm, whole, whole, whole, whole, hbm, hbm, hbm, whole, hbm, whole, hbm, whole, whole, whole],
        out_specs=[hbm, hbm, whole, whole, whole, hbm, whole, whole],
        out_shape=[
            out((shards * seqs, width // shards, length), BF16),
            out((shards * seqs, local_rows, width_lat), BF16),
            out((1, cols, rows), F32),
            out((2, cols, width), BF16),
            out((3, cols, width_lat), BF16),
            out((rows, width_lat), BF16),
            out((1, width // shards, 256), F32),
            out((local_rows // shards, width_lat), F32),
        ],
        scratch_shapes=[
            vmem((seqs, width, length), BF16),
            vmem((seqs, width, length), BF16),
            vmem((width, rows_in.shape[0]), F32),
            vmem((2, 2, head_dim, length), BF16),
            vmem((seqs, 2, width_lat, length), BF16),
            vmem((heads, rows, head_dim), BF16),
            vmem((heads, rows, head_dim), BF16),
            vmem((128, rows), F32),
            vmem((rows, 128), F32),
            vmem((1, shards, cols, rows), F32),
            vmem((2, shards, cols, width), BF16),
        ] + reduce_buffers(3, width_lat, BF16)[::2] + reduce_buffers(3, width_lat, BF16)[3:] + reduce_buffers(2, width, BF16)[:2]
        + reduce_buffers(2, width, BF16)[3:] + reduce_buffers(1, rows, F32)
        + reduce_buffers(1, 256, F32, width // shards) + [
            vmem((width, 2), F32),
            vmem((width, seqs), F32),
            vmem((1, shards, width // shards, 256), F32),
            vmem((local_rows, width_lat // 2), F32),
            vmem((local_rows, width_lat // 2), F32),
            vmem((local_rows, width_lat // 2), F32),
            vmem((local_rows, width_lat // 2), F32),
            vmem((shards - 1, local_rows // shards, width_lat // 2), F32),
        ] + [sem((11,))] * 8 + [sem((6,))] * 2 + [sem((seqs,))] * 2 + [sem((2,))] * 2 + [sem((shards,))] * 2 + [sem((seqs, shards))] * 2
        + [sem((6 + seqs,)), sem((2,))],
        compiler_params=pltpu.CompilerParams(vmem_limit_bytes=VMEM_LIMIT, collective_id=2, has_side_effects=True),
        name="second",
    )(x_cols, rows_in, mask, w_cols, qt, pairs, xn, grad_out, stats, mixed, lat_low, grads, vectors, lang_rows, lat_sum)


def third_kernel(dq_ref, wq_ref, lat_ref, gain_ref, latn_ref, sum_ref, grad_ref, dwq_ref, vec_ref,
                 part_ref, got_ref, piece_ref, all_ref, vec_all, z_ss, z_rs, p_ss, p_rs, v_ss, v_rs):
    _, blk, me, _, _ = places()
    shards = lax.axis_size("heads")
    local_rows, width = lat_ref.shape
    share = local_rows // shards
    other = 1 - blk
    z_of = [lax.rem(me + d, shards) for d in range(shards)]
    z_back = [lax.rem(me + shards - d, shards) for d in range(shards)]
    greet([mesh_at(dh=z_of[d]) for d in range(1, shards)] + [mesh_at(db=other, dh=z_of[d]) for d in range(shards)])
    pending = []

    def arrived(where, ss, rs):
        pltpu.make_async_remote_copy(src_ref=where, dst_ref=where, send_sem=ss, recv_sem=rs,
                                     device_id=mesh_at(db=other), device_id_type=pl.DeviceIdType.MESH).wait_recv()

    query = dq_ref[0].astype(BF16)
    own = dq_ref[0, :, pl.ds(pl.multiple_of(blk * local_rows, 128), local_rows)]
    part = dot_nt(jnp.transpose(own).astype(BF16), wq_ref[...]).astype(BF16)
    part_ref[...] = part.reshape(shards, share, width)
    for d in range(1, shards):
        pending.append(send(part_ref.at[z_back[d]], got_ref.at[d - 1], z_ss.at[d], z_rs.at[d], mesh_at(dh=z_back[d])))
    for i in range(0, width, 256):
        dwq_ref[i:i + 256] = dot_nt(jnp.transpose(latn_ref[:, i:i + 256]), query)
    mine = pl.ds(pl.multiple_of(me * share, 8), share)
    grad = part_ref[me].astype(F32)
    for d in range(1, shards):
        arrived(got_ref.at[d - 1], z_ss.at[d], z_rs.at[d])
        grad += got_ref[d - 1].astype(F32)
    _, normed, inverse = norm_keep(lat_ref[mine].astype(F32), 1.0, 0.0)
    piece_ref[...] = (sum_ref[...] + norm_back(grad, normed, inverse, gain_ref[...])).astype(BF16)
    for d in range(1, shards):
        pending.append(send(piece_ref, all_ref.at[me], p_ss.at[d], p_rs.at[d], mesh_at(dh=z_back[d])))
    at = blk * shards + me
    vec_all[at] = jnp.zeros_like(vec_all[0])
    vec_all[at, 0:1] = jnp.sum(grad * normed, axis=0, keepdims=True)
    vec_all[at, 1:2] = jnp.sum(grad, axis=0, keepdims=True)
    for b in range(2):
        for d in range(1 - b, shards):
            target = mesh_at(db=other, dh=z_back[d]) if b else mesh_at(dh=z_back[d])
            pending.append(send(vec_all.at[at], vec_all.at[at], v_ss.at[b, d], v_rs.at[b, d], target))
    all_ref[me] = piece_ref[...]
    for d in range(1, shards):
        arrived(all_ref.at[z_of[d]], p_ss.at[d], p_rs.at[d])
    grad_ref[...] = all_ref[...].reshape(local_rows, width).astype(F32)
    for b in range(2):
        for d in range(1 - b, shards):
            arrived(vec_all.at[(other if b else blk) * shards + z_of[d]], v_ss.at[b, d], v_rs.at[b, d])
    total = vec_all[0]
    for i in range(1, 2 * shards):
        total += vec_all[i]
    vec_ref[...] = total
    for copy in pending:
        copy.wait_send()


def third_call(dq, w_query, latents, lat_gain, lat_low_all, lat_sum):
    local_rows, width = latents.shape
    shards = lax.axis_size("heads")
    share = local_rows // shards
    whole = pl.BlockSpec(memory_space=pltpu.VMEM)
    out, vmem, sem = jax.ShapeDtypeStruct, pltpu.VMEM, pltpu.SemaphoreType.DMA
    return pl.pallas_call(
        third_kernel,
        in_specs=[whole] * 6,
        out_specs=[whole] * 3,
        out_shape=[out((local_rows, width), F32), out(w_query.shape, F32), out((8, width), F32)],
        scratch_shapes=[
            vmem((shards, share, width), BF16), vmem((shards - 1, share, width), BF16), vmem((share, width), BF16),
            vmem((shards, share, width), BF16), vmem((2 * shards, 8, width), F32),
            sem((shards,)), sem((shards,)), sem((shards,)), sem((shards,)), sem((2, shards)), sem((2, shards)),
        ],
        compiler_params=pltpu.CompilerParams(vmem_limit_bytes=VMEM_LIMIT, collective_id=3, has_side_effects=True),
        name="third",
    )(dq, w_query, latents, lat_gain, lat_low_all, lat_sum)


def middle_kernel(att_ref, lat_ref, cot_ref, all_ref, bup_ref, bdown_ref, gain_ref, bias_ref, lse_ref,
                  mixed_ref, do_ref, stat_ref, half_ref, vec_ref, sum_ref,
                  rows_ref, mid_ref, low_ref, hid_ref, norm_ref, a_ref, b_src, b_ref, a_ss, a_rs, b_ss, b_rs):
    items, _, _, _, core = places()
    to_sib = mesh_at(di=items + 1 - 2 * core)
    seqs, width, local_rows = att_ref.shape
    rows = seqs * local_rows
    heads = lse_ref.shape[1]
    head_dim = width // heads
    half = width // 2
    block = 256
    pending = []
    greet([to_sib])

    def block_loop(body):
        def step(i, _):
            body(pl.ds(pl.multiple_of(i * block, block), block))
            return 0
        lax.fori_loop(0, width // block, step, 0)

    def share_a(i):
        pending.append(send(a_ref.at[i, 0], a_ref.at[i, 1], a_ss.at[i], a_rs.at[i], to_sib))

    def share_b(i):
        theirs = b_src.at[i, :, pl.ds(pl.multiple_of((1 - core) * half, 128), half)]
        pending.append(send(theirs, b_ref.at[i, 1], b_ss.at[i], b_rs.at[i], to_sib))
        b_ref[i, 0] = b_src[i, :, pl.ds(pl.multiple_of(core * half, 128), half)]

    cot = cot_ref[...]
    b_src[2] = cot
    share_b(2)
    for s in range(seqs):
        at = slice(s * local_rows, (s + 1) * local_rows)
        low = att_ref[s].astype(BF16)
        a_ref[0, 0, :, at] = low
        rows_ref[at] = jnp.transpose(att_ref[s]).astype(BF16)
    share_a(0)

    def branch(at):
        latent = lat_ref[:, at].astype(F32)
        mid_ref[:, at] = dot(rows_ref[...], all_ref[0, :, at]) + jnp.concatenate([latent] * seqs, axis=0)
    block_loop(branch)
    mid_out, normed, inverse = norm_keep(mid_ref[...], gain_ref[...], bias_ref[...])
    norm_ref[...] = normed
    b_src[1] = mid_out.astype(BF16)
    share_b(1)

    def up(at):
        value = dot_nt(b_src[1], all_ref[1, at]) + bup_ref[:, at]
        square = value * value
        bend = jnp.tanh(0.7978845608028654 * (value + 0.044715 * (square * value)))
        active = 0.5 * value * (1.0 + bend)
        slope = 0.5 * (1.0 + bend) + 0.5 * value * (1.0 - bend * bend) * (0.7978845608028654 * (1.0 + 0.134145 * square))
        rows_ref[:, at] = active.astype(BF16)
        grad = (dot_nt(cot_ref[...], all_ref[2, at]) * slope).astype(BF16)
        low_ref[:, at] = grad
        vec_ref[2:3, at] = jnp.sum(grad.astype(F32), axis=0, keepdims=True)
        a_ref[2, 0, at] = jnp.transpose(active.astype(BF16))
        a_ref[1, 0, at] = jnp.transpose(grad)
    block_loop(up)
    share_a(2)
    share_a(1)

    def down(at):
        hid_ref[:, at] = dot(low_ref[...], all_ref[1, :, at])
        out = mid_ref[:, at] + dot(rows_ref[...], all_ref[2, :, at]) + bdown_ref[:, at]
        for s in range(seqs):
            mixed_ref[s, :, at] = out[s * local_rows:(s + 1) * local_rows].astype(BF16)
    block_loop(down)
    grad = hid_ref[...]
    normed = norm_ref[...]
    vec_ref[0:1] = jnp.sum(grad * normed, axis=0, keepdims=True)
    vec_ref[1:2] = jnp.sum(grad, axis=0, keepdims=True)
    vec_ref[3:4] = jnp.sum(cot_ref[...].astype(F32), axis=0, keepdims=True)
    grad = cot_ref[...].astype(F32) + norm_back(grad, normed, inverse, gain_ref[...])
    b_src[0] = grad.astype(BF16)
    share_b(0)
    total = grad[:local_rows]
    for s in range(1, seqs):
        total += grad[s * local_rows:(s + 1) * local_rows]
    sum_ref[...] = total

    def out(h, _):
        at = pl.ds(pl.multiple_of(h * head_dim, 16), head_dim)
        grad = dot_nt(all_ref[0, at], b_src[0]).astype(BF16)
        for s in range(seqs):
            part = grad[:, s * local_rows:(s + 1) * local_rows]
            do_ref[s, at] = part
            delta = jnp.sum(part.astype(F32) * att_ref[s, at], axis=0, keepdims=True)
            stat_ref[pl.ds((2 * s + 1) * heads + h, 1)] = delta
        return 0
    lax.fori_loop(0, heads, out, 0)
    for s in range(seqs):
        stat_ref[2 * s * heads:(2 * s + 1) * heads] = lse_ref[s]

    def arrived(where, ss, rs):
        pltpu.make_async_remote_copy(src_ref=where, dst_ref=where, send_sem=ss, recv_sem=rs,
                                     device_id=to_sib, device_id_type=pl.DeviceIdType.MESH).wait_recv()

    shards, cols = half_ref.shape[1:3]
    for i in (2, 1, 0):
        arrived(a_ref.at[i, 1], a_ss.at[i], a_rs.at[i])
        arrived(b_ref.at[i, 1], b_ss.at[i], b_rs.at[i])

        def weight(h, _):
            at = pl.ds(pl.multiple_of(h * cols, 16), cols)
            half_ref[i, h] = (dot(a_ref[i, 0, at], b_ref[i, 0]) + dot(a_ref[i, 1, at], b_ref[i, 1])).astype(BF16)
            return 0
        lax.fori_loop(0, shards, weight, 0)
    for copy in pending:
        copy.wait_send()


def middle_call(att, latents, cot, weights, b_up, b_down, gain, bias, lse):
    seqs, width, local_rows = att.shape
    rows = seqs * local_rows
    heads = lse.shape[1]
    shards = lax.axis_size("heads")
    whole = pl.BlockSpec(memory_space=pltpu.VMEM)
    out, vmem, sem = jax.ShapeDtypeStruct, pltpu.VMEM, pltpu.SemaphoreType.DMA
    return pl.pallas_call(
        middle_kernel,
        in_specs=[whole] * 9,
        out_specs=[whole] * 6,
        out_shape=[
            out((seqs, local_rows, width), BF16),
            out((seqs, width, local_rows), BF16),
            out((2 * seqs * heads, local_rows), F32),
            out((3, shards, width // shards, width // 2), BF16),
            out((4, width), F32),
            out((local_rows, width), F32),
        ],
        scratch_shapes=[
            vmem((rows, width), BF16), vmem((rows, width), F32), vmem((rows, width), BF16), vmem((rows, width), F32), vmem((rows, width), F32),
            vmem((3, 2, width, rows), BF16), vmem((3, rows, width), BF16), vmem((3, 2, rows, width // 2), BF16),
            sem((3,)), sem((3,)), sem((3,)), sem((3,)),
        ],
        compiler_params=pltpu.CompilerParams(vmem_limit_bytes=VMEM_LIMIT, collective_id=4, has_side_effects=True),
        name="middle",
    )(att, latents, cot, weights, b_up, b_down, gain, bias, lse)


REST = ("items", "blk")
ALL = ("heads", "items", "blk")


def gather_rows(shard):
    count = lax.axis_size("items") * lax.axis_size("blk")
    me = lax.axis_index("items") * lax.axis_size("blk") + lax.axis_index("blk")
    share = shard.shape[0] // count
    part = lax.dynamic_slice_in_dim(shard, me * share, share, 0)
    return lax.all_gather(part, ALL, axis=0, tiled=True)


def scatter_rows(whole):
    part = lax.psum_scatter(whole.astype(BF16), ALL, scatter_dimension=0, tiled=True)
    return lax.all_gather(part, REST, axis=0, tiled=True)


def general_device(inputs, padding, language, lang_table, latents, in_gain, in_bias, lat_gain, lat_bias, mid_gain, mid_bias,
              w_query, w_key, w_value, w_out, w_up, b_up, w_down, b_down, cotangent):
    length, local_seqs, width = inputs.shape
    local_rows, width_lat = latents.shape
    cols = w_query.shape[1]
    head_dim = width_lat // HEADS
    per_shard = cols // head_dim
    shards = lax.axis_size("heads")
    blocks = lax.axis_size("blk")
    rows = local_rows * blocks
    seqs = local_seqs // shards
    me = lax.axis_index("heads")
    first = me * seqs

    pair_shard = jnp.concatenate([w_key.T, w_value.T], axis=0)
    pair_rows = gather_rows(pair_shard)
    latent_shard = jnp.concatenate([w_out, w_up.T, w_down], axis=0)
    lat_all = gather_rows(latent_shard).reshape(shards, 3, cols, width_lat)
    out_all, up_all, down_all = (lat_all[:, i].reshape(width_lat, width_lat) for i in range(3))

    all_latents = lax.all_gather(latents, "blk", axis=0, tiled=True).astype(F32)
    lat_out, _, _ = norm_keep(all_latents, lat_gain, lat_bias)
    lat_low = lat_out.astype(BF16)
    query_part = dot(lat_low, w_query).astype(BF16)
    queries = lax.all_gather(query_part, "heads", axis=1, tiled=True)
    q = queries.reshape(rows, HEADS, head_dim).transpose(1, 0, 2)

    own = lax.dynamic_slice_in_dim(inputs, first, seqs, 1)
    x_cols = jnp.transpose(own, (1, 2, 0))
    live = jnp.transpose(lax.dynamic_slice_in_dim(padding, first, seqs, 1))
    mask = jnp.where(live > 0, 0.0, MASKED).astype(F32)[:, None, :]
    own_lang = lax.dynamic_slice_in_dim(language, first, seqs, 0)
    onehot = (own_lang[:, None] == jnp.arange(lang_table.shape[0], dtype=jnp.int32)[None, :]).astype(F32)
    emb = jnp.dot(onehot, lang_table.astype(F32), precision=lax.Precision.HIGHEST)[:, :, None]
    gain_col, bias_col = in_gain[:, None], in_bias[:, None]

    pairs, o_cols, lse = forward_call(x_cols, emb, gain_col, bias_col, pair_rows, q, mask, per_shard)

    parts = o_cols.reshape(seqs, width_lat, blocks, local_rows).transpose(2, 0, 3, 1)
    parts = lax.all_to_all(parts, "blk", 0, 0, tiled=True).astype(F32)
    lse_parts = lse.reshape(seqs, HEADS, blocks, local_rows).transpose(2, 0, 3, 1)
    lse_parts = lax.all_to_all(lse_parts, "blk", 0, 0, tiled=True)
    top = jnp.max(lse_parts, axis=0)
    shares = jnp.exp2(lse_parts - top)
    total = jnp.sum(shares, axis=0)
    own_lse = top + jnp.log2(total)
    shares = shares / total
    attended = jnp.sum(parts.reshape(blocks, seqs, local_rows, HEADS, head_dim) * shares[..., None], axis=0)
    att_low = attended.reshape(seqs * local_rows, width_lat).astype(BF16)

    cot = lax.dynamic_slice_in_dim(cotangent, first, seqs, 0).reshape(seqs * local_rows, width_lat)
    lat_f32 = latents.astype(F32)
    middle = (lat_f32[None] + dot(att_low, out_all).reshape(seqs, local_rows, width_lat)).reshape(seqs * local_rows, width_lat)
    mid_out, mid_normed, mid_inverse = norm_keep(middle, mid_gain, mid_bias)
    mid_low = mid_out.astype(BF16)
    b_up_all = lax.all_gather(b_up, "heads", axis=0, tiled=True)
    hidden = dot_nt(mid_low, up_all) + b_up_all
    active, gelu_back = jax.vjp(jax.nn.gelu, hidden)
    active_low = active.astype(BF16)
    own_mixed = (middle + dot(active_low, down_all) + b_down).astype(BF16).reshape(seqs, local_rows, width_lat)
    mixed_latents = lax.all_gather(own_mixed, "heads", axis=0, tiled=True)

    grad_b_down = jnp.sum(cot.astype(F32), axis=0)
    grad_w_down = dot(active_low.T, cot)
    grad_active = dot_nt(cot, down_all)
    grad_hidden = gelu_back(grad_active)[0].astype(BF16)
    grad_b_up = jnp.sum(grad_hidden.astype(F32), axis=0)
    grad_w_up = dot(grad_hidden.T, mid_low)
    grad_mid_norm = dot(grad_hidden, up_all)
    grad_mid_gain = jnp.sum(grad_mid_norm * mid_normed, axis=0)
    grad_mid_bias = jnp.sum(grad_mid_norm, axis=0)
    grad_middle = cot.astype(F32) + norm_back(grad_mid_norm, mid_normed, mid_inverse, mid_gain)
    grad_branch = grad_middle.astype(BF16)
    grad_w_out = dot(att_low.T, grad_branch)
    grad_att = dot_nt(grad_branch, out_all).astype(BF16).reshape(seqs, local_rows, width_lat)
    grad_att_heads = grad_att.reshape(seqs, local_rows, HEADS, head_dim)
    delta = jnp.sum(grad_att_heads.astype(F32) * attended, axis=-1)
    lat_sum = jnp.sum(grad_middle.reshape(seqs, local_rows, width_lat), axis=0)

    all_grad_att = lax.all_gather(grad_att, "blk", axis=1, tiled=True).reshape(seqs, rows, HEADS, head_dim)
    stats = lax.all_gather(jnp.concatenate([own_lse, delta], axis=-1), "blk", axis=1, tiled=True)
    stats = jnp.transpose(stats, (0, 2, 1))[..., None]
    g_cols, dw_pair, dq, dgain, dbias, demb = backward_call(
        x_cols, emb, gain_col, bias_col, pair_rows.T, q, q.transpose(0, 2, 1),
        all_grad_att.transpose(0, 2, 1, 3), all_grad_att.transpose(0, 2, 3, 1),
        stats[:, :HEADS], stats[:, HEADS:], mask, pairs, per_shard)

    send = g_cols.reshape(seqs, shards, width // shards, length).transpose(1, 0, 2, 3)
    got = lax.all_to_all(send, "heads", 0, 0, tiled=True)
    grad_inputs = got.reshape(local_seqs, width // shards, length).transpose(2, 0, 1)

    grad_rows = jnp.stack([grad_w_out, grad_w_up, grad_w_down], axis=0).reshape(3, shards, cols, width_lat)
    lat_total = scatter_rows(grad_rows.transpose(1, 0, 2, 3).reshape(-1, width_lat)).astype(F32)
    pair_total = scatter_rows(dw_pair).astype(F32)

    dq_part = lax.psum_scatter(dq.reshape(width_lat, rows).astype(BF16), "heads", scatter_dimension=0, tiled=True)
    query_low = lax.psum(dq_part, REST)
    grad_w_query = dot(lat_low.T, query_low.T)
    lat_mine = lax.dynamic_slice_in_dim(query_low, lax.axis_index("blk") * local_rows, local_rows, 1)
    grad_lat_part = dot(lat_mine.T, w_query.T)
    grad_lat_norm = lax.psum(grad_lat_part.astype(BF16), "heads").astype(F32)
    lat_sum = lax.psum(lat_sum.astype(BF16), ("heads", "items")).astype(F32)
    _, own_normed, own_inverse = norm_keep(lat_f32, lat_gain, lat_bias)
    grad_latents = lat_sum + norm_back(grad_lat_norm, own_normed, own_inverse, lat_gain)
    lat_small = jnp.concatenate([jnp.sum(grad_lat_norm * own_normed, axis=0), jnp.sum(grad_lat_norm, axis=0)])
    lat_small = lax.psum(lat_small, "blk")

    table = jnp.dot(onehot.T, demb[:, :, 0], precision=lax.Precision.HIGHEST)
    small = jnp.concatenate([table.reshape(-1), dgain[:, 0], dbias[:, 0], grad_mid_gain, grad_mid_bias, grad_b_up, grad_b_down])
    small = lax.psum(small, ALL)
    sizes = [table.size, width, width, width_lat, width_lat, width_lat, width_lat]
    ends = [sum(sizes[:i]) for i in range(len(sizes) + 1)]
    table, dgain, dbias, dmid_gain, dmid_bias, db_up, db_down = (small[ends[i]:ends[i + 1]] for i in range(7))
    share = width // shards
    table = lax.dynamic_slice_in_dim(table.reshape(-1, width), me * share, share, 1)
    return (
        mixed_latents,
        grad_inputs,
        grad_latents,
        table,
        lax.dynamic_slice_in_dim(dgain, me * share, share, 0),
        lax.dynamic_slice_in_dim(dbias, me * share, share, 0),
        lat_small[:width_lat],
        lat_small[width_lat:],
        dmid_gain,
        dmid_bias,
        grad_w_query,
        pair_total[:cols].T,
        pair_total[cols:].T,
        lat_total[:cols],
        lat_total[cols:2 * cols].T,
        lax.dynamic_slice_in_dim(db_up, me * cols, cols, 0),
        lat_total[2 * cols:],
        db_down,
    )


def fast_device(inputs, padding, language, lang_table, latents, in_gain, in_bias, lat_gain, lat_bias, mid_gain, mid_bias,
              w_query, w_key, w_value, w_out, w_up, b_up, w_down, b_down, cotangent):
    length, local_seqs, width = inputs.shape
    local_rows, width_lat = latents.shape
    cols = w_query.shape[1]
    head_dim = width_lat // HEADS
    per_shard = cols // head_dim
    shards = lax.axis_size("heads")
    blocks = lax.axis_size("blk")
    rows = local_rows * blocks
    seqs = local_seqs // shards
    me = lax.axis_index("heads")
    first = me * seqs

    own = lax.dynamic_slice_in_dim(inputs, first, seqs, 1)
    x_cols = jnp.transpose(own, (1, 2, 0))
    live = jnp.transpose(lax.dynamic_slice_in_dim(padding, first, seqs, 1))
    mask = jnp.where(live > 0, 0.0, MASKED).astype(F32)[:, None, :]
    own_lang = lax.dynamic_slice_in_dim(language, first, seqs, 0)
    onehot = (own_lang[:, None] == jnp.arange(lang_table.shape[0], dtype=jnp.int32)[None, :]).astype(F32)
    emb = jnp.dot(onehot, lang_table.astype(F32), precision=lax.Precision.HIGHEST)
    rows_in = jnp.concatenate([in_gain[None], in_bias[None], emb, jnp.zeros((6 - seqs, width), F32)], axis=0)
    b_up_tile = jnp.pad(b_up[None, :], ((0, 7), (0, -cols % 128)))
    w_cols, lat_all, pairs, xn, att_cols, lse_cols, queries_t, lat_low, b_up_tiles = first_call(
        x_cols, rows_in, mask, latents, lat_gain[None], lat_bias[None], w_query.T,
        jnp.stack([w_key.T, w_value.T]), jnp.stack([w_out, w_up.T, w_down]), b_up_tile, rows)
    b_up_all = b_up_tiles[:, 0, :cols].reshape(1, -1)
    cot = lax.dynamic_slice_in_dim(cotangent, first, seqs, 0).reshape(seqs * local_rows, width_lat)
    own_mixed, grad_att, stats, grads, vectors, lat_sum = middle_call(
        att_cols, latents, cot, lat_all, b_up_all, b_down[None], mid_gain[None], mid_bias[None], lse_cols)
    grad_att = grad_att.reshape(seqs, shards, cols, local_rows)
    vectors = vectors.reshape(-1, 128)
    lang_rows = jnp.pad(onehot, ((0, 8 - seqs), (0, 128 - lang_table.shape[0])))
    g_cols, mixed_latents, dq, pair_total, lat_total, lat_low_all, small, lat_sum = second_call(
        x_cols, rows_in, mask, w_cols, queries_t, pairs, xn, grad_att, stats, own_mixed, lat_low, grads, vectors, lang_rows, lat_sum)
    grad_latents, grad_w_query, lat_small = third_call(dq, w_query, latents, lat_gain[None], lat_low_all, lat_sum)
    grad_inputs = g_cols.transpose(2, 0, 1)
    lat_total, pair_total = lat_total.astype(F32), pair_total.astype(F32)
    table = small[0, :, :lang_table.shape[0]].T
    dmid_gain, dmid_bias, db_up, db_down = small[0, :vectors.shape[0], 128:].reshape(4, width_lat)
    return (
        mixed_latents,
        grad_inputs,
        grad_latents,
        table,
        small[0, :, 32],
        small[0, :, 33],
        lat_small[0],
        lat_small[1],
        dmid_gain,
        dmid_bias,
        grad_w_query,
        pair_total[0].T,
        pair_total[1].T,
        lat_total[0],
        lat_total[1].T,
        lax.dynamic_slice_in_dim(db_up, me * cols, cols, 0),
        lat_total[2],
        db_down,
    )


def solution(mesh):
    placed = (
        P("blk", "items", None), P("blk", "items"), P("items"), P(), P("blk", None), P(), P(), P(), P(), P(), P(),
        P(None, "heads"), P(None, "heads"), P(None, "heads"), P("heads", None), P(None, "heads"), P("heads"),
        P("heads", None), P(), P("items", "blk", None),
    )
    out = (
        P("items", "blk", None), P("blk", "items", "heads"), P("blk", None), P(None, "heads"), P("heads"), P("heads"),
        P(), P(), P(), P(), P(None, "heads"), P(None, "heads"), P(None, "heads"), P("heads", None), P(None, "heads"),
        P("heads"), P("heads", None), P(),
    )
    fits = mesh.shape["blk"] == 2 and mesh.shape["items"] == 4 and mesh.shape["heads"] == 4
    return jax.shard_map(fast_device if fits else general_device, mesh=mesh, in_specs=placed, out_specs=out, check_vma=False)
```

```python
import functools

import jax
import jax.numpy as jnp
from jax import lax
from jax.experimental import pallas as pl
from jax.experimental.pallas import tpu as pltpu
from jax.sharding import PartitionSpec as P

HEADS = 8
EPS = 1e-05
MASKED = -1e30
LOG2E = 1.4426950408889634
F32 = jnp.float32
BF16 = jnp.bfloat16
NT = (((1,), (1,)), ((), ()))
VMEM_LIMIT = 60 * 1024 * 1024


def dot(a, b):
    return jnp.dot(a, b, preferred_element_type=F32)


def dot_nt(a, b):
    return lax.dot_general(a, b, NT, preferred_element_type=F32)


def norm_keep(values, gain, bias):
    average = jnp.mean(values, axis=-1, keepdims=True)
    centred = values - average
    inverse = lax.rsqrt(jnp.mean(centred * centred, axis=-1, keepdims=True) + EPS)
    normed = centred * inverse
    return (normed * gain + bias, normed, inverse)


def norm_back(grad_norm, normed, inverse, gain):
    scaled = grad_norm * gain
    first = jnp.mean(scaled, axis=-1, keepdims=True)
    second = jnp.mean(scaled * normed, axis=-1, keepdims=True)
    return (scaled - first - normed * second) * inverse


def norm_columns(x, emb):
    shifted = x.astype(F32) + emb
    centred = shifted - jnp.mean(shifted, axis=0, keepdims=True)
    inverse = lax.rsqrt(jnp.mean(centred * centred, axis=0, keepdims=True) + EPS)
    return centred * inverse, inverse


def head_rows(h, per_shard, head_dim):
    key = (h // per_shard) * 2 * per_shard + lax.rem(h, per_shard)
    key_at = pl.multiple_of(key * head_dim, head_dim)
    return pl.ds(key_at, head_dim), pl.ds(pl.multiple_of(key_at + per_shard * head_dim, head_dim), head_dim)


def forward_kernel(per_shard, x_ref, emb_ref, gain_ref, bias_ref, w_ref, q_ref, mask_ref, kv_ref, o_ref, lse_ref, xn_ref, stat_ref):
    heads, rows, head_dim = q_ref.shape
    length = x_ref.shape[1]
    piece = min(256, length)

    def norm_step(i, _):
        at = pl.ds(pl.multiple_of(i * piece, piece), piece)
        normed, _unused = norm_columns(x_ref[:, at], emb_ref[...])
        xn_ref[:, at] = (normed * gain_ref[...] + bias_ref[...]).astype(BF16)
        return 0

    lax.fori_loop(0, length // piece, norm_step, 0)
    block = 512 if w_ref.shape[0] % 512 == 0 else 160

    def pair_step(i, _):
        at = pl.ds(pl.multiple_of(i * block, block), block)
        kv_ref[at] = dot(w_ref[at], xn_ref[...]).astype(BF16)
        return 0

    lax.fori_loop(0, w_ref.shape[0] // block, pair_step, 0)
    factor = LOG2E * head_dim ** (-0.5)
    lane = lax.broadcasted_iota(jnp.int32, (rows, 128), 1)
    stat_ref[...] = jnp.zeros_like(stat_ref)

    def head_step(h, _):
        at_key, at_value = head_rows(h, per_shard, head_dim)
        scores = dot(q_ref[h], kv_ref[at_key]) * factor + mask_ref[...]
        top = jnp.max(scores, axis=1, keepdims=True)
        weights = jnp.exp2(scores - top)
        total = jnp.sum(weights, axis=1, keepdims=True)
        out = dot_nt(kv_ref[at_value], weights.astype(BF16))
        stat_ref[...] = jnp.where(lane == h, top + jnp.log2(total), stat_ref[...])
        inverse = jnp.transpose(jnp.broadcast_to(1.0 / total, (rows, 128)))[:1]
        o_ref[pl.ds(pl.multiple_of(h * head_dim, head_dim), head_dim)] = (out * inverse).astype(BF16)
        return 0

    lax.fori_loop(0, heads, head_step, 0)
    lse_ref[...] = jnp.transpose(stat_ref[...])[:heads]


def forward_call(x_cols, emb, gain, bias, w_rows, q, mask, per_shard):
    seqs, width, length = x_cols.shape
    heads, rows, head_dim = q.shape
    pair_rows = w_rows.shape[0]
    whole = pl.BlockSpec(memory_space=pltpu.VMEM)

    def per_seq(*dims):
        return pl.BlockSpec((None,) + dims, lambda s: (s, 0, 0))

    return pl.pallas_call(
        functools.partial(forward_kernel, per_shard),
        grid=(seqs,),
        in_specs=[per_seq(width, length), per_seq(width, 1), whole, whole, whole, whole, per_seq(1, length)],
        out_specs=[per_seq(pair_rows, length), per_seq(heads * head_dim, rows), per_seq(heads, rows)],
        out_shape=[
            jax.ShapeDtypeStruct((seqs, pair_rows, length), BF16),
            jax.ShapeDtypeStruct((seqs, heads * head_dim, rows), BF16),
            jax.ShapeDtypeStruct((seqs, heads, rows), F32),
        ],
        scratch_shapes=[pltpu.VMEM((width, length), BF16), pltpu.VMEM((rows, 128), F32)],
        compiler_params=pltpu.CompilerParams(vmem_limit_bytes=VMEM_LIMIT),
        name="attend",
    )(x_cols, emb, gain, bias, w_rows, q, mask)


def backward_kernel(per_shard, x_ref, emb_ref, gain_ref, bias_ref, w_ref, q_ref, qt_ref, do_ref, dot_ref, lse_ref, delta_ref, mask_ref, kv_ref,
                    g_ref, dw_ref, dq_ref, dgain_ref, dbias_ref, demb_ref, xn_ref, dkv_ref):
    heads, rows, head_dim = q_ref.shape
    width, length = x_ref.shape
    piece = min(256, length)

    @pl.when(pl.program_id(0) == 0)
    def _():
        dw_ref[...] = jnp.zeros_like(dw_ref)
        dq_ref[...] = jnp.zeros_like(dq_ref)
        dgain_ref[...] = jnp.zeros_like(dgain_ref)
        dbias_ref[...] = jnp.zeros_like(dbias_ref)

    def norm_step(i, _):
        at = pl.ds(pl.multiple_of(i * piece, piece), piece)
        normed, _unused = norm_columns(x_ref[:, at], emb_ref[...])
        xn_ref[:, at] = (normed * gain_ref[...] + bias_ref[...]).astype(BF16)
        return 0

    lax.fori_loop(0, length // piece, norm_step, 0)
    scale = head_dim ** (-0.5)
    factor = LOG2E * scale

    def head_step(h, _):
        at_key, at_value = head_rows(h, per_shard, head_dim)
        keys = kv_ref[at_key]
        weights = jnp.exp2(dot(q_ref[h], keys) * factor + mask_ref[...] - lse_ref[h])
        dkv_ref[at_value] = dot(dot_ref[h], weights.astype(BF16)).astype(BF16)
        grad = dot(do_ref[h], kv_ref[at_value]) - delta_ref[h]
        grad = (weights * grad).astype(BF16)
        dkv_ref[at_key] = (dot(qt_ref[h], grad) * scale).astype(BF16)
        dq_ref[h] += dot_nt(keys, grad) * scale
        return 0

    lax.fori_loop(0, heads, head_step, 0)
    block = 512 if dw_ref.shape[0] % 512 == 0 else 160

    def weight_step(i, _):
        at = pl.ds(pl.multiple_of(i * block, block), block)
        dw_ref[at] += dot_nt(dkv_ref[at], xn_ref[...])
        return 0

    lax.fori_loop(0, dw_ref.shape[0] // block, weight_step, 0)

    def byte_step(i, carry):
        at = pl.ds(pl.multiple_of(i * piece, piece), piece)
        grad = dot(w_ref[...], dkv_ref[:, at])
        normed, inverse = norm_columns(x_ref[:, at], emb_ref[...])
        dbias_ref[...] += jnp.sum(grad, axis=1, keepdims=True)
        dgain_ref[...] += jnp.sum(grad * normed, axis=1, keepdims=True)
        scaled = grad * gain_ref[...]
        first = jnp.mean(scaled, axis=0, keepdims=True)
        second = jnp.mean(scaled * normed, axis=0, keepdims=True)
        shifted = (scaled - first - normed * second) * inverse
        g_ref[:, at] = shifted.astype(BF16)
        return carry + jnp.sum(shifted, axis=1, keepdims=True)

    demb_ref[...] = lax.fori_loop(0, length // piece, byte_step, jnp.zeros((width, 1), F32))


def backward_call(x_cols, emb, gain, bias, w, q, qt, grad_out, grad_out_t, lse, delta, mask, pairs, per_shard):
    seqs, width, length = x_cols.shape
    heads, rows, head_dim = q.shape
    pair_rows = w.shape[1]
    whole = pl.BlockSpec(memory_space=pltpu.VMEM)

    def per_seq(*dims):
        return pl.BlockSpec((None,) + dims, lambda s: (s,) + (0,) * len(dims))

    return pl.pallas_call(
        functools.partial(backward_kernel, per_shard),
        grid=(seqs,),
        in_specs=[
            per_seq(width, length), per_seq(width, 1), whole, whole, whole, whole, whole,
            per_seq(heads, rows, head_dim), per_seq(heads, head_dim, rows),
            per_seq(heads, rows, 1), per_seq(heads, rows, 1), per_seq(1, length), per_seq(pair_rows, length),
        ],
        out_specs=[per_seq(width, length), whole, whole, whole, whole, per_seq(width, 1)],
        out_shape=[
            jax.ShapeDtypeStruct((seqs, width, length), BF16),
            jax.ShapeDtypeStruct((pair_rows, width), F32),
            jax.ShapeDtypeStruct((heads, head_dim, rows), F32),
            jax.ShapeDtypeStruct((width, 1), F32),
            jax.ShapeDtypeStruct((width, 1), F32),
            jax.ShapeDtypeStruct((seqs, width, 1), F32),
        ],
        scratch_shapes=[pltpu.VMEM((width, length), BF16), pltpu.VMEM((pair_rows, length), BF16)],
        compiler_params=pltpu.CompilerParams(vmem_limit_bytes=VMEM_LIMIT),
        name="attend_back",
    )(x_cols, emb, gain, bias, w, q, qt, grad_out, grad_out_t, lse, delta, mask, pairs)


def mesh_at(di=None, db=None, dh=None, core=None):
    items, blk, heads = lax.axis_index("items"), lax.axis_index("blk"), lax.axis_index("heads")
    return (items if di is None else di, blk if db is None else db, heads if dh is None else dh)


def places():
    items, blk, heads = lax.axis_index("items"), lax.axis_index("blk"), lax.axis_index("heads")
    core = lax.rem(items, 2)
    return items, blk, heads, items // 2, core


def send(src, dst, sems, recvs, target):
    copy = pltpu.make_async_remote_copy(
        src_ref=src, dst_ref=dst, send_sem=sems, recv_sem=recvs, device_id=target, device_id_type=pl.DeviceIdType.MESH)
    copy.start()
    return copy


def greet(targets):
    barrier = pltpu.get_barrier_semaphore()
    for target in targets:
        pl.semaphore_signal(barrier, inc=1, device_id=target, device_id_type=pl.DeviceIdType.MESH)
    pl.semaphore_wait(barrier, len(targets))


def first_kernel(x_ref, rows_ref, mask_ref, lat_ref, lgain_ref, lbias_ref, wq_ref, pair_shard, lat_shard, bup_ref,
                 wcols_ref, all_ref, kv_out, xn_out, att_ref, lse_ref, qt_ref, latn_ref, bup_all,
                 xn_ref, pair_ref, kv_ref, cols_ref, q_ref, o_tmp, o_own, o_send, o_got, stat_ref, stat_send, stat_own, stat_got,
                 pair_ss, pair_rs, lat_ss, lat_rs, q_ss, q_rs, misc_ss, misc_rs, o_ss, o_rs, own_sem, xn_sem, kv_sem):
    items, blk, me, hi, core = places()
    shards = lax.axis_size("heads")
    seqs, width, length = x_ref.shape
    rows = qt_ref.shape[3]
    local_rows = rows // 2
    heads, _, head_dim = q_ref.shape
    cols = heads * head_dim // shards
    per_shard = heads // shards
    sibling = items + 1 - 2 * core
    other = 1 - blk
    to_sib, to_x, to_y = mesh_at(di=sibling), mesh_at(db=other), mesh_at(di=(1 - hi) * 2 + core)
    z_of = [lax.rem(me + d, shards) for d in range(shards)]
    z_back = [lax.rem(me + shards - d, shards) for d in range(shards)]
    greet([to_sib, to_x, to_y] + [mesh_at(dh=z_of[d]) for d in range(1, shards)])

    share = cols // 4
    chip = hi * 2 + blk
    chip_x, chip_y, chip_xy = hi * 2 + other, (1 - hi) * 2 + blk, (1 - hi) * 2 + other

    def region(ref, shard, chip_at, lanes_of):
        half = ref.shape[2] // 2
        return ref.at[:, pl.ds(pl.multiple_of(shard * cols + chip_at * share, 16), share), pl.ds(pl.multiple_of(lanes_of * half, 128), half)]

    def lane_half(ref, shard, lanes_of):
        half = ref.shape[2] // 2
        return ref.at[:, pl.ds(pl.multiple_of(shard * cols, 16), cols), pl.ds(pl.multiple_of(lanes_of * half, 128), half)]

    pending = []
    local = []
    kinds = {"pair": (pair_shard, pair_ref, pair_ss, pair_rs), "lat": (lat_shard, all_ref, lat_ss, lat_rs)}

    def recv(kind, d, stage, where):
        _, dst, ss, rs = kinds[kind]
        pltpu.make_async_remote_copy(src_ref=where, dst_ref=where, send_sem=ss.at[d, stage], recv_sem=rs.at[d, stage],
                                     device_id=to_sib, device_id_type=pl.DeviceIdType.MESH).wait_recv()

    def out_z(kind, d):
        src, dst, ss, rs = kinds[kind]
        pending.append(send(region(src, 0, chip, core), region(dst, me, chip, core), ss.at[d, 0], rs.at[d, 0], mesh_at(dh=z_back[d])))

    def after_z(kind, d):
        _, dst, ss, rs = kinds[kind]
        mine = region(dst, z_of[d], chip, core)
        recv(kind, d, 0, mine)
        pending.append(send(mine, mine, ss.at[d, 1], rs.at[d, 1], to_x))
        pending.append(send(mine, mine, ss.at[d, 2], rs.at[d, 2], to_y))

    def after_x(kind, d):
        _, dst, ss, rs = kinds[kind]
        got = region(dst, z_of[d], chip_x, core)
        recv(kind, d, 1, got)
        pending.append(send(got, got, ss.at[d, 3], rs.at[d, 3], to_y))

    def after_y(kind, d):
        _, dst, ss, rs = kinds[kind]
        recv(kind, d, 2, region(dst, z_of[d], chip_y, core))
        recv(kind, d, 3, region(dst, z_of[d], chip_xy, core))
        half = lane_half(dst, z_of[d], core)
        pending.append(send(half, half, ss.at[d, 4], rs.at[d, 4], to_sib))

    def after_sib(kind, d):
        _, dst, ss, rs = kinds[kind]
        recv(kind, d, 4, lane_half(dst, z_of[d], 1 - core))

    for d in range(1, shards):
        out_z("pair", d)
    own_pair = pltpu.make_async_copy(pair_shard, pair_ref.at[:, pl.ds(pl.multiple_of(me * cols, 16), cols)], own_sem.at[0])
    own_lat = pltpu.make_async_copy(lat_shard, all_ref.at[:, pl.ds(pl.multiple_of(me * cols, 16), cols)], own_sem.at[1])
    own_pair.start()
    own_lat.start()
    my_rows = pl.ds(pl.multiple_of(blk * local_rows, 128), local_rows)
    other_rows = pl.ds(pl.multiple_of(other * local_rows, 128), local_rows)

    lat_out, _, _ = norm_keep(lat_ref[...].astype(F32), lgain_ref[...], lbias_ref[...])
    lat_low = lat_out.astype(BF16)
    latn_ref[...] = lat_low
    at_head = pl.ds(pl.multiple_of(core * head_dim, 16), head_dim)
    qt_ref[core, me, :, my_rows] = dot_nt(wq_ref[at_head], lat_low).astype(BF16)
    bup_all[me] = bup_ref[...]
    for d in range(1, shards):
        my_q = qt_ref.at[core, me, :, my_rows]
        pending.append(send(my_q, my_q, q_ss.at[0, d], q_rs.at[0, d], mesh_at(dh=z_back[d])))
    for d in range(1, shards):
        pending.append(send(bup_ref, bup_all.at[me], misc_ss.at[d], misc_rs.at[d], mesh_at(dh=z_back[d])))
    cols_ref[...] = jnp.transpose(rows_ref[...])

    def queries_z():
        for d in range(1, shards):
            wait_plain(qt_ref.at[core, z_of[d], :, my_rows], q_ss.at[0, d], q_rs.at[0, d])
        part = qt_ref.at[core, :, :, my_rows]
        pending.append(send(part, part, q_ss.at[1, 0], q_rs.at[1, 0], to_x))

    def queries_x():
        wait_plain(qt_ref.at[core, :, :, other_rows], q_ss.at[1, 0], q_rs.at[1, 0])
        pending.append(send(qt_ref.at[core], qt_ref.at[core], q_ss.at[1, 1], q_rs.at[1, 1], to_sib))

    def queries_sib():
        wait_plain(qt_ref.at[1 - core], q_ss.at[1, 1], q_rs.at[1, 1])

    def wait_plain(where, ss, rs):
        pltpu.make_async_remote_copy(src_ref=where, dst_ref=where, send_sem=ss, recv_sem=rs,
                                     device_id=to_sib, device_id_type=pl.DeviceIdType.MESH).wait_recv()

    piece = min(256, length)

    def norm_bytes(s):
        def norm_step(i, _):
            at = pl.ds(pl.multiple_of(i * piece, piece), piece)
            normed, _unused = norm_columns(x_ref[s, :, at], cols_ref[:, 2 + s:3 + s])
            xn_ref[s, :, at] = (normed * cols_ref[:, 0:1] + cols_ref[:, 1:2]).astype(BF16)
            return 0
        lax.fori_loop(0, length // piece, norm_step, 0)
        copy = pltpu.make_async_copy(xn_ref.at[s], xn_out.at[s], xn_sem.at[s])
        copy.start()
        local.append(copy)

    def project(d):
        at = pl.ds(pl.multiple_of(z_of[d] * cols, 16), cols)

        def step(i, _):
            s, part = i // 2, lax.rem(i, 2)
            kv_ref[s, part, at] = dot(pair_ref[part, at], xn_ref[s]).astype(BF16)
            return 0
        lax.fori_loop(0, 2 * seqs, step, 0)
        copy = pltpu.make_async_copy(kv_ref.at[:, :, at], kv_out.at[:, :, at], kv_sem.at[d])
        copy.start()
        local.append(copy)

    factor = LOG2E * head_dim ** (-0.5)
    lane = lax.broadcasted_iota(jnp.int32, (rows, 128), 1)
    stat_ref[...] = jnp.zeros_like(stat_ref)

    def turn_queries(d):
        for j in range(per_shard):
            h = z_of[d] * per_shard + j
            q_ref[h] = jnp.transpose(qt_ref[j, z_of[d]])

    def attend(d, s):
        def head_step(j, _):
            h = z_of[d] * per_shard + j
            at = pl.ds(pl.multiple_of(h * head_dim, 16), head_dim)
            scores = dot(q_ref[h], kv_ref[s, 0, at]) * factor + mask_ref[s]
            top = jnp.max(scores, axis=1, keepdims=True)
            weights = jnp.exp2(scores - top)
            total = jnp.sum(weights, axis=1, keepdims=True)
            out = dot_nt(kv_ref[s, 1, at], weights.astype(BF16))
            stat_ref[s] = jnp.where(lane == h, top + jnp.log2(total), stat_ref[s])
            inverse = jnp.transpose(jnp.broadcast_to(1.0 / total, (rows, 128)))[:1]
            o_tmp[...] = out * inverse
            o_own[s, at] = o_tmp[:, my_rows]
            o_send[s, at] = o_tmp[:, other_rows].astype(BF16)
            return 0
        lax.fori_loop(0, per_shard, head_step, 0)
        part = pl.ds(pl.multiple_of(z_of[d] * cols, 16), cols)
        pending.append(send(o_send.at[s, part], o_got.at[s, part], o_ss.at[d, s], o_rs.at[d, s], to_x))

    norm_bytes(0)
    after_z("pair", 1)
    queries_z()
    for s in range(1, seqs):
        norm_bytes(s)
    after_z("pair", 2)
    after_x("pair", 1)
    after_z("pair", 3)
    out_z("lat", 1)
    own_pair.wait()
    project(0)
    queries_x()
    after_x("pair", 2)
    after_y("pair", 1)
    after_x("pair", 3)
    queries_sib()
    turn_queries(0)
    attend(0, 0)
    after_y("pair", 2)
    after_y("pair", 3)
    after_z("lat", 1)
    out_z("lat", 2)
    for s in range(1, seqs):
        attend(0, s)
    after_z("lat", 2)
    out_z("lat", 3)
    after_x("lat", 1)
    after_sib("pair", 1)
    project(1)
    turn_queries(1)
    after_z("lat", 3)
    attend(1, 0)
    after_x("lat", 2)
    for s in range(1, seqs):
        attend(1, s)
    after_x("lat", 3)
    after_y("lat", 1)
    after_sib("pair", 2)
    project(2)
    turn_queries(2)
    for s in range(seqs):
        attend(2, s)
    after_y("lat", 2)
    after_sib("pair", 3)
    project(3)
    turn_queries(3)
    for s in range(seqs):
        attend(3, s)

    for s in range(seqs):
        at = pl.ds(s * heads, heads)
        stats = jnp.transpose(stat_ref[s])[:heads]
        stat_send[...] = stats
        stat_own[at] = stat_send[:, my_rows]
        stat_got[0, at] = stat_send[:, other_rows]
    pending.append(send(stat_got.at[0], stat_got.at[1], o_ss.at[shards, 0], o_rs.at[shards, 0], to_x))
    block = 256
    for part in range(2):
        for i in range(pair_ref.shape[1] // block):
            wcols_ref[part, :, i * block:(i + 1) * block] = jnp.transpose(pair_ref[part, i * block:(i + 1) * block])
    after_y("lat", 3)
    wait_plain(stat_got.at[1], o_ss.at[shards, 0], o_rs.at[shards, 0])
    own_lse, got_lse = stat_own[...], stat_got[1]
    top = jnp.maximum(own_lse, got_lse)
    own_share, got_share = jnp.exp2(own_lse - top), jnp.exp2(got_lse - top)
    total = own_share + got_share
    lse = top + jnp.log2(total)
    own_share, got_share = own_share / total, got_share / total
    for s in range(seqs):
        lse_ref[s] = lse[s * heads:(s + 1) * heads]
        for d in range(shards):
            part = pl.ds(pl.multiple_of(z_of[d] * cols, 16), cols)
            wait_plain(o_got.at[s, part], o_ss.at[d, s], o_rs.at[d, s])
    for s in range(seqs):
        for h in range(heads):
            at = slice(h * head_dim, (h + 1) * head_dim)
            n = s * heads + h
            att_ref[s, at] = o_own[s, at] * own_share[n:n + 1] + o_got[s, at].astype(F32) * got_share[n:n + 1]
    for d in range(1, shards):
        wait_plain(bup_all.at[z_of[d]], misc_ss.at[d], misc_rs.at[d])
    for d in range(1, shards):
        after_sib("lat", d)
    own_lat.wait()
    for copy in local:
        copy.wait()
    for copy in pending:
        copy.wait_send()


def first_call(x_cols, rows_in, mask, latents, lat_gain, lat_bias, wq_rows, pair_shard, lat_shard, b_up, rows):
    seqs, width, length = x_cols.shape
    local_rows, width_lat = latents.shape
    shards = lax.axis_size("heads")
    heads = HEADS
    head_dim = width_lat // heads
    whole = pl.BlockSpec(memory_space=pltpu.VMEM)
    hbm = pl.BlockSpec(memory_space=pl.ANY)
    out = jax.ShapeDtypeStruct
    sem = pltpu.SemaphoreType.DMA
    return pl.pallas_call(
        first_kernel,
        in_specs=[whole] * 10,
        out_specs=[whole, hbm, hbm, hbm] + [whole] * 5,
        out_shape=[
            out((2, width, width_lat), BF16),
            out((3, width_lat, width_lat), BF16),
            out((seqs, 2, width_lat, length), BF16),
            out((seqs, width, length), BF16),
            out((seqs, width_lat, local_rows), F32),
            out((seqs, heads, local_rows), F32),
            out((heads // shards, shards, head_dim, rows), BF16),
            out((local_rows, width_lat), BF16),
            out((shards,) + b_up.shape, F32),
        ],
        scratch_shapes=[
            pltpu.VMEM((seqs, width, length), BF16),
            pltpu.VMEM((2, width_lat, width), BF16),
            pltpu.VMEM((seqs, 2, width_lat, length), BF16),
            pltpu.VMEM((width, rows_in.shape[0]), F32),
            pltpu.VMEM((heads, rows, head_dim), BF16),
            pltpu.VMEM((head_dim, rows), F32),
            pltpu.VMEM((seqs, width_lat, local_rows), F32),
            pltpu.VMEM((seqs, width_lat, local_rows), BF16),
            pltpu.VMEM((seqs, width_lat, local_rows), BF16),
            pltpu.VMEM((seqs, rows, 128), F32),
            pltpu.VMEM((heads, rows), F32),
            pltpu.VMEM((seqs * heads, local_rows), F32),
            pltpu.VMEM((2, seqs * heads, local_rows), F32),
            sem((shards, 5)), sem((shards, 5)), sem((shards, 5)), sem((shards, 5)),
            sem((2, shards)), sem((2, shards)), sem((shards,)), sem((shards,)),
            sem((shards + 1, seqs)), sem((shards + 1, seqs)), sem((2,)), sem((seqs,)), sem((shards,)),
        ],
        compiler_params=pltpu.CompilerParams(vmem_limit_bytes=VMEM_LIMIT, collective_id=1, has_side_effects=True),
        name="first",
    )(x_cols, rows_in, mask, latents, lat_gain, lat_bias, wq_rows, pair_shard, lat_shard, b_up)


class Reduce:
    def __init__(self, src, half, got_sib, got_chip, got_z, out, ss, rs, pending, x_first=True, stage=None, stage_sem=None):
        self.src, self.half, self.got_sib, self.got_chip, self.got_z, self.out = src, half, got_sib, got_chip, got_z, out
        self.ss, self.rs, self.pending, self.x_first = ss, rs, pending, x_first
        self.stage, self.stage_sem, self.kept = stage, stage_sem, None
        self.split = src is not None and src.shape[3] == half.shape[3]
        items, blk, self.me, hi, self.core = places()
        self.shards = lax.axis_size("heads")
        other = 1 - blk
        self.chip = hi * 2 + blk
        self.chip_x, self.chip_y, self.chip_xy = hi * 2 + other, (1 - hi) * 2 + blk, (1 - hi) * 2 + other
        self.to_x, self.to_y = mesh_at(db=other), mesh_at(di=(1 - hi) * 2 + self.core)
        self.to_sib = mesh_at(di=items + 1 - 2 * self.core)
        self.n, _, self.cols, self.width = half.shape
        self.share = self.cols // 4
        self.near = self.me + 1 - 2 * lax.rem(self.me, 2)
        self.far, self.cross = lax.rem(self.me + 2, 4), lax.rem(self.near + 2, 4)

    def rows(self, chip):
        return pl.ds(pl.multiple_of(chip * self.share, 16), self.share)

    def lanes(self, core):
        return pl.ds(pl.multiple_of(core * self.width, 128), self.width)

    def go(self, src, dst, i, target):
        self.pending.append(send(src, dst, self.ss.at[i], self.rs.at[i], target))

    def arrived(self, where, i):
        pltpu.make_async_remote_copy(src_ref=where, dst_ref=where, send_sem=self.ss.at[i], recv_sem=self.rs.at[i],
                                     device_id=self.to_sib, device_id_type=pl.DeviceIdType.MESH).wait_recv()

    def start(self):
        theirs = self.src if self.split else self.src.at[:, :, :, self.lanes(1 - self.core)]
        self.go(theirs, self.got_sib, 0, self.to_sib)

    def join_sib(self):
        self.arrived(self.got_sib, 0)

        def step(i, _):
            n, h = i // self.shards, lax.rem(i, self.shards)
            own = self.half[n, h] if self.split else self.src[n, h, :, self.lanes(self.core)]
            self.half[n, h] = (own.astype(F32) + self.got_sib[n, h].astype(F32)).astype(self.half.dtype)
            return 0
        lax.fori_loop(0, self.n * self.shards, step, 0)

    def send_chips(self):
        low, high = pl.ds(0, 2), pl.ds(2, 2)
        self.go(self.half.at[:, low, self.rows(self.chip_x)], self.got_chip.at[0], 1, self.to_x)
        self.go(self.half.at[:, high, self.rows(self.chip_y)], self.got_chip.at[2], 3, self.to_y)
        self.go(self.half.at[:, low, self.rows(self.chip_xy)], self.got_chip.at[1], 2, self.to_x)
        self.go(self.half.at[:, high, self.rows(self.chip_xy)], self.got_chip.at[3], 4, self.to_y)

    def add(self, slot, first, rows):
        self.arrived(self.got_chip.at[slot], 1 + slot)
        for n in range(self.n):
            for h in range(2):
                total = self.half[n, first + h, rows].astype(F32) + self.got_chip[slot, n, h].astype(F32)
                self.half[n, first + h, rows] = total.astype(self.half.dtype)

    def join_first(self):
        self.add(1, 0, self.rows(self.chip_y))
        self.go(self.half.at[:, pl.ds(0, 2), self.rows(self.chip_y)], self.got_chip.at[4], 5, self.to_y)
        self.add(3, 2, self.rows(self.chip_x))
        self.go(self.half.at[:, pl.ds(2, 2), self.rows(self.chip_x)], self.got_chip.at[5], 6, self.to_x)
        self.add(0, 0, self.rows(self.chip))
        self.add(2, 2, self.rows(self.chip))

    def join_chips(self):
        mine = self.rows(self.chip)
        self.add(4, 0, mine)
        self.add(5, 2, mine)
        for i, shard in enumerate((self.near, self.cross)):
            self.go(self.half.at[:, shard, mine], self.got_z.at[i], 7 + i, mesh_at(dh=self.near))

    def join_near(self):
        mine = self.rows(self.chip)
        for i, shard in enumerate((self.me, self.far)):
            self.arrived(self.got_z.at[i], 7 + i)
            for n in range(self.n):
                total = self.half[n, shard, mine].astype(F32) + self.got_z[i, n].astype(F32)
                self.half[n, shard, mine] = total.astype(self.half.dtype)
        self.go(self.half.at[:, self.far, mine], self.got_z.at[2], 9, mesh_at(dh=self.far))

    def join_z(self):
        self.arrived(self.got_z.at[2], 9)
        mine = self.rows(self.chip)
        for n in range(self.n):
            total = self.half[n, self.me, mine].astype(F32) + self.got_z[2, n].astype(F32)
            if self.stage is None:
                self.out[n, mine, self.lanes(self.core)] = total.astype(self.out.dtype)
            else:
                self.stage[n] = total.astype(self.out.dtype)
        src = self.piece(self.chip)
        if self.stage is not None:
            self.kept = pltpu.make_async_copy(self.stage, src, self.stage_sem)
            self.kept.start()
            src = self.stage
        self.go(src, self.piece(self.chip), 10, self.to_x)
        self.go(src, self.piece(self.chip), 11, self.to_y)

    def piece(self, chip):
        return self.out.at[:, self.rows(chip), self.lanes(self.core)]

    def pass_on(self, chip, i, target):
        self.go(self.piece(chip), self.piece(chip), i, target)

    def share_chips(self):
        if self.x_first:
            self.arrived(self.piece(self.chip_x), 10)
            self.pass_on(self.chip_x, 12, self.to_y)
        else:
            self.arrived(self.piece(self.chip_y), 11)
            self.pass_on(self.chip_y, 12, self.to_x)

    def share_sib(self):
        if self.x_first:
            self.arrived(self.piece(self.chip_y), 11)
        else:
            self.arrived(self.piece(self.chip_x), 10)
        self.arrived(self.piece(self.chip_xy), 12)
        if self.kept is not None:
            self.kept.wait()
        half = self.out.at[:, :, self.lanes(self.core)]
        self.go(half, half, 13, self.to_sib)

    def finish(self):
        self.arrived(self.out.at[:, :, self.lanes(1 - self.core)], 13)


def second_kernel(x_hbm, rows_ref, mask_ref, w_ref, qt_ref, kv_hbm, xn_hbm, do_in, stat_in, mixed_in, lat_in, grads_hbm, vec_in, lang_in, latsum_in, wq_ref, lat_raw, lgain_ref,
                  g_out, mixed_out, dw_out, dlat_out, small_out, glat_out, vec_out, dwq_out,
                  x_ref, xn_ref, cols_ref, kv_ref, dkv_ref, q_ref, do_ref, stat_ref, stat_cols, dq_ref, dw_ref, dw_tmp,
                  g_half, g_chip, g_z, w_half, w_sib, w_chip, w_z, q_half, q_sib, q_chip, q_z, s_half, s_sib, s_chip, s_z,
                  small_ref, s_ref, l_sib, l_half, l_y, l_sum, l_z, l_tot, dq_out, latn_ref, lat8_ref,
                  g_stage, w_stage, tq_ref, t_part, t_got, t_z, y_buf, c_buf, x_buf, dwq_ref,
                  g_ss, g_rs, w_ss, w_rs, q_ss, q_rs, s_ss, s_rs, l_ss, l_rs, t_ss, t_rs, do_ss, do_rs, misc_ss, misc_rs, mix_ss, mix_rs, a_ss, a_rs, load_sem, kv_sem, stage_sem):
    items, blk, me, hi, core = places()
    shards = lax.axis_size("heads")
    seqs, width, length = x_ref.shape
    heads, rows, head_dim = q_ref.shape
    local_rows = rows // 2
    per_shard = heads // shards
    cols = per_shard * head_dim
    stat_rows = stat_in.shape[0]
    other = 1 - blk
    to_x, to_sib = mesh_at(db=other), mesh_at(di=items + 1 - 2 * core)
    to_y = mesh_at(di=(1 - hi) * 2 + core)
    z_of = [lax.rem(me + d, shards) for d in range(shards)]
    z_back = [lax.rem(me + shards - d, shards) for d in range(shards)]
    my_rows = pl.ds(pl.multiple_of(blk * local_rows, 128), local_rows)
    other_rows = pl.ds(pl.multiple_of(other * local_rows, 128), local_rows)
    pending = []
    dot_ref = w_sib.at[:, :, :, pl.ds(0, rows)]
    grads = [Reduce(None, g_half.at[pl.ds(m, 1)], None, g_chip.at[:, pl.ds(m, 1)], g_z.at[m], dlat_out.at[pl.ds(m, 1)], g_ss.at[m], g_rs.at[m], pending, m != 1,
                        g_stage.at[pl.ds(m, 1)], stage_sem.at[m])
             for m in range(3)]
    pair = [Reduce(dw_ref.at[pl.ds(m, 1)], w_half.at[pl.ds(m, 1)], w_sib.at[pl.ds(m, 1)], w_chip.at[:, pl.ds(m, 1)], w_z.at[m],
                   dw_out.at[pl.ds(m, 1)], w_ss.at[m], w_rs.at[m], pending, m == 0, w_stage.at[pl.ds(m, 1)], stage_sem.at[3 + m]) for m in range(2)]
    query = Reduce(dq_ref, q_half, q_sib, q_chip, q_z, dq_out, q_ss, q_rs, pending, False)
    small = Reduce(s_ref, s_half, s_sib, s_chip, s_z, small_out, s_ss, s_rs, pending)
    greet([to_sib, to_x, to_y] + [mesh_at(dh=z_of[d]) for d in range(1, shards)])

    def arrived(where, ss, rs):
        pltpu.make_async_remote_copy(src_ref=where, dst_ref=where, send_sem=ss, recv_sem=rs,
                                     device_id=to_sib, device_id_type=pl.DeviceIdType.MESH).wait_recv()

    pending.append(send(stat_in, stat_ref.at[pl.ds(0, stat_rows), my_rows], misc_ss.at[0], misc_rs.at[0], to_x))

    def send_do(s):
        pending.append(send(do_in.at[s], dot_ref.at[s, :, :, my_rows], do_ss.at[s], do_rs.at[s], to_x))

    mine = pl.ds(me * seqs, seqs)
    near = me + 1 - 2 * lax.rem(me, 2)
    far, cross = lax.rem(me + 2, 4), lax.rem(near + 2, 4)
    far_rows, near_rows, cross_rows = (pl.ds(at * seqs, seqs) for at in (far, near, cross))

    def mixed_far():
        pending.append(send(mixed_in, mixed_out.at[mine], mix_ss.at[0], mix_rs.at[0], mesh_at(dh=far)))

    def mixed_near():
        pending.append(send(mixed_in, mixed_out.at[mine], mix_ss.at[1], mix_rs.at[1], mesh_at(dh=near)))

    def mixed_cross():
        arrived(mixed_out.at[far_rows], mix_ss.at[0], mix_rs.at[0])
        pending.append(send(mixed_out.at[far_rows], mixed_out.at[far_rows], mix_ss.at[2], mix_rs.at[2], mesh_at(dh=near)))

    def latents_share():
        pending.append(send(lat_in, latn_ref.at[my_rows], misc_ss.at[1], misc_rs.at[1], to_x))

    loads = [
        pltpu.make_async_copy(xn_hbm, xn_ref, load_sem.at[0]),
        pltpu.make_async_copy(x_hbm, x_ref, load_sem.at[1]),
        pltpu.make_async_copy(grads_hbm, g_half, load_sem.at[2]),
        pltpu.make_async_copy(mixed_in, mixed_out.at[mine], load_sem.at[3]),
        pltpu.make_async_copy(lat_raw.at[pl.ds(pl.multiple_of(core * 64 + hi * 32 + me * 8, 8), 8)], lat8_ref, load_sem.at[4]),
    ]
    own_sum = pltpu.make_async_copy(latsum_in.at[pl.ds(pl.multiple_of(core * (local_rows // 2), 8), local_rows // 2)], l_half, load_sem.at[13])
    own_sum.start()
    latn_ref[my_rows] = lat_in[...]
    own_do = pltpu.make_async_copy(do_in, dot_ref.at[:, :, :, my_rows], load_sem.at[5])

    def load_pair(n, start):
        s, h = n // heads, lax.rem(n, heads)
        slot = lax.rem(n, 2)
        copy = pltpu.make_async_copy(kv_hbm.at[s, :, pl.ds(pl.multiple_of(h * head_dim, 16), head_dim)], kv_ref.at[slot], kv_sem.at[slot])
        copy.start() if start else copy.wait()

    load_pair(0, True)
    for copy in loads:
        copy.start()
    own_do.start()
    stat_ref[:stat_rows, my_rows] = stat_in[...]
    stat_ref[stat_rows:] = jnp.zeros((128 - stat_rows, rows), F32)
    for h in range(heads):
        q_ref[h] = jnp.transpose(qt_ref[h % per_shard, h // per_shard])
    dq_ref[...] = jnp.zeros_like(dq_ref)
    small_ref[...] = jnp.zeros_like(small_ref)

    def stats_ready():
        arrived(stat_ref.at[pl.ds(0, stat_rows), other_rows], misc_ss.at[0], misc_rs.at[0])
        stat_cols[...] = jnp.transpose(stat_ref[...])

    scale = head_dim ** (-0.5)
    factor = LOG2E * scale
    lane = lax.broadcasted_iota(jnp.int32, (rows, 128), 1)
    cols_ref[...] = jnp.transpose(rows_ref[...])
    gain = cols_ref[:, 0:1]

    def turn_grads(s):
        arrived(dot_ref.at[s, :, :, other_rows], do_ss.at[s], do_rs.at[s])
        for h in range(heads):
            inner = h % per_shard * head_dim
            do_ref[h] = jnp.transpose(dot_ref[s, h // per_shard, inner:inner + head_dim])

    def head_steps(s, group):
        def head_step(h, _):
            n = s * heads + h
            slot = lax.rem(n, 2)
            load_pair(n, False)

            @pl.when(n + 1 < seqs * heads)
            def _():
                load_pair(n + 1, True)

            at = pl.ds(pl.multiple_of(h * head_dim, 16), head_dim)
            lse = jnp.sum(jnp.where(lane == s * 2 * heads + h, stat_cols[...], 0.0), axis=1, keepdims=True)
            delta = jnp.sum(jnp.where(lane == s * 2 * heads + heads + h, stat_cols[...], 0.0), axis=1, keepdims=True)
            keys = kv_ref[slot, 0]
            weights = jnp.exp2(dot(q_ref[h], keys) * factor + mask_ref[s] - lse)
            part = pl.ds(pl.multiple_of(lax.rem(h, per_shard) * head_dim, 16), head_dim)
            dkv_ref[s, 1, at] = dot(dot_ref[s, h // per_shard, part], weights.astype(BF16)).astype(BF16)
            grad = dot(do_ref[h], kv_ref[slot, 1]) - delta
            grad = (weights * grad).astype(BF16)
            dkv_ref[s, 0, at] = (dot(qt_ref[lax.rem(h, per_shard), h // per_shard], grad) * scale).astype(BF16)
            dq_ref[0, h // per_shard, part] += dot_nt(keys, grad) * scale
            return 0

        lax.fori_loop(2 * group, 2 * group + 2, head_step, 0)

    piece = min(256, length)

    def byte_steps(s):
        def byte_step(i, carry):
            at = pl.ds(pl.multiple_of(i * piece, piece), piece)
            grad = dot(w_ref[0], dkv_ref[s, 0, :, at]) + dot(w_ref[1], dkv_ref[s, 1, :, at])
            normed, inverse = norm_columns(x_ref[s, :, at], cols_ref[:, 2 + s:3 + s])
            small_ref[:, 0:1] += jnp.sum(grad * normed, axis=1, keepdims=True)
            small_ref[:, 1:2] += jnp.sum(grad, axis=1, keepdims=True)
            scaled = grad * gain
            first = jnp.mean(scaled, axis=0, keepdims=True)
            second = jnp.mean(scaled * normed, axis=0, keepdims=True)
            shifted = (scaled - first - normed * second) * inverse
            x_ref[s, :, at] = shifted.astype(BF16)
            return carry + jnp.sum(shifted, axis=1, keepdims=True)

        small_ref[:, 2 + s:3 + s] = lax.fori_loop(0, length // piece, byte_step, jnp.zeros((width, 1), F32))
        share = width // shards
        own = pltpu.make_async_copy(x_ref.at[s, pl.ds(pl.multiple_of(me * share, 16), share)], g_out.at[me * seqs + s], load_sem.at[6 + s])
        own.start()
        loads.append(own)

    def bytes_send(s, d):
        share = width // shards
        there = pl.ds(pl.multiple_of(z_back[d] * share, 16), share)
        pending.append(send(x_ref.at[s, there], g_out.at[me * seqs + s], a_ss.at[s, d], a_rs.at[s, d], mesh_at(dh=z_back[d])))

    half_rows, quarter = local_rows // 2, local_rows // 4
    piece_rows = quarter // shards

    def latents_send():
        theirs = latsum_in.at[pl.ds(pl.multiple_of((1 - core) * half_rows, 8), half_rows)]
        pending.append(send(theirs, l_sib, l_ss.at[0], l_rs.at[0], to_sib))

    def latents_sib():
        arrived(l_sib, l_ss.at[0], l_rs.at[0])
        own_sum.wait()
        l_half[...] += l_sib[...]
        pending.append(send(l_half.at[pl.ds(pl.multiple_of((1 - hi) * quarter, 8), quarter)], l_y, l_ss.at[1], l_rs.at[1], to_y))

    def latents_y():
        arrived(l_y, l_ss.at[1], l_rs.at[1])
        l_sum[...] = (l_half[pl.ds(pl.multiple_of(hi * quarter, 8), quarter)] + l_y[...]).reshape(l_sum.shape)
        for d in range(1, shards):
            pending.append(send(l_sum.at[z_back[d]], l_z.at[d - 1], l_ss.at[1 + d], l_rs.at[1 + d], mesh_at(dh=z_back[d])))

    def latents_z():
        total = l_sum[me]
        for d in range(1, shards):
            arrived(l_z.at[d - 1], l_ss.at[1 + d], l_rs.at[1 + d])
            total += l_z[d - 1]
        l_tot[...] = total

    def third_first():
        tq_ref[...] = jnp.transpose(dq_out[0, :, my_rows])
        rows_here = tq_ref[pl.ds(pl.multiple_of(core * half_rows + hi * quarter, 8), quarter)].astype(BF16)
        t_part[...] = dot_nt(rows_here, wq_ref[...]).reshape(t_part.shape)
        for d in range(1, shards):
            pending.append(send(t_part.at[z_back[d]], t_got.at[d - 1], t_ss.at[0, d], t_rs.at[0, d], mesh_at(dh=z_back[d])))

    def third_z():
        grad = t_part[me]
        for d in range(1, shards):
            arrived(t_got.at[d - 1], t_ss.at[0, d], t_rs.at[0, d])
            grad += t_got[d - 1]
        loads[4].wait()
        _, normed, inverse = norm_keep(lat8_ref[...], 1.0, 0.0)
        t_z[me, :piece_rows] = l_tot[...] + norm_back(grad, normed, inverse, lgain_ref[...])
        t_z[me, piece_rows:] = jnp.zeros((8, lat8_ref.shape[1]), F32)
        t_z[me, piece_rows:piece_rows + 1] = jnp.sum(grad * normed, axis=0, keepdims=True)
        t_z[me, piece_rows + 1:piece_rows + 2] = jnp.sum(grad, axis=0, keepdims=True)
        for d in range(1, shards):
            pending.append(send(t_z.at[me], t_z.at[me], t_ss.at[1, d], t_rs.at[1, d], mesh_at(dh=z_back[d])))

    def third_y():
        for d in range(1, shards):
            arrived(t_z.at[z_of[d]], t_ss.at[1, d], t_rs.at[1, d])
        y_buf[hi, :quarter] = t_z[:, :piece_rows].reshape(quarter, t_z.shape[2])
        y_buf[hi, quarter:] = t_z[0, piece_rows:] + t_z[1, piece_rows:] + t_z[2, piece_rows:] + t_z[3, piece_rows:]
        pending.append(send(y_buf.at[hi], y_buf.at[hi], t_ss.at[2, 0], t_rs.at[2, 0], to_y))

    def third_core():
        arrived(y_buf.at[1 - hi], t_ss.at[2, 0], t_rs.at[2, 0])
        c_buf[core, :quarter] = y_buf[0, :quarter]
        c_buf[core, quarter:half_rows] = y_buf[1, :quarter]
        c_buf[core, half_rows:] = y_buf[0, quarter:] + y_buf[1, quarter:]
        pending.append(send(c_buf.at[core], c_buf.at[core], t_ss.at[2, 1], t_rs.at[2, 1], to_sib))

    def third_x():
        arrived(c_buf.at[1 - core], t_ss.at[2, 1], t_rs.at[2, 1])
        glat_out[:half_rows] = c_buf[0, :half_rows]
        glat_out[half_rows:] = c_buf[1, :half_rows]
        x_buf[blk] = c_buf[0, half_rows:] + c_buf[1, half_rows:]
        pending.append(send(x_buf.at[blk], x_buf.at[blk], t_ss.at[2, 2], t_rs.at[2, 2], to_x))

    def third_end():
        arrived(x_buf.at[other], t_ss.at[2, 2], t_rs.at[2, 2])
        vec_out[...] = x_buf[0] + x_buf[1]

    def query_weights():
        arrived(latn_ref.at[other_rows], misc_ss.at[1], misc_rs.at[1])
        query_low = dq_out[0].astype(BF16)
        for i in range(dwq_out.shape[0] // 256):
            if i:
                loads[-1].wait()
            dwq_ref[...] = dot_nt(jnp.transpose(latn_ref[:, i * 256:(i + 1) * 256]), query_low)
            copy = pltpu.make_async_copy(dwq_ref, dwq_out.at[pl.ds(i * 256, 256)], load_sem.at[8 + i])
            copy.start()
            loads.append(copy)

    def small_start():
        wide_lane = lax.broadcasted_iota(jnp.int32, (width, 128), 1)
        block = jnp.where(wide_lane == 32, small_ref[:, 0:1], 0.0) + jnp.where(wide_lane == 33, small_ref[:, 1:2], 0.0)
        for s in range(seqs):
            block += small_ref[:, 2 + s:3 + s] * lang_in[s:s + 1]
        share = width // shards
        for h in range(shards):
            s_ref[0, h, :, :128] = block[h * share:(h + 1) * share]
            s_ref[0, h, :, 128:] = jnp.zeros((share, 128), F32)
            s_ref[0, h, :vec_in.shape[0], 128:] = vec_in[...]
        small.start()

    def weight_steps(part):
        def weight_step(h, _):
            at = pl.ds(pl.multiple_of(h * cols, 16), cols)
            total = dot_nt(dkv_ref[0, part, at], xn_ref[0])
            for s in range(1, seqs):
                total += dot_nt(dkv_ref[s, part, at], xn_ref[s])
            dw_tmp[...] = total.astype(BF16)
            w_half[part, h] = dw_tmp[:, pl.ds(pl.multiple_of(core * (width // 2), 128), width // 2)]
            dw_ref[part, h] = dw_tmp[:, pl.ds(pl.multiple_of((1 - core) * (width // 2), 128), width // 2)]
            return 0
        lax.fori_loop(0, shards, weight_step, 0)

    mixed_far()
    send_do(0)
    mixed_near()
    own_do.wait()
    stats_ready()
    turn_grads(0)
    send_do(1)
    head_steps(0, 0)
    head_steps(0, 1)
    loads[2].wait()
    grads[0].send_chips()
    head_steps(0, 2)
    head_steps(0, 3)
    loads[1].wait()
    byte_steps(0)
    bytes_send(0, 3)
    grads[2].send_chips()
    bytes_send(0, 1)
    turn_grads(1)
    head_steps(1, 0)
    head_steps(1, 1)
    head_steps(1, 2)
    head_steps(1, 3)
    query.start()
    grads[2].join_first()
    bytes_send(0, 2)
    loads[0].wait()
    weight_steps(0)
    latents_send()
    query.join_sib()
    query.send_chips()
    grads[2].join_chips()
    latents_sib()
    byte_steps(1)
    grads[0].join_first()
    small_start()
    query.join_first()
    query.join_chips()
    pair[0].start()
    grads[0].join_chips()
    grads[1].send_chips()
    small.join_sib()
    small.send_chips()
    grads[2].join_near()
    pair[0].join_sib()
    pair[0].send_chips()
    bytes_send(1, 3)
    bytes_send(1, 1)
    query.join_near()
    small.join_first()
    query.join_z()
    latents_y()
    weight_steps(1)
    pair[0].join_first()
    grads[1].join_first()
    pair[1].start()
    grads[0].join_near()
    grads[2].join_z()
    pair[0].join_chips()
    latents_z()
    query.share_chips()
    query.share_sib()
    query.finish()
    small.join_chips()
    grads[0].join_z()
    grads[1].join_chips()
    small.join_near()
    latents_share()
    grads[2].share_chips()
    grads[0].share_chips()
    pair[0].join_near()
    small.join_z()
    third_first()
    pair[1].join_sib()
    mixed_cross()
    pair[1].send_chips()
    grads[1].join_near()
    third_z()
    pair[0].join_z()
    pair[1].join_first()
    pair[1].join_chips()
    small.share_chips()
    bytes_send(1, 2)
    third_y()
    grads[1].join_z()
    pair[1].join_near()
    small.share_sib()
    grads[1].share_chips()
    pair[0].share_chips()
    query_weights()
    grads[2].share_sib()
    pair[1].join_z()
    grads[1].share_sib()
    grads[0].share_sib()
    third_core()
    pair[1].share_chips()
    third_x()
    small.finish()
    pair[0].share_sib()
    pair[1].share_sib()
    pair[0].finish()
    third_end()
    pair[1].finish()
    grads[2].finish()
    grads[0].finish()
    grads[1].finish()
    arrived(mixed_out.at[near_rows], mix_ss.at[1], mix_rs.at[1])
    arrived(mixed_out.at[cross_rows], mix_ss.at[2], mix_rs.at[2])
    for d in range(1, shards):
        for s in range(seqs):
            arrived(g_out.at[z_of[d] * seqs + s], a_ss.at[s, d], a_rs.at[s, d])
    loads[3].wait()
    for own in loads[5:5 + seqs] + loads[-1:]:
        own.wait()
    for copy in pending:
        copy.wait_send()


def second_call(x_cols, rows_in, mask, w_cols, qt, pairs, xn, grad_out, stats, mixed, lat_low, grads, vectors, lang_rows, lat_sum, w_query, lat_f32, lat_gain):
    seqs, width, length = x_cols.shape
    rows, width_lat = qt.shape[3], pairs.shape[2]
    local_rows = lat_low.shape[0]
    shards = lax.axis_size("heads")
    heads = HEADS
    head_dim = width_lat // heads
    cols = width_lat // shards
    share = cols // 4
    whole = pl.BlockSpec(memory_space=pltpu.VMEM)
    hbm = pl.BlockSpec(memory_space=pl.ANY)
    out = jax.ShapeDtypeStruct
    vmem = pltpu.VMEM
    sem = pltpu.SemaphoreType.DMA

    assert seqs == 2

    def reduce_buffers(n, lanes, kind, cols=cols):
        half, share = lanes // 2, cols // 4
        return [vmem((n, shards, cols, half), kind), vmem((n, shards, cols, half), kind), vmem((6, n, 2, share, half), kind),
                vmem((shards - 1, n, share, half), kind)]

    return pl.pallas_call(
        second_kernel,
        in_specs=[hbm, whole, whole, whole, whole, hbm, hbm, hbm, whole, hbm, whole, hbm, whole, whole, hbm, whole, hbm, whole],
        out_specs=[hbm, hbm, hbm, hbm, whole, whole, whole, hbm],
        out_shape=[
            out((shards * seqs, width // shards, length), BF16),
            out((shards * seqs, local_rows, width_lat), BF16),
            out((2, cols, width), BF16),
            out((3, cols, width_lat), BF16),
            out((1, width // shards, 256), F32),
            out((local_rows, width_lat), F32),
            out((8, width_lat), F32),
            out((width_lat, cols), F32),
        ],
        scratch_shapes=[
            vmem((seqs, width, length), BF16),
            vmem((seqs, width, length), BF16),
            vmem((width, rows_in.shape[0]), F32),
            vmem((2, 2, head_dim, length), BF16),
            vmem((seqs, 2, width_lat, length), BF16),
            vmem((heads, rows, head_dim), BF16),
            vmem((heads, rows, head_dim), BF16),
            vmem((128, rows), F32),
            vmem((rows, 128), F32),
            vmem((1, shards, cols, rows), F32),
            vmem((2, shards, cols, width // 2), BF16),
            vmem((cols, width), BF16),
        ] + [
            vmem((3, shards, cols, width_lat // 2), BF16),
            vmem((6, 3, 2, share, width_lat // 2), BF16),
            vmem((3, 3, 1, share, width_lat // 2), BF16),
        ] + reduce_buffers(2, width, BF16)[:3] + [vmem((2, 3, 1, share, width // 2), BF16)]
        + reduce_buffers(1, rows, F32)
        + reduce_buffers(1, 256, F32, width // shards) + [
            vmem((width, 8), F32),
            vmem((1, shards, width // shards, 256), F32),
            vmem((local_rows // 2, width_lat), F32),
            vmem((local_rows // 2, width_lat), F32),
            vmem((local_rows // 4, width_lat), F32),
            vmem((shards, local_rows // 16, width_lat), F32),
            vmem((shards - 1, local_rows // 16, width_lat), F32),
            vmem((local_rows // 16, width_lat), F32),
            vmem((1, cols, rows), F32),
            vmem((rows, width_lat), BF16),
            vmem((local_rows // 16, width_lat), F32),
            vmem((3, share, width_lat // 2), BF16),
            vmem((2, share, width // 2), BF16),
            vmem((local_rows, cols), F32),
            vmem((shards, local_rows // 16, width_lat), F32),
            vmem((shards - 1, local_rows // 16, width_lat), F32),
            vmem((shards, local_rows // 16 + 8, width_lat), F32),
            vmem((2, local_rows // 4 + 8, width_lat), F32),
            vmem((2, local_rows // 2 + 8, width_lat), F32),
            vmem((2, 8, width_lat), F32),
            vmem((256, cols), F32),
        ] + [sem((3, 14))] * 2 + [sem((2, 14))] * 2 + [sem((14,))] * 4 + [sem((6,))] * 2 + [sem((3, shards))] * 2 + [sem((seqs,))] * 2 + [sem((2,))] * 2 + [sem((shards,))] * 2 + [sem((seqs, shards))] * 2
        + [sem((16,)), sem((2,)), sem((5,))],
        compiler_params=pltpu.CompilerParams(vmem_limit_bytes=VMEM_LIMIT, collective_id=2, has_side_effects=True),
        name="second",
    )(x_cols, rows_in, mask, w_cols, qt, pairs, xn, grad_out, stats, mixed, lat_low, grads, vectors, lang_rows, lat_sum, w_query, lat_f32, lat_gain)


def middle_kernel(att_ref, lat_ref, cot_ref, all_ref, bup_ref, bdown_ref, gain_ref, bias_ref, lse_ref,
                  mixed_ref, do_ref, stat_ref, half_ref, vec_ref, sum_ref,
                  rows_ref, mid_ref, low_ref, hid_ref, norm_ref, a_ref, b_src, b_ref, a_ss, a_rs, b_ss, b_rs):
    items, _, _, _, core = places()
    to_sib = mesh_at(di=items + 1 - 2 * core)
    seqs, width, local_rows = att_ref.shape
    rows = seqs * local_rows
    heads = lse_ref.shape[1]
    head_dim = width // heads
    half = width // 2
    block = 256
    pending = []
    greet([to_sib])

    def block_loop(body):
        def step(i, _):
            body(pl.ds(pl.multiple_of(i * block, block), block))
            return 0
        lax.fori_loop(0, width // block, step, 0)

    def share_a(i):
        pending.append(send(a_ref.at[i, 0], a_ref.at[i, 1], a_ss.at[i], a_rs.at[i], to_sib))

    def share_b(i):
        theirs = b_src.at[i, :, pl.ds(pl.multiple_of((1 - core) * half, 128), half)]
        pending.append(send(theirs, b_ref.at[i, 1], b_ss.at[i], b_rs.at[i], to_sib))
        b_ref[i, 0] = b_src[i, :, pl.ds(pl.multiple_of(core * half, 128), half)]

    cot = cot_ref[...]
    b_src[2] = cot
    share_b(2)
    for s in range(seqs):
        at = slice(s * local_rows, (s + 1) * local_rows)
        low = att_ref[s].astype(BF16)
        a_ref[0, 0, :, at] = low
        rows_ref[at] = jnp.transpose(att_ref[s]).astype(BF16)
    share_a(0)

    def branch(at):
        latent = lat_ref[:, at].astype(F32)
        mid_ref[:, at] = dot(rows_ref[...], all_ref[0, :, at]) + jnp.concatenate([latent] * seqs, axis=0)
    block_loop(branch)
    mid_out, normed, inverse = norm_keep(mid_ref[...], gain_ref[...], bias_ref[...])
    norm_ref[...] = normed
    b_src[1] = mid_out.astype(BF16)
    share_b(1)

    def up(at):
        value = dot_nt(b_src[1], all_ref[1, at]) + bup_ref[:, at]
        square = value * value
        bend = jnp.tanh(0.7978845608028654 * (value + 0.044715 * (square * value)))
        active = 0.5 * value * (1.0 + bend)
        slope = 0.5 * (1.0 + bend) + 0.5 * value * (1.0 - bend * bend) * (0.7978845608028654 * (1.0 + 0.134145 * square))
        rows_ref[:, at] = active.astype(BF16)
        grad = (dot_nt(cot_ref[...], all_ref[2, at]) * slope).astype(BF16)
        low_ref[:, at] = grad
        vec_ref[2:3, at] = jnp.sum(grad.astype(F32), axis=0, keepdims=True)
        a_ref[2, 0, at] = jnp.transpose(active.astype(BF16))
        a_ref[1, 0, at] = jnp.transpose(grad)
    block_loop(up)
    share_a(2)
    share_a(1)

    def down(at):
        hid_ref[:, at] = dot(low_ref[...], all_ref[1, :, at])
        out = mid_ref[:, at] + dot(rows_ref[...], all_ref[2, :, at]) + bdown_ref[:, at]
        for s in range(seqs):
            mixed_ref[s, :, at] = out[s * local_rows:(s + 1) * local_rows].astype(BF16)
    block_loop(down)
    grad = hid_ref[...]
    normed = norm_ref[...]
    vec_ref[0:1] = jnp.sum(grad * normed, axis=0, keepdims=True)
    vec_ref[1:2] = jnp.sum(grad, axis=0, keepdims=True)
    vec_ref[3:4] = jnp.sum(cot_ref[...].astype(F32), axis=0, keepdims=True)
    grad = cot_ref[...].astype(F32) + norm_back(grad, normed, inverse, gain_ref[...])
    b_src[0] = grad.astype(BF16)
    share_b(0)
    total = grad[:local_rows]
    for s in range(1, seqs):
        total += grad[s * local_rows:(s + 1) * local_rows]
    sum_ref[...] = total

    def out(h, _):
        at = pl.ds(pl.multiple_of(h * head_dim, 16), head_dim)
        grad = dot_nt(all_ref[0, at], b_src[0]).astype(BF16)
        for s in range(seqs):
            part = grad[:, s * local_rows:(s + 1) * local_rows]
            do_ref[s, at] = part
            delta = jnp.sum(part.astype(F32) * att_ref[s, at], axis=0, keepdims=True)
            stat_ref[pl.ds((2 * s + 1) * heads + h, 1)] = delta
        return 0
    lax.fori_loop(0, heads, out, 0)
    for s in range(seqs):
        stat_ref[2 * s * heads:(2 * s + 1) * heads] = lse_ref[s]

    def arrived(where, ss, rs):
        pltpu.make_async_remote_copy(src_ref=where, dst_ref=where, send_sem=ss, recv_sem=rs,
                                     device_id=to_sib, device_id_type=pl.DeviceIdType.MESH).wait_recv()

    shards, cols = half_ref.shape[1:3]
    for i in (2, 1, 0):
        arrived(a_ref.at[i, 1], a_ss.at[i], a_rs.at[i])
        arrived(b_ref.at[i, 1], b_ss.at[i], b_rs.at[i])

        def weight(h, _):
            at = pl.ds(pl.multiple_of(h * cols, 16), cols)
            half_ref[i, h] = (dot(a_ref[i, 0, at], b_ref[i, 0]) + dot(a_ref[i, 1, at], b_ref[i, 1])).astype(BF16)
            return 0
        lax.fori_loop(0, shards, weight, 0)
    for copy in pending:
        copy.wait_send()


def middle_call(att, latents, cot, weights, b_up, b_down, gain, bias, lse):
    seqs, width, local_rows = att.shape
    rows = seqs * local_rows
    heads = lse.shape[1]
    shards = lax.axis_size("heads")
    whole = pl.BlockSpec(memory_space=pltpu.VMEM)
    out, vmem, sem = jax.ShapeDtypeStruct, pltpu.VMEM, pltpu.SemaphoreType.DMA
    return pl.pallas_call(
        middle_kernel,
        in_specs=[whole] * 9,
        out_specs=[whole] * 6,
        out_shape=[
            out((seqs, local_rows, width), BF16),
            out((seqs, width, local_rows), BF16),
            out((2 * seqs * heads, local_rows), F32),
            out((3, shards, width // shards, width // 2), BF16),
            out((4, width), F32),
            out((local_rows, width), F32),
        ],
        scratch_shapes=[
            vmem((rows, width), BF16), vmem((rows, width), F32), vmem((rows, width), BF16), vmem((rows, width), F32), vmem((rows, width), F32),
            vmem((3, 2, width, rows), BF16), vmem((3, rows, width), BF16), vmem((3, 2, rows, width // 2), BF16),
            sem((3,)), sem((3,)), sem((3,)), sem((3,)),
        ],
        compiler_params=pltpu.CompilerParams(vmem_limit_bytes=VMEM_LIMIT, collective_id=4, has_side_effects=True),
        name="middle",
    )(att, latents, cot, weights, b_up, b_down, gain, bias, lse)


REST = ("items", "blk")
ALL = ("heads", "items", "blk")


def gather_rows(shard):
    count = lax.axis_size("items") * lax.axis_size("blk")
    me = lax.axis_index("items") * lax.axis_size("blk") + lax.axis_index("blk")
    share = shard.shape[0] // count
    part = lax.dynamic_slice_in_dim(shard, me * share, share, 0)
    return lax.all_gather(part, ALL, axis=0, tiled=True)


def scatter_rows(whole):
    part = lax.psum_scatter(whole.astype(BF16), ALL, scatter_dimension=0, tiled=True)
    return lax.all_gather(part, REST, axis=0, tiled=True)


def general_device(inputs, padding, language, lang_table, latents, in_gain, in_bias, lat_gain, lat_bias, mid_gain, mid_bias,
              w_query, w_key, w_value, w_out, w_up, b_up, w_down, b_down, cotangent):
    length, local_seqs, width = inputs.shape
    local_rows, width_lat = latents.shape
    cols = w_query.shape[1]
    head_dim = width_lat // HEADS
    per_shard = cols // head_dim
    shards = lax.axis_size("heads")
    blocks = lax.axis_size("blk")
    rows = local_rows * blocks
    seqs = local_seqs // shards
    me = lax.axis_index("heads")
    first = me * seqs

    pair_shard = jnp.concatenate([w_key.T, w_value.T], axis=0)
    pair_rows = gather_rows(pair_shard)
    latent_shard = jnp.concatenate([w_out, w_up.T, w_down], axis=0)
    lat_all = gather_rows(latent_shard).reshape(shards, 3, cols, width_lat)
    out_all, up_all, down_all = (lat_all[:, i].reshape(width_lat, width_lat) for i in range(3))

    all_latents = lax.all_gather(latents, "blk", axis=0, tiled=True).astype(F32)
    lat_out, _, _ = norm_keep(all_latents, lat_gain, lat_bias)
    lat_low = lat_out.astype(BF16)
    query_part = dot(lat_low, w_query).astype(BF16)
    queries = lax.all_gather(query_part, "heads", axis=1, tiled=True)
    q = queries.reshape(rows, HEADS, head_dim).transpose(1, 0, 2)

    own = lax.dynamic_slice_in_dim(inputs, first, seqs, 1)
    x_cols = jnp.transpose(own, (1, 2, 0))
    live = jnp.transpose(lax.dynamic_slice_in_dim(padding, first, seqs, 1))
    mask = jnp.where(live > 0, 0.0, MASKED).astype(F32)[:, None, :]
    own_lang = lax.dynamic_slice_in_dim(language, first, seqs, 0)
    onehot = (own_lang[:, None] == jnp.arange(lang_table.shape[0], dtype=jnp.int32)[None, :]).astype(F32)
    emb = jnp.dot(onehot, lang_table.astype(F32), precision=lax.Precision.HIGHEST)[:, :, None]
    gain_col, bias_col = in_gain[:, None], in_bias[:, None]

    pairs, o_cols, lse = forward_call(x_cols, emb, gain_col, bias_col, pair_rows, q, mask, per_shard)

    parts = o_cols.reshape(seqs, width_lat, blocks, local_rows).transpose(2, 0, 3, 1)
    parts = lax.all_to_all(parts, "blk", 0, 0, tiled=True).astype(F32)
    lse_parts = lse.reshape(seqs, HEADS, blocks, local_rows).transpose(2, 0, 3, 1)
    lse_parts = lax.all_to_all(lse_parts, "blk", 0, 0, tiled=True)
    top = jnp.max(lse_parts, axis=0)
    shares = jnp.exp2(lse_parts - top)
    total = jnp.sum(shares, axis=0)
    own_lse = top + jnp.log2(total)
    shares = shares / total
    attended = jnp.sum(parts.reshape(blocks, seqs, local_rows, HEADS, head_dim) * shares[..., None], axis=0)
    att_low = attended.reshape(seqs * local_rows, width_lat).astype(BF16)

    cot = lax.dynamic_slice_in_dim(cotangent, first, seqs, 0).reshape(seqs * local_rows, width_lat)
    lat_f32 = latents.astype(F32)
    middle = (lat_f32[None] + dot(att_low, out_all).reshape(seqs, local_rows, width_lat)).reshape(seqs * local_rows, width_lat)
    mid_out, mid_normed, mid_inverse = norm_keep(middle, mid_gain, mid_bias)
    mid_low = mid_out.astype(BF16)
    b_up_all = lax.all_gather(b_up, "heads", axis=0, tiled=True)
    hidden = dot_nt(mid_low, up_all) + b_up_all
    active, gelu_back = jax.vjp(jax.nn.gelu, hidden)
    active_low = active.astype(BF16)
    own_mixed = (middle + dot(active_low, down_all) + b_down).astype(BF16).reshape(seqs, local_rows, width_lat)
    mixed_latents = lax.all_gather(own_mixed, "heads", axis=0, tiled=True)

    grad_b_down = jnp.sum(cot.astype(F32), axis=0)
    grad_w_down = dot(active_low.T, cot)
    grad_active = dot_nt(cot, down_all)
    grad_hidden = gelu_back(grad_active)[0].astype(BF16)
    grad_b_up = jnp.sum(grad_hidden.astype(F32), axis=0)
    grad_w_up = dot(grad_hidden.T, mid_low)
    grad_mid_norm = dot(grad_hidden, up_all)
    grad_mid_gain = jnp.sum(grad_mid_norm * mid_normed, axis=0)
    grad_mid_bias = jnp.sum(grad_mid_norm, axis=0)
    grad_middle = cot.astype(F32) + norm_back(grad_mid_norm, mid_normed, mid_inverse, mid_gain)
    grad_branch = grad_middle.astype(BF16)
    grad_w_out = dot(att_low.T, grad_branch)
    grad_att = dot_nt(grad_branch, out_all).astype(BF16).reshape(seqs, local_rows, width_lat)
    grad_att_heads = grad_att.reshape(seqs, local_rows, HEADS, head_dim)
    delta = jnp.sum(grad_att_heads.astype(F32) * attended, axis=-1)
    lat_sum = jnp.sum(grad_middle.reshape(seqs, local_rows, width_lat), axis=0)

    all_grad_att = lax.all_gather(grad_att, "blk", axis=1, tiled=True).reshape(seqs, rows, HEADS, head_dim)
    stats = lax.all_gather(jnp.concatenate([own_lse, delta], axis=-1), "blk", axis=1, tiled=True)
    stats = jnp.transpose(stats, (0, 2, 1))[..., None]
    g_cols, dw_pair, dq, dgain, dbias, demb = backward_call(
        x_cols, emb, gain_col, bias_col, pair_rows.T, q, q.transpose(0, 2, 1),
        all_grad_att.transpose(0, 2, 1, 3), all_grad_att.transpose(0, 2, 3, 1),
        stats[:, :HEADS], stats[:, HEADS:], mask, pairs, per_shard)

    send = g_cols.reshape(seqs, shards, width // shards, length).transpose(1, 0, 2, 3)
    got = lax.all_to_all(send, "heads", 0, 0, tiled=True)
    grad_inputs = got.reshape(local_seqs, width // shards, length).transpose(2, 0, 1)

    grad_rows = jnp.stack([grad_w_out, grad_w_up, grad_w_down], axis=0).reshape(3, shards, cols, width_lat)
    lat_total = scatter_rows(grad_rows.transpose(1, 0, 2, 3).reshape(-1, width_lat)).astype(F32)
    pair_total = scatter_rows(dw_pair).astype(F32)

    dq_part = lax.psum_scatter(dq.reshape(width_lat, rows).astype(BF16), "heads", scatter_dimension=0, tiled=True)
    query_low = lax.psum(dq_part, REST)
    grad_w_query = dot(lat_low.T, query_low.T)
    lat_mine = lax.dynamic_slice_in_dim(query_low, lax.axis_index("blk") * local_rows, local_rows, 1)
    grad_lat_part = dot(lat_mine.T, w_query.T)
    grad_lat_norm = lax.psum(grad_lat_part.astype(BF16), "heads").astype(F32)
    lat_sum = lax.psum(lat_sum.astype(BF16), ("heads", "items")).astype(F32)
    _, own_normed, own_inverse = norm_keep(lat_f32, lat_gain, lat_bias)
    grad_latents = lat_sum + norm_back(grad_lat_norm, own_normed, own_inverse, lat_gain)
    lat_small = jnp.concatenate([jnp.sum(grad_lat_norm * own_normed, axis=0), jnp.sum(grad_lat_norm, axis=0)])
    lat_small = lax.psum(lat_small, "blk")

    table = jnp.dot(onehot.T, demb[:, :, 0], precision=lax.Precision.HIGHEST)
    small = jnp.concatenate([table.reshape(-1), dgain[:, 0], dbias[:, 0], grad_mid_gain, grad_mid_bias, grad_b_up, grad_b_down])
    small = lax.psum(small, ALL)
    sizes = [table.size, width, width, width_lat, width_lat, width_lat, width_lat]
    ends = [sum(sizes[:i]) for i in range(len(sizes) + 1)]
    table, dgain, dbias, dmid_gain, dmid_bias, db_up, db_down = (small[ends[i]:ends[i + 1]] for i in range(7))
    share = width // shards
    table = lax.dynamic_slice_in_dim(table.reshape(-1, width), me * share, share, 1)
    return (
        mixed_latents,
        grad_inputs,
        grad_latents,
        table,
        lax.dynamic_slice_in_dim(dgain, me * share, share, 0),
        lax.dynamic_slice_in_dim(dbias, me * share, share, 0),
        lat_small[:width_lat],
        lat_small[width_lat:],
        dmid_gain,
        dmid_bias,
        grad_w_query,
        pair_total[:cols].T,
        pair_total[cols:].T,
        lat_total[:cols],
        lat_total[cols:2 * cols].T,
        lax.dynamic_slice_in_dim(db_up, me * cols, cols, 0),
        lat_total[2 * cols:],
        db_down,
    )


def fast_device(inputs, padding, language, lang_table, latents, in_gain, in_bias, lat_gain, lat_bias, mid_gain, mid_bias,
              w_query, w_key, w_value, w_out, w_up, b_up, w_down, b_down, cotangent):
    length, local_seqs, width = inputs.shape
    local_rows, width_lat = latents.shape
    cols = w_query.shape[1]
    head_dim = width_lat // HEADS
    per_shard = cols // head_dim
    shards = lax.axis_size("heads")
    blocks = lax.axis_size("blk")
    rows = local_rows * blocks
    seqs = local_seqs // shards
    me = lax.axis_index("heads")
    first = me * seqs

    own = lax.dynamic_slice_in_dim(inputs, first, seqs, 1)
    x_cols = jnp.transpose(own, (1, 2, 0))
    live = jnp.transpose(lax.dynamic_slice_in_dim(padding, first, seqs, 1))
    mask = jnp.where(live > 0, 0.0, MASKED).astype(F32)[:, None, :]
    own_lang = lax.dynamic_slice_in_dim(language, first, seqs, 0)
    onehot = (own_lang[:, None] == jnp.arange(lang_table.shape[0], dtype=jnp.int32)[None, :]).astype(F32)
    emb = jnp.dot(onehot, lang_table.astype(F32), precision=lax.Precision.HIGHEST)
    rows_in = jnp.concatenate([in_gain[None], in_bias[None], emb, jnp.zeros((6 - seqs, width), F32)], axis=0)
    b_up_tile = jnp.pad(b_up[None, :], ((0, 7), (0, -cols % 128)))
    w_cols, lat_all, pairs, xn, att_cols, lse_cols, queries_t, lat_low, b_up_tiles = first_call(
        x_cols, rows_in, mask, latents, lat_gain[None], lat_bias[None], w_query.T,
        jnp.stack([w_key.T, w_value.T]), jnp.stack([w_out, w_up.T, w_down]), b_up_tile, rows)
    b_up_all = b_up_tiles[:, 0, :cols].reshape(1, -1)
    cot = lax.dynamic_slice_in_dim(cotangent, first, seqs, 0).reshape(seqs * local_rows, width_lat)
    own_mixed, grad_att, stats, grads, vectors, lat_sum = middle_call(
        att_cols, latents, cot, lat_all, b_up_all, b_down[None], mid_gain[None], mid_bias[None], lse_cols)
    grad_att = grad_att.reshape(seqs, shards, cols, local_rows)
    vectors = vectors.reshape(-1, 128)
    lang_rows = jnp.pad(onehot, ((0, 8 - seqs), (0, 128 - lang_table.shape[0])))
    g_cols, mixed_latents, pair_total, lat_total, small, grad_latents, lat_small, grad_w_query = second_call(
        x_cols, rows_in, mask, w_cols, queries_t, pairs, xn, grad_att, stats, own_mixed, lat_low, grads, vectors, lang_rows, lat_sum,
        w_query, latents.astype(F32), lat_gain[None])
    grad_inputs = g_cols.transpose(2, 0, 1)
    lat_total, pair_total = lat_total.astype(F32), pair_total.astype(F32)
    table = small[0, :, :lang_table.shape[0]].T
    dmid_gain, dmid_bias, db_up, db_down = small[0, :vectors.shape[0], 128:].reshape(4, width_lat)
    return (
        mixed_latents,
        grad_inputs,
        grad_latents,
        table,
        small[0, :, 32],
        small[0, :, 33],
        lat_small[0],
        lat_small[1],
        dmid_gain,
        dmid_bias,
        grad_w_query,
        pair_total[0].T,
        pair_total[1].T,
        lat_total[0],
        lat_total[1].T,
        lax.dynamic_slice_in_dim(db_up, me * cols, cols, 0),
        lat_total[2],
        db_down,
    )


def solution(mesh):
    placed = (
        P("blk", "items", None), P("blk", "items"), P("items"), P(), P("blk", None), P(), P(), P(), P(), P(), P(),
        P(None, "heads"), P(None, "heads"), P(None, "heads"), P("heads", None), P(None, "heads"), P("heads"),
        P("heads", None), P(), P("items", "blk", None),
    )
    out = (
        P("items", "blk", None), P("blk", "items", "heads"), P("blk", None), P(None, "heads"), P("heads"), P("heads"),
        P(), P(), P(), P(), P(None, "heads"), P(None, "heads"), P(None, "heads"), P("heads", None), P(None, "heads"),
        P("heads"), P("heads", None), P(),
    )
    fits = mesh.shape["blk"] == 2 and mesh.shape["items"] == 4 and mesh.shape["heads"] == 4
    return jax.shard_map(fast_device if fits else general_device, mesh=mesh, in_specs=placed, out_specs=out, check_vma=False)
```

```python
import functools

import jax
import jax.numpy as jnp
from jax import lax
from jax.experimental import pallas as pl
from jax.experimental.pallas import tpu as pltpu
from jax.sharding import PartitionSpec as P

HEADS = 8
EPS = 1e-05
MASKED = -1e30
LOG2E = 1.4426950408889634
F32 = jnp.float32
BF16 = jnp.bfloat16
NT = (((1,), (1,)), ((), ()))
VMEM_LIMIT = 60 * 1024 * 1024


def dot(a, b):
    return jnp.dot(a, b, preferred_element_type=F32)


def dot_nt(a, b):
    return lax.dot_general(a, b, NT, preferred_element_type=F32)


def norm_keep(values, gain, bias):
    average = jnp.mean(values, axis=-1, keepdims=True)
    centred = values - average
    inverse = lax.rsqrt(jnp.mean(centred * centred, axis=-1, keepdims=True) + EPS)
    normed = centred * inverse
    return (normed * gain + bias, normed, inverse)


def norm_back(grad_norm, normed, inverse, gain):
    scaled = grad_norm * gain
    first = jnp.mean(scaled, axis=-1, keepdims=True)
    second = jnp.mean(scaled * normed, axis=-1, keepdims=True)
    return (scaled - first - normed * second) * inverse


def norm_columns(x, emb):
    shifted = x.astype(F32) + emb
    centred = shifted - jnp.mean(shifted, axis=0, keepdims=True)
    inverse = lax.rsqrt(jnp.mean(centred * centred, axis=0, keepdims=True) + EPS)
    return centred * inverse, inverse


def head_rows(h, per_shard, head_dim):
    key = (h // per_shard) * 2 * per_shard + lax.rem(h, per_shard)
    key_at = pl.multiple_of(key * head_dim, head_dim)
    return pl.ds(key_at, head_dim), pl.ds(pl.multiple_of(key_at + per_shard * head_dim, head_dim), head_dim)


def forward_kernel(per_shard, x_ref, emb_ref, gain_ref, bias_ref, w_ref, q_ref, mask_ref, kv_ref, o_ref, lse_ref, xn_ref, stat_ref):
    heads, rows, head_dim = q_ref.shape
    length = x_ref.shape[1]
    piece = min(256, length)

    def norm_step(i, _):
        at = pl.ds(pl.multiple_of(i * piece, piece), piece)
        normed, _unused = norm_columns(x_ref[:, at], emb_ref[...])
        xn_ref[:, at] = (normed * gain_ref[...] + bias_ref[...]).astype(BF16)
        return 0

    lax.fori_loop(0, length // piece, norm_step, 0)
    block = 512 if w_ref.shape[0] % 512 == 0 else 160

    def pair_step(i, _):
        at = pl.ds(pl.multiple_of(i * block, block), block)
        kv_ref[at] = dot(w_ref[at], xn_ref[...]).astype(BF16)
        return 0

    lax.fori_loop(0, w_ref.shape[0] // block, pair_step, 0)
    factor = LOG2E * head_dim ** (-0.5)
    lane = lax.broadcasted_iota(jnp.int32, (rows, 128), 1)
    stat_ref[...] = jnp.zeros_like(stat_ref)

    def head_step(h, _):
        at_key, at_value = head_rows(h, per_shard, head_dim)
        scores = dot(q_ref[h], kv_ref[at_key]) * factor + mask_ref[...]
        top = jnp.max(scores, axis=1, keepdims=True)
        weights = jnp.exp2(scores - top)
        total = jnp.sum(weights, axis=1, keepdims=True)
        out = dot_nt(kv_ref[at_value], weights.astype(BF16))
        stat_ref[...] = jnp.where(lane == h, top + jnp.log2(total), stat_ref[...])
        inverse = jnp.transpose(jnp.broadcast_to(1.0 / total, (rows, 128)))[:1]
        o_ref[pl.ds(pl.multiple_of(h * head_dim, head_dim), head_dim)] = (out * inverse).astype(BF16)
        return 0

    lax.fori_loop(0, heads, head_step, 0)
    lse_ref[...] = jnp.transpose(stat_ref[...])[:heads]


def forward_call(x_cols, emb, gain, bias, w_rows, q, mask, per_shard):
    seqs, width, length = x_cols.shape
    heads, rows, head_dim = q.shape
    pair_rows = w_rows.shape[0]
    whole = pl.BlockSpec(memory_space=pltpu.VMEM)

    def per_seq(*dims):
        return pl.BlockSpec((None,) + dims, lambda s: (s, 0, 0))

    return pl.pallas_call(
        functools.partial(forward_kernel, per_shard),
        grid=(seqs,),
        in_specs=[per_seq(width, length), per_seq(width, 1), whole, whole, whole, whole, per_seq(1, length)],
        out_specs=[per_seq(pair_rows, length), per_seq(heads * head_dim, rows), per_seq(heads, rows)],
        out_shape=[
            jax.ShapeDtypeStruct((seqs, pair_rows, length), BF16),
            jax.ShapeDtypeStruct((seqs, heads * head_dim, rows), BF16),
            jax.ShapeDtypeStruct((seqs, heads, rows), F32),
        ],
        scratch_shapes=[pltpu.VMEM((width, length), BF16), pltpu.VMEM((rows, 128), F32)],
        compiler_params=pltpu.CompilerParams(vmem_limit_bytes=VMEM_LIMIT),
        name="attend",
    )(x_cols, emb, gain, bias, w_rows, q, mask)


def backward_kernel(per_shard, x_ref, emb_ref, gain_ref, bias_ref, w_ref, q_ref, qt_ref, do_ref, dot_ref, lse_ref, delta_ref, mask_ref, kv_ref,
                    g_ref, dw_ref, dq_ref, dgain_ref, dbias_ref, demb_ref, xn_ref, dkv_ref):
    heads, rows, head_dim = q_ref.shape
    width, length = x_ref.shape
    piece = min(256, length)

    @pl.when(pl.program_id(0) == 0)
    def _():
        dw_ref[...] = jnp.zeros_like(dw_ref)
        dq_ref[...] = jnp.zeros_like(dq_ref)
        dgain_ref[...] = jnp.zeros_like(dgain_ref)
        dbias_ref[...] = jnp.zeros_like(dbias_ref)

    def norm_step(i, _):
        at = pl.ds(pl.multiple_of(i * piece, piece), piece)
        normed, _unused = norm_columns(x_ref[:, at], emb_ref[...])
        xn_ref[:, at] = (normed * gain_ref[...] + bias_ref[...]).astype(BF16)
        return 0

    lax.fori_loop(0, length // piece, norm_step, 0)
    scale = head_dim ** (-0.5)
    factor = LOG2E * scale

    def head_step(h, _):
        at_key, at_value = head_rows(h, per_shard, head_dim)
        keys = kv_ref[at_key]
        weights = jnp.exp2(dot(q_ref[h], keys) * factor + mask_ref[...] - lse_ref[h])
        dkv_ref[at_value] = dot(dot_ref[h], weights.astype(BF16)).astype(BF16)
        grad = dot(do_ref[h], kv_ref[at_value]) - delta_ref[h]
        grad = (weights * grad).astype(BF16)
        dkv_ref[at_key] = (dot(qt_ref[h], grad) * scale).astype(BF16)
        dq_ref[h] += dot_nt(keys, grad) * scale
        return 0

    lax.fori_loop(0, heads, head_step, 0)
    block = 512 if dw_ref.shape[0] % 512 == 0 else 160

    def weight_step(i, _):
        at = pl.ds(pl.multiple_of(i * block, block), block)
        dw_ref[at] += dot_nt(dkv_ref[at], xn_ref[...])
        return 0

    lax.fori_loop(0, dw_ref.shape[0] // block, weight_step, 0)

    def byte_step(i, carry):
        at = pl.ds(pl.multiple_of(i * piece, piece), piece)
        grad = dot(w_ref[...], dkv_ref[:, at])
        normed, inverse = norm_columns(x_ref[:, at], emb_ref[...])
        dbias_ref[...] += jnp.sum(grad, axis=1, keepdims=True)
        dgain_ref[...] += jnp.sum(grad * normed, axis=1, keepdims=True)
        scaled = grad * gain_ref[...]
        first = jnp.mean(scaled, axis=0, keepdims=True)
        second = jnp.mean(scaled * normed, axis=0, keepdims=True)
        shifted = (scaled - first - normed * second) * inverse
        g_ref[:, at] = shifted.astype(BF16)
        return carry + jnp.sum(shifted, axis=1, keepdims=True)

    demb_ref[...] = lax.fori_loop(0, length // piece, byte_step, jnp.zeros((width, 1), F32))


def backward_call(x_cols, emb, gain, bias, w, q, qt, grad_out, grad_out_t, lse, delta, mask, pairs, per_shard):
    seqs, width, length = x_cols.shape
    heads, rows, head_dim = q.shape
    pair_rows = w.shape[1]
    whole = pl.BlockSpec(memory_space=pltpu.VMEM)

    def per_seq(*dims):
        return pl.BlockSpec((None,) + dims, lambda s: (s,) + (0,) * len(dims))

    return pl.pallas_call(
        functools.partial(backward_kernel, per_shard),
        grid=(seqs,),
        in_specs=[
            per_seq(width, length), per_seq(width, 1), whole, whole, whole, whole, whole,
            per_seq(heads, rows, head_dim), per_seq(heads, head_dim, rows),
            per_seq(heads, rows, 1), per_seq(heads, rows, 1), per_seq(1, length), per_seq(pair_rows, length),
        ],
        out_specs=[per_seq(width, length), whole, whole, whole, whole, per_seq(width, 1)],
        out_shape=[
            jax.ShapeDtypeStruct((seqs, width, length), BF16),
            jax.ShapeDtypeStruct((pair_rows, width), F32),
            jax.ShapeDtypeStruct((heads, head_dim, rows), F32),
            jax.ShapeDtypeStruct((width, 1), F32),
            jax.ShapeDtypeStruct((width, 1), F32),
            jax.ShapeDtypeStruct((seqs, width, 1), F32),
        ],
        scratch_shapes=[pltpu.VMEM((width, length), BF16), pltpu.VMEM((pair_rows, length), BF16)],
        compiler_params=pltpu.CompilerParams(vmem_limit_bytes=VMEM_LIMIT),
        name="attend_back",
    )(x_cols, emb, gain, bias, w, q, qt, grad_out, grad_out_t, lse, delta, mask, pairs)


def mesh_at(di=None, db=None, dh=None, core=None):
    items, blk, heads = lax.axis_index("items"), lax.axis_index("blk"), lax.axis_index("heads")
    return (items if di is None else di, blk if db is None else db, heads if dh is None else dh)


def places():
    items, blk, heads = lax.axis_index("items"), lax.axis_index("blk"), lax.axis_index("heads")
    core = lax.rem(items, 2)
    return items, blk, heads, items // 2, core


def send(src, dst, sems, recvs, target):
    copy = pltpu.make_async_remote_copy(
        src_ref=src, dst_ref=dst, send_sem=sems, recv_sem=recvs, device_id=target, device_id_type=pl.DeviceIdType.MESH)
    copy.start()
    return copy


def greet(targets):
    barrier = pltpu.get_barrier_semaphore()
    for target in targets:
        pl.semaphore_signal(barrier, inc=1, device_id=target, device_id_type=pl.DeviceIdType.MESH)
    pl.semaphore_wait(barrier, len(targets))


def first_kernel(x_hbm, pad_ref, lang_ref, table_ref, vecs_ref, lat_ref, wq_ref, pair_shard, lat_shard,
                 wcols_ref, all_ref, kv_out, xn_out, att_ref, lse_ref, qt_ref, latn_ref, bup_all, x_out, rows_ref, mask_ref, lang_out, latf_ref,
                 x_ref, xbuf, x32, xn_ref, pair_ref, kv_ref, cols_ref, q_ref, o_tmp, o_own, o_send, o_got, stat_ref, stat_send, stat_own, stat_got,
                 pair_ss, pair_rs, lat_ss, lat_rs, q_ss, q_rs, misc_ss, misc_rs, o_ss, o_rs, own_sem, xn_sem, kv_sem, x_sem):
    items, blk, me, hi, core = places()
    shards = lax.axis_size("heads")
    seqs, width, length = x_ref.shape
    rows = qt_ref.shape[3]
    local_rows = rows // 2
    heads, _, head_dim = q_ref.shape
    cols = heads * head_dim // shards
    per_shard = heads // shards
    sibling = items + 1 - 2 * core
    other = 1 - blk
    to_sib, to_x, to_y = mesh_at(di=sibling), mesh_at(db=other), mesh_at(di=(1 - hi) * 2 + core)
    z_of = [lax.rem(me + d, shards) for d in range(shards)]
    z_back = [lax.rem(me + shards - d, shards) for d in range(shards)]
    greet([to_sib, to_x, to_y] + [mesh_at(dh=z_of[d]) for d in range(1, shards)])

    share = cols // 4
    chip = hi * 2 + blk
    chip_x, chip_y, chip_xy = hi * 2 + other, (1 - hi) * 2 + blk, (1 - hi) * 2 + other

    def region(ref, shard, chip_at, lanes_of):
        half = ref.shape[2] // 2
        return ref.at[:, pl.ds(pl.multiple_of(shard * cols + chip_at * share, 16), share), pl.ds(pl.multiple_of(lanes_of * half, 128), half)]

    def lane_half(ref, shard, lanes_of):
        half = ref.shape[2] // 2
        return ref.at[:, pl.ds(pl.multiple_of(shard * cols, 16), cols), pl.ds(pl.multiple_of(lanes_of * half, 128), half)]

    pending = []
    local = []
    near = me + 1 - 2 * lax.rem(me, 2)
    far, cross = lax.rem(me + 2, 4), lax.rem(near + 2, 4)
    shard_at = [me, near, far, cross]
    kinds = {"pair": (pair_shard, pair_ref, pair_ss, pair_rs)}
    for m in range(3):
        one = pl.ds(m, 1)
        kinds[f"l{m}"] = (lat_shard.at[one], all_ref.at[one], lat_ss.at[m], lat_rs.at[m])

    def recv(kind, d, stage, where):
        _, dst, ss, rs = kinds[kind]
        pltpu.make_async_remote_copy(src_ref=where, dst_ref=where, send_sem=ss.at[d, stage], recv_sem=rs.at[d, stage],
                                     device_id=to_sib, device_id_type=pl.DeviceIdType.MESH).wait_recv()

    def out_z(kind, d):
        src, dst, ss, rs = kinds[kind]
        if d == 3:
            block = region(dst, far, chip, core)
            pending.append(send(block, block, ss.at[d, 0], rs.at[d, 0], mesh_at(dh=near)))
        else:
            pending.append(send(region(src, 0, chip, core), region(dst, me, chip, core), ss.at[d, 0], rs.at[d, 0], mesh_at(dh=shard_at[d])))

    def after_z(kind, d):
        _, dst, ss, rs = kinds[kind]
        mine = region(dst, shard_at[d], chip, core)
        recv(kind, d, 0, mine)
        pending.append(send(mine, mine, ss.at[d, 1], rs.at[d, 1], to_x))
        pending.append(send(mine, mine, ss.at[d, 2], rs.at[d, 2], to_y))

    def after_x(kind, d):
        _, dst, ss, rs = kinds[kind]
        x_first = kind != "l1"
        got = region(dst, shard_at[d], chip_x if x_first else chip_y, core)
        recv(kind, d, 1 if x_first else 2, got)
        pending.append(send(got, got, ss.at[d, 3], rs.at[d, 3], to_y if x_first else to_x))

    def after_y(kind, d):
        _, dst, ss, rs = kinds[kind]
        x_first = kind != "l1"
        recv(kind, d, 2 if x_first else 1, region(dst, shard_at[d], chip_y if x_first else chip_x, core))
        recv(kind, d, 3, region(dst, shard_at[d], chip_xy, core))
        half = lane_half(dst, shard_at[d], core)
        pending.append(send(half, half, ss.at[d, 4], rs.at[d, 4], to_sib))

    def after_sib(kind, d):
        _, dst, ss, rs = kinds[kind]
        recv(kind, d, 4, lane_half(dst, shard_at[d], 1 - core))

    own_pair = pltpu.make_async_copy(pair_shard, pair_ref.at[:, pl.ds(pl.multiple_of(me * cols, 16), cols)], own_sem.at[0])
    own_lat = pltpu.make_async_copy(lat_shard, all_ref.at[:, pl.ds(pl.multiple_of(me * cols, 16), cols)], own_sem.at[1])
    own_pair.start()
    own_lat.start()
    my_rows = pl.ds(pl.multiple_of(blk * local_rows, 128), local_rows)
    other_rows = pl.ds(pl.multiple_of(other * local_rows, 128), local_rows)

    def queries_start():
        latf_ref[...] = lat_ref[...].astype(F32)
        lat_out, _, _ = norm_keep(latf_ref[...], vecs_ref[0:1], vecs_ref[1:2])
        lat_low = lat_out.astype(BF16)
        latn_ref[...] = lat_low
        at_head = pl.ds(pl.multiple_of(core * head_dim, 16), head_dim)
        qt_ref[core, me, :, my_rows] = dot_nt(wq_ref[at_head], lat_low).astype(BF16)
        bup_ref = vecs_ref.at[:, pl.ds(0, bup_all.shape[2])]
        bup_all[me] = bup_ref[...]
        for d in range(1, shards):
            my_q = qt_ref.at[core, me, :, my_rows]
            pending.append(send(my_q, my_q, q_ss.at[0, d], q_rs.at[0, d], mesh_at(dh=z_back[d])))
        for d in range(1, shards):
            pending.append(send(bup_ref, bup_all.at[me], misc_ss.at[d], misc_rs.at[d], mesh_at(dh=z_back[d])))

    rows_ref[0:1] = vecs_ref[5:6, :width]
    rows_ref[1:2] = vecs_ref[6:7, :width]
    rows_ref[4:8] = jnp.zeros((4, width), F32)
    lang_out[...] = jnp.zeros_like(lang_out)
    for s in range(seqs):
        lang = lang_ref[me * seqs + s]
        picked = lax.broadcasted_iota(jnp.int32, table_ref.shape, 0) == lang
        rows_ref[2 + s:3 + s] = jnp.sum(jnp.where(picked, table_ref[...].astype(F32), 0.0), axis=0, keepdims=True)
        lang_out[s:s + 1] = jnp.where(lax.broadcasted_iota(jnp.int32, (1, 128), 1) == lang, 1.0, 0.0)
        mask_ref[s] = jnp.where(pad_ref[pl.ds(me * seqs + s, 1)] > 0, 0.0, MASKED)
    cols_ref[...] = jnp.transpose(rows_ref[...])
    step_rows = xbuf.shape[1]

    def load_bytes(c):
        return pltpu.make_async_copy(x_hbm.at[pl.ds(c * step_rows, step_rows)], xbuf.at[c % 2], x_sem.at[c % 2])

    load_bytes(0).start()

    def pick_bytes(c):
        load_bytes(c).wait()
        if (c + 1) * step_rows < length:
            load_bytes(c + 1).start()
        at = slice(c * step_rows, (c + 1) * step_rows)
        for j in range(x32.shape[0]):
            lanes = slice(j * 128, (j + 1) * 128)
            x32[j] = xbuf[c % 2, :, :, lanes].astype(F32).reshape(x32.shape[1:])
            for s in range(seqs):
                x_ref[s, lanes, at] = jnp.transpose(x32[j, pl.ds(me * seqs + s, step_rows, stride=x_hbm.shape[1])]).astype(BF16)
        if (c + 1) * step_rows == length:
            copy = pltpu.make_async_copy(x_ref, x_out, x_sem.at[2])
            copy.start()
            local.append(copy)


    def queries_z():
        for d in range(1, shards):
            wait_plain(qt_ref.at[core, z_of[d], :, my_rows], q_ss.at[0, d], q_rs.at[0, d])
        part = qt_ref.at[core, :, :, my_rows]
        pending.append(send(part, part, q_ss.at[1, 0], q_rs.at[1, 0], to_x))

    def queries_x():
        wait_plain(qt_ref.at[core, :, :, other_rows], q_ss.at[1, 0], q_rs.at[1, 0])
        pending.append(send(qt_ref.at[core], qt_ref.at[core], q_ss.at[1, 1], q_rs.at[1, 1], to_sib))

    def queries_sib():
        wait_plain(qt_ref.at[1 - core], q_ss.at[1, 1], q_rs.at[1, 1])

    def wait_plain(where, ss, rs):
        pltpu.make_async_remote_copy(src_ref=where, dst_ref=where, send_sem=ss, recv_sem=rs,
                                     device_id=to_sib, device_id_type=pl.DeviceIdType.MESH).wait_recv()

    piece = min(256, length)

    def norm_bytes(s):
        def norm_step(i, _):
            at = pl.ds(pl.multiple_of(i * piece, piece), piece)
            normed, _unused = norm_columns(x_ref[s, :, at], cols_ref[:, 2 + s:3 + s])
            xn_ref[s, :, at] = (normed * cols_ref[:, 0:1] + cols_ref[:, 1:2]).astype(BF16)
            return 0
        lax.fori_loop(0, length // piece, norm_step, 0)
        copy = pltpu.make_async_copy(xn_ref.at[s], xn_out.at[s], xn_sem.at[s])
        copy.start()
        local.append(copy)

    def project(d):
        at = pl.ds(pl.multiple_of(shard_at[d] * cols, 16), cols)

        def step(i, _):
            s, part = i // 2, lax.rem(i, 2)
            kv_ref[s, part, at] = dot(pair_ref[part, at], xn_ref[s]).astype(BF16)
            return 0
        lax.fori_loop(0, 2 * seqs, step, 0)
        copy = pltpu.make_async_copy(kv_ref.at[:, :, at], kv_out.at[:, :, at], kv_sem.at[d])
        copy.start()
        local.append(copy)

    factor = LOG2E * head_dim ** (-0.5)
    lane = lax.broadcasted_iota(jnp.int32, (rows, 128), 1)
    stat_ref[...] = jnp.zeros_like(stat_ref)

    def turn_queries(d):
        for j in range(per_shard):
            h = shard_at[d] * per_shard + j
            q_ref[h] = jnp.transpose(qt_ref[j, shard_at[d]])

    def attend(d, s):
        def head_step(j, _):
            h = shard_at[d] * per_shard + j
            at = pl.ds(pl.multiple_of(h * head_dim, 16), head_dim)
            scores = dot(q_ref[h], kv_ref[s, 0, at]) * factor + mask_ref[s]
            top = jnp.max(scores, axis=1, keepdims=True)
            weights = jnp.exp2(scores - top)
            total = jnp.sum(weights, axis=1, keepdims=True)
            out = dot_nt(kv_ref[s, 1, at], weights.astype(BF16))
            stat_ref[s] = jnp.where(lane == h, top + jnp.log2(total), stat_ref[s])
            inverse = jnp.transpose(jnp.broadcast_to(1.0 / total, (rows, 128)))[:1]
            o_tmp[...] = out * inverse
            o_own[s, at] = o_tmp[:, my_rows]
            o_send[s, at] = o_tmp[:, other_rows].astype(BF16)
            return 0
        lax.fori_loop(0, per_shard, head_step, 0)
        part = pl.ds(pl.multiple_of(shard_at[d] * cols, 16), cols)
        pending.append(send(o_send.at[s, part], o_got.at[s, part], o_ss.at[d, s], o_rs.at[d, s], to_x))

    def stats_send():
        for s in range(seqs):
            at = pl.ds(s * heads, heads)
            stats = jnp.transpose(stat_ref[s])[:heads]
            stat_send[...] = stats
            stat_own[at] = stat_send[:, my_rows]
            stat_got[0, at] = stat_send[:, other_rows]
        pending.append(send(stat_got.at[0], stat_got.at[1], o_ss.at[shards, 0], o_rs.at[shards, 0], to_x))

    def turn_weights():
        block = 256
        for part in range(2):
            for i in range(pair_ref.shape[1] // block):
                wcols_ref[part, :, i * block:(i + 1) * block] = jnp.transpose(pair_ref[part, i * block:(i + 1) * block])

    out_z("pair", 1)
    out_z("pair", 2)
    queries_start()
    pick_bytes(0)
    pick_bytes(1)
    pick_bytes(2)
    pick_bytes(3)
    pick_bytes(4)
    pick_bytes(5)
    pick_bytes(6)
    after_z("pair", 1)
    out_z("l0", 1)
    pick_bytes(7)
    queries_z()
    norm_bytes(0)
    after_z("pair", 2)
    out_z("pair", 3)
    norm_bytes(1)
    after_z("l0", 1)
    out_z("l0", 2)
    own_pair.wait()
    project(0)
    after_x("pair", 1)
    after_z("pair", 3)
    out_z("l1", 1)
    after_z("l0", 2)
    out_z("l0", 3)
    after_z("l1", 1)
    out_z("l1", 2)
    after_x("pair", 2)
    queries_x()
    after_x("l0", 1)
    after_y("pair", 1)
    queries_sib()
    turn_queries(0)
    attend(0, 0)
    after_sib("pair", 1)
    after_z("l0", 3)
    out_z("l2", 1)
    attend(0, 1)
    after_x("pair", 3)
    after_x("l0", 2)
    after_z("l1", 2)
    out_z("l1", 3)
    project(1)
    turn_queries(1)
    attend(1, 0)
    after_z("l2", 1)
    out_z("l2", 2)
    attend(1, 1)
    after_z("l1", 3)
    after_x("l1", 1)
    after_x("l0", 3)
    after_y("l0", 1)
    after_z("l2", 2)
    out_z("l2", 3)
    after_y("pair", 2)
    after_sib("l0", 1)
    after_sib("pair", 2)
    project(2)
    after_z("l2", 3)
    turn_queries(2)
    attend(2, 0)
    after_y("l0", 2)
    after_x("l1", 2)
    after_x("l2", 1)
    attend(2, 1)
    after_y("l1", 1)
    after_y("pair", 3)
    after_sib("l0", 2)
    after_x("l2", 2)
    after_x("l1", 3)
    after_sib("l1", 1)
    after_y("l0", 3)
    after_sib("pair", 3)
    project(3)
    after_sib("l0", 3)
    turn_queries(3)
    attend(3, 0)
    after_y("l2", 1)
    after_x("l2", 3)
    attend(3, 1)
    after_y("l1", 2)
    after_y("l2", 2)
    stats_send()
    turn_weights()
    after_y("l1", 3)
    after_y("l2", 3)
    after_sib("l2", 1)
    after_sib("l1", 2)
    after_sib("l2", 2)
    after_sib("l1", 3)
    after_sib("l2", 3)

    wait_plain(stat_got.at[1], o_ss.at[shards, 0], o_rs.at[shards, 0])
    own_lse, got_lse = stat_own[...], stat_got[1]
    top = jnp.maximum(own_lse, got_lse)
    own_share, got_share = jnp.exp2(own_lse - top), jnp.exp2(got_lse - top)
    total = own_share + got_share
    lse = top + jnp.log2(total)
    own_share, got_share = own_share / total, got_share / total
    for s in range(seqs):
        lse_ref[s] = lse[s * heads:(s + 1) * heads]
        for d in range(shards):
            part = pl.ds(pl.multiple_of(shard_at[d] * cols, 16), cols)
            wait_plain(o_got.at[s, part], o_ss.at[d, s], o_rs.at[d, s])
    for s in range(seqs):
        for h in range(heads):
            at = slice(h * head_dim, (h + 1) * head_dim)
            n = s * heads + h
            att_ref[s, at] = o_own[s, at] * own_share[n:n + 1] + o_got[s, at].astype(F32) * got_share[n:n + 1]
    for d in range(1, shards):
        wait_plain(bup_all.at[z_of[d]], misc_ss.at[d], misc_rs.at[d])
    own_lat.wait()
    for copy in local:
        copy.wait()
    for copy in pending:
        copy.wait_send()


def first_call(inputs, padding, language, table, vecs, latents, wq_rows, pair_shard, lat_shard, rows, seqs):
    length, local_seqs, width = inputs.shape
    local_rows, width_lat = latents.shape
    shards = lax.axis_size("heads")
    heads = HEADS
    head_dim = width_lat // heads
    whole = pl.BlockSpec(memory_space=pltpu.VMEM)
    hbm = pl.BlockSpec(memory_space=pl.ANY)
    out = jax.ShapeDtypeStruct
    sem = pltpu.SemaphoreType.DMA
    return pl.pallas_call(
        first_kernel,
        in_specs=[hbm, whole, pl.BlockSpec(memory_space=pltpu.SMEM)] + [whole] * 6,
        out_specs=[whole, hbm, hbm, hbm] + [whole] * 5 + [hbm] + [whole] * 4,
        out_shape=[
            out((2, width, width_lat), BF16),
            out((3, width_lat, width_lat), BF16),
            out((seqs, 2, width_lat, length), BF16),
            out((seqs, width, length), BF16),
            out((seqs, width_lat, local_rows), F32),
            out((seqs, heads, local_rows), F32),
            out((heads // shards, shards, head_dim, rows), BF16),
            out((local_rows, width_lat), BF16),
            out((shards, 8, 384), F32),
            out((seqs, width, length), BF16),
            out((8, width), F32),
            out((seqs, 1, length), F32),
            out((8, 128), F32),
            out((local_rows, width_lat), F32),
        ],
        scratch_shapes=[
            pltpu.VMEM((seqs, width, length), BF16),
            pltpu.VMEM((2, 128, local_seqs, width), BF16),
            pltpu.VMEM((width // 128, 128 * local_seqs, 128), F32),
            pltpu.VMEM((seqs, width, length), BF16),
            pltpu.VMEM((2, width_lat, width), BF16),
            pltpu.VMEM((seqs, 2, width_lat, length), BF16),
            pltpu.VMEM((width, 8), F32),
            pltpu.VMEM((heads, rows, head_dim), BF16),
            pltpu.VMEM((head_dim, rows), F32),
            pltpu.VMEM((seqs, width_lat, local_rows), F32),
            pltpu.VMEM((seqs, width_lat, local_rows), BF16),
            pltpu.VMEM((seqs, width_lat, local_rows), BF16),
            pltpu.VMEM((seqs, rows, 128), F32),
            pltpu.VMEM((heads, rows), F32),
            pltpu.VMEM((seqs * heads, local_rows), F32),
            pltpu.VMEM((2, seqs * heads, local_rows), F32),
            sem((shards, 5)), sem((shards, 5)), sem((3, shards, 5)), sem((3, shards, 5)),
            sem((2, shards)), sem((2, shards)), sem((shards,)), sem((shards,)),
            sem((shards + 1, seqs)), sem((shards + 1, seqs)), sem((2,)), sem((seqs,)), sem((shards,)), sem((3,)),
        ],
        compiler_params=pltpu.CompilerParams(vmem_limit_bytes=VMEM_LIMIT, collective_id=1, has_side_effects=True),
        name="first",
    )(inputs, padding, language, table, vecs, latents, wq_rows, pair_shard, lat_shard)


class Reduce:
    def __init__(self, src, half, got_sib, got_chip, got_z, out, ss, rs, pending, x_first=True, stage=None, stage_sem=None):
        self.src, self.half, self.got_sib, self.got_chip, self.got_z, self.out = src, half, got_sib, got_chip, got_z, out
        self.ss, self.rs, self.pending, self.x_first = ss, rs, pending, x_first
        self.stage, self.stage_sem, self.kept = stage, stage_sem, None
        self.split = src is not None and src.shape[3] == half.shape[3]
        items, blk, self.me, hi, self.core = places()
        self.shards = lax.axis_size("heads")
        other = 1 - blk
        self.chip = hi * 2 + blk
        self.chip_x, self.chip_y, self.chip_xy = hi * 2 + other, (1 - hi) * 2 + blk, (1 - hi) * 2 + other
        self.to_x, self.to_y = mesh_at(db=other), mesh_at(di=(1 - hi) * 2 + self.core)
        self.to_sib = mesh_at(di=items + 1 - 2 * self.core)
        self.n, _, self.cols, self.width = half.shape
        self.share = self.cols // 4
        self.near = self.me + 1 - 2 * lax.rem(self.me, 2)
        self.far, self.cross = lax.rem(self.me + 2, 4), lax.rem(self.near + 2, 4)

    def rows(self, chip):
        return pl.ds(pl.multiple_of(chip * self.share, 16), self.share)

    def lanes(self, core):
        return pl.ds(pl.multiple_of(core * self.width, 128), self.width)

    def go(self, src, dst, i, target):
        self.pending.append(send(src, dst, self.ss.at[i], self.rs.at[i], target))

    def arrived(self, where, i):
        pltpu.make_async_remote_copy(src_ref=where, dst_ref=where, send_sem=self.ss.at[i], recv_sem=self.rs.at[i],
                                     device_id=self.to_sib, device_id_type=pl.DeviceIdType.MESH).wait_recv()

    def start(self):
        theirs = self.src if self.split else self.src.at[:, :, :, self.lanes(1 - self.core)]
        self.go(theirs, self.got_sib, 0, self.to_sib)

    def join_sib(self):
        self.arrived(self.got_sib, 0)

        def step(i, _):
            n, h = i // self.shards, lax.rem(i, self.shards)
            own = self.half[n, h] if self.split else self.src[n, h, :, self.lanes(self.core)]
            self.half[n, h] = (own.astype(F32) + self.got_sib[n, h].astype(F32)).astype(self.half.dtype)
            return 0
        lax.fori_loop(0, self.n * self.shards, step, 0)

    def send_chips(self):
        low, high = pl.ds(0, 2), pl.ds(2, 2)
        self.go(self.half.at[:, low, self.rows(self.chip_x)], self.got_chip.at[0], 1, self.to_x)
        self.go(self.half.at[:, high, self.rows(self.chip_y)], self.got_chip.at[2], 3, self.to_y)
        self.go(self.half.at[:, low, self.rows(self.chip_xy)], self.got_chip.at[1], 2, self.to_x)
        self.go(self.half.at[:, high, self.rows(self.chip_xy)], self.got_chip.at[3], 4, self.to_y)

    def add(self, slot, first, rows):
        self.arrived(self.got_chip.at[slot], 1 + slot)
        for n in range(self.n):
            for h in range(2):
                total = self.half[n, first + h, rows].astype(F32) + self.got_chip[slot, n, h].astype(F32)
                self.half[n, first + h, rows] = total.astype(self.half.dtype)

    def join_first(self):
        self.add(1, 0, self.rows(self.chip_y))
        self.go(self.half.at[:, pl.ds(0, 2), self.rows(self.chip_y)], self.got_chip.at[4], 5, self.to_y)
        self.add(3, 2, self.rows(self.chip_x))
        self.go(self.half.at[:, pl.ds(2, 2), self.rows(self.chip_x)], self.got_chip.at[5], 6, self.to_x)
        self.add(0, 0, self.rows(self.chip))
        self.add(2, 2, self.rows(self.chip))

    def join_chips(self):
        mine = self.rows(self.chip)
        self.add(4, 0, mine)
        self.add(5, 2, mine)
        for i, shard in enumerate((self.near, self.cross)):
            self.go(self.half.at[:, shard, mine], self.got_z.at[i], 7 + i, mesh_at(dh=self.near))

    def join_near(self):
        mine = self.rows(self.chip)
        for i, shard in enumerate((self.me, self.far)):
            self.arrived(self.got_z.at[i], 7 + i)
            for n in range(self.n):
                total = self.half[n, shard, mine].astype(F32) + self.got_z[i, n].astype(F32)
                self.half[n, shard, mine] = total.astype(self.half.dtype)
        self.go(self.half.at[:, self.far, mine], self.got_z.at[2], 9, mesh_at(dh=self.far))

    def join_z(self):
        self.arrived(self.got_z.at[2], 9)
        mine = self.rows(self.chip)
        for n in range(self.n):
            total = self.half[n, self.me, mine].astype(F32) + self.got_z[2, n].astype(F32)
            if self.stage is None:
                self.out[n, mine, self.lanes(self.core)] = total.astype(self.out.dtype)
            else:
                self.stage[n] = total.astype(self.out.dtype)
        src = self.piece(self.chip)
        if self.stage is not None:
            self.kept = pltpu.make_async_copy(self.stage, src, self.stage_sem)
            self.kept.start()
            src = self.stage
        self.go(src, self.piece(self.chip), 10, self.to_x)
        self.go(src, self.piece(self.chip), 11, self.to_y)

    def piece(self, chip):
        return self.out.at[:, self.rows(chip), self.lanes(self.core)]

    def pass_on(self, chip, i, target):
        self.go(self.piece(chip), self.piece(chip), i, target)

    def share_chips(self):
        if self.x_first:
            self.arrived(self.piece(self.chip_x), 10)
            self.pass_on(self.chip_x, 12, self.to_y)
        else:
            self.arrived(self.piece(self.chip_y), 11)
            self.pass_on(self.chip_y, 12, self.to_x)

    def share_sib(self):
        if self.x_first:
            self.arrived(self.piece(self.chip_y), 11)
        else:
            self.arrived(self.piece(self.chip_x), 10)
        self.arrived(self.piece(self.chip_xy), 12)
        if self.kept is not None:
            self.kept.wait()
        half = self.out.at[:, :, self.lanes(self.core)]
        self.go(half, half, 13, self.to_sib)

    def finish(self):
        self.arrived(self.out.at[:, :, self.lanes(1 - self.core)], 13)


def second_kernel(x_hbm, rows_ref, mask_ref, w_ref, qt_ref, kv_hbm, xn_hbm, do_in, stat_in, mixed_in, lat_in, grads_hbm, vec_in, lang_in, latsum_in, wq_ref, lat_raw, lgain_ref,
                  g_out, mixed_out, dw_out, dlat_out, small_out, glat_out, vec_out, dwq_out,
                  x_ref, xn_ref, cols_ref, kv_ref, dkv_ref, q_ref, do_ref, stat_ref, stat_cols, dq_ref, dw_ref, dw_tmp,
                  g_half, g_chip, g_z, w_half, w_sib, w_chip, w_z, q_half, q_sib, q_chip, q_z, s_half, s_sib, s_chip, s_z,
                  small_ref, s_ref, l_sib, l_half, l_y, l_sum, l_z, l_tot, dq_out, latn_ref, lat8_ref,
                  g_stage, w_stage, tq_ref, t_part, t_got, t_z, y_buf, c_buf, x_buf, dwq_ref,
                  g_ss, g_rs, w_ss, w_rs, q_ss, q_rs, s_ss, s_rs, l_ss, l_rs, t_ss, t_rs, do_ss, do_rs, misc_ss, misc_rs, mix_ss, mix_rs, a_ss, a_rs, load_sem, kv_sem, stage_sem):
    items, blk, me, hi, core = places()
    shards = lax.axis_size("heads")
    seqs, width, length = x_ref.shape
    heads, rows, head_dim = q_ref.shape
    local_rows = rows // 2
    per_shard = heads // shards
    cols = per_shard * head_dim
    stat_rows = stat_in.shape[0]
    other = 1 - blk
    to_x, to_sib = mesh_at(db=other), mesh_at(di=items + 1 - 2 * core)
    to_y = mesh_at(di=(1 - hi) * 2 + core)
    z_of = [lax.rem(me + d, shards) for d in range(shards)]
    z_back = [lax.rem(me + shards - d, shards) for d in range(shards)]
    my_rows = pl.ds(pl.multiple_of(blk * local_rows, 128), local_rows)
    other_rows = pl.ds(pl.multiple_of(other * local_rows, 128), local_rows)
    pending = []
    dot_ref = w_sib.at[:, :, :, pl.ds(0, rows)]
    grads = [Reduce(None, g_half.at[pl.ds(m, 1)], None, g_chip.at[:, pl.ds(m, 1)], g_z.at[m], dlat_out.at[pl.ds(m, 1)], g_ss.at[m], g_rs.at[m], pending, m != 1,
                        g_stage.at[pl.ds(m, 1)], stage_sem.at[m])
             for m in range(3)]
    pair = [Reduce(dw_ref.at[pl.ds(m, 1)], w_half.at[pl.ds(m, 1)], w_sib.at[pl.ds(m, 1)], w_chip.at[:, pl.ds(m, 1)], w_z.at[m],
                   dw_out.at[pl.ds(m, 1)], w_ss.at[m], w_rs.at[m], pending, m == 0, w_stage.at[pl.ds(m, 1)], stage_sem.at[3 + m]) for m in range(2)]
    query = Reduce(dq_ref, q_half, q_sib, q_chip, q_z, dq_out, q_ss, q_rs, pending, False)
    small = Reduce(s_ref, s_half, s_sib, s_chip, s_z, small_out, s_ss, s_rs, pending)
    greet([to_sib, to_x, to_y] + [mesh_at(dh=z_of[d]) for d in range(1, shards)])

    def arrived(where, ss, rs):
        pltpu.make_async_remote_copy(src_ref=where, dst_ref=where, send_sem=ss, recv_sem=rs,
                                     device_id=to_sib, device_id_type=pl.DeviceIdType.MESH).wait_recv()

    pending.append(send(stat_in, stat_ref.at[pl.ds(0, stat_rows), my_rows], misc_ss.at[0], misc_rs.at[0], to_x))

    def send_do(s):
        pending.append(send(do_in.at[s], dot_ref.at[s, :, :, my_rows], do_ss.at[s], do_rs.at[s], to_x))

    mine = pl.ds(me * seqs, seqs)
    near = me + 1 - 2 * lax.rem(me, 2)
    far, cross = lax.rem(me + 2, 4), lax.rem(near + 2, 4)
    far_rows, near_rows, cross_rows = (pl.ds(at * seqs, seqs) for at in (far, near, cross))

    def mixed_far():
        pending.append(send(mixed_in, mixed_out.at[mine], mix_ss.at[0], mix_rs.at[0], mesh_at(dh=far)))

    def mixed_near():
        pending.append(send(mixed_in, mixed_out.at[mine], mix_ss.at[1], mix_rs.at[1], mesh_at(dh=near)))

    def mixed_cross():
        arrived(mixed_out.at[far_rows], mix_ss.at[0], mix_rs.at[0])
        pending.append(send(mixed_out.at[far_rows], mixed_out.at[far_rows], mix_ss.at[2], mix_rs.at[2], mesh_at(dh=near)))

    def latents_share():
        pending.append(send(lat_in, latn_ref.at[my_rows], misc_ss.at[1], misc_rs.at[1], to_x))

    loads = [
        pltpu.make_async_copy(xn_hbm, xn_ref, load_sem.at[0]),
        pltpu.make_async_copy(x_hbm, x_ref, load_sem.at[1]),
        pltpu.make_async_copy(grads_hbm, g_half, load_sem.at[2]),
        pltpu.make_async_copy(mixed_in, mixed_out.at[mine], load_sem.at[3]),
        pltpu.make_async_copy(lat_raw.at[pl.ds(pl.multiple_of(core * 64 + hi * 32 + me * 8, 8), 8)], lat8_ref, load_sem.at[4]),
    ]
    own_sum = pltpu.make_async_copy(latsum_in.at[pl.ds(pl.multiple_of(core * (local_rows // 2), 8), local_rows // 2)], l_half, load_sem.at[13])
    own_sum.start()
    latn_ref[my_rows] = lat_in[...]
    own_do = pltpu.make_async_copy(do_in, dot_ref.at[:, :, :, my_rows], load_sem.at[5])

    def load_pair(n, start):
        s, h = n // heads, lax.rem(n, heads)
        slot = lax.rem(n, 2)
        copy = pltpu.make_async_copy(kv_hbm.at[s, :, pl.ds(pl.multiple_of(h * head_dim, 16), head_dim)], kv_ref.at[slot], kv_sem.at[slot])
        copy.start() if start else copy.wait()

    load_pair(0, True)
    for copy in loads:
        copy.start()
    own_do.start()
    stat_ref[:stat_rows, my_rows] = stat_in[...]
    stat_ref[stat_rows:] = jnp.zeros((128 - stat_rows, rows), F32)
    for h in range(heads):
        q_ref[h] = jnp.transpose(qt_ref[h % per_shard, h // per_shard])
    dq_ref[...] = jnp.zeros_like(dq_ref)
    small_ref[...] = jnp.zeros_like(small_ref)

    def stats_ready():
        arrived(stat_ref.at[pl.ds(0, stat_rows), other_rows], misc_ss.at[0], misc_rs.at[0])
        stat_cols[...] = jnp.transpose(stat_ref[...])

    scale = head_dim ** (-0.5)
    factor = LOG2E * scale
    lane = lax.broadcasted_iota(jnp.int32, (rows, 128), 1)
    cols_ref[...] = jnp.transpose(rows_ref[...])
    gain = cols_ref[:, 0:1]

    def turn_grads(s):
        arrived(dot_ref.at[s, :, :, other_rows], do_ss.at[s], do_rs.at[s])
        for h in range(heads):
            inner = h % per_shard * head_dim
            do_ref[h] = jnp.transpose(dot_ref[s, h // per_shard, inner:inner + head_dim])

    def head_steps(s, group):
        def head_step(h, _):
            n = s * heads + h
            slot = lax.rem(n, 2)
            load_pair(n, False)

            @pl.when(n + 1 < seqs * heads)
            def _():
                load_pair(n + 1, True)

            at = pl.ds(pl.multiple_of(h * head_dim, 16), head_dim)
            lse = jnp.sum(jnp.where(lane == s * 2 * heads + h, stat_cols[...], 0.0), axis=1, keepdims=True)
            delta = jnp.sum(jnp.where(lane == s * 2 * heads + heads + h, stat_cols[...], 0.0), axis=1, keepdims=True)
            keys = kv_ref[slot, 0]
            weights = jnp.exp2(dot(q_ref[h], keys) * factor + mask_ref[s] - lse)
            part = pl.ds(pl.multiple_of(lax.rem(h, per_shard) * head_dim, 16), head_dim)
            dkv_ref[s, 1, at] = dot(dot_ref[s, h // per_shard, part], weights.astype(BF16)).astype(BF16)
            grad = dot(do_ref[h], kv_ref[slot, 1]) - delta
            grad = (weights * grad).astype(BF16)
            dkv_ref[s, 0, at] = (dot(qt_ref[lax.rem(h, per_shard), h // per_shard], grad) * scale).astype(BF16)
            dq_ref[0, h // per_shard, part] += dot_nt(keys, grad) * scale
            return 0

        lax.fori_loop(2 * group, 2 * group + 2, head_step, 0)

    piece = min(256, length)

    def byte_steps(s):
        def byte_step(i, carry):
            at = pl.ds(pl.multiple_of(i * piece, piece), piece)
            grad = dot(w_ref[0], dkv_ref[s, 0, :, at]) + dot(w_ref[1], dkv_ref[s, 1, :, at])
            normed, inverse = norm_columns(x_ref[s, :, at], cols_ref[:, 2 + s:3 + s])
            small_ref[:, 0:1] += jnp.sum(grad * normed, axis=1, keepdims=True)
            small_ref[:, 1:2] += jnp.sum(grad, axis=1, keepdims=True)
            scaled = grad * gain
            first = jnp.mean(scaled, axis=0, keepdims=True)
            second = jnp.mean(scaled * normed, axis=0, keepdims=True)
            shifted = (scaled - first - normed * second) * inverse
            x_ref[s, :, at] = shifted.astype(BF16)
            return carry + jnp.sum(shifted, axis=1, keepdims=True)

        small_ref[:, 2 + s:3 + s] = lax.fori_loop(0, length // piece, byte_step, jnp.zeros((width, 1), F32))
        share = width // shards
        own = pltpu.make_async_copy(x_ref.at[s, pl.ds(pl.multiple_of(me * share, 16), share)], g_out.at[me * seqs + s], load_sem.at[6 + s])
        own.start()
        loads.append(own)

    def bytes_send(s, d):
        share = width // shards
        there = pl.ds(pl.multiple_of(z_back[d] * share, 16), share)
        pending.append(send(x_ref.at[s, there], g_out.at[me * seqs + s], a_ss.at[s, d], a_rs.at[s, d], mesh_at(dh=z_back[d])))

    half_rows, quarter = local_rows // 2, local_rows // 4
    piece_rows = quarter // shards

    def latents_send():
        theirs = latsum_in.at[pl.ds(pl.multiple_of((1 - core) * half_rows, 8), half_rows)]
        pending.append(send(theirs, l_sib, l_ss.at[0], l_rs.at[0], to_sib))

    def latents_sib():
        arrived(l_sib, l_ss.at[0], l_rs.at[0])
        own_sum.wait()
        l_half[...] += l_sib[...]
        pending.append(send(l_half.at[pl.ds(pl.multiple_of((1 - hi) * quarter, 8), quarter)], l_y, l_ss.at[1], l_rs.at[1], to_y))

    def latents_y():
        arrived(l_y, l_ss.at[1], l_rs.at[1])
        l_sum[...] = (l_half[pl.ds(pl.multiple_of(hi * quarter, 8), quarter)] + l_y[...]).reshape(l_sum.shape)
        for d in range(1, shards):
            pending.append(send(l_sum.at[z_back[d]], l_z.at[d - 1], l_ss.at[1 + d], l_rs.at[1 + d], mesh_at(dh=z_back[d])))

    def latents_z():
        total = l_sum[me]
        for d in range(1, shards):
            arrived(l_z.at[d - 1], l_ss.at[1 + d], l_rs.at[1 + d])
            total += l_z[d - 1]
        l_tot[...] = total

    def third_first():
        tq_ref[...] = jnp.transpose(dq_out[0, :, my_rows])
        rows_here = tq_ref[pl.ds(pl.multiple_of(core * half_rows + hi * quarter, 8), quarter)].astype(BF16)
        t_part[...] = dot(rows_here, wq_ref[...]).reshape(t_part.shape)
        for d in range(1, shards):
            pending.append(send(t_part.at[z_back[d]], t_got.at[d - 1], t_ss.at[0, d], t_rs.at[0, d], mesh_at(dh=z_back[d])))

    def third_z():
        grad = t_part[me]
        for d in range(1, shards):
            arrived(t_got.at[d - 1], t_ss.at[0, d], t_rs.at[0, d])
            grad += t_got[d - 1]
        loads[4].wait()
        _, normed, inverse = norm_keep(lat8_ref[...], 1.0, 0.0)
        t_z[me, :piece_rows] = l_tot[...] + norm_back(grad, normed, inverse, lgain_ref[0:1])
        t_z[me, piece_rows:] = jnp.zeros((8, lat8_ref.shape[1]), F32)
        t_z[me, piece_rows:piece_rows + 1] = jnp.sum(grad * normed, axis=0, keepdims=True)
        t_z[me, piece_rows + 1:piece_rows + 2] = jnp.sum(grad, axis=0, keepdims=True)
        for d in range(1, shards):
            pending.append(send(t_z.at[me], t_z.at[me], t_ss.at[1, d], t_rs.at[1, d], mesh_at(dh=z_back[d])))

    def third_y():
        for d in range(1, shards):
            arrived(t_z.at[z_of[d]], t_ss.at[1, d], t_rs.at[1, d])
        y_buf[hi, :quarter] = t_z[:, :piece_rows].reshape(quarter, t_z.shape[2])
        y_buf[hi, quarter:] = t_z[0, piece_rows:] + t_z[1, piece_rows:] + t_z[2, piece_rows:] + t_z[3, piece_rows:]
        pending.append(send(y_buf.at[hi], y_buf.at[hi], t_ss.at[2, 0], t_rs.at[2, 0], to_y))

    def third_core():
        arrived(y_buf.at[1 - hi], t_ss.at[2, 0], t_rs.at[2, 0])
        c_buf[core, :quarter] = y_buf[0, :quarter]
        c_buf[core, quarter:half_rows] = y_buf[1, :quarter]
        c_buf[core, half_rows:] = y_buf[0, quarter:] + y_buf[1, quarter:]
        pending.append(send(c_buf.at[core], c_buf.at[core], t_ss.at[2, 1], t_rs.at[2, 1], to_sib))

    def third_x():
        arrived(c_buf.at[1 - core], t_ss.at[2, 1], t_rs.at[2, 1])
        glat_out[:half_rows] = c_buf[0, :half_rows]
        glat_out[half_rows:] = c_buf[1, :half_rows]
        x_buf[blk] = c_buf[0, half_rows:] + c_buf[1, half_rows:]
        pending.append(send(x_buf.at[blk], x_buf.at[blk], t_ss.at[2, 2], t_rs.at[2, 2], to_x))

    def third_end():
        arrived(x_buf.at[other], t_ss.at[2, 2], t_rs.at[2, 2])
        vec_out[...] = x_buf[0] + x_buf[1]

    def query_weights():
        arrived(latn_ref.at[other_rows], misc_ss.at[1], misc_rs.at[1])
        query_low = dq_out[0].astype(BF16)
        for i in range(dwq_out.shape[0] // 256):
            if i:
                loads[-1].wait()
            dwq_ref[...] = dot_nt(jnp.transpose(latn_ref[:, i * 256:(i + 1) * 256]), query_low)
            copy = pltpu.make_async_copy(dwq_ref, dwq_out.at[pl.ds(i * 256, 256)], load_sem.at[8 + i])
            copy.start()
            loads.append(copy)

    def small_start():
        wide_lane = lax.broadcasted_iota(jnp.int32, (width, 128), 1)
        block = jnp.where(wide_lane == 32, small_ref[:, 0:1], 0.0) + jnp.where(wide_lane == 33, small_ref[:, 1:2], 0.0)
        for s in range(seqs):
            block += small_ref[:, 2 + s:3 + s] * lang_in[s:s + 1]
        share = width // shards
        for h in range(shards):
            s_ref[0, h, :, :128] = block[h * share:(h + 1) * share]
            s_ref[0, h, :, 128:] = jnp.zeros((share, 128), F32)
            for v in range(vec_in.shape[0]):
                for b in range(vec_in.shape[1] // 128):
                    s_ref[0, h, v * 10 + b:v * 10 + b + 1, 128:] = vec_in[v:v + 1, b * 128:(b + 1) * 128]
        small.start()

    def weight_steps(part):
        def weight_step(h, _):
            at = pl.ds(pl.multiple_of(h * cols, 16), cols)
            total = dot_nt(dkv_ref[0, part, at], xn_ref[0])
            for s in range(1, seqs):
                total += dot_nt(dkv_ref[s, part, at], xn_ref[s])
            dw_tmp[...] = total.astype(BF16)
            w_half[part, h] = dw_tmp[:, pl.ds(pl.multiple_of(core * (width // 2), 128), width // 2)]
            dw_ref[part, h] = dw_tmp[:, pl.ds(pl.multiple_of((1 - core) * (width // 2), 128), width // 2)]
            return 0
        lax.fori_loop(0, shards, weight_step, 0)

    mixed_far()
    send_do(0)
    mixed_near()
    own_do.wait()
    stats_ready()
    turn_grads(0)
    send_do(1)
    head_steps(0, 0)
    head_steps(0, 1)
    loads[2].wait()
    grads[0].send_chips()
    head_steps(0, 2)
    head_steps(0, 3)
    loads[1].wait()
    byte_steps(0)
    bytes_send(0, 3)
    grads[2].send_chips()
    bytes_send(0, 1)
    turn_grads(1)
    head_steps(1, 0)
    head_steps(1, 1)
    head_steps(1, 2)
    head_steps(1, 3)
    query.start()
    grads[2].join_first()
    bytes_send(0, 2)
    loads[0].wait()
    weight_steps(0)
    latents_send()
    query.join_sib()
    query.send_chips()
    grads[2].join_chips()
    latents_sib()
    byte_steps(1)
    grads[0].join_first()
    small_start()
    query.join_first()
    query.join_chips()
    pair[0].start()
    grads[0].join_chips()
    grads[1].send_chips()
    small.join_sib()
    small.send_chips()
    grads[2].join_near()
    pair[0].join_sib()
    pair[0].send_chips()
    bytes_send(1, 3)
    bytes_send(1, 1)
    query.join_near()
    small.join_first()
    query.join_z()
    latents_y()
    weight_steps(1)
    pair[0].join_first()
    grads[1].join_first()
    pair[1].start()
    grads[0].join_near()
    grads[2].join_z()
    pair[0].join_chips()
    latents_z()
    query.share_chips()
    query.share_sib()
    query.finish()
    small.join_chips()
    grads[0].join_z()
    grads[1].join_chips()
    small.join_near()
    latents_share()
    grads[2].share_chips()
    grads[0].share_chips()
    pair[0].join_near()
    small.join_z()
    third_first()
    pair[1].join_sib()
    mixed_cross()
    pair[1].send_chips()
    grads[1].join_near()
    third_z()
    pair[0].join_z()
    pair[1].join_first()
    pair[1].join_chips()
    small.share_chips()
    bytes_send(1, 2)
    third_y()
    grads[1].join_z()
    pair[1].join_near()
    small.share_sib()
    grads[1].share_chips()
    pair[0].share_chips()
    query_weights()
    grads[2].share_sib()
    pair[1].join_z()
    grads[1].share_sib()
    grads[0].share_sib()
    third_core()
    pair[1].share_chips()
    third_x()
    small.finish()
    pair[0].share_sib()
    pair[1].share_sib()
    pair[0].finish()
    third_end()
    pair[1].finish()
    grads[2].finish()
    grads[0].finish()
    grads[1].finish()
    arrived(mixed_out.at[near_rows], mix_ss.at[1], mix_rs.at[1])
    arrived(mixed_out.at[cross_rows], mix_ss.at[2], mix_rs.at[2])
    for d in range(1, shards):
        for s in range(seqs):
            arrived(g_out.at[z_of[d] * seqs + s], a_ss.at[s, d], a_rs.at[s, d])
    loads[3].wait()
    for own in loads[5:5 + seqs] + loads[-1:]:
        own.wait()
    for copy in pending:
        copy.wait_send()


def second_call(x_cols, rows_in, mask, w_cols, qt, pairs, xn, grad_out, stats, mixed, lat_low, grads, vectors, lang_rows, lat_sum, w_query, lat_f32, lat_gain):
    seqs, width, length = x_cols.shape
    rows, width_lat = qt.shape[3], pairs.shape[2]
    local_rows = lat_low.shape[0]
    shards = lax.axis_size("heads")
    heads = HEADS
    head_dim = width_lat // heads
    cols = width_lat // shards
    share = cols // 4
    whole = pl.BlockSpec(memory_space=pltpu.VMEM)
    hbm = pl.BlockSpec(memory_space=pl.ANY)
    out = jax.ShapeDtypeStruct
    vmem = pltpu.VMEM
    sem = pltpu.SemaphoreType.DMA

    assert seqs == 2

    def reduce_buffers(n, lanes, kind, cols=cols):
        half, share = lanes // 2, cols // 4
        return [vmem((n, shards, cols, half), kind), vmem((n, shards, cols, half), kind), vmem((6, n, 2, share, half), kind),
                vmem((shards - 1, n, share, half), kind)]

    return pl.pallas_call(
        second_kernel,
        in_specs=[hbm, whole, whole, whole, whole, hbm, hbm, hbm, whole, hbm, whole, hbm, whole, whole, hbm, whole, hbm, whole],
        out_specs=[hbm, hbm, hbm, hbm, whole, whole, whole, hbm],
        out_shape=[
            out((shards * seqs, width // shards, length), BF16),
            out((shards * seqs, local_rows, width_lat), BF16),
            out((2, cols, width), BF16),
            out((3, cols, width_lat), BF16),
            out((1, width // shards, 256), F32),
            out((local_rows, width_lat), F32),
            out((8, width_lat), F32),
            out((width_lat, cols), F32),
        ],
        scratch_shapes=[
            vmem((seqs, width, length), BF16),
            vmem((seqs, width, length), BF16),
            vmem((width, rows_in.shape[0]), F32),
            vmem((2, 2, head_dim, length), BF16),
            vmem((seqs, 2, width_lat, length), BF16),
            vmem((heads, rows, head_dim), BF16),
            vmem((heads, rows, head_dim), BF16),
            vmem((128, rows), F32),
            vmem((rows, 128), F32),
            vmem((1, shards, cols, rows), F32),
            vmem((2, shards, cols, width // 2), BF16),
            vmem((cols, width), BF16),
        ] + [
            vmem((3, shards, cols, width_lat // 2), BF16),
            vmem((6, 3, 2, share, width_lat // 2), BF16),
            vmem((3, 3, 1, share, width_lat // 2), BF16),
        ] + reduce_buffers(2, width, BF16)[:3] + [vmem((2, 3, 1, share, width // 2), BF16)]
        + reduce_buffers(1, rows, F32)
        + reduce_buffers(1, 256, F32, width // shards) + [
            vmem((width, 8), F32),
            vmem((1, shards, width // shards, 256), F32),
            vmem((local_rows // 2, width_lat), F32),
            vmem((local_rows // 2, width_lat), F32),
            vmem((local_rows // 4, width_lat), F32),
            vmem((shards, local_rows // 16, width_lat), F32),
            vmem((shards - 1, local_rows // 16, width_lat), F32),
            vmem((local_rows // 16, width_lat), F32),
            vmem((1, cols, rows), F32),
            vmem((rows, width_lat), BF16),
            vmem((local_rows // 16, width_lat), F32),
            vmem((3, share, width_lat // 2), BF16),
            vmem((2, share, width // 2), BF16),
            vmem((local_rows, cols), F32),
            vmem((shards, local_rows // 16, width_lat), F32),
            vmem((shards - 1, local_rows // 16, width_lat), F32),
            vmem((shards, local_rows // 16 + 8, width_lat), F32),
            vmem((2, local_rows // 4 + 8, width_lat), F32),
            vmem((2, local_rows // 2 + 8, width_lat), F32),
            vmem((2, 8, width_lat), F32),
            vmem((256, cols), F32),
        ] + [sem((3, 14))] * 2 + [sem((2, 14))] * 2 + [sem((14,))] * 4 + [sem((6,))] * 2 + [sem((3, shards))] * 2 + [sem((seqs,))] * 2 + [sem((2,))] * 2 + [sem((shards,))] * 2 + [sem((seqs, shards))] * 2
        + [sem((16,)), sem((2,)), sem((5,))],
        compiler_params=pltpu.CompilerParams(vmem_limit_bytes=VMEM_LIMIT, collective_id=2, has_side_effects=True),
        name="second",
    )(x_cols, rows_in, mask, w_cols, qt, pairs, xn, grad_out, stats, mixed, lat_low, grads, vectors, lang_rows, lat_sum, w_query, lat_f32, lat_gain)


def middle_kernel(att_ref, lat_ref, cot_ref, all_hbm, bup_tiles, vecs_ref, lse_ref,
                  mixed_ref, do_ref, stat_ref, half_ref, vec_ref, sum_ref,
                  rows_ref, mid_ref, low_ref, hid_ref, norm_ref, a_ref, b_src, b_ref, bup_ref, all_ref, a_ss, a_rs, b_ss, b_rs, load_sem):
    items, _, _, _, core = places()
    to_sib = mesh_at(di=items + 1 - 2 * core)
    seqs, width, local_rows = att_ref.shape
    rows = seqs * local_rows
    heads = lse_ref.shape[1]
    head_dim = width // heads
    half = width // 2
    block = 256
    pending = []
    loads = [pltpu.make_async_copy(all_hbm.at[i], all_ref.at[i], load_sem.at[i]) for i in range(3)]
    for copy in loads:
        copy.start()
    greet([to_sib])
    shards, cols = half_ref.shape[1:3]
    for h in range(shards):
        bup_ref[:, h * cols:(h + 1) * cols] = bup_tiles[h, 7:8, :cols]
    gain_ref, bias_ref, bdown_ref = vecs_ref.at[pl.ds(2, 1)], vecs_ref.at[pl.ds(3, 1)], vecs_ref.at[pl.ds(4, 1)]

    def block_loop(body):
        def step(i, _):
            body(pl.ds(pl.multiple_of(i * block, block), block))
            return 0
        lax.fori_loop(0, width // block, step, 0)

    def share_a(i):
        pending.append(send(a_ref.at[i, 0], a_ref.at[i, 1], a_ss.at[i], a_rs.at[i], to_sib))

    def share_b(i):
        theirs = b_src.at[i, :, pl.ds(pl.multiple_of((1 - core) * half, 128), half)]
        pending.append(send(theirs, b_ref.at[i, 1], b_ss.at[i], b_rs.at[i], to_sib))
        b_ref[i, 0] = b_src[i, :, pl.ds(pl.multiple_of(core * half, 128), half)]

    cot = cot_ref[...]
    b_src[2] = cot
    share_b(2)
    for s in range(seqs):
        at = slice(s * local_rows, (s + 1) * local_rows)
        low = att_ref[s].astype(BF16)
        a_ref[0, 0, :, at] = low
        rows_ref[at] = jnp.transpose(att_ref[s]).astype(BF16)
    share_a(0)

    def branch(at):
        latent = lat_ref[:, at].astype(F32)
        mid_ref[:, at] = dot(rows_ref[...], all_ref[0, :, at]) + jnp.concatenate([latent] * seqs, axis=0)
    loads[0].wait()
    block_loop(branch)
    mid_out, normed, inverse = norm_keep(mid_ref[...], gain_ref[...], bias_ref[...])
    norm_ref[...] = normed
    b_src[1] = mid_out.astype(BF16)
    share_b(1)

    def up(at):
        value = dot_nt(b_src[1], all_ref[1, at]) + bup_ref[:, at]
        square = value * value
        bend = jnp.tanh(0.7978845608028654 * (value + 0.044715 * (square * value)))
        active = 0.5 * value * (1.0 + bend)
        slope = 0.5 * (1.0 + bend) + 0.5 * value * (1.0 - bend * bend) * (0.7978845608028654 * (1.0 + 0.134145 * square))
        rows_ref[:, at] = active.astype(BF16)
        grad = (dot_nt(cot_ref[...], all_ref[2, at]) * slope).astype(BF16)
        low_ref[:, at] = grad
        vec_ref[2:3, at] = jnp.sum(grad.astype(F32), axis=0, keepdims=True)
        a_ref[2, 0, at] = jnp.transpose(active.astype(BF16))
        a_ref[1, 0, at] = jnp.transpose(grad)
    loads[1].wait()
    loads[2].wait()
    block_loop(up)
    share_a(2)
    share_a(1)

    def down(at):
        hid_ref[:, at] = dot(low_ref[...], all_ref[1, :, at])
        out = mid_ref[:, at] + dot(rows_ref[...], all_ref[2, :, at]) + bdown_ref[:, at]
        for s in range(seqs):
            mixed_ref[s, :, at] = out[s * local_rows:(s + 1) * local_rows].astype(BF16)
    block_loop(down)
    grad = hid_ref[...]
    normed = norm_ref[...]
    vec_ref[0:1] = jnp.sum(grad * normed, axis=0, keepdims=True)
    vec_ref[1:2] = jnp.sum(grad, axis=0, keepdims=True)
    vec_ref[3:4] = jnp.sum(cot_ref[...].astype(F32), axis=0, keepdims=True)
    grad = cot_ref[...].astype(F32) + norm_back(grad, normed, inverse, gain_ref[...])
    b_src[0] = grad.astype(BF16)
    share_b(0)
    total = grad[:local_rows]
    for s in range(1, seqs):
        total += grad[s * local_rows:(s + 1) * local_rows]
    sum_ref[...] = total

    def out(h, _):
        at = pl.ds(pl.multiple_of(h * head_dim, 16), head_dim)
        grad = dot_nt(all_ref[0, at], b_src[0]).astype(BF16)
        for s in range(seqs):
            part = grad[:, s * local_rows:(s + 1) * local_rows]
            do_ref[s, at] = part
            delta = jnp.sum(part.astype(F32) * att_ref[s, at], axis=0, keepdims=True)
            stat_ref[pl.ds((2 * s + 1) * heads + h, 1)] = delta
        return 0
    lax.fori_loop(0, heads, out, 0)
    for s in range(seqs):
        stat_ref[2 * s * heads:(2 * s + 1) * heads] = lse_ref[s]

    def arrived(where, ss, rs):
        pltpu.make_async_remote_copy(src_ref=where, dst_ref=where, send_sem=ss, recv_sem=rs,
                                     device_id=to_sib, device_id_type=pl.DeviceIdType.MESH).wait_recv()

    for i in (2, 1, 0):
        arrived(a_ref.at[i, 1], a_ss.at[i], a_rs.at[i])
        arrived(b_ref.at[i, 1], b_ss.at[i], b_rs.at[i])

        def weight(h, _):
            at = pl.ds(pl.multiple_of(h * cols, 16), cols)
            half_ref[i, h] = (dot(a_ref[i, 0, at], b_ref[i, 0]) + dot(a_ref[i, 1, at], b_ref[i, 1])).astype(BF16)
            return 0
        lax.fori_loop(0, shards, weight, 0)
    for copy in pending:
        copy.wait_send()


def middle_call(att, latents, cot, weights, b_up, vecs, lse):
    seqs, width, local_rows = att.shape
    rows = seqs * local_rows
    heads = lse.shape[1]
    shards = lax.axis_size("heads")
    whole = pl.BlockSpec(memory_space=pltpu.VMEM)
    out, vmem, sem = jax.ShapeDtypeStruct, pltpu.VMEM, pltpu.SemaphoreType.DMA
    return pl.pallas_call(
        middle_kernel,
        in_specs=[whole, whole, whole, pl.BlockSpec(memory_space=pl.ANY), whole, whole, whole],
        out_specs=[whole] * 6,
        out_shape=[
            out((seqs, local_rows, width), BF16),
            out((seqs, width, local_rows), BF16),
            out((2 * seqs * heads, local_rows), F32),
            out((3, shards, width // shards, width // 2), BF16),
            out((4, width), F32),
            out((local_rows, width), F32),
        ],
        scratch_shapes=[
            vmem((rows, width), BF16), vmem((rows, width), F32), vmem((rows, width), BF16), vmem((rows, width), F32), vmem((rows, width), F32),
            vmem((3, 2, width, rows), BF16), vmem((3, rows, width), BF16), vmem((3, 2, rows, width // 2), BF16),
            vmem((1, width), F32), vmem((3, width, width), BF16),
            sem((3,)), sem((3,)), sem((3,)), sem((3,)), sem((3,)),
        ],
        compiler_params=pltpu.CompilerParams(vmem_limit_bytes=VMEM_LIMIT, collective_id=4, has_side_effects=True),
        name="middle",
    )(att, latents, cot, weights, b_up, vecs, lse)


REST = ("items", "blk")
ALL = ("heads", "items", "blk")


def gather_rows(shard):
    count = lax.axis_size("items") * lax.axis_size("blk")
    me = lax.axis_index("items") * lax.axis_size("blk") + lax.axis_index("blk")
    share = shard.shape[0] // count
    part = lax.dynamic_slice_in_dim(shard, me * share, share, 0)
    return lax.all_gather(part, ALL, axis=0, tiled=True)


def scatter_rows(whole):
    part = lax.psum_scatter(whole.astype(BF16), ALL, scatter_dimension=0, tiled=True)
    return lax.all_gather(part, REST, axis=0, tiled=True)


def general_device(inputs, padding, language, lang_table, latents, in_gain, in_bias, lat_gain, lat_bias, mid_gain, mid_bias,
              w_query, w_key, w_value, w_out, w_up, b_up, w_down, b_down, cotangent):
    length, local_seqs, width = inputs.shape
    local_rows, width_lat = latents.shape
    cols = w_query.shape[1]
    head_dim = width_lat // HEADS
    per_shard = cols // head_dim
    shards = lax.axis_size("heads")
    blocks = lax.axis_size("blk")
    rows = local_rows * blocks
    seqs = local_seqs // shards
    me = lax.axis_index("heads")
    first = me * seqs

    pair_shard = jnp.concatenate([w_key.T, w_value.T], axis=0)
    pair_rows = gather_rows(pair_shard)
    latent_shard = jnp.concatenate([w_out, w_up.T, w_down], axis=0)
    lat_all = gather_rows(latent_shard).reshape(shards, 3, cols, width_lat)
    out_all, up_all, down_all = (lat_all[:, i].reshape(width_lat, width_lat) for i in range(3))

    all_latents = lax.all_gather(latents, "blk", axis=0, tiled=True).astype(F32)
    lat_out, _, _ = norm_keep(all_latents, lat_gain, lat_bias)
    lat_low = lat_out.astype(BF16)
    query_part = dot(lat_low, w_query).astype(BF16)
    queries = lax.all_gather(query_part, "heads", axis=1, tiled=True)
    q = queries.reshape(rows, HEADS, head_dim).transpose(1, 0, 2)

    own = lax.dynamic_slice_in_dim(inputs, first, seqs, 1)
    x_cols = jnp.transpose(own, (1, 2, 0))
    live = jnp.transpose(lax.dynamic_slice_in_dim(padding, first, seqs, 1))
    mask = jnp.where(live > 0, 0.0, MASKED).astype(F32)[:, None, :]
    own_lang = lax.dynamic_slice_in_dim(language, first, seqs, 0)
    onehot = (own_lang[:, None] == jnp.arange(lang_table.shape[0], dtype=jnp.int32)[None, :]).astype(F32)
    emb = jnp.dot(onehot, lang_table.astype(F32), precision=lax.Precision.HIGHEST)[:, :, None]
    gain_col, bias_col = in_gain[:, None], in_bias[:, None]

    pairs, o_cols, lse = forward_call(x_cols, emb, gain_col, bias_col, pair_rows, q, mask, per_shard)

    parts = o_cols.reshape(seqs, width_lat, blocks, local_rows).transpose(2, 0, 3, 1)
    parts = lax.all_to_all(parts, "blk", 0, 0, tiled=True).astype(F32)
    lse_parts = lse.reshape(seqs, HEADS, blocks, local_rows).transpose(2, 0, 3, 1)
    lse_parts = lax.all_to_all(lse_parts, "blk", 0, 0, tiled=True)
    top = jnp.max(lse_parts, axis=0)
    shares = jnp.exp2(lse_parts - top)
    total = jnp.sum(shares, axis=0)
    own_lse = top + jnp.log2(total)
    shares = shares / total
    attended = jnp.sum(parts.reshape(blocks, seqs, local_rows, HEADS, head_dim) * shares[..., None], axis=0)
    att_low = attended.reshape(seqs * local_rows, width_lat).astype(BF16)

    cot = lax.dynamic_slice_in_dim(cotangent, first, seqs, 0).reshape(seqs * local_rows, width_lat)
    lat_f32 = latents.astype(F32)
    middle = (lat_f32[None] + dot(att_low, out_all).reshape(seqs, local_rows, width_lat)).reshape(seqs * local_rows, width_lat)
    mid_out, mid_normed, mid_inverse = norm_keep(middle, mid_gain, mid_bias)
    mid_low = mid_out.astype(BF16)
    b_up_all = lax.all_gather(b_up, "heads", axis=0, tiled=True)
    hidden = dot_nt(mid_low, up_all) + b_up_all
    active, gelu_back = jax.vjp(jax.nn.gelu, hidden)
    active_low = active.astype(BF16)
    own_mixed = (middle + dot(active_low, down_all) + b_down).astype(BF16).reshape(seqs, local_rows, width_lat)
    mixed_latents = lax.all_gather(own_mixed, "heads", axis=0, tiled=True)

    grad_b_down = jnp.sum(cot.astype(F32), axis=0)
    grad_w_down = dot(active_low.T, cot)
    grad_active = dot_nt(cot, down_all)
    grad_hidden = gelu_back(grad_active)[0].astype(BF16)
    grad_b_up = jnp.sum(grad_hidden.astype(F32), axis=0)
    grad_w_up = dot(grad_hidden.T, mid_low)
    grad_mid_norm = dot(grad_hidden, up_all)
    grad_mid_gain = jnp.sum(grad_mid_norm * mid_normed, axis=0)
    grad_mid_bias = jnp.sum(grad_mid_norm, axis=0)
    grad_middle = cot.astype(F32) + norm_back(grad_mid_norm, mid_normed, mid_inverse, mid_gain)
    grad_branch = grad_middle.astype(BF16)
    grad_w_out = dot(att_low.T, grad_branch)
    grad_att = dot_nt(grad_branch, out_all).astype(BF16).reshape(seqs, local_rows, width_lat)
    grad_att_heads = grad_att.reshape(seqs, local_rows, HEADS, head_dim)
    delta = jnp.sum(grad_att_heads.astype(F32) * attended, axis=-1)
    lat_sum = jnp.sum(grad_middle.reshape(seqs, local_rows, width_lat), axis=0)

    all_grad_att = lax.all_gather(grad_att, "blk", axis=1, tiled=True).reshape(seqs, rows, HEADS, head_dim)
    stats = lax.all_gather(jnp.concatenate([own_lse, delta], axis=-1), "blk", axis=1, tiled=True)
    stats = jnp.transpose(stats, (0, 2, 1))[..., None]
    g_cols, dw_pair, dq, dgain, dbias, demb = backward_call(
        x_cols, emb, gain_col, bias_col, pair_rows.T, q, q.transpose(0, 2, 1),
        all_grad_att.transpose(0, 2, 1, 3), all_grad_att.transpose(0, 2, 3, 1),
        stats[:, :HEADS], stats[:, HEADS:], mask, pairs, per_shard)

    send = g_cols.reshape(seqs, shards, width // shards, length).transpose(1, 0, 2, 3)
    got = lax.all_to_all(send, "heads", 0, 0, tiled=True)
    grad_inputs = got.reshape(local_seqs, width // shards, length).transpose(2, 0, 1)

    grad_rows = jnp.stack([grad_w_out, grad_w_up, grad_w_down], axis=0).reshape(3, shards, cols, width_lat)
    lat_total = scatter_rows(grad_rows.transpose(1, 0, 2, 3).reshape(-1, width_lat)).astype(F32)
    pair_total = scatter_rows(dw_pair).astype(F32)

    dq_part = lax.psum_scatter(dq.reshape(width_lat, rows).astype(BF16), "heads", scatter_dimension=0, tiled=True)
    query_low = lax.psum(dq_part, REST)
    grad_w_query = dot(lat_low.T, query_low.T)
    lat_mine = lax.dynamic_slice_in_dim(query_low, lax.axis_index("blk") * local_rows, local_rows, 1)
    grad_lat_part = dot(lat_mine.T, w_query.T)
    grad_lat_norm = lax.psum(grad_lat_part.astype(BF16), "heads").astype(F32)
    lat_sum = lax.psum(lat_sum.astype(BF16), ("heads", "items")).astype(F32)
    _, own_normed, own_inverse = norm_keep(lat_f32, lat_gain, lat_bias)
    grad_latents = lat_sum + norm_back(grad_lat_norm, own_normed, own_inverse, lat_gain)
    lat_small = jnp.concatenate([jnp.sum(grad_lat_norm * own_normed, axis=0), jnp.sum(grad_lat_norm, axis=0)])
    lat_small = lax.psum(lat_small, "blk")

    table = jnp.dot(onehot.T, demb[:, :, 0], precision=lax.Precision.HIGHEST)
    small = jnp.concatenate([table.reshape(-1), dgain[:, 0], dbias[:, 0], grad_mid_gain, grad_mid_bias, grad_b_up, grad_b_down])
    small = lax.psum(small, ALL)
    sizes = [table.size, width, width, width_lat, width_lat, width_lat, width_lat]
    ends = [sum(sizes[:i]) for i in range(len(sizes) + 1)]
    table, dgain, dbias, dmid_gain, dmid_bias, db_up, db_down = (small[ends[i]:ends[i + 1]] for i in range(7))
    share = width // shards
    table = lax.dynamic_slice_in_dim(table.reshape(-1, width), me * share, share, 1)
    return (
        mixed_latents,
        grad_inputs,
        grad_latents,
        table,
        lax.dynamic_slice_in_dim(dgain, me * share, share, 0),
        lax.dynamic_slice_in_dim(dbias, me * share, share, 0),
        lat_small[:width_lat],
        lat_small[width_lat:],
        dmid_gain,
        dmid_bias,
        grad_w_query,
        pair_total[:cols].T,
        pair_total[cols:].T,
        lat_total[:cols],
        lat_total[cols:2 * cols].T,
        lax.dynamic_slice_in_dim(db_up, me * cols, cols, 0),
        lat_total[2 * cols:],
        db_down,
    )


def fast_device(inputs, padding, language, lang_table, latents, in_gain, in_bias, lat_gain, lat_bias, mid_gain, mid_bias,
              w_query, w_key, w_value, w_out, w_up, b_up, w_down, b_down, cotangent):
    length, local_seqs, width = inputs.shape
    local_rows, width_lat = latents.shape
    cols = w_query.shape[1]
    head_dim = width_lat // HEADS
    per_shard = cols // head_dim
    shards = lax.axis_size("heads")
    blocks = lax.axis_size("blk")
    rows = local_rows * blocks
    seqs = local_seqs // shards
    me = lax.axis_index("heads")
    first = me * seqs

    vecs = (lat_gain, lat_bias, mid_gain, mid_bias, b_down, in_gain, in_bias, b_up)
    vecs = jnp.concatenate([jnp.pad(v, (0, width_lat - v.shape[0])) for v in vecs]).reshape(len(vecs), width_lat)
    wq_rows = w_query.T
    w_cols, lat_all, pairs, xn, att_cols, lse_cols, queries_t, lat_low, b_up_tiles, x_cols, rows_in, mask, lang_rows, lat_f32 = first_call(
        inputs, padding.T, language, lang_table, vecs, latents, wq_rows,
        jnp.stack([w_key.T, w_value.T]), jnp.stack([w_out, w_up.T, w_down]), rows, seqs)
    cot = lax.dynamic_slice_in_dim(cotangent, first, seqs, 0).reshape(seqs * local_rows, width_lat)
    own_mixed, grad_att, stats, grads, vectors, lat_sum = middle_call(att_cols, latents, cot, lat_all, b_up_tiles, vecs, lse_cols)
    grad_att = grad_att.reshape(seqs, shards, cols, local_rows)
    g_cols, mixed_latents, pair_total, lat_total, small, grad_latents, lat_small, grad_w_query = second_call(
        x_cols, rows_in, mask, w_cols, queries_t, pairs, xn, grad_att, stats, own_mixed, lat_low, grads, vectors, lang_rows, lat_sum,
        wq_rows, lat_f32, vecs)
    grad_inputs = g_cols.transpose(2, 0, 1)
    lat_total, pair_total = lat_total.astype(F32), pair_total.astype(F32)
    table = small[0, :, :lang_table.shape[0]].T
    dmid_gain, dmid_bias, db_up, db_down = small[0, :40, 128:].reshape(4, width_lat)
    return (
        mixed_latents,
        grad_inputs,
        grad_latents,
        table,
        small[0, :, 32],
        small[0, :, 33],
        lat_small[0],
        lat_small[1],
        dmid_gain,
        dmid_bias,
        grad_w_query,
        pair_total[0].T,
        pair_total[1].T,
        lat_total[0],
        lat_total[1].T,
        lax.dynamic_slice_in_dim(db_up, me * cols, cols, 0),
        lat_total[2],
        db_down,
    )


def solution(mesh):
    placed = (
        P("blk", "items", None), P("blk", "items"), P("items"), P(), P("blk", None), P(), P(), P(), P(), P(), P(),
        P(None, "heads"), P(None, "heads"), P(None, "heads"), P("heads", None), P(None, "heads"), P("heads"),
        P("heads", None), P(), P("items", "blk", None),
    )
    out = (
        P("items", "blk", None), P("blk", "items", "heads"), P("blk", None), P(None, "heads"), P("heads"), P("heads"),
        P(), P(), P(), P(), P(None, "heads"), P(None, "heads"), P(None, "heads"), P("heads", None), P(None, "heads"),
        P("heads"), P("heads", None), P(),
    )
    fits = mesh.shape["blk"] == 2 and mesh.shape["items"] == 4 and mesh.shape["heads"] == 4
    return jax.shard_map(fast_device if fits else general_device, mesh=mesh, in_specs=placed, out_specs=out, check_vma=False)
```

```python
import functools

import jax
import jax.numpy as jnp
from jax import lax
from jax.experimental import pallas as pl
from jax.experimental.pallas import tpu as pltpu
from jax.sharding import PartitionSpec as P

HEADS = 8
EPS = 1e-05
MASKED = -1e30
LOG2E = 1.4426950408889634
F32 = jnp.float32
BF16 = jnp.bfloat16
NT = (((1,), (1,)), ((), ()))
VMEM_LIMIT = 60 * 1024 * 1024


def dot(a, b):
    return jnp.dot(a, b, preferred_element_type=F32)


def dot_nt(a, b):
    return lax.dot_general(a, b, NT, preferred_element_type=F32)


def norm_keep(values, gain, bias):
    average = jnp.mean(values, axis=-1, keepdims=True)
    centred = values - average
    inverse = lax.rsqrt(jnp.mean(centred * centred, axis=-1, keepdims=True) + EPS)
    normed = centred * inverse
    return (normed * gain + bias, normed, inverse)


def norm_back(grad_norm, normed, inverse, gain):
    scaled = grad_norm * gain
    first = jnp.mean(scaled, axis=-1, keepdims=True)
    second = jnp.mean(scaled * normed, axis=-1, keepdims=True)
    return (scaled - first - normed * second) * inverse


def norm_columns(x, emb):
    shifted = x.astype(F32) + emb
    centred = shifted - jnp.mean(shifted, axis=0, keepdims=True)
    inverse = lax.rsqrt(jnp.mean(centred * centred, axis=0, keepdims=True) + EPS)
    return centred * inverse, inverse


def head_rows(h, per_shard, head_dim):
    key = (h // per_shard) * 2 * per_shard + lax.rem(h, per_shard)
    key_at = pl.multiple_of(key * head_dim, head_dim)
    return pl.ds(key_at, head_dim), pl.ds(pl.multiple_of(key_at + per_shard * head_dim, head_dim), head_dim)


def forward_kernel(per_shard, x_ref, emb_ref, gain_ref, bias_ref, w_ref, q_ref, mask_ref, kv_ref, o_ref, lse_ref, xn_ref, stat_ref):
    heads, rows, head_dim = q_ref.shape
    length = x_ref.shape[1]
    piece = min(256, length)

    def norm_step(i, _):
        at = pl.ds(pl.multiple_of(i * piece, piece), piece)
        normed, _unused = norm_columns(x_ref[:, at], emb_ref[...])
        xn_ref[:, at] = (normed * gain_ref[...] + bias_ref[...]).astype(BF16)
        return 0

    lax.fori_loop(0, length // piece, norm_step, 0)
    block = 512 if w_ref.shape[0] % 512 == 0 else 160

    def pair_step(i, _):
        at = pl.ds(pl.multiple_of(i * block, block), block)
        kv_ref[at] = dot(w_ref[at], xn_ref[...]).astype(BF16)
        return 0

    lax.fori_loop(0, w_ref.shape[0] // block, pair_step, 0)
    factor = LOG2E * head_dim ** (-0.5)
    lane = lax.broadcasted_iota(jnp.int32, (rows, 128), 1)
    stat_ref[...] = jnp.zeros_like(stat_ref)

    def head_step(h, _):
        at_key, at_value = head_rows(h, per_shard, head_dim)
        scores = dot(q_ref[h], kv_ref[at_key]) * factor + mask_ref[...]
        top = jnp.max(scores, axis=1, keepdims=True)
        weights = jnp.exp2(scores - top)
        total = jnp.sum(weights, axis=1, keepdims=True)
        out = dot_nt(kv_ref[at_value], weights.astype(BF16))
        stat_ref[...] = jnp.where(lane == h, top + jnp.log2(total), stat_ref[...])
        inverse = jnp.transpose(jnp.broadcast_to(1.0 / total, (rows, 128)))[:1]
        o_ref[pl.ds(pl.multiple_of(h * head_dim, head_dim), head_dim)] = (out * inverse).astype(BF16)
        return 0

    lax.fori_loop(0, heads, head_step, 0)
    lse_ref[...] = jnp.transpose(stat_ref[...])[:heads]


def forward_call(x_cols, emb, gain, bias, w_rows, q, mask, per_shard):
    seqs, width, length = x_cols.shape
    heads, rows, head_dim = q.shape
    pair_rows = w_rows.shape[0]
    whole = pl.BlockSpec(memory_space=pltpu.VMEM)

    def per_seq(*dims):
        return pl.BlockSpec((None,) + dims, lambda s: (s, 0, 0))

    return pl.pallas_call(
        functools.partial(forward_kernel, per_shard),
        grid=(seqs,),
        in_specs=[per_seq(width, length), per_seq(width, 1), whole, whole, whole, whole, per_seq(1, length)],
        out_specs=[per_seq(pair_rows, length), per_seq(heads * head_dim, rows), per_seq(heads, rows)],
        out_shape=[
            jax.ShapeDtypeStruct((seqs, pair_rows, length), BF16),
            jax.ShapeDtypeStruct((seqs, heads * head_dim, rows), BF16),
            jax.ShapeDtypeStruct((seqs, heads, rows), F32),
        ],
        scratch_shapes=[pltpu.VMEM((width, length), BF16), pltpu.VMEM((rows, 128), F32)],
        compiler_params=pltpu.CompilerParams(vmem_limit_bytes=VMEM_LIMIT),
        name="attend",
    )(x_cols, emb, gain, bias, w_rows, q, mask)


def backward_kernel(per_shard, x_ref, emb_ref, gain_ref, bias_ref, w_ref, q_ref, qt_ref, do_ref, dot_ref, lse_ref, delta_ref, mask_ref, kv_ref,
                    g_ref, dw_ref, dq_ref, dgain_ref, dbias_ref, demb_ref, xn_ref, dkv_ref):
    heads, rows, head_dim = q_ref.shape
    width, length = x_ref.shape
    piece = min(256, length)

    @pl.when(pl.program_id(0) == 0)
    def _():
        dw_ref[...] = jnp.zeros_like(dw_ref)
        dq_ref[...] = jnp.zeros_like(dq_ref)
        dgain_ref[...] = jnp.zeros_like(dgain_ref)
        dbias_ref[...] = jnp.zeros_like(dbias_ref)

    def norm_step(i, _):
        at = pl.ds(pl.multiple_of(i * piece, piece), piece)
        normed, _unused = norm_columns(x_ref[:, at], emb_ref[...])
        xn_ref[:, at] = (normed * gain_ref[...] + bias_ref[...]).astype(BF16)
        return 0

    lax.fori_loop(0, length // piece, norm_step, 0)
    scale = head_dim ** (-0.5)
    factor = LOG2E * scale

    def head_step(h, _):
        at_key, at_value = head_rows(h, per_shard, head_dim)
        keys = kv_ref[at_key]
        weights = jnp.exp2(dot(q_ref[h], keys) * factor + mask_ref[...] - lse_ref[h])
        dkv_ref[at_value] = dot(dot_ref[h], weights.astype(BF16)).astype(BF16)
        grad = dot(do_ref[h], kv_ref[at_value]) - delta_ref[h]
        grad = (weights * grad).astype(BF16)
        dkv_ref[at_key] = (dot(qt_ref[h], grad) * scale).astype(BF16)
        dq_ref[h] += dot_nt(keys, grad) * scale
        return 0

    lax.fori_loop(0, heads, head_step, 0)
    block = 512 if dw_ref.shape[0] % 512 == 0 else 160

    def weight_step(i, _):
        at = pl.ds(pl.multiple_of(i * block, block), block)
        dw_ref[at] += dot_nt(dkv_ref[at], xn_ref[...])
        return 0

    lax.fori_loop(0, dw_ref.shape[0] // block, weight_step, 0)

    def byte_step(i, carry):
        at = pl.ds(pl.multiple_of(i * piece, piece), piece)
        grad = dot(w_ref[...], dkv_ref[:, at])
        normed, inverse = norm_columns(x_ref[:, at], emb_ref[...])
        dbias_ref[...] += jnp.sum(grad, axis=1, keepdims=True)
        dgain_ref[...] += jnp.sum(grad * normed, axis=1, keepdims=True)
        scaled = grad * gain_ref[...]
        first = jnp.mean(scaled, axis=0, keepdims=True)
        second = jnp.mean(scaled * normed, axis=0, keepdims=True)
        shifted = (scaled - first - normed * second) * inverse
        g_ref[:, at] = shifted.astype(BF16)
        return carry + jnp.sum(shifted, axis=1, keepdims=True)

    demb_ref[...] = lax.fori_loop(0, length // piece, byte_step, jnp.zeros((width, 1), F32))


def backward_call(x_cols, emb, gain, bias, w, q, qt, grad_out, grad_out_t, lse, delta, mask, pairs, per_shard):
    seqs, width, length = x_cols.shape
    heads, rows, head_dim = q.shape
    pair_rows = w.shape[1]
    whole = pl.BlockSpec(memory_space=pltpu.VMEM)

    def per_seq(*dims):
        return pl.BlockSpec((None,) + dims, lambda s: (s,) + (0,) * len(dims))

    return pl.pallas_call(
        functools.partial(backward_kernel, per_shard),
        grid=(seqs,),
        in_specs=[
            per_seq(width, length), per_seq(width, 1), whole, whole, whole, whole, whole,
            per_seq(heads, rows, head_dim), per_seq(heads, head_dim, rows),
            per_seq(heads, rows, 1), per_seq(heads, rows, 1), per_seq(1, length), per_seq(pair_rows, length),
        ],
        out_specs=[per_seq(width, length), whole, whole, whole, whole, per_seq(width, 1)],
        out_shape=[
            jax.ShapeDtypeStruct((seqs, width, length), BF16),
            jax.ShapeDtypeStruct((pair_rows, width), F32),
            jax.ShapeDtypeStruct((heads, head_dim, rows), F32),
            jax.ShapeDtypeStruct((width, 1), F32),
            jax.ShapeDtypeStruct((width, 1), F32),
            jax.ShapeDtypeStruct((seqs, width, 1), F32),
        ],
        scratch_shapes=[pltpu.VMEM((width, length), BF16), pltpu.VMEM((pair_rows, length), BF16)],
        compiler_params=pltpu.CompilerParams(vmem_limit_bytes=VMEM_LIMIT),
        name="attend_back",
    )(x_cols, emb, gain, bias, w, q, qt, grad_out, grad_out_t, lse, delta, mask, pairs)


def mesh_at(di=None, db=None, dh=None, core=None):
    items, blk, heads = lax.axis_index("items"), lax.axis_index("blk"), lax.axis_index("heads")
    return (items if di is None else di, blk if db is None else db, heads if dh is None else dh)


def places():
    items, blk, heads = lax.axis_index("items"), lax.axis_index("blk"), lax.axis_index("heads")
    core = lax.rem(items, 2)
    return items, blk, heads, items // 2, core


def send(src, dst, sems, recvs, target):
    copy = pltpu.make_async_remote_copy(
        src_ref=src, dst_ref=dst, send_sem=sems, recv_sem=recvs, device_id=target, device_id_type=pl.DeviceIdType.MESH)
    copy.start()
    return copy


def greet(targets):
    barrier = pltpu.get_barrier_semaphore()
    for target in targets:
        pl.semaphore_signal(barrier, inc=1, device_id=target, device_id_type=pl.DeviceIdType.MESH)
    pl.semaphore_wait(barrier, len(targets))


def first_kernel(x_hbm, pad_ref, lang_ref, table_ref, lgain, lbias, mgain, mbias, bdown, igain, ibias, bup, lat_ref, wq_ref, pair_shard, lat_shard,
                 wcols_ref, all_ref, kv_out, xn_out, att_ref, lse_ref, qt_ref, latn_ref, bup_all, x_out, rows_ref, mask_ref, lang_out, latf_ref, vecs_ref,
                 x_ref, xbuf, x32, xn_ref, pair_ref, kv_ref, cols_ref, q_ref, o_tmp, o_own, o_send, o_got, stat_ref, stat_send, stat_own, stat_got,
                 pair_ss, pair_rs, lat_ss, lat_rs, q_ss, q_rs, misc_ss, misc_rs, o_ss, o_rs, own_sem, xn_sem, kv_sem, x_sem):
    items, blk, me, hi, core = places()
    shards = lax.axis_size("heads")
    seqs, width, length = x_ref.shape
    rows = qt_ref.shape[3]
    local_rows = rows // 2
    heads, _, head_dim = q_ref.shape
    cols = heads * head_dim // shards
    per_shard = heads // shards
    sibling = items + 1 - 2 * core
    other = 1 - blk
    to_sib, to_x, to_y = mesh_at(di=sibling), mesh_at(db=other), mesh_at(di=(1 - hi) * 2 + core)
    z_of = [lax.rem(me + d, shards) for d in range(shards)]
    z_back = [lax.rem(me + shards - d, shards) for d in range(shards)]
    greet([to_sib, to_x, to_y] + [mesh_at(dh=z_of[d]) for d in range(1, shards)])

    share = cols // 4
    chip = hi * 2 + blk
    chip_x, chip_y, chip_xy = hi * 2 + other, (1 - hi) * 2 + blk, (1 - hi) * 2 + other

    def region(ref, shard, chip_at, lanes_of):
        half = ref.shape[2] // 2
        return ref.at[:, pl.ds(pl.multiple_of(shard * cols + chip_at * share, 16), share), pl.ds(pl.multiple_of(lanes_of * half, 128), half)]

    def lane_half(ref, shard, lanes_of):
        half = ref.shape[2] // 2
        return ref.at[:, pl.ds(pl.multiple_of(shard * cols, 16), cols), pl.ds(pl.multiple_of(lanes_of * half, 128), half)]

    pending = []
    local = []
    near = me + 1 - 2 * lax.rem(me, 2)
    far, cross = lax.rem(me + 2, 4), lax.rem(near + 2, 4)
    shard_at = [me, near, far, cross]
    kinds = {"pair": (pair_shard, pair_ref, pair_ss, pair_rs)}
    for m in range(3):
        one = pl.ds(m, 1)
        kinds[f"l{m}"] = (lat_shard.at[one], all_ref.at[one], lat_ss.at[m], lat_rs.at[m])

    def recv(kind, d, stage, where):
        _, dst, ss, rs = kinds[kind]
        pltpu.make_async_remote_copy(src_ref=where, dst_ref=where, send_sem=ss.at[d, stage], recv_sem=rs.at[d, stage],
                                     device_id=to_sib, device_id_type=pl.DeviceIdType.MESH).wait_recv()

    def out_z(kind, d):
        src, dst, ss, rs = kinds[kind]
        if d == 3:
            block = region(dst, far, chip, core)
            pending.append(send(block, block, ss.at[d, 0], rs.at[d, 0], mesh_at(dh=near)))
        else:
            pending.append(send(region(src, 0, chip, core), region(dst, me, chip, core), ss.at[d, 0], rs.at[d, 0], mesh_at(dh=shard_at[d])))

    def after_z(kind, d):
        _, dst, ss, rs = kinds[kind]
        mine = region(dst, shard_at[d], chip, core)
        recv(kind, d, 0, mine)
        pending.append(send(mine, mine, ss.at[d, 1], rs.at[d, 1], to_x))
        pending.append(send(mine, mine, ss.at[d, 2], rs.at[d, 2], to_y))

    def after_x(kind, d):
        _, dst, ss, rs = kinds[kind]
        x_first = kind != "l1"
        got = region(dst, shard_at[d], chip_x if x_first else chip_y, core)
        recv(kind, d, 1 if x_first else 2, got)
        pending.append(send(got, got, ss.at[d, 3], rs.at[d, 3], to_y if x_first else to_x))

    def after_y(kind, d):
        _, dst, ss, rs = kinds[kind]
        x_first = kind != "l1"
        recv(kind, d, 2 if x_first else 1, region(dst, shard_at[d], chip_y if x_first else chip_x, core))
        recv(kind, d, 3, region(dst, shard_at[d], chip_xy, core))
        half = lane_half(dst, shard_at[d], core)
        pending.append(send(half, half, ss.at[d, 4], rs.at[d, 4], to_sib))

    def after_sib(kind, d):
        _, dst, ss, rs = kinds[kind]
        recv(kind, d, 4, lane_half(dst, shard_at[d], 1 - core))

    own_pair = pltpu.make_async_copy(pair_shard, pair_ref.at[:, pl.ds(pl.multiple_of(me * cols, 16), cols)], own_sem.at[0])
    own_lat = pltpu.make_async_copy(lat_shard, all_ref.at[:, pl.ds(pl.multiple_of(me * cols, 16), cols)], own_sem.at[1])
    own_pair.start()
    own_lat.start()
    my_rows = pl.ds(pl.multiple_of(blk * local_rows, 128), local_rows)
    other_rows = pl.ds(pl.multiple_of(other * local_rows, 128), local_rows)

    vecs_ref[...] = jnp.zeros_like(vecs_ref)
    for i, vector in enumerate((lgain, lbias, mgain, mbias, bdown, igain, ibias, bup)):
        vecs_ref[i:i + 1, :vector.shape[0]] = vector[...].reshape(1, vector.shape[0])
    rows_ref[0:1] = vecs_ref[5:6, :width]
    rows_ref[1:2] = vecs_ref[6:7, :width]
    rows_ref[4:8] = jnp.zeros((4, width), F32)
    lang_out[...] = jnp.zeros_like(lang_out)
    for s in range(seqs):
        lang = lang_ref[me * seqs + s]
        picked = lax.broadcasted_iota(jnp.int32, table_ref.shape, 0) == lang
        rows_ref[2 + s:3 + s] = jnp.sum(jnp.where(picked, table_ref[...].astype(F32), 0.0), axis=0, keepdims=True)
        lang_out[s:s + 1] = jnp.where(lax.broadcasted_iota(jnp.int32, (1, 128), 1) == lang, 1.0, 0.0)
        mask_ref[s] = jnp.where(pad_ref[pl.ds(me * seqs + s, 1)] > 0, 0.0, MASKED)

    def queries_start():
        latf_ref[...] = lat_ref[...].astype(F32)
        lat_out, _, _ = norm_keep(latf_ref[...], vecs_ref[0:1], vecs_ref[1:2])
        lat_low = lat_out.astype(BF16)
        latn_ref[...] = lat_low
        at_head = pl.ds(pl.multiple_of(core * head_dim, 16), head_dim)
        qt_ref[core, me, :, my_rows] = dot_nt(wq_ref[at_head], lat_low).astype(BF16)
        bup_ref = vecs_ref.at[:, pl.ds(0, bup_all.shape[2])]
        bup_all[me] = bup_ref[...]
        for d in range(1, shards):
            my_q = qt_ref.at[core, me, :, my_rows]
            pending.append(send(my_q, my_q, q_ss.at[0, d], q_rs.at[0, d], mesh_at(dh=z_back[d])))
        for d in range(1, shards):
            pending.append(send(bup_ref, bup_all.at[me], misc_ss.at[d], misc_rs.at[d], mesh_at(dh=z_back[d])))

    cols_ref[...] = jnp.transpose(rows_ref[...])
    step_rows = xbuf.shape[1]

    def load_bytes(c):
        return pltpu.make_async_copy(x_hbm.at[pl.ds(c * step_rows, step_rows)], xbuf.at[c % 2], x_sem.at[c % 2])

    load_bytes(0).start()

    def pick_bytes(c):
        load_bytes(c).wait()
        if (c + 1) * step_rows < length:
            load_bytes(c + 1).start()
        at = slice(c * step_rows, (c + 1) * step_rows)
        for j in range(x32.shape[0]):
            lanes = slice(j * 128, (j + 1) * 128)
            x32[j] = xbuf[c % 2, :, :, lanes].astype(F32).reshape(x32.shape[1:])
            for s in range(seqs):
                x_ref[s, lanes, at] = jnp.transpose(x32[j, pl.ds(me * seqs + s, step_rows, stride=x_hbm.shape[1])]).astype(BF16)
        if (c + 1) * step_rows == length:
            copy = pltpu.make_async_copy(x_ref, x_out, x_sem.at[2])
            copy.start()
            local.append(copy)


    def queries_z():
        for d in range(1, shards):
            wait_plain(qt_ref.at[core, z_of[d], :, my_rows], q_ss.at[0, d], q_rs.at[0, d])
        part = qt_ref.at[core, :, :, my_rows]
        pending.append(send(part, part, q_ss.at[1, 0], q_rs.at[1, 0], to_x))

    def queries_x():
        wait_plain(qt_ref.at[core, :, :, other_rows], q_ss.at[1, 0], q_rs.at[1, 0])
        pending.append(send(qt_ref.at[core], qt_ref.at[core], q_ss.at[1, 1], q_rs.at[1, 1], to_sib))

    def queries_sib():
        wait_plain(qt_ref.at[1 - core], q_ss.at[1, 1], q_rs.at[1, 1])

    def wait_plain(where, ss, rs):
        pltpu.make_async_remote_copy(src_ref=where, dst_ref=where, send_sem=ss, recv_sem=rs,
                                     device_id=to_sib, device_id_type=pl.DeviceIdType.MESH).wait_recv()

    piece = min(256, length)

    def norm_bytes(s):
        def norm_step(i, _):
            at = pl.ds(pl.multiple_of(i * piece, piece), piece)
            normed, _unused = norm_columns(x_ref[s, :, at], cols_ref[:, 2 + s:3 + s])
            xn_ref[s, :, at] = (normed * cols_ref[:, 0:1] + cols_ref[:, 1:2]).astype(BF16)
            return 0
        lax.fori_loop(0, length // piece, norm_step, 0)
        copy = pltpu.make_async_copy(xn_ref.at[s], xn_out.at[s], xn_sem.at[s])
        copy.start()
        local.append(copy)

    def project(d):
        at = pl.ds(pl.multiple_of(shard_at[d] * cols, 16), cols)

        def step(i, _):
            s, part = i // 2, lax.rem(i, 2)
            kv_ref[s, part, at] = dot(pair_ref[part, at], xn_ref[s]).astype(BF16)
            return 0
        lax.fori_loop(0, 2 * seqs, step, 0)
        copy = pltpu.make_async_copy(kv_ref.at[:, :, at], kv_out.at[:, :, at], kv_sem.at[d])
        copy.start()
        local.append(copy)

    factor = LOG2E * head_dim ** (-0.5)
    lane = lax.broadcasted_iota(jnp.int32, (rows, 128), 1)
    stat_ref[...] = jnp.zeros_like(stat_ref)

    def turn_queries(d):
        for j in range(per_shard):
            h = shard_at[d] * per_shard + j
            q_ref[h] = jnp.transpose(qt_ref[j, shard_at[d]])

    def attend(d, s):
        def head_step(j, _):
            h = shard_at[d] * per_shard + j
            at = pl.ds(pl.multiple_of(h * head_dim, 16), head_dim)
            scores = dot(q_ref[h], kv_ref[s, 0, at]) * factor + mask_ref[s]
            top = jnp.max(scores, axis=1, keepdims=True)
            weights = jnp.exp2(scores - top)
            total = jnp.sum(weights, axis=1, keepdims=True)
            out = dot_nt(kv_ref[s, 1, at], weights.astype(BF16))
            stat_ref[s] = jnp.where(lane == h, top + jnp.log2(total), stat_ref[s])
            inverse = jnp.transpose(jnp.broadcast_to(1.0 / total, (rows, 128)))[:1]
            o_tmp[...] = out * inverse
            o_own[s, at] = o_tmp[:, my_rows]
            o_send[s, at] = o_tmp[:, other_rows].astype(BF16)
            return 0
        lax.fori_loop(0, per_shard, head_step, 0)
        part = pl.ds(pl.multiple_of(shard_at[d] * cols, 16), cols)
        pending.append(send(o_send.at[s, part], o_got.at[s, part], o_ss.at[d, s], o_rs.at[d, s], to_x))

    def stats_send():
        for s in range(seqs):
            at = pl.ds(s * heads, heads)
            stats = jnp.transpose(stat_ref[s])[:heads]
            stat_send[...] = stats
            stat_own[at] = stat_send[:, my_rows]
            stat_got[0, at] = stat_send[:, other_rows]
        pending.append(send(stat_got.at[0], stat_got.at[1], o_ss.at[shards, 0], o_rs.at[shards, 0], to_x))

    def turn_weights():
        block = 256
        for part in range(2):
            for i in range(pair_ref.shape[1] // block):
                wcols_ref[part, :, i * block:(i + 1) * block] = jnp.transpose(pair_ref[part, i * block:(i + 1) * block])

    out_z("pair", 1)
    out_z("pair", 2)
    queries_start()
    pick_bytes(0)
    pick_bytes(1)
    pick_bytes(2)
    pick_bytes(3)
    pick_bytes(4)
    pick_bytes(5)
    pick_bytes(6)
    after_z("pair", 1)
    out_z("l0", 1)
    pick_bytes(7)
    queries_z()
    norm_bytes(0)
    after_z("pair", 2)
    out_z("pair", 3)
    norm_bytes(1)
    after_z("l0", 1)
    out_z("l0", 2)
    own_pair.wait()
    project(0)
    after_x("pair", 1)
    after_z("pair", 3)
    out_z("l1", 1)
    after_z("l0", 2)
    out_z("l0", 3)
    after_z("l1", 1)
    out_z("l1", 2)
    after_x("pair", 2)
    queries_x()
    after_x("l0", 1)
    after_y("pair", 1)
    queries_sib()
    turn_queries(0)
    attend(0, 0)
    after_sib("pair", 1)
    after_z("l0", 3)
    out_z("l2", 1)
    attend(0, 1)
    after_x("pair", 3)
    after_x("l0", 2)
    after_z("l1", 2)
    out_z("l1", 3)
    project(1)
    turn_queries(1)
    attend(1, 0)
    after_z("l2", 1)
    out_z("l2", 2)
    attend(1, 1)
    after_z("l1", 3)
    after_x("l1", 1)
    after_x("l0", 3)
    after_y("l0", 1)
    after_z("l2", 2)
    out_z("l2", 3)
    after_y("pair", 2)
    after_sib("l0", 1)
    after_sib("pair", 2)
    project(2)
    after_z("l2", 3)
    turn_queries(2)
    attend(2, 0)
    after_y("l0", 2)
    after_x("l1", 2)
    after_x("l2", 1)
    attend(2, 1)
    after_y("l1", 1)
    after_y("pair", 3)
    after_sib("l0", 2)
    after_x("l2", 2)
    after_x("l1", 3)
    after_sib("l1", 1)
    after_y("l0", 3)
    after_sib("pair", 3)
    project(3)
    after_sib("l0", 3)
    turn_queries(3)
    attend(3, 0)
    after_y("l2", 1)
    after_x("l2", 3)
    attend(3, 1)
    after_y("l1", 2)
    after_y("l2", 2)
    stats_send()
    turn_weights()
    after_y("l1", 3)
    after_y("l2", 3)
    after_sib("l2", 1)
    after_sib("l1", 2)
    after_sib("l2", 2)
    after_sib("l1", 3)
    after_sib("l2", 3)

    wait_plain(stat_got.at[1], o_ss.at[shards, 0], o_rs.at[shards, 0])
    own_lse, got_lse = stat_own[...], stat_got[1]
    top = jnp.maximum(own_lse, got_lse)
    own_share, got_share = jnp.exp2(own_lse - top), jnp.exp2(got_lse - top)
    total = own_share + got_share
    lse = top + jnp.log2(total)
    own_share, got_share = own_share / total, got_share / total
    for s in range(seqs):
        lse_ref[s] = lse[s * heads:(s + 1) * heads]
        for d in range(shards):
            part = pl.ds(pl.multiple_of(shard_at[d] * cols, 16), cols)
            wait_plain(o_got.at[s, part], o_ss.at[d, s], o_rs.at[d, s])
    for s in range(seqs):
        for h in range(heads):
            at = slice(h * head_dim, (h + 1) * head_dim)
            n = s * heads + h
            att_ref[s, at] = o_own[s, at] * own_share[n:n + 1] + o_got[s, at].astype(F32) * got_share[n:n + 1]
    for d in range(1, shards):
        wait_plain(bup_all.at[z_of[d]], misc_ss.at[d], misc_rs.at[d])
    own_lat.wait()
    for copy in local:
        copy.wait()
    for copy in pending:
        copy.wait_send()


def first_call(inputs, padding, language, table, vectors, latents, wq_rows, pair_shard, lat_shard, rows, seqs):
    length, local_seqs, width = inputs.shape
    local_rows, width_lat = latents.shape
    shards = lax.axis_size("heads")
    heads = HEADS
    head_dim = width_lat // heads
    whole = pl.BlockSpec(memory_space=pltpu.VMEM)
    hbm = pl.BlockSpec(memory_space=pl.ANY)
    out = jax.ShapeDtypeStruct
    sem = pltpu.SemaphoreType.DMA
    return pl.pallas_call(
        first_kernel,
        in_specs=[hbm, whole, pl.BlockSpec(memory_space=pltpu.SMEM)] + [whole] * 13,
        out_specs=[whole, hbm, hbm, hbm] + [whole] * 5 + [hbm] + [whole] * 5,
        out_shape=[
            out((2, width, width_lat), BF16),
            out((3, width_lat, width_lat), BF16),
            out((seqs, 2, width_lat, length), BF16),
            out((seqs, width, length), BF16),
            out((seqs, width_lat, local_rows), F32),
            out((seqs, heads, local_rows), F32),
            out((heads // shards, shards, head_dim, rows), BF16),
            out((local_rows, width_lat), BF16),
            out((shards, 8, 384), F32),
            out((seqs, width, length), BF16),
            out((8, width), F32),
            out((seqs, 1, length), F32),
            out((8, 128), F32),
            out((local_rows, width_lat), F32),
            out((8, width_lat), F32),
        ],
        scratch_shapes=[
            pltpu.VMEM((seqs, width, length), BF16),
            pltpu.VMEM((2, 128, local_seqs, width), BF16),
            pltpu.VMEM((width // 128, 128 * local_seqs, 128), F32),
            pltpu.VMEM((seqs, width, length), BF16),
            pltpu.VMEM((2, width_lat, width), BF16),
            pltpu.VMEM((seqs, 2, width_lat, length), BF16),
            pltpu.VMEM((width, 8), F32),
            pltpu.VMEM((heads, rows, head_dim), BF16),
            pltpu.VMEM((head_dim, rows), F32),
            pltpu.VMEM((seqs, width_lat, local_rows), F32),
            pltpu.VMEM((seqs, width_lat, local_rows), BF16),
            pltpu.VMEM((seqs, width_lat, local_rows), BF16),
            pltpu.VMEM((seqs, rows, 128), F32),
            pltpu.VMEM((heads, rows), F32),
            pltpu.VMEM((seqs * heads, local_rows), F32),
            pltpu.VMEM((2, seqs * heads, local_rows), F32),
            sem((shards, 5)), sem((shards, 5)), sem((3, shards, 5)), sem((3, shards, 5)),
            sem((2, shards)), sem((2, shards)), sem((shards,)), sem((shards,)),
            sem((shards + 1, seqs)), sem((shards + 1, seqs)), sem((2,)), sem((seqs,)), sem((shards,)), sem((3,)),
        ],
        compiler_params=pltpu.CompilerParams(vmem_limit_bytes=VMEM_LIMIT, collective_id=1, has_side_effects=True),
        name="first",
    )(inputs, padding, language, table, *vectors, latents, wq_rows, pair_shard, lat_shard)


class Reduce:
    def __init__(self, src, half, got_sib, got_chip, got_z, out, ss, rs, pending, x_first=True, stage=None, stage_sem=None):
        self.src, self.half, self.got_sib, self.got_chip, self.got_z, self.out = src, half, got_sib, got_chip, got_z, out
        self.ss, self.rs, self.pending, self.x_first = ss, rs, pending, x_first
        self.stage, self.stage_sem, self.kept = stage, stage_sem, None
        self.split = src is not None and src.shape[3] == half.shape[3]
        items, blk, self.me, hi, self.core = places()
        self.shards = lax.axis_size("heads")
        other = 1 - blk
        self.chip = hi * 2 + blk
        self.chip_x, self.chip_y, self.chip_xy = hi * 2 + other, (1 - hi) * 2 + blk, (1 - hi) * 2 + other
        self.to_x, self.to_y = mesh_at(db=other), mesh_at(di=(1 - hi) * 2 + self.core)
        self.to_sib = mesh_at(di=items + 1 - 2 * self.core)
        self.n, _, self.cols, self.width = half.shape
        self.share = self.cols // 4
        self.near = self.me + 1 - 2 * lax.rem(self.me, 2)
        self.far, self.cross = lax.rem(self.me + 2, 4), lax.rem(self.near + 2, 4)

    def rows(self, chip):
        return pl.ds(pl.multiple_of(chip * self.share, 16), self.share)

    def lanes(self, core):
        return pl.ds(pl.multiple_of(core * self.width, 128), self.width)

    def go(self, src, dst, i, target):
        self.pending.append(send(src, dst, self.ss.at[i], self.rs.at[i], target))

    def arrived(self, where, i):
        pltpu.make_async_remote_copy(src_ref=where, dst_ref=where, send_sem=self.ss.at[i], recv_sem=self.rs.at[i],
                                     device_id=self.to_sib, device_id_type=pl.DeviceIdType.MESH).wait_recv()

    def start(self):
        theirs = self.src if self.split else self.src.at[:, :, :, self.lanes(1 - self.core)]
        self.go(theirs, self.got_sib, 0, self.to_sib)

    def join_sib(self):
        self.arrived(self.got_sib, 0)

        def step(i, _):
            n, h = i // self.shards, lax.rem(i, self.shards)
            own = self.half[n, h] if self.split else self.src[n, h, :, self.lanes(self.core)]
            self.half[n, h] = (own.astype(F32) + self.got_sib[n, h].astype(F32)).astype(self.half.dtype)
            return 0
        lax.fori_loop(0, self.n * self.shards, step, 0)

    def send_chips(self):
        low, high = pl.ds(0, 2), pl.ds(2, 2)
        self.go(self.half.at[:, low, self.rows(self.chip_x)], self.got_chip.at[0], 1, self.to_x)
        self.go(self.half.at[:, high, self.rows(self.chip_y)], self.got_chip.at[2], 3, self.to_y)
        self.go(self.half.at[:, low, self.rows(self.chip_xy)], self.got_chip.at[1], 2, self.to_x)
        self.go(self.half.at[:, high, self.rows(self.chip_xy)], self.got_chip.at[3], 4, self.to_y)

    def add(self, slot, first, rows):
        self.arrived(self.got_chip.at[slot], 1 + slot)
        for n in range(self.n):
            for h in range(2):
                total = self.half[n, first + h, rows].astype(F32) + self.got_chip[slot, n, h].astype(F32)
                self.half[n, first + h, rows] = total.astype(self.half.dtype)

    def join_first(self):
        self.add(1, 0, self.rows(self.chip_y))
        self.go(self.half.at[:, pl.ds(0, 2), self.rows(self.chip_y)], self.got_chip.at[4], 5, self.to_y)
        self.add(3, 2, self.rows(self.chip_x))
        self.go(self.half.at[:, pl.ds(2, 2), self.rows(self.chip_x)], self.got_chip.at[5], 6, self.to_x)
        self.add(0, 0, self.rows(self.chip))
        self.add(2, 2, self.rows(self.chip))

    def join_chips(self):
        mine = self.rows(self.chip)
        self.add(4, 0, mine)
        self.add(5, 2, mine)
        for i, shard in enumerate((self.near, self.cross)):
            self.go(self.half.at[:, shard, mine], self.got_z.at[i], 7 + i, mesh_at(dh=self.near))

    def join_near(self):
        mine = self.rows(self.chip)
        for i, shard in enumerate((self.me, self.far)):
            self.arrived(self.got_z.at[i], 7 + i)
            for n in range(self.n):
                total = self.half[n, shard, mine].astype(F32) + self.got_z[i, n].astype(F32)
                self.half[n, shard, mine] = total.astype(self.half.dtype)
        self.go(self.half.at[:, self.far, mine], self.got_z.at[2], 9, mesh_at(dh=self.far))

    def join_z(self):
        self.arrived(self.got_z.at[2], 9)
        mine = self.rows(self.chip)
        for n in range(self.n):
            total = self.half[n, self.me, mine].astype(F32) + self.got_z[2, n].astype(F32)
            if self.stage is None:
                self.out[n, mine, self.lanes(self.core)] = total.astype(self.out.dtype)
            else:
                self.stage[n] = total.astype(self.out.dtype)
        src = self.piece(self.chip)
        if self.stage is not None:
            self.kept = pltpu.make_async_copy(self.stage, src, self.stage_sem)
            self.kept.start()
            src = self.stage
        self.go(src, self.piece(self.chip), 10, self.to_x)
        self.go(src, self.piece(self.chip), 11, self.to_y)

    def piece(self, chip):
        return self.out.at[:, self.rows(chip), self.lanes(self.core)]

    def pass_on(self, chip, i, target):
        self.go(self.piece(chip), self.piece(chip), i, target)

    def share_chips(self):
        if self.x_first:
            self.arrived(self.piece(self.chip_x), 10)
            self.pass_on(self.chip_x, 12, self.to_y)
        else:
            self.arrived(self.piece(self.chip_y), 11)
            self.pass_on(self.chip_y, 12, self.to_x)

    def share_sib(self):
        if self.x_first:
            self.arrived(self.piece(self.chip_y), 11)
        else:
            self.arrived(self.piece(self.chip_x), 10)
        self.arrived(self.piece(self.chip_xy), 12)
        if self.kept is not None:
            self.kept.wait()
        half = self.out.at[:, :, self.lanes(self.core)]
        self.go(half, half, 13, self.to_sib)

    def finish(self):
        self.arrived(self.out.at[:, :, self.lanes(1 - self.core)], 13)


def second_kernel(x_hbm, rows_ref, mask_ref, w_ref, qt_ref, kv_hbm, xn_hbm, do_in, stat_in, mixed_in, lat_in, grads_hbm, vec_in, lang_in, latsum_in, wq_ref, lat_raw, lgain_ref,
                  g_out, mixed_out, dw_out, dlat_out, small_out, glat_out, vec_out, dq_out, latn_ref,
                  x_ref, xn_ref, cols_ref, kv_ref, dkv_ref, q_ref, do_ref, stat_ref, stat_cols, dq_ref, dw_ref, dw_tmp,
                  g_half, g_chip, g_z, w_half, w_sib, w_chip, w_z, q_half, q_sib, q_chip, q_z, s_half, s_sib, s_chip, s_z,
                  small_ref, s_ref, l_sib, l_half, l_y, l_sum, l_z, l_tot, lat8_ref,
                  g_stage, w_stage, tq_ref, t_part, t_got, t_z, y_buf, c_buf, x_buf,
                  g_ss, g_rs, w_ss, w_rs, q_ss, q_rs, s_ss, s_rs, l_ss, l_rs, t_ss, t_rs, do_ss, do_rs, misc_ss, misc_rs, mix_ss, mix_rs, a_ss, a_rs, load_sem, kv_sem, stage_sem):
    items, blk, me, hi, core = places()
    shards = lax.axis_size("heads")
    seqs, width, length = x_ref.shape
    heads, rows, head_dim = q_ref.shape
    local_rows = rows // 2
    per_shard = heads // shards
    cols = per_shard * head_dim
    stat_rows = stat_in.shape[0]
    other = 1 - blk
    to_x, to_sib = mesh_at(db=other), mesh_at(di=items + 1 - 2 * core)
    to_y = mesh_at(di=(1 - hi) * 2 + core)
    z_of = [lax.rem(me + d, shards) for d in range(shards)]
    z_back = [lax.rem(me + shards - d, shards) for d in range(shards)]
    my_rows = pl.ds(pl.multiple_of(blk * local_rows, 128), local_rows)
    other_rows = pl.ds(pl.multiple_of(other * local_rows, 128), local_rows)
    pending = []
    dot_ref = w_sib.at[:, :, :, pl.ds(0, rows)]
    grads = [Reduce(None, g_half.at[pl.ds(m, 1)], None, g_chip.at[:, pl.ds(m, 1)], g_z.at[m], dlat_out.at[pl.ds(m, 1)], g_ss.at[m], g_rs.at[m], pending, m != 1,
                        g_stage.at[pl.ds(m, 1)], stage_sem.at[m])
             for m in range(3)]
    pair = [Reduce(dw_ref.at[pl.ds(m, 1)], w_half.at[pl.ds(m, 1)], w_sib.at[pl.ds(m, 1)], w_chip.at[:, pl.ds(m, 1)], w_z.at[m],
                   dw_out.at[pl.ds(m, 1)], w_ss.at[m], w_rs.at[m], pending, m == 0, w_stage.at[pl.ds(m, 1)], stage_sem.at[3 + m]) for m in range(2)]
    query = Reduce(dq_ref, q_half, q_sib, q_chip, q_z, dq_out, q_ss, q_rs, pending, False)
    small = Reduce(s_ref, s_half, s_sib, s_chip, s_z, small_out, s_ss, s_rs, pending)
    greet([to_sib, to_x, to_y] + [mesh_at(dh=z_of[d]) for d in range(1, shards)])

    def arrived(where, ss, rs):
        pltpu.make_async_remote_copy(src_ref=where, dst_ref=where, send_sem=ss, recv_sem=rs,
                                     device_id=to_sib, device_id_type=pl.DeviceIdType.MESH).wait_recv()

    pending.append(send(stat_in, stat_ref.at[pl.ds(0, stat_rows), my_rows], misc_ss.at[0], misc_rs.at[0], to_x))

    def send_do(s):
        pending.append(send(do_in.at[s], dot_ref.at[s, :, :, my_rows], do_ss.at[s], do_rs.at[s], to_x))

    near = me + 1 - 2 * lax.rem(me, 2)
    far, cross = lax.rem(me + 2, 4), lax.rem(near + 2, 4)

    def mixed_pass(block, i, there):
        pending.append(send(mixed_out.at[block], mixed_out.at[block], mix_ss.at[i], mix_rs.at[i], mesh_at(dh=there)))

    def mixed_far():
        mixed_pass(me * seqs + 1, 0, far)

    def mixed_near():
        mixed_pass(me * seqs + 1, 1, near)

    def mixed_cross_0():
        mixed_pass(far * seqs, 2, near)

    def mixed_cross_1():
        arrived(mixed_out.at[far * seqs + 1], mix_ss.at[0], mix_rs.at[0])
        mixed_pass(far * seqs + 1, 3, near)

    def latents_share():
        pending.append(send(lat_in, latn_ref.at[my_rows], misc_ss.at[1], misc_rs.at[1], to_x))

    loads = [
        pltpu.make_async_copy(xn_hbm, xn_ref, load_sem.at[0]),
        pltpu.make_async_copy(x_hbm, x_ref, load_sem.at[1]),
        pltpu.make_async_copy(grads_hbm, g_half, load_sem.at[2]),
        pltpu.make_async_copy(lat_raw.at[pl.ds(pl.multiple_of(core * 64 + hi * 32 + me * 8, 8), 8)], lat8_ref, load_sem.at[4]),
    ]
    own_sum = pltpu.make_async_copy(latsum_in.at[pl.ds(pl.multiple_of(core * (local_rows // 2), 8), local_rows // 2)], l_half, load_sem.at[13])
    own_sum.start()
    latn_ref[my_rows] = lat_in[...]
    own_do = pltpu.make_async_copy(do_in, dot_ref.at[:, :, :, my_rows], load_sem.at[5])

    def load_pair(n, start):
        s, h = n // heads, lax.rem(n, heads)
        slot = lax.rem(n, 2)
        copy = pltpu.make_async_copy(kv_hbm.at[s, :, pl.ds(pl.multiple_of(h * head_dim, 16), head_dim)], kv_ref.at[slot], kv_sem.at[slot])
        copy.start() if start else copy.wait()

    load_pair(0, True)
    for copy in loads:
        copy.start()
    own_do.start()
    stat_ref[:stat_rows, my_rows] = stat_in[...]
    stat_ref[stat_rows:] = jnp.zeros((128 - stat_rows, rows), F32)
    for h in range(heads):
        q_ref[h] = jnp.transpose(qt_ref[h % per_shard, h // per_shard])
    dq_ref[...] = jnp.zeros_like(dq_ref)
    small_ref[...] = jnp.zeros_like(small_ref)

    def stats_ready():
        arrived(stat_ref.at[pl.ds(0, stat_rows), other_rows], misc_ss.at[0], misc_rs.at[0])
        stat_cols[...] = jnp.transpose(stat_ref[...])

    scale = head_dim ** (-0.5)
    factor = LOG2E * scale
    lane = lax.broadcasted_iota(jnp.int32, (rows, 128), 1)
    cols_ref[...] = jnp.transpose(rows_ref[...])
    gain = cols_ref[:, 0:1]

    def turn_grads(s):
        arrived(dot_ref.at[s, :, :, other_rows], do_ss.at[s], do_rs.at[s])
        for h in range(heads):
            inner = h % per_shard * head_dim
            do_ref[h] = jnp.transpose(dot_ref[s, h // per_shard, inner:inner + head_dim])

    def head_steps(s, group):
        def head_step(h, _):
            n = s * heads + h
            slot = lax.rem(n, 2)
            load_pair(n, False)

            @pl.when(n + 1 < seqs * heads)
            def _():
                load_pair(n + 1, True)

            at = pl.ds(pl.multiple_of(h * head_dim, 16), head_dim)
            lse = jnp.sum(jnp.where(lane == s * 2 * heads + h, stat_cols[...], 0.0), axis=1, keepdims=True)
            delta = jnp.sum(jnp.where(lane == s * 2 * heads + heads + h, stat_cols[...], 0.0), axis=1, keepdims=True)
            keys = kv_ref[slot, 0]
            weights = jnp.exp2(dot(q_ref[h], keys) * factor + mask_ref[s] - lse)
            part = pl.ds(pl.multiple_of(lax.rem(h, per_shard) * head_dim, 16), head_dim)
            dkv_ref[s, 1, at] = dot(dot_ref[s, h // per_shard, part], weights.astype(BF16)).astype(BF16)
            grad = dot(do_ref[h], kv_ref[slot, 1]) - delta
            grad = (weights * grad).astype(BF16)
            dkv_ref[s, 0, at] = (dot(qt_ref[lax.rem(h, per_shard), h // per_shard], grad) * scale).astype(BF16)
            dq_ref[0, h // per_shard, part] += dot_nt(keys, grad) * scale
            return 0

        lax.fori_loop(2 * group, 2 * group + 2, head_step, 0)

    piece = min(256, length)

    def byte_steps(s):
        def byte_step(i, carry):
            at = pl.ds(pl.multiple_of(i * piece, piece), piece)
            grad = dot(w_ref[0], dkv_ref[s, 0, :, at]) + dot(w_ref[1], dkv_ref[s, 1, :, at])
            normed, inverse = norm_columns(x_ref[s, :, at], cols_ref[:, 2 + s:3 + s])
            small_ref[:, 0:1] += jnp.sum(grad * normed, axis=1, keepdims=True)
            small_ref[:, 1:2] += jnp.sum(grad, axis=1, keepdims=True)
            scaled = grad * gain
            first = jnp.mean(scaled, axis=0, keepdims=True)
            second = jnp.mean(scaled * normed, axis=0, keepdims=True)
            shifted = (scaled - first - normed * second) * inverse
            x_ref[s, :, at] = shifted.astype(BF16)
            return carry + jnp.sum(shifted, axis=1, keepdims=True)

        small_ref[:, 2 + s:3 + s] = lax.fori_loop(0, length // piece, byte_step, jnp.zeros((width, 1), F32))
        share = width // shards
        own = pltpu.make_async_copy(x_ref.at[s, pl.ds(pl.multiple_of(me * share, 16), share)], g_out.at[me * seqs + s], load_sem.at[6 + s])
        own.start()
        loads.append(own)

    def bytes_send(s, d):
        share = width // shards
        there = pl.ds(pl.multiple_of(z_back[d] * share, 16), share)
        pending.append(send(x_ref.at[s, there], g_out.at[me * seqs + s], a_ss.at[s, d], a_rs.at[s, d], mesh_at(dh=z_back[d])))

    half_rows, quarter = local_rows // 2, local_rows // 4
    piece_rows = quarter // shards

    def latents_send():
        theirs = latsum_in.at[pl.ds(pl.multiple_of((1 - core) * half_rows, 8), half_rows)]
        pending.append(send(theirs, l_sib, l_ss.at[0], l_rs.at[0], to_sib))

    def latents_sib():
        arrived(l_sib, l_ss.at[0], l_rs.at[0])
        own_sum.wait()
        l_half[...] += l_sib[...]
        pending.append(send(l_half.at[pl.ds(pl.multiple_of((1 - hi) * quarter, 8), quarter)], l_y, l_ss.at[1], l_rs.at[1], to_y))

    def latents_y():
        arrived(l_y, l_ss.at[1], l_rs.at[1])
        l_sum[...] = (l_half[pl.ds(pl.multiple_of(hi * quarter, 8), quarter)] + l_y[...]).reshape(l_sum.shape)
        for d in range(1, shards):
            pending.append(send(l_sum.at[z_back[d]], l_z.at[d - 1], l_ss.at[1 + d], l_rs.at[1 + d], mesh_at(dh=z_back[d])))

    def latents_z():
        total = l_sum[me]
        for d in range(1, shards):
            arrived(l_z.at[d - 1], l_ss.at[1 + d], l_rs.at[1 + d])
            total += l_z[d - 1]
        l_tot[...] = total

    def third_first():
        tq_ref[...] = jnp.transpose(dq_out[0, :, my_rows])
        rows_here = tq_ref[pl.ds(pl.multiple_of(core * half_rows + hi * quarter, 8), quarter)].astype(BF16)
        t_part[...] = dot(rows_here, wq_ref[...]).reshape(t_part.shape)
        for d in range(1, shards):
            pending.append(send(t_part.at[z_back[d]], t_got.at[d - 1], t_ss.at[0, d], t_rs.at[0, d], mesh_at(dh=z_back[d])))

    def third_z():
        grad = t_part[me]
        for d in range(1, shards):
            arrived(t_got.at[d - 1], t_ss.at[0, d], t_rs.at[0, d])
            grad += t_got[d - 1]
        loads[3].wait()
        _, normed, inverse = norm_keep(lat8_ref[...], 1.0, 0.0)
        t_z[me, :piece_rows] = l_tot[...] + norm_back(grad, normed, inverse, lgain_ref[0:1])
        t_z[me, piece_rows:] = jnp.zeros((8, lat8_ref.shape[1]), F32)
        t_z[me, piece_rows:piece_rows + 1] = jnp.sum(grad * normed, axis=0, keepdims=True)
        t_z[me, piece_rows + 1:piece_rows + 2] = jnp.sum(grad, axis=0, keepdims=True)
        for d in range(1, shards):
            pending.append(send(t_z.at[me], t_z.at[me], t_ss.at[1, d], t_rs.at[1, d], mesh_at(dh=z_back[d])))

    def third_y():
        for d in range(1, shards):
            arrived(t_z.at[z_of[d]], t_ss.at[1, d], t_rs.at[1, d])
        y_buf[hi, :quarter] = t_z[:, :piece_rows].reshape(quarter, t_z.shape[2])
        y_buf[hi, quarter:] = t_z[0, piece_rows:] + t_z[1, piece_rows:] + t_z[2, piece_rows:] + t_z[3, piece_rows:]
        pending.append(send(y_buf.at[hi], y_buf.at[hi], t_ss.at[2, 0], t_rs.at[2, 0], to_y))

    def third_core():
        arrived(y_buf.at[1 - hi], t_ss.at[2, 0], t_rs.at[2, 0])
        c_buf[core, :quarter] = y_buf[0, :quarter]
        c_buf[core, quarter:half_rows] = y_buf[1, :quarter]
        c_buf[core, half_rows:] = y_buf[0, quarter:] + y_buf[1, quarter:]
        pending.append(send(c_buf.at[core], c_buf.at[core], t_ss.at[2, 1], t_rs.at[2, 1], to_sib))

    def third_x():
        arrived(c_buf.at[1 - core], t_ss.at[2, 1], t_rs.at[2, 1])
        glat_out[:half_rows] = c_buf[0, :half_rows]
        glat_out[half_rows:] = c_buf[1, :half_rows]
        x_buf[blk] = c_buf[0, half_rows:] + c_buf[1, half_rows:]
        pending.append(send(x_buf.at[blk], x_buf.at[blk], t_ss.at[2, 2], t_rs.at[2, 2], to_x))

    def third_end():
        arrived(x_buf.at[other], t_ss.at[2, 2], t_rs.at[2, 2])
        vec_out[...] = x_buf[0] + x_buf[1]

    def small_start():
        wide_lane = lax.broadcasted_iota(jnp.int32, (width, 128), 1)
        block = jnp.where(wide_lane == 32, small_ref[:, 0:1], 0.0) + jnp.where(wide_lane == 33, small_ref[:, 1:2], 0.0)
        for s in range(seqs):
            block += small_ref[:, 2 + s:3 + s] * lang_in[s:s + 1]
        share = width // shards
        for h in range(shards):
            s_ref[0, h, :, :128] = block[h * share:(h + 1) * share]
            s_ref[0, h, :, 128:] = jnp.zeros((share, 128), F32)
            for v in range(vec_in.shape[0]):
                for b in range(vec_in.shape[1] // 128):
                    s_ref[0, h, v * 10 + b:v * 10 + b + 1, 128:] = vec_in[v:v + 1, b * 128:(b + 1) * 128]
        small.start()

    def weight_steps(part):
        def weight_step(h, _):
            at = pl.ds(pl.multiple_of(h * cols, 16), cols)
            total = dot_nt(dkv_ref[0, part, at], xn_ref[0])
            for s in range(1, seqs):
                total += dot_nt(dkv_ref[s, part, at], xn_ref[s])
            dw_tmp[...] = total.astype(BF16)
            w_half[part, h] = dw_tmp[:, pl.ds(pl.multiple_of(core * (width // 2), 128), width // 2)]
            dw_ref[part, h] = dw_tmp[:, pl.ds(pl.multiple_of((1 - core) * (width // 2), 128), width // 2)]
            return 0
        lax.fori_loop(0, shards, weight_step, 0)

    send_do(0)
    mixed_near()
    own_do.wait()
    stats_ready()
    turn_grads(0)
    send_do(1)
    mixed_far()
    head_steps(0, 0)
    latents_send()
    head_steps(0, 1)
    head_steps(0, 2)
    loads[2].wait()
    grads[2].send_chips()
    head_steps(0, 3)
    loads[1].wait()
    byte_steps(0)
    grads[1].send_chips()
    mixed_cross_0()
    bytes_send(0, 1)
    bytes_send(0, 3)
    turn_grads(1)
    head_steps(1, 0)
    head_steps(1, 1)
    bytes_send(0, 2)
    grads[0].send_chips()
    head_steps(1, 2)
    head_steps(1, 3)
    grads[2].join_first()
    query.start()
    loads[0].wait()
    weight_steps(0)
    latents_sib()
    byte_steps(1)
    query.join_sib()
    small_start()
    grads[0].join_first()
    grads[2].join_chips()
    small.join_sib()
    small.send_chips()
    query.send_chips()
    grads[1].join_first()
    pair[0].start()
    latents_y()
    weight_steps(1)
    pair[1].start()
    grads[0].join_chips()
    pair[0].join_sib()
    bytes_send(1, 3)
    query.join_first()
    pair[0].send_chips()
    grads[2].join_near()
    query.join_chips()
    latents_share()
    grads[1].join_chips()
    pair[1].join_sib()
    pair[1].send_chips()
    pair[0].join_first()
    query.join_near()
    grads[0].join_near()
    small.join_first()
    query.join_z()
    query.share_chips()
    grads[1].join_near()
    pair[1].join_first()
    small.join_chips()
    grads[2].join_z()
    bytes_send(1, 2)
    pair[0].join_chips()
    query.share_sib()
    query.finish()
    third_first()
    grads[0].join_z()
    small.join_near()
    pair[0].join_near()
    grads[0].share_chips()
    grads[2].share_chips()
    small.join_z()
    pair[1].join_chips()
    latents_z()
    grads[1].join_z()
    grads[2].share_sib()
    third_z()
    grads[0].share_sib()
    grads[1].share_chips()
    pair[0].join_z()
    pair[1].join_near()
    mixed_cross_1()
    small.share_chips()
    pair[0].share_chips()
    pair[0].share_sib()
    small.share_sib()
    grads[1].share_sib()
    third_y()
    bytes_send(1, 1)
    grads[2].finish()
    pair[1].join_z()
    grads[0].finish()
    third_core()
    pair[0].finish()
    grads[1].finish()
    pair[1].share_chips()
    pair[1].share_sib()
    third_x()
    pair[1].finish()
    small.finish()
    third_end()
    arrived(latn_ref.at[other_rows], misc_ss.at[1], misc_rs.at[1])
    arrived(mixed_out.at[near * seqs + 1], mix_ss.at[1], mix_rs.at[1])
    arrived(mixed_out.at[cross * seqs], mix_ss.at[2], mix_rs.at[2])
    arrived(mixed_out.at[cross * seqs + 1], mix_ss.at[3], mix_rs.at[3])
    for d in range(1, shards):
        for s in range(seqs):
            arrived(g_out.at[z_of[d] * seqs + s], a_ss.at[s, d], a_rs.at[s, d])
    for own in loads[4:]:
        own.wait()
    for copy in pending:
        copy.wait_send()


def second_call(x_cols, rows_in, mask, w_cols, qt, pairs, xn, grad_out, stats, mixed, lat_low, grads, vectors, lang_rows, lat_sum, w_query, lat_f32, lat_gain):
    seqs, width, length = x_cols.shape
    rows, width_lat = qt.shape[3], pairs.shape[2]
    local_rows = lat_low.shape[0]
    shards = lax.axis_size("heads")
    heads = HEADS
    head_dim = width_lat // heads
    cols = width_lat // shards
    share = cols // 4
    whole = pl.BlockSpec(memory_space=pltpu.VMEM)
    hbm = pl.BlockSpec(memory_space=pl.ANY)
    out = jax.ShapeDtypeStruct
    vmem = pltpu.VMEM
    sem = pltpu.SemaphoreType.DMA

    assert seqs == 2

    def reduce_buffers(n, lanes, kind, cols=cols):
        half, share = lanes // 2, cols // 4
        return [vmem((n, shards, cols, half), kind), vmem((n, shards, cols, half), kind), vmem((6, n, 2, share, half), kind),
                vmem((shards - 1, n, share, half), kind)]

    return pl.pallas_call(
        second_kernel,
        in_specs=[hbm, whole, whole, whole, whole, hbm, hbm, hbm, whole, hbm, whole, hbm, whole, whole, hbm, whole, hbm, whole],
        out_specs=[hbm, hbm, hbm, hbm, whole, whole, whole, whole, whole],
        input_output_aliases={9: 1},
        out_shape=[
            out((shards * seqs, width // shards, length), BF16),
            out((shards * seqs, local_rows, width_lat), BF16),
            out((2, cols, width), BF16),
            out((3, cols, width_lat), BF16),
            out((1, width // shards, 256), F32),
            out((local_rows, width_lat), F32),
            out((8, width_lat), F32),
            out((1, cols, rows), F32),
            out((rows, width_lat), BF16),
        ],
        scratch_shapes=[
            vmem((seqs, width, length), BF16),
            vmem((seqs, width, length), BF16),
            vmem((width, rows_in.shape[0]), F32),
            vmem((2, 2, head_dim, length), BF16),
            vmem((seqs, 2, width_lat, length), BF16),
            vmem((heads, rows, head_dim), BF16),
            vmem((heads, rows, head_dim), BF16),
            vmem((128, rows), F32),
            vmem((rows, 128), F32),
            vmem((1, shards, cols, rows), F32),
            vmem((2, shards, cols, width // 2), BF16),
            vmem((cols, width), BF16),
        ] + [
            vmem((3, shards, cols, width_lat // 2), BF16),
            vmem((6, 3, 2, share, width_lat // 2), BF16),
            vmem((3, 3, 1, share, width_lat // 2), BF16),
        ] + reduce_buffers(2, width, BF16)[:3] + [vmem((2, 3, 1, share, width // 2), BF16)]
        + reduce_buffers(1, rows, F32)
        + reduce_buffers(1, 256, F32, width // shards) + [
            vmem((width, 8), F32),
            vmem((1, shards, width // shards, 256), F32),
            vmem((local_rows // 2, width_lat), F32),
            vmem((local_rows // 2, width_lat), F32),
            vmem((local_rows // 4, width_lat), F32),
            vmem((shards, local_rows // 16, width_lat), F32),
            vmem((shards - 1, local_rows // 16, width_lat), F32),
            vmem((local_rows // 16, width_lat), F32),
            vmem((local_rows // 16, width_lat), F32),
            vmem((3, share, width_lat // 2), BF16),
            vmem((2, share, width // 2), BF16),
            vmem((local_rows, cols), F32),
            vmem((shards, local_rows // 16, width_lat), F32),
            vmem((shards - 1, local_rows // 16, width_lat), F32),
            vmem((shards, local_rows // 16 + 8, width_lat), F32),
            vmem((2, local_rows // 4 + 8, width_lat), F32),
            vmem((2, local_rows // 2 + 8, width_lat), F32),
            vmem((2, 8, width_lat), F32),
        ] + [sem((3, 14))] * 2 + [sem((2, 14))] * 2 + [sem((14,))] * 4 + [sem((6,))] * 2 + [sem((3, shards))] * 2 + [sem((seqs,))] * 2 + [sem((2,))] * 2 + [sem((shards,))] * 2 + [sem((seqs, shards))] * 2
        + [sem((16,)), sem((2,)), sem((5,))],
        compiler_params=pltpu.CompilerParams(vmem_limit_bytes=VMEM_LIMIT, collective_id=2, has_side_effects=True),
        name="second",
    )(x_cols, rows_in, mask, w_cols, qt, pairs, xn, grad_out, stats, mixed, lat_low, grads, vectors, lang_rows, lat_sum, w_query, lat_f32, lat_gain)


def middle_kernel(att_ref, lat_ref, cot_ref, all_hbm, bup_tiles, vecs_ref, lse_ref,
                  mixed_all, do_ref, stat_ref, half_ref, vec_ref, sum_ref,
                  rows_ref, mid_ref, low_ref, hid_ref, norm_ref, a_ref, b_src, b_ref, bup_ref, all_ref, mixed_ref, a_ss, a_rs, b_ss, b_rs, load_sem, mix_ss, mix_rs):
    items, _, me, _, core = places()
    near = me + 1 - 2 * lax.rem(me, 2)
    far = lax.rem(me + 2, 4)
    to_sib = mesh_at(di=items + 1 - 2 * core)
    seqs, width, local_rows = att_ref.shape
    rows = seqs * local_rows
    heads = lse_ref.shape[1]
    head_dim = width // heads
    half = width // 2
    block = 256
    pending = []
    loads = [pltpu.make_async_copy(all_hbm.at[i], all_ref.at[i], load_sem.at[i]) for i in range(3)]
    for copy in loads:
        copy.start()
    greet([to_sib, mesh_at(dh=near), mesh_at(dh=far)])
    shards, cols = half_ref.shape[1:3]
    for h in range(shards):
        bup_ref[:, h * cols:(h + 1) * cols] = bup_tiles[h, 7:8, :cols]
    gain_ref, bias_ref, bdown_ref = vecs_ref.at[pl.ds(2, 1)], vecs_ref.at[pl.ds(3, 1)], vecs_ref.at[pl.ds(4, 1)]

    def block_loop(body):
        def step(i, _):
            body(pl.ds(pl.multiple_of(i * block, block), block))
            return 0
        lax.fori_loop(0, width // block, step, 0)

    def share_a(i):
        pending.append(send(a_ref.at[i, 0], a_ref.at[i, 1], a_ss.at[i], a_rs.at[i], to_sib))

    def share_b(i):
        theirs = b_src.at[i, :, pl.ds(pl.multiple_of((1 - core) * half, 128), half)]
        pending.append(send(theirs, b_ref.at[i, 1], b_ss.at[i], b_rs.at[i], to_sib))
        b_ref[i, 0] = b_src[i, :, pl.ds(pl.multiple_of(core * half, 128), half)]

    cot = cot_ref[...]
    b_src[2] = cot
    share_b(2)
    for s in range(seqs):
        at = slice(s * local_rows, (s + 1) * local_rows)
        low = att_ref[s].astype(BF16)
        a_ref[0, 0, :, at] = low
        rows_ref[at] = jnp.transpose(att_ref[s]).astype(BF16)
    share_a(0)

    def branch(at):
        latent = lat_ref[:, at].astype(F32)
        mid_ref[:, at] = dot(rows_ref[...], all_ref[0, :, at]) + jnp.concatenate([latent] * seqs, axis=0)
    loads[0].wait()
    block_loop(branch)
    mid_out, normed, inverse = norm_keep(mid_ref[...], gain_ref[...], bias_ref[...])
    norm_ref[...] = normed
    b_src[1] = mid_out.astype(BF16)
    share_b(1)

    def up(at):
        value = dot_nt(b_src[1], all_ref[1, at]) + bup_ref[:, at]
        square = value * value
        bend = jnp.tanh(0.7978845608028654 * (value + 0.044715 * (square * value)))
        active = 0.5 * value * (1.0 + bend)
        slope = 0.5 * (1.0 + bend) + 0.5 * value * (1.0 - bend * bend) * (0.7978845608028654 * (1.0 + 0.134145 * square))
        rows_ref[:, at] = active.astype(BF16)
        grad = (dot_nt(cot_ref[...], all_ref[2, at]) * slope).astype(BF16)
        low_ref[:, at] = grad
        vec_ref[2:3, at] = jnp.sum(grad.astype(F32), axis=0, keepdims=True)
        a_ref[2, 0, at] = jnp.transpose(active.astype(BF16))
        a_ref[1, 0, at] = jnp.transpose(grad)
    loads[1].wait()
    loads[2].wait()
    block_loop(up)
    share_a(2)
    share_a(1)

    def down(at):
        hid_ref[:, at] = dot(low_ref[...], all_ref[1, :, at])
        out = mid_ref[:, at] + dot(rows_ref[...], all_ref[2, :, at]) + bdown_ref[:, at]
        for s in range(seqs):
            mixed_ref[s, :, at] = out[s * local_rows:(s + 1) * local_rows].astype(BF16)
    block_loop(down)
    own_mixed = pltpu.make_async_copy(mixed_ref, mixed_all.at[pl.ds(me * seqs, seqs)], load_sem.at[3])
    own_mixed.start()
    for i, there in enumerate((far, near)):
        pending.append(send(mixed_ref.at[0], mixed_all.at[me * seqs], mix_ss.at[i], mix_rs.at[i], mesh_at(dh=there)))
    grad = hid_ref[...]
    normed = norm_ref[...]
    vec_ref[0:1] = jnp.sum(grad * normed, axis=0, keepdims=True)
    vec_ref[1:2] = jnp.sum(grad, axis=0, keepdims=True)
    vec_ref[3:4] = jnp.sum(cot_ref[...].astype(F32), axis=0, keepdims=True)
    grad = cot_ref[...].astype(F32) + norm_back(grad, normed, inverse, gain_ref[...])
    b_src[0] = grad.astype(BF16)
    share_b(0)
    total = grad[:local_rows]
    for s in range(1, seqs):
        total += grad[s * local_rows:(s + 1) * local_rows]
    sum_ref[...] = total

    def out(h, _):
        at = pl.ds(pl.multiple_of(h * head_dim, 16), head_dim)
        grad = dot_nt(all_ref[0, at], b_src[0]).astype(BF16)
        for s in range(seqs):
            part = grad[:, s * local_rows:(s + 1) * local_rows]
            do_ref[s, at] = part
            delta = jnp.sum(part.astype(F32) * att_ref[s, at], axis=0, keepdims=True)
            stat_ref[pl.ds((2 * s + 1) * heads + h, 1)] = delta
        return 0
    lax.fori_loop(0, heads, out, 0)
    for s in range(seqs):
        stat_ref[2 * s * heads:(2 * s + 1) * heads] = lse_ref[s]

    def arrived(where, ss, rs):
        pltpu.make_async_remote_copy(src_ref=where, dst_ref=where, send_sem=ss, recv_sem=rs,
                                     device_id=to_sib, device_id_type=pl.DeviceIdType.MESH).wait_recv()

    for i in (2, 1, 0):
        arrived(a_ref.at[i, 1], a_ss.at[i], a_rs.at[i])
        arrived(b_ref.at[i, 1], b_ss.at[i], b_rs.at[i])

        def weight(h, _):
            at = pl.ds(pl.multiple_of(h * cols, 16), cols)
            half_ref[i, h] = (dot(a_ref[i, 0, at], b_ref[i, 0]) + dot(a_ref[i, 1, at], b_ref[i, 1])).astype(BF16)
            return 0
        lax.fori_loop(0, shards, weight, 0)
    own_mixed.wait()
    for i, there in enumerate((far, near)):
        arrived(mixed_all.at[there * seqs], mix_ss.at[i], mix_rs.at[i])
    for copy in pending:
        copy.wait_send()


def middle_call(att, latents, cot, weights, b_up, vecs, lse):
    seqs, width, local_rows = att.shape
    rows = seqs * local_rows
    heads = lse.shape[1]
    shards = lax.axis_size("heads")
    whole = pl.BlockSpec(memory_space=pltpu.VMEM)
    out, vmem, sem = jax.ShapeDtypeStruct, pltpu.VMEM, pltpu.SemaphoreType.DMA
    return pl.pallas_call(
        middle_kernel,
        in_specs=[whole, whole, whole, pl.BlockSpec(memory_space=pl.ANY), whole, whole, whole],
        out_specs=[pl.BlockSpec(memory_space=pl.ANY)] + [whole] * 5,
        out_shape=[
            out((shards * seqs, local_rows, width), BF16),
            out((seqs, width, local_rows), BF16),
            out((2 * seqs * heads, local_rows), F32),
            out((3, shards, width // shards, width // 2), BF16),
            out((4, width), F32),
            out((local_rows, width), F32),
        ],
        scratch_shapes=[
            vmem((rows, width), BF16), vmem((rows, width), F32), vmem((rows, width), BF16), vmem((rows, width), F32), vmem((rows, width), F32),
            vmem((3, 2, width, rows), BF16), vmem((3, rows, width), BF16), vmem((3, 2, rows, width // 2), BF16),
            vmem((1, width), F32), vmem((3, width, width), BF16), vmem((seqs, local_rows, width), BF16),
            sem((3,)), sem((3,)), sem((3,)), sem((3,)), sem((4,)), sem((2,)), sem((2,)),
        ],
        compiler_params=pltpu.CompilerParams(vmem_limit_bytes=VMEM_LIMIT, collective_id=4, has_side_effects=True),
        name="middle",
    )(att, latents, cot, weights, b_up, vecs, lse)


def finish_kernel(lat_ref, pair_ref, small_ref, vec_ref, query_ref, latn_ref,
                  table_out, igain_out, ibias_out, lgain_out, lbias_out, mgain_out, mbias_out, wq_out, wk_out, wv_out, wo_out, wu_out,
                  bup_out, wd_out, bdown_out, wq_ref, wk_ref, wv_ref, wo_ref, wu_ref, wd_ref, row_ref, sems):
    me = lax.axis_index("heads")
    copies = []

    def store(ref, out):
        copy = pltpu.make_async_copy(ref, out, sems.at[len(copies)])
        copy.start()
        copies.append(copy)

    wo_ref[...] = lat_ref[0].astype(F32)
    store(wo_ref, wo_out)
    wd_ref[...] = lat_ref[2].astype(F32)
    store(wd_ref, wd_out)
    wu_ref[...] = jnp.transpose(lat_ref[1]).astype(F32)
    store(wu_ref, wu_out)
    wk_ref[...] = jnp.transpose(pair_ref[0]).astype(F32)
    store(wk_ref, wk_out)
    wv_ref[...] = jnp.transpose(pair_ref[1]).astype(F32)
    store(wv_ref, wv_out)
    query = query_ref[0].astype(BF16)
    for i in range(0, latn_ref.shape[1], 256):
        wq_ref[i:i + 256] = dot_nt(jnp.transpose(latn_ref[:, i:i + 256]), query)
    store(wq_ref, wq_out)
    turned = jnp.transpose(small_ref[0, :, :128])
    table_out[...] = turned[:table_out.shape[0]]
    igain_out[...] = turned[32]
    ibias_out[...] = turned[33]
    lgain_out[...] = vec_ref[0]
    lbias_out[...] = vec_ref[1]
    blocks = row_ref.shape[1] // 128
    for v, out in enumerate((mgain_out, mbias_out, None, bdown_out)):
        for b in range(blocks):
            row_ref[:, b * 128:(b + 1) * 128] = small_ref[0, v * blocks + b:v * blocks + b + 1, 128:]
        if out is not None:
            out[...] = row_ref[0]
        else:
            cols = bup_out.shape[0]
            total = jnp.zeros((1, cols), F32)
            for h in range(row_ref.shape[1] // cols):
                total += jnp.where(me == h, row_ref[:, h * cols:(h + 1) * cols], 0.0)
            bup_out[...] = total[0]
    for copy in copies:
        copy.wait()


def finish_call(lat_total, pair_total, small, vec, query, latn, langs):
    _, cols, width_lat = lat_total.shape
    width = pair_total.shape[2]
    share = small.shape[1]
    whole = pl.BlockSpec(memory_space=pltpu.VMEM)
    hbm = pl.BlockSpec(memory_space=pl.ANY)
    out, vmem = jax.ShapeDtypeStruct, pltpu.VMEM
    big = [(width_lat, cols), (width, cols), (width, cols), (cols, width_lat), (width_lat, cols), (cols, width_lat)]
    return pl.pallas_call(
        finish_kernel,
        in_specs=[whole] * 6,
        out_specs=[whole] * 7 + [hbm] * 5 + [whole, hbm, whole],
        out_shape=[out(shape, F32) for shape in [(langs, share), (share,), (share,)] + [(width_lat,)] * 4 + big[:5] + [(cols,)] + big[5:] + [(width_lat,)]],
        scratch_shapes=[vmem(shape, F32) for shape in big] + [vmem((1, width_lat), F32), pltpu.SemaphoreType.DMA((6,))],
        compiler_params=pltpu.CompilerParams(vmem_limit_bytes=VMEM_LIMIT),
        name="finish",
    )(lat_total, pair_total, small, vec, query, latn)


REST = ("items", "blk")
ALL = ("heads", "items", "blk")


def gather_rows(shard):
    count = lax.axis_size("items") * lax.axis_size("blk")
    me = lax.axis_index("items") * lax.axis_size("blk") + lax.axis_index("blk")
    share = shard.shape[0] // count
    part = lax.dynamic_slice_in_dim(shard, me * share, share, 0)
    return lax.all_gather(part, ALL, axis=0, tiled=True)


def scatter_rows(whole):
    part = lax.psum_scatter(whole.astype(BF16), ALL, scatter_dimension=0, tiled=True)
    return lax.all_gather(part, REST, axis=0, tiled=True)


def general_device(inputs, padding, language, lang_table, latents, in_gain, in_bias, lat_gain, lat_bias, mid_gain, mid_bias,
              w_query, w_key, w_value, w_out, w_up, b_up, w_down, b_down, cotangent):
    length, local_seqs, width = inputs.shape
    local_rows, width_lat = latents.shape
    cols = w_query.shape[1]
    head_dim = width_lat // HEADS
    per_shard = cols // head_dim
    shards = lax.axis_size("heads")
    blocks = lax.axis_size("blk")
    rows = local_rows * blocks
    seqs = local_seqs // shards
    me = lax.axis_index("heads")
    first = me * seqs

    pair_shard = jnp.concatenate([w_key.T, w_value.T], axis=0)
    pair_rows = gather_rows(pair_shard)
    latent_shard = jnp.concatenate([w_out, w_up.T, w_down], axis=0)
    lat_all = gather_rows(latent_shard).reshape(shards, 3, cols, width_lat)
    out_all, up_all, down_all = (lat_all[:, i].reshape(width_lat, width_lat) for i in range(3))

    all_latents = lax.all_gather(latents, "blk", axis=0, tiled=True).astype(F32)
    lat_out, _, _ = norm_keep(all_latents, lat_gain, lat_bias)
    lat_low = lat_out.astype(BF16)
    query_part = dot(lat_low, w_query).astype(BF16)
    queries = lax.all_gather(query_part, "heads", axis=1, tiled=True)
    q = queries.reshape(rows, HEADS, head_dim).transpose(1, 0, 2)

    own = lax.dynamic_slice_in_dim(inputs, first, seqs, 1)
    x_cols = jnp.transpose(own, (1, 2, 0))
    live = jnp.transpose(lax.dynamic_slice_in_dim(padding, first, seqs, 1))
    mask = jnp.where(live > 0, 0.0, MASKED).astype(F32)[:, None, :]
    own_lang = lax.dynamic_slice_in_dim(language, first, seqs, 0)
    onehot = (own_lang[:, None] == jnp.arange(lang_table.shape[0], dtype=jnp.int32)[None, :]).astype(F32)
    emb = jnp.dot(onehot, lang_table.astype(F32), precision=lax.Precision.HIGHEST)[:, :, None]
    gain_col, bias_col = in_gain[:, None], in_bias[:, None]

    pairs, o_cols, lse = forward_call(x_cols, emb, gain_col, bias_col, pair_rows, q, mask, per_shard)

    parts = o_cols.reshape(seqs, width_lat, blocks, local_rows).transpose(2, 0, 3, 1)
    parts = lax.all_to_all(parts, "blk", 0, 0, tiled=True).astype(F32)
    lse_parts = lse.reshape(seqs, HEADS, blocks, local_rows).transpose(2, 0, 3, 1)
    lse_parts = lax.all_to_all(lse_parts, "blk", 0, 0, tiled=True)
    top = jnp.max(lse_parts, axis=0)
    shares = jnp.exp2(lse_parts - top)
    total = jnp.sum(shares, axis=0)
    own_lse = top + jnp.log2(total)
    shares = shares / total
    attended = jnp.sum(parts.reshape(blocks, seqs, local_rows, HEADS, head_dim) * shares[..., None], axis=0)
    att_low = attended.reshape(seqs * local_rows, width_lat).astype(BF16)

    cot = lax.dynamic_slice_in_dim(cotangent, first, seqs, 0).reshape(seqs * local_rows, width_lat)
    lat_f32 = latents.astype(F32)
    middle = (lat_f32[None] + dot(att_low, out_all).reshape(seqs, local_rows, width_lat)).reshape(seqs * local_rows, width_lat)
    mid_out, mid_normed, mid_inverse = norm_keep(middle, mid_gain, mid_bias)
    mid_low = mid_out.astype(BF16)
    b_up_all = lax.all_gather(b_up, "heads", axis=0, tiled=True)
    hidden = dot_nt(mid_low, up_all) + b_up_all
    active, gelu_back = jax.vjp(jax.nn.gelu, hidden)
    active_low = active.astype(BF16)
    own_mixed = (middle + dot(active_low, down_all) + b_down).astype(BF16).reshape(seqs, local_rows, width_lat)
    mixed_latents = lax.all_gather(own_mixed, "heads", axis=0, tiled=True)

    grad_b_down = jnp.sum(cot.astype(F32), axis=0)
    grad_w_down = dot(active_low.T, cot)
    grad_active = dot_nt(cot, down_all)
    grad_hidden = gelu_back(grad_active)[0].astype(BF16)
    grad_b_up = jnp.sum(grad_hidden.astype(F32), axis=0)
    grad_w_up = dot(grad_hidden.T, mid_low)
    grad_mid_norm = dot(grad_hidden, up_all)
    grad_mid_gain = jnp.sum(grad_mid_norm * mid_normed, axis=0)
    grad_mid_bias = jnp.sum(grad_mid_norm, axis=0)
    grad_middle = cot.astype(F32) + norm_back(grad_mid_norm, mid_normed, mid_inverse, mid_gain)
    grad_branch = grad_middle.astype(BF16)
    grad_w_out = dot(att_low.T, grad_branch)
    grad_att = dot_nt(grad_branch, out_all).astype(BF16).reshape(seqs, local_rows, width_lat)
    grad_att_heads = grad_att.reshape(seqs, local_rows, HEADS, head_dim)
    delta = jnp.sum(grad_att_heads.astype(F32) * attended, axis=-1)
    lat_sum = jnp.sum(grad_middle.reshape(seqs, local_rows, width_lat), axis=0)

    all_grad_att = lax.all_gather(grad_att, "blk", axis=1, tiled=True).reshape(seqs, rows, HEADS, head_dim)
    stats = lax.all_gather(jnp.concatenate([own_lse, delta], axis=-1), "blk", axis=1, tiled=True)
    stats = jnp.transpose(stats, (0, 2, 1))[..., None]
    g_cols, dw_pair, dq, dgain, dbias, demb = backward_call(
        x_cols, emb, gain_col, bias_col, pair_rows.T, q, q.transpose(0, 2, 1),
        all_grad_att.transpose(0, 2, 1, 3), all_grad_att.transpose(0, 2, 3, 1),
        stats[:, :HEADS], stats[:, HEADS:], mask, pairs, per_shard)

    send = g_cols.reshape(seqs, shards, width // shards, length).transpose(1, 0, 2, 3)
    got = lax.all_to_all(send, "heads", 0, 0, tiled=True)
    grad_inputs = got.reshape(local_seqs, width // shards, length).transpose(2, 0, 1)

    grad_rows = jnp.stack([grad_w_out, grad_w_up, grad_w_down], axis=0).reshape(3, shards, cols, width_lat)
    lat_total = scatter_rows(grad_rows.transpose(1, 0, 2, 3).reshape(-1, width_lat)).astype(F32)
    pair_total = scatter_rows(dw_pair).astype(F32)

    dq_part = lax.psum_scatter(dq.reshape(width_lat, rows).astype(BF16), "heads", scatter_dimension=0, tiled=True)
    query_low = lax.psum(dq_part, REST)
    grad_w_query = dot(lat_low.T, query_low.T)
    lat_mine = lax.dynamic_slice_in_dim(query_low, lax.axis_index("blk") * local_rows, local_rows, 1)
    grad_lat_part = dot(lat_mine.T, w_query.T)
    grad_lat_norm = lax.psum(grad_lat_part.astype(BF16), "heads").astype(F32)
    lat_sum = lax.psum(lat_sum.astype(BF16), ("heads", "items")).astype(F32)
    _, own_normed, own_inverse = norm_keep(lat_f32, lat_gain, lat_bias)
    grad_latents = lat_sum + norm_back(grad_lat_norm, own_normed, own_inverse, lat_gain)
    lat_small = jnp.concatenate([jnp.sum(grad_lat_norm * own_normed, axis=0), jnp.sum(grad_lat_norm, axis=0)])
    lat_small = lax.psum(lat_small, "blk")

    table = jnp.dot(onehot.T, demb[:, :, 0], precision=lax.Precision.HIGHEST)
    small = jnp.concatenate([table.reshape(-1), dgain[:, 0], dbias[:, 0], grad_mid_gain, grad_mid_bias, grad_b_up, grad_b_down])
    small = lax.psum(small, ALL)
    sizes = [table.size, width, width, width_lat, width_lat, width_lat, width_lat]
    ends = [sum(sizes[:i]) for i in range(len(sizes) + 1)]
    table, dgain, dbias, dmid_gain, dmid_bias, db_up, db_down = (small[ends[i]:ends[i + 1]] for i in range(7))
    share = width // shards
    table = lax.dynamic_slice_in_dim(table.reshape(-1, width), me * share, share, 1)
    return (
        mixed_latents,
        grad_inputs,
        grad_latents,
        table,
        lax.dynamic_slice_in_dim(dgain, me * share, share, 0),
        lax.dynamic_slice_in_dim(dbias, me * share, share, 0),
        lat_small[:width_lat],
        lat_small[width_lat:],
        dmid_gain,
        dmid_bias,
        grad_w_query,
        pair_total[:cols].T,
        pair_total[cols:].T,
        lat_total[:cols],
        lat_total[cols:2 * cols].T,
        lax.dynamic_slice_in_dim(db_up, me * cols, cols, 0),
        lat_total[2 * cols:],
        db_down,
    )


def fast_device(inputs, padding, language, lang_table, latents, in_gain, in_bias, lat_gain, lat_bias, mid_gain, mid_bias,
              w_query, w_key, w_value, w_out, w_up, b_up, w_down, b_down, cotangent):
    length, local_seqs, width = inputs.shape
    local_rows, width_lat = latents.shape
    cols = w_query.shape[1]
    head_dim = width_lat // HEADS
    per_shard = cols // head_dim
    shards = lax.axis_size("heads")
    blocks = lax.axis_size("blk")
    rows = local_rows * blocks
    seqs = local_seqs // shards
    me = lax.axis_index("heads")
    first = me * seqs

    vectors = (lat_gain, lat_bias, mid_gain, mid_bias, b_down, in_gain, in_bias, b_up)
    wq_rows = w_query.T
    w_cols, lat_all, pairs, xn, att_cols, lse_cols, queries_t, lat_low, b_up_tiles, x_cols, rows_in, mask, lang_rows, lat_f32, vecs = first_call(
        inputs, padding.T, language, lang_table, vectors, latents, wq_rows,
        jnp.stack([w_key.T, w_value.T]), jnp.stack([w_out, w_up.T, w_down]), rows, seqs)
    cot = lax.dynamic_slice_in_dim(cotangent, first, seqs, 0).reshape(seqs * local_rows, width_lat)
    mixed, grad_att, stats, grads, vectors, lat_sum = middle_call(att_cols, latents, cot, lat_all, b_up_tiles, vecs, lse_cols)
    grad_att = grad_att.reshape(seqs, shards, cols, local_rows)
    g_cols, mixed_latents, pair_total, lat_total, small, grad_latents, lat_small, dq, lat_low_all = second_call(
        x_cols, rows_in, mask, w_cols, queries_t, pairs, xn, grad_att, stats, mixed, lat_low, grads, vectors, lang_rows, lat_sum,
        wq_rows, lat_f32, vecs)
    grad_inputs = g_cols.transpose(2, 0, 1)
    rest = finish_call(lat_total, pair_total, small, lat_small, dq, lat_low_all, lang_table.shape[0])
    return (mixed_latents, grad_inputs, grad_latents) + tuple(rest)


def solution(mesh):
    placed = (
        P("blk", "items", None), P("blk", "items"), P("items"), P(), P("blk", None), P(), P(), P(), P(), P(), P(),
        P(None, "heads"), P(None, "heads"), P(None, "heads"), P("heads", None), P(None, "heads"), P("heads"),
        P("heads", None), P(), P("items", "blk", None),
    )
    out = (
        P("items", "blk", None), P("blk", "items", "heads"), P("blk", None), P(None, "heads"), P("heads"), P("heads"),
        P(), P(), P(), P(), P(None, "heads"), P(None, "heads"), P(None, "heads"), P("heads", None), P(None, "heads"),
        P("heads"), P("heads", None), P(),
    )
    fits = mesh.shape["blk"] == 2 and mesh.shape["items"] == 4 and mesh.shape["heads"] == 4
    return jax.shard_map(fast_device if fits else general_device, mesh=mesh, in_specs=placed, out_specs=out, check_vma=False)
```

```python
import functools

import jax
import jax.numpy as jnp
from jax import lax
from jax.experimental import pallas as pl
from jax.experimental.pallas import tpu as pltpu
from jax.sharding import PartitionSpec as P

HEADS = 8
EPS = 1e-05
MASKED = -1e30
LOG2E = 1.4426950408889634
F32 = jnp.float32
BF16 = jnp.bfloat16
NT = (((1,), (1,)), ((), ()))
VMEM_LIMIT = 60 * 1024 * 1024


def dot(a, b):
    return jnp.dot(a, b, preferred_element_type=F32)


def dot_nt(a, b):
    return lax.dot_general(a, b, NT, preferred_element_type=F32)


def norm_keep(values, gain, bias):
    average = jnp.mean(values, axis=-1, keepdims=True)
    centred = values - average
    inverse = lax.rsqrt(jnp.mean(centred * centred, axis=-1, keepdims=True) + EPS)
    normed = centred * inverse
    return (normed * gain + bias, normed, inverse)


def norm_back(grad_norm, normed, inverse, gain):
    scaled = grad_norm * gain
    first = jnp.mean(scaled, axis=-1, keepdims=True)
    second = jnp.mean(scaled * normed, axis=-1, keepdims=True)
    return (scaled - first - normed * second) * inverse


def norm_columns(x, emb):
    shifted = x.astype(F32) + emb
    centred = shifted - jnp.mean(shifted, axis=0, keepdims=True)
    inverse = lax.rsqrt(jnp.mean(centred * centred, axis=0, keepdims=True) + EPS)
    return centred * inverse, inverse


def head_rows(h, per_shard, head_dim):
    key = (h // per_shard) * 2 * per_shard + lax.rem(h, per_shard)
    key_at = pl.multiple_of(key * head_dim, head_dim)
    return pl.ds(key_at, head_dim), pl.ds(pl.multiple_of(key_at + per_shard * head_dim, head_dim), head_dim)


def forward_kernel(per_shard, x_ref, emb_ref, gain_ref, bias_ref, w_ref, q_ref, mask_ref, kv_ref, o_ref, lse_ref, xn_ref, stat_ref):
    heads, rows, head_dim = q_ref.shape
    length = x_ref.shape[1]
    piece = min(256, length)

    def norm_step(i, _):
        at = pl.ds(pl.multiple_of(i * piece, piece), piece)
        normed, _unused = norm_columns(x_ref[:, at], emb_ref[...])
        xn_ref[:, at] = (normed * gain_ref[...] + bias_ref[...]).astype(BF16)
        return 0

    lax.fori_loop(0, length // piece, norm_step, 0)
    block = 512 if w_ref.shape[0] % 512 == 0 else 160

    def pair_step(i, _):
        at = pl.ds(pl.multiple_of(i * block, block), block)
        kv_ref[at] = dot(w_ref[at], xn_ref[...]).astype(BF16)
        return 0

    lax.fori_loop(0, w_ref.shape[0] // block, pair_step, 0)
    factor = LOG2E * head_dim ** (-0.5)
    lane = lax.broadcasted_iota(jnp.int32, (rows, 128), 1)
    stat_ref[...] = jnp.zeros_like(stat_ref)

    def head_step(h, _):
        at_key, at_value = head_rows(h, per_shard, head_dim)
        scores = dot(q_ref[h], kv_ref[at_key]) * factor + mask_ref[...]
        top = jnp.max(scores, axis=1, keepdims=True)
        weights = jnp.exp2(scores - top)
        total = jnp.sum(weights, axis=1, keepdims=True)
        out = dot_nt(kv_ref[at_value], weights.astype(BF16))
        stat_ref[...] = jnp.where(lane == h, top + jnp.log2(total), stat_ref[...])
        inverse = jnp.transpose(jnp.broadcast_to(1.0 / total, (rows, 128)))[:1]
        o_ref[pl.ds(pl.multiple_of(h * head_dim, head_dim), head_dim)] = (out * inverse).astype(BF16)
        return 0

    lax.fori_loop(0, heads, head_step, 0)
    lse_ref[...] = jnp.transpose(stat_ref[...])[:heads]


def forward_call(x_cols, emb, gain, bias, w_rows, q, mask, per_shard):
    seqs, width, length = x_cols.shape
    heads, rows, head_dim = q.shape
    pair_rows = w_rows.shape[0]
    whole = pl.BlockSpec(memory_space=pltpu.VMEM)

    def per_seq(*dims):
        return pl.BlockSpec((None,) + dims, lambda s: (s, 0, 0))

    return pl.pallas_call(
        functools.partial(forward_kernel, per_shard),
        grid=(seqs,),
        in_specs=[per_seq(width, length), per_seq(width, 1), whole, whole, whole, whole, per_seq(1, length)],
        out_specs=[per_seq(pair_rows, length), per_seq(heads * head_dim, rows), per_seq(heads, rows)],
        out_shape=[
            jax.ShapeDtypeStruct((seqs, pair_rows, length), BF16),
            jax.ShapeDtypeStruct((seqs, heads * head_dim, rows), BF16),
            jax.ShapeDtypeStruct((seqs, heads, rows), F32),
        ],
        scratch_shapes=[pltpu.VMEM((width, length), BF16), pltpu.VMEM((rows, 128), F32)],
        compiler_params=pltpu.CompilerParams(vmem_limit_bytes=VMEM_LIMIT),
        name="attend",
    )(x_cols, emb, gain, bias, w_rows, q, mask)


def backward_kernel(per_shard, x_ref, emb_ref, gain_ref, bias_ref, w_ref, q_ref, qt_ref, do_ref, dot_ref, lse_ref, delta_ref, mask_ref, kv_ref,
                    g_ref, dw_ref, dq_ref, dgain_ref, dbias_ref, demb_ref, xn_ref, dkv_ref):
    heads, rows, head_dim = q_ref.shape
    width, length = x_ref.shape
    piece = min(256, length)

    @pl.when(pl.program_id(0) == 0)
    def _():
        dw_ref[...] = jnp.zeros_like(dw_ref)
        dq_ref[...] = jnp.zeros_like(dq_ref)
        dgain_ref[...] = jnp.zeros_like(dgain_ref)
        dbias_ref[...] = jnp.zeros_like(dbias_ref)

    def norm_step(i, _):
        at = pl.ds(pl.multiple_of(i * piece, piece), piece)
        normed, _unused = norm_columns(x_ref[:, at], emb_ref[...])
        xn_ref[:, at] = (normed * gain_ref[...] + bias_ref[...]).astype(BF16)
        return 0

    lax.fori_loop(0, length // piece, norm_step, 0)
    scale = head_dim ** (-0.5)
    factor = LOG2E * scale

    def head_step(h, _):
        at_key, at_value = head_rows(h, per_shard, head_dim)
        keys = kv_ref[at_key]
        weights = jnp.exp2(dot(q_ref[h], keys) * factor + mask_ref[...] - lse_ref[h])
        dkv_ref[at_value] = dot(dot_ref[h], weights.astype(BF16)).astype(BF16)
        grad = dot(do_ref[h], kv_ref[at_value]) - delta_ref[h]
        grad = (weights * grad).astype(BF16)
        dkv_ref[at_key] = (dot(qt_ref[h], grad) * scale).astype(BF16)
        dq_ref[h] += dot_nt(keys, grad) * scale
        return 0

    lax.fori_loop(0, heads, head_step, 0)
    block = 512 if dw_ref.shape[0] % 512 == 0 else 160

    def weight_step(i, _):
        at = pl.ds(pl.multiple_of(i * block, block), block)
        dw_ref[at] += dot_nt(dkv_ref[at], xn_ref[...])
        return 0

    lax.fori_loop(0, dw_ref.shape[0] // block, weight_step, 0)

    def byte_step(i, carry):
        at = pl.ds(pl.multiple_of(i * piece, piece), piece)
        grad = dot(w_ref[...], dkv_ref[:, at])
        normed, inverse = norm_columns(x_ref[:, at], emb_ref[...])
        dbias_ref[...] += jnp.sum(grad, axis=1, keepdims=True)
        dgain_ref[...] += jnp.sum(grad * normed, axis=1, keepdims=True)
        scaled = grad * gain_ref[...]
        first = jnp.mean(scaled, axis=0, keepdims=True)
        second = jnp.mean(scaled * normed, axis=0, keepdims=True)
        shifted = (scaled - first - normed * second) * inverse
        g_ref[:, at] = shifted.astype(BF16)
        return carry + jnp.sum(shifted, axis=1, keepdims=True)

    demb_ref[...] = lax.fori_loop(0, length // piece, byte_step, jnp.zeros((width, 1), F32))


def backward_call(x_cols, emb, gain, bias, w, q, qt, grad_out, grad_out_t, lse, delta, mask, pairs, per_shard):
    seqs, width, length = x_cols.shape
    heads, rows, head_dim = q.shape
    pair_rows = w.shape[1]
    whole = pl.BlockSpec(memory_space=pltpu.VMEM)

    def per_seq(*dims):
        return pl.BlockSpec((None,) + dims, lambda s: (s,) + (0,) * len(dims))

    return pl.pallas_call(
        functools.partial(backward_kernel, per_shard),
        grid=(seqs,),
        in_specs=[
            per_seq(width, length), per_seq(width, 1), whole, whole, whole, whole, whole,
            per_seq(heads, rows, head_dim), per_seq(heads, head_dim, rows),
            per_seq(heads, rows, 1), per_seq(heads, rows, 1), per_seq(1, length), per_seq(pair_rows, length),
        ],
        out_specs=[per_seq(width, length), whole, whole, whole, whole, per_seq(width, 1)],
        out_shape=[
            jax.ShapeDtypeStruct((seqs, width, length), BF16),
            jax.ShapeDtypeStruct((pair_rows, width), F32),
            jax.ShapeDtypeStruct((heads, head_dim, rows), F32),
            jax.ShapeDtypeStruct((width, 1), F32),
            jax.ShapeDtypeStruct((width, 1), F32),
            jax.ShapeDtypeStruct((seqs, width, 1), F32),
        ],
        scratch_shapes=[pltpu.VMEM((width, length), BF16), pltpu.VMEM((pair_rows, length), BF16)],
        compiler_params=pltpu.CompilerParams(vmem_limit_bytes=VMEM_LIMIT),
        name="attend_back",
    )(x_cols, emb, gain, bias, w, q, qt, grad_out, grad_out_t, lse, delta, mask, pairs)


def mesh_at(di=None, db=None, dh=None, core=None):
    items, blk, heads = lax.axis_index("items"), lax.axis_index("blk"), lax.axis_index("heads")
    return (items if di is None else di, blk if db is None else db, heads if dh is None else dh)


def places():
    items, blk, heads = lax.axis_index("items"), lax.axis_index("blk"), lax.axis_index("heads")
    core = lax.rem(items, 2)
    return items, blk, heads, items // 2, core


def send(src, dst, sems, recvs, target):
    copy = pltpu.make_async_remote_copy(
        src_ref=src, dst_ref=dst, send_sem=sems, recv_sem=recvs, device_id=target, device_id_type=pl.DeviceIdType.MESH)
    copy.start()
    return copy


def greet(targets):
    barrier = pltpu.get_barrier_semaphore()
    for target in targets:
        pl.semaphore_signal(barrier, inc=1, device_id=target, device_id_type=pl.DeviceIdType.MESH)
    pl.semaphore_wait(barrier, len(targets))


def first_kernel(x_hbm, pad_ref, lang_ref, table_ref, lgain, lbias, mgain, mbias, bdown, igain, ibias, bup, lat_ref, wq_ref, wk_hbm, wv_hbm, wo_hbm, wu_hbm, wd_hbm,
                 wcols_ref, all_ref, kv_out, xn_out, att_ref, lse_ref, qt_ref, latn_ref, bup_all, x_out, rows_ref, mask_ref, lang_out, latf_ref, vecs_ref,
                 pair_shard, lat_shard, x_ref, xbuf, x32, xn_ref, pair_ref, kv_ref, cols_ref, q_ref, o_tmp, o_own, o_send, o_got, stat_ref, stat_send, stat_own, stat_got,
                 pair_ss, pair_rs, lat_ss, lat_rs, q_ss, q_rs, misc_ss, misc_rs, o_ss, o_rs, own_sem, xn_sem, kv_sem, x_sem, w_sem):
    items, blk, me, hi, core = places()
    shards = lax.axis_size("heads")
    seqs, width, length = x_ref.shape
    rows = qt_ref.shape[3]
    local_rows = rows // 2
    heads, _, head_dim = q_ref.shape
    cols = heads * head_dim // shards
    per_shard = heads // shards
    sibling = items + 1 - 2 * core
    other = 1 - blk
    to_sib, to_x, to_y = mesh_at(di=sibling), mesh_at(db=other), mesh_at(di=(1 - hi) * 2 + core)
    z_of = [lax.rem(me + d, shards) for d in range(shards)]
    z_back = [lax.rem(me + shards - d, shards) for d in range(shards)]
    weights = [pltpu.make_async_copy(src, dst, w_sem.at[n]) for n, (src, dst) in enumerate((
        (wk_hbm, pair_shard.at[0]), (wv_hbm, pair_shard.at[1]), (wo_hbm, lat_shard.at[0]), (wu_hbm, lat_shard.at[1]), (wd_hbm, lat_shard.at[2])))]
    for copy in weights:
        copy.start()
    greet([to_sib, to_x, to_y] + [mesh_at(dh=z_of[d]) for d in range(1, shards)])

    share = cols // 4
    chip = hi * 2 + blk
    chip_x, chip_y, chip_xy = hi * 2 + other, (1 - hi) * 2 + blk, (1 - hi) * 2 + other

    def region(ref, shard, chip_at, lanes_of):
        half = ref.shape[2] // 2
        return ref.at[:, pl.ds(pl.multiple_of(shard * cols + chip_at * share, 16), share), pl.ds(pl.multiple_of(lanes_of * half, 128), half)]

    def lane_half(ref, shard, lanes_of):
        half = ref.shape[2] // 2
        return ref.at[:, pl.ds(pl.multiple_of(shard * cols, 16), cols), pl.ds(pl.multiple_of(lanes_of * half, 128), half)]

    pending = []
    local = []
    near = me + 1 - 2 * lax.rem(me, 2)
    far, cross = lax.rem(me + 2, 4), lax.rem(near + 2, 4)
    shard_at = [me, near, far, cross]
    kinds = {"pair": (pair_shard, pair_ref, pair_ss, pair_rs)}
    for m in range(3):
        one = pl.ds(m, 1)
        kinds[f"l{m}"] = (lat_shard.at[one], all_ref.at[one], lat_ss.at[m], lat_rs.at[m])

    def recv(kind, d, stage, where):
        _, dst, ss, rs = kinds[kind]
        pltpu.make_async_remote_copy(src_ref=where, dst_ref=where, send_sem=ss.at[d, stage], recv_sem=rs.at[d, stage],
                                     device_id=to_sib, device_id_type=pl.DeviceIdType.MESH).wait_recv()

    def out_z(kind, d):
        src, dst, ss, rs = kinds[kind]
        if d == 3:
            block = region(dst, far, chip, core)
            pending.append(send(block, block, ss.at[d, 0], rs.at[d, 0], mesh_at(dh=near)))
        else:
            pending.append(send(region(src, 0, chip, core), region(dst, me, chip, core), ss.at[d, 0], rs.at[d, 0], mesh_at(dh=shard_at[d])))

    def after_z(kind, d):
        _, dst, ss, rs = kinds[kind]
        mine = region(dst, shard_at[d], chip, core)
        recv(kind, d, 0, mine)
        pending.append(send(mine, mine, ss.at[d, 1], rs.at[d, 1], to_x))
        pending.append(send(mine, mine, ss.at[d, 2], rs.at[d, 2], to_y))

    def after_x(kind, d):
        _, dst, ss, rs = kinds[kind]
        x_first = kind != "l1"
        got = region(dst, shard_at[d], chip_x if x_first else chip_y, core)
        recv(kind, d, 1 if x_first else 2, got)
        pending.append(send(got, got, ss.at[d, 3], rs.at[d, 3], to_y if x_first else to_x))

    def after_y(kind, d):
        _, dst, ss, rs = kinds[kind]
        x_first = kind != "l1"
        recv(kind, d, 2 if x_first else 1, region(dst, shard_at[d], chip_y if x_first else chip_x, core))
        recv(kind, d, 3, region(dst, shard_at[d], chip_xy, core))
        half = lane_half(dst, shard_at[d], core)
        pending.append(send(half, half, ss.at[d, 4], rs.at[d, 4], to_sib))

    def after_sib(kind, d):
        _, dst, ss, rs = kinds[kind]
        recv(kind, d, 4, lane_half(dst, shard_at[d], 1 - core))

    for copy in weights:
        copy.wait()
    own_pair = pltpu.make_async_copy(pair_shard, pair_ref.at[:, pl.ds(pl.multiple_of(me * cols, 16), cols)], own_sem.at[0])
    own_lat = pltpu.make_async_copy(lat_shard, all_ref.at[:, pl.ds(pl.multiple_of(me * cols, 16), cols)], own_sem.at[1])
    own_pair.start()
    own_lat.start()
    my_rows = pl.ds(pl.multiple_of(blk * local_rows, 128), local_rows)
    other_rows = pl.ds(pl.multiple_of(other * local_rows, 128), local_rows)

    vecs_ref[...] = jnp.zeros_like(vecs_ref)
    for i, vector in enumerate((lgain, lbias, mgain, mbias, bdown, igain, ibias, bup)):
        vecs_ref[i:i + 1, :vector.shape[0]] = vector[...].reshape(1, vector.shape[0])
    rows_ref[0:1] = vecs_ref[5:6, :width]
    rows_ref[1:2] = vecs_ref[6:7, :width]
    rows_ref[4:8] = jnp.zeros((4, width), F32)
    lang_out[...] = jnp.zeros_like(lang_out)
    for s in range(seqs):
        lang = lang_ref[me * seqs + s]
        picked = lax.broadcasted_iota(jnp.int32, table_ref.shape, 0) == lang
        rows_ref[2 + s:3 + s] = jnp.sum(jnp.where(picked, table_ref[...].astype(F32), 0.0), axis=0, keepdims=True)
        lang_out[s:s + 1] = jnp.where(lax.broadcasted_iota(jnp.int32, (1, 128), 1) == lang, 1.0, 0.0)
        mask_ref[s] = jnp.where(pad_ref[pl.ds(me * seqs + s, 1)] > 0, 0.0, MASKED)

    def queries_start():
        latf_ref[...] = lat_ref[...].astype(F32)
        lat_out, _, _ = norm_keep(latf_ref[...], vecs_ref[0:1], vecs_ref[1:2])
        lat_low = lat_out.astype(BF16)
        latn_ref[...] = lat_low
        at_head = pl.ds(pl.multiple_of(core * head_dim, 16), head_dim)
        qt_ref[core, me, :, my_rows] = dot_nt(wq_ref[at_head], lat_low).astype(BF16)
        bup_ref = vecs_ref.at[:, pl.ds(0, bup_all.shape[2])]
        bup_all[me] = bup_ref[...]
        for d in range(1, shards):
            my_q = qt_ref.at[core, me, :, my_rows]
            pending.append(send(my_q, my_q, q_ss.at[0, d], q_rs.at[0, d], mesh_at(dh=z_back[d])))
        for d in range(1, shards):
            pending.append(send(bup_ref, bup_all.at[me], misc_ss.at[d], misc_rs.at[d], mesh_at(dh=z_back[d])))

    cols_ref[...] = jnp.transpose(rows_ref[...])
    step_rows = xbuf.shape[1]

    def load_bytes(c):
        return pltpu.make_async_copy(x_hbm.at[pl.ds(c * step_rows, step_rows)], xbuf.at[c % 2], x_sem.at[c % 2])

    load_bytes(0).start()

    def pick_bytes(c):
        load_bytes(c).wait()
        if (c + 1) * step_rows < length:
            load_bytes(c + 1).start()
        at = slice(c * step_rows, (c + 1) * step_rows)
        for j in range(x32.shape[0]):
            lanes = slice(j * 128, (j + 1) * 128)
            x32[j] = xbuf[c % 2, :, :, lanes].astype(F32).reshape(x32.shape[1:])
            for s in range(seqs):
                x_ref[s, lanes, at] = jnp.transpose(x32[j, pl.ds(me * seqs + s, step_rows, stride=x_hbm.shape[1])]).astype(BF16)
        if (c + 1) * step_rows == length:
            copy = pltpu.make_async_copy(x_ref, x_out, x_sem.at[2])
            copy.start()
            local.append(copy)


    def queries_z():
        for d in range(1, shards):
            wait_plain(qt_ref.at[core, z_of[d], :, my_rows], q_ss.at[0, d], q_rs.at[0, d])
        part = qt_ref.at[core, :, :, my_rows]
        pending.append(send(part, part, q_ss.at[1, 0], q_rs.at[1, 0], to_x))

    def queries_x():
        wait_plain(qt_ref.at[core, :, :, other_rows], q_ss.at[1, 0], q_rs.at[1, 0])
        pending.append(send(qt_ref.at[core], qt_ref.at[core], q_ss.at[1, 1], q_rs.at[1, 1], to_sib))

    def queries_sib():
        wait_plain(qt_ref.at[1 - core], q_ss.at[1, 1], q_rs.at[1, 1])

    def wait_plain(where, ss, rs):
        pltpu.make_async_remote_copy(src_ref=where, dst_ref=where, send_sem=ss, recv_sem=rs,
                                     device_id=to_sib, device_id_type=pl.DeviceIdType.MESH).wait_recv()

    piece = min(256, length)

    def norm_bytes(s):
        def norm_step(i, _):
            at = pl.ds(pl.multiple_of(i * piece, piece), piece)
            normed, _unused = norm_columns(x_ref[s, :, at], cols_ref[:, 2 + s:3 + s])
            xn_ref[s, :, at] = (normed * cols_ref[:, 0:1] + cols_ref[:, 1:2]).astype(BF16)
            return 0
        lax.fori_loop(0, length // piece, norm_step, 0)
        copy = pltpu.make_async_copy(xn_ref.at[s], xn_out.at[s], xn_sem.at[s])
        copy.start()
        local.append(copy)

    def project(d):
        at = pl.ds(pl.multiple_of(shard_at[d] * cols, 16), cols)

        def step(i, _):
            s, part = i // 2, lax.rem(i, 2)
            kv_ref[s, part, at] = dot(pair_ref[part, at], xn_ref[s]).astype(BF16)
            return 0
        lax.fori_loop(0, 2 * seqs, step, 0)
        copy = pltpu.make_async_copy(kv_ref.at[:, :, at], kv_out.at[:, :, at], kv_sem.at[d])
        copy.start()
        local.append(copy)

    factor = LOG2E * head_dim ** (-0.5)
    lane = lax.broadcasted_iota(jnp.int32, (rows, 128), 1)
    stat_ref[...] = jnp.zeros_like(stat_ref)

    def turn_queries(d):
        for j in range(per_shard):
            h = shard_at[d] * per_shard + j
            q_ref[h] = jnp.transpose(qt_ref[j, shard_at[d]])

    def attend(d, s):
        def head_step(j, _):
            h = shard_at[d] * per_shard + j
            at = pl.ds(pl.multiple_of(h * head_dim, 16), head_dim)
            scores = dot(q_ref[h], kv_ref[s, 0, at]) * factor + mask_ref[s]
            top = jnp.max(scores, axis=1, keepdims=True)
            weights = jnp.exp2(scores - top)
            total = jnp.sum(weights, axis=1, keepdims=True)
            out = dot_nt(kv_ref[s, 1, at], weights.astype(BF16))
            stat_ref[s] = jnp.where(lane == h, top + jnp.log2(total), stat_ref[s])
            inverse = jnp.transpose(jnp.broadcast_to(1.0 / total, (rows, 128)))[:1]
            o_tmp[...] = out * inverse
            o_own[s, at] = o_tmp[:, my_rows]
            o_send[s, at] = o_tmp[:, other_rows].astype(BF16)
            return 0
        lax.fori_loop(0, per_shard, head_step, 0)
        part = pl.ds(pl.multiple_of(shard_at[d] * cols, 16), cols)
        pending.append(send(o_send.at[s, part], o_got.at[s, part], o_ss.at[d, s], o_rs.at[d, s], to_x))

    def stats_send():
        for s in range(seqs):
            at = pl.ds(s * heads, heads)
            stats = jnp.transpose(stat_ref[s])[:heads]
            stat_send[...] = stats
            stat_own[at] = stat_send[:, my_rows]
            stat_got[0, at] = stat_send[:, other_rows]
        pending.append(send(stat_got.at[0], stat_got.at[1], o_ss.at[shards, 0], o_rs.at[shards, 0], to_x))

    def turn_weights():
        block = 256
        for part in range(2):
            for i in range(pair_ref.shape[1] // block):
                wcols_ref[part, :, i * block:(i + 1) * block] = jnp.transpose(pair_ref[part, i * block:(i + 1) * block])

    out_z("pair", 1)
    out_z("pair", 2)
    queries_start()
    pick_bytes(0)
    pick_bytes(1)
    pick_bytes(2)
    pick_bytes(3)
    pick_bytes(4)
    pick_bytes(5)
    pick_bytes(6)
    after_z("pair", 1)
    out_z("l0", 1)
    pick_bytes(7)
    queries_z()
    norm_bytes(0)
    after_z("pair", 2)
    out_z("pair", 3)
    norm_bytes(1)
    after_z("l0", 1)
    out_z("l0", 2)
    own_pair.wait()
    project(0)
    after_x("pair", 1)
    after_z("pair", 3)
    out_z("l1", 1)
    after_z("l0", 2)
    out_z("l0", 3)
    after_z("l1", 1)
    out_z("l1", 2)
    after_x("pair", 2)
    queries_x()
    after_x("l0", 1)
    after_y("pair", 1)
    queries_sib()
    turn_queries(0)
    attend(0, 0)
    after_sib("pair", 1)
    after_z("l0", 3)
    out_z("l2", 1)
    attend(0, 1)
    after_x("pair", 3)
    after_x("l0", 2)
    after_z("l1", 2)
    out_z("l1", 3)
    project(1)
    turn_queries(1)
    attend(1, 0)
    after_z("l2", 1)
    out_z("l2", 2)
    attend(1, 1)
    after_z("l1", 3)
    after_x("l1", 1)
    after_x("l0", 3)
    after_y("l0", 1)
    after_z("l2", 2)
    out_z("l2", 3)
    after_y("pair", 2)
    after_sib("l0", 1)
    after_sib("pair", 2)
    project(2)
    after_z("l2", 3)
    turn_queries(2)
    attend(2, 0)
    after_y("l0", 2)
    after_x("l1", 2)
    after_x("l2", 1)
    attend(2, 1)
    after_y("l1", 1)
    after_y("pair", 3)
    after_sib("l0", 2)
    after_x("l2", 2)
    after_x("l1", 3)
    after_sib("l1", 1)
    after_y("l0", 3)
    after_sib("pair", 3)
    project(3)
    after_sib("l0", 3)
    turn_queries(3)
    attend(3, 0)
    after_y("l2", 1)
    after_x("l2", 3)
    attend(3, 1)
    after_y("l1", 2)
    after_y("l2", 2)
    stats_send()
    turn_weights()
    after_y("l1", 3)
    after_y("l2", 3)
    after_sib("l2", 1)
    after_sib("l1", 2)
    after_sib("l2", 2)
    after_sib("l1", 3)
    after_sib("l2", 3)

    wait_plain(stat_got.at[1], o_ss.at[shards, 0], o_rs.at[shards, 0])
    own_lse, got_lse = stat_own[...], stat_got[1]
    top = jnp.maximum(own_lse, got_lse)
    own_share, got_share = jnp.exp2(own_lse - top), jnp.exp2(got_lse - top)
    total = own_share + got_share
    lse = top + jnp.log2(total)
    own_share, got_share = own_share / total, got_share / total
    for s in range(seqs):
        lse_ref[s] = lse[s * heads:(s + 1) * heads]
        for d in range(shards):
            part = pl.ds(pl.multiple_of(shard_at[d] * cols, 16), cols)
            wait_plain(o_got.at[s, part], o_ss.at[d, s], o_rs.at[d, s])
    for s in range(seqs):
        for h in range(heads):
            at = slice(h * head_dim, (h + 1) * head_dim)
            n = s * heads + h
            att_ref[s, at] = o_own[s, at] * own_share[n:n + 1] + o_got[s, at].astype(F32) * got_share[n:n + 1]
    for d in range(1, shards):
        wait_plain(bup_all.at[z_of[d]], misc_ss.at[d], misc_rs.at[d])
    own_lat.wait()
    for copy in local:
        copy.wait()
    for copy in pending:
        copy.wait_send()


def first_call(inputs, padding, language, table, vectors, latents, wq_rows, weights, rows, seqs):
    length, local_seqs, width = inputs.shape
    local_rows, width_lat = latents.shape
    shards = lax.axis_size("heads")
    heads = HEADS
    head_dim = width_lat // heads
    whole = pl.BlockSpec(memory_space=pltpu.VMEM)
    hbm = pl.BlockSpec(memory_space=pl.ANY)
    out = jax.ShapeDtypeStruct
    sem = pltpu.SemaphoreType.DMA
    return pl.pallas_call(
        first_kernel,
        in_specs=[hbm, whole, pl.BlockSpec(memory_space=pltpu.SMEM)] + [whole] * 11 + [hbm] * 5,
        out_specs=[whole, hbm, hbm, hbm] + [whole] * 5 + [hbm] + [whole] * 5,
        out_shape=[
            out((2, width, width_lat), BF16),
            out((3, width_lat, width_lat), BF16),
            out((seqs, 2, width_lat, length), BF16),
            out((seqs, width, length), BF16),
            out((seqs, width_lat, local_rows), F32),
            out((seqs, heads, local_rows), F32),
            out((heads // shards, shards, head_dim, rows), BF16),
            out((local_rows, width_lat), BF16),
            out((shards, 8, 384), F32),
            out((seqs, width, length), BF16),
            out((8, width), F32),
            out((seqs, 1, length), F32),
            out((8, 128), F32),
            out((local_rows, width_lat), F32),
            out((8, width_lat), F32),
        ],
        scratch_shapes=[
            pltpu.VMEM((2, width_lat // shards, width), BF16),
            pltpu.VMEM((3, width_lat // shards, width_lat), BF16),
            pltpu.VMEM((seqs, width, length), BF16),
            pltpu.VMEM((2, 128, local_seqs, width), BF16),
            pltpu.VMEM((width // 128, 128 * local_seqs, 128), F32),
            pltpu.VMEM((seqs, width, length), BF16),
            pltpu.VMEM((2, width_lat, width), BF16),
            pltpu.VMEM((seqs, 2, width_lat, length), BF16),
            pltpu.VMEM((width, 8), F32),
            pltpu.VMEM((heads, rows, head_dim), BF16),
            pltpu.VMEM((head_dim, rows), F32),
            pltpu.VMEM((seqs, width_lat, local_rows), F32),
            pltpu.VMEM((seqs, width_lat, local_rows), BF16),
            pltpu.VMEM((seqs, width_lat, local_rows), BF16),
            pltpu.VMEM((seqs, rows, 128), F32),
            pltpu.VMEM((heads, rows), F32),
            pltpu.VMEM((seqs * heads, local_rows), F32),
            pltpu.VMEM((2, seqs * heads, local_rows), F32),
            sem((shards, 5)), sem((shards, 5)), sem((3, shards, 5)), sem((3, shards, 5)),
            sem((2, shards)), sem((2, shards)), sem((shards,)), sem((shards,)),
            sem((shards + 1, seqs)), sem((shards + 1, seqs)), sem((2,)), sem((seqs,)), sem((shards,)), sem((3,)), sem((5,)),
        ],
        compiler_params=pltpu.CompilerParams(vmem_limit_bytes=VMEM_LIMIT, collective_id=1, has_side_effects=True),
        name="first",
    )(inputs, padding, language, table, *vectors, latents, wq_rows, *weights)


class Reduce:
    def __init__(self, src, half, got_sib, got_chip, got_z, out, ss, rs, pending, x_first=True, stage=None, stage_sem=None):
        self.src, self.half, self.got_sib, self.got_chip, self.got_z, self.out = src, half, got_sib, got_chip, got_z, out
        self.ss, self.rs, self.pending, self.x_first = ss, rs, pending, x_first
        self.stage, self.stage_sem, self.kept = stage, stage_sem, None
        self.split = src is not None and src.shape[3] == half.shape[3]
        items, blk, self.me, hi, self.core = places()
        self.shards = lax.axis_size("heads")
        other = 1 - blk
        self.chip = hi * 2 + blk
        self.chip_x, self.chip_y, self.chip_xy = hi * 2 + other, (1 - hi) * 2 + blk, (1 - hi) * 2 + other
        self.to_x, self.to_y = mesh_at(db=other), mesh_at(di=(1 - hi) * 2 + self.core)
        self.to_sib = mesh_at(di=items + 1 - 2 * self.core)
        self.n, _, self.cols, self.width = half.shape
        self.share = self.cols // 4
        self.near = self.me + 1 - 2 * lax.rem(self.me, 2)
        self.far, self.cross = lax.rem(self.me + 2, 4), lax.rem(self.near + 2, 4)

    def rows(self, chip):
        return pl.ds(pl.multiple_of(chip * self.share, 16), self.share)

    def lanes(self, core):
        return pl.ds(pl.multiple_of(core * self.width, 128), self.width)

    def go(self, src, dst, i, target):
        self.pending.append(send(src, dst, self.ss.at[i], self.rs.at[i], target))

    def arrived(self, where, i):
        pltpu.make_async_remote_copy(src_ref=where, dst_ref=where, send_sem=self.ss.at[i], recv_sem=self.rs.at[i],
                                     device_id=self.to_sib, device_id_type=pl.DeviceIdType.MESH).wait_recv()

    def start(self):
        theirs = self.src if self.split else self.src.at[:, :, :, self.lanes(1 - self.core)]
        self.go(theirs, self.got_sib, 0, self.to_sib)

    def join_sib(self):
        self.arrived(self.got_sib, 0)

        def step(i, _):
            n, h = i // self.shards, lax.rem(i, self.shards)
            own = self.half[n, h] if self.split else self.src[n, h, :, self.lanes(self.core)]
            self.half[n, h] = (own.astype(F32) + self.got_sib[n, h].astype(F32)).astype(self.half.dtype)
            return 0
        lax.fori_loop(0, self.n * self.shards, step, 0)

    def send_chips(self):
        low, high = pl.ds(0, 2), pl.ds(2, 2)
        self.go(self.half.at[:, low, self.rows(self.chip_x)], self.got_chip.at[0], 1, self.to_x)
        self.go(self.half.at[:, high, self.rows(self.chip_y)], self.got_chip.at[2], 3, self.to_y)
        self.go(self.half.at[:, low, self.rows(self.chip_xy)], self.got_chip.at[1], 2, self.to_x)
        self.go(self.half.at[:, high, self.rows(self.chip_xy)], self.got_chip.at[3], 4, self.to_y)

    def add(self, slot, first, rows):
        self.arrived(self.got_chip.at[slot], 1 + slot)
        for n in range(self.n):
            for h in range(2):
                total = self.half[n, first + h, rows].astype(F32) + self.got_chip[slot, n, h].astype(F32)
                self.half[n, first + h, rows] = total.astype(self.half.dtype)

    def join_first(self):
        self.add(1, 0, self.rows(self.chip_y))
        self.go(self.half.at[:, pl.ds(0, 2), self.rows(self.chip_y)], self.got_chip.at[4], 5, self.to_y)
        self.add(3, 2, self.rows(self.chip_x))
        self.go(self.half.at[:, pl.ds(2, 2), self.rows(self.chip_x)], self.got_chip.at[5], 6, self.to_x)
        self.add(0, 0, self.rows(self.chip))
        self.add(2, 2, self.rows(self.chip))

    def join_chips(self):
        mine = self.rows(self.chip)
        self.add(4, 0, mine)
        self.add(5, 2, mine)
        for i, shard in enumerate((self.near, self.cross)):
            self.go(self.half.at[:, shard, mine], self.got_z.at[i], 7 + i, mesh_at(dh=self.near))

    def join_near(self):
        mine = self.rows(self.chip)
        for i, shard in enumerate((self.me, self.far)):
            self.arrived(self.got_z.at[i], 7 + i)
            for n in range(self.n):
                total = self.half[n, shard, mine].astype(F32) + self.got_z[i, n].astype(F32)
                self.half[n, shard, mine] = total.astype(self.half.dtype)
        self.go(self.half.at[:, self.far, mine], self.got_z.at[2], 9, mesh_at(dh=self.far))

    def join_z(self):
        self.arrived(self.got_z.at[2], 9)
        mine = self.rows(self.chip)
        for n in range(self.n):
            total = self.half[n, self.me, mine].astype(F32) + self.got_z[2, n].astype(F32)
            if self.stage is None:
                self.out[n, mine, self.lanes(self.core)] = total.astype(self.out.dtype)
            else:
                self.stage[n] = total.astype(self.out.dtype)
        src = self.piece(self.chip)
        if self.stage is not None:
            self.kept = pltpu.make_async_copy(self.stage, src, self.stage_sem)
            self.kept.start()
            src = self.stage
        self.go(src, self.piece(self.chip), 10, self.to_x)
        self.go(src, self.piece(self.chip), 11, self.to_y)

    def piece(self, chip):
        return self.out.at[:, self.rows(chip), self.lanes(self.core)]

    def pass_on(self, chip, i, target):
        self.go(self.piece(chip), self.piece(chip), i, target)

    def share_chips(self):
        if self.x_first:
            self.arrived(self.piece(self.chip_x), 10)
            self.pass_on(self.chip_x, 12, self.to_y)
        else:
            self.arrived(self.piece(self.chip_y), 11)
            self.pass_on(self.chip_y, 12, self.to_x)

    def share_sib(self):
        if self.x_first:
            self.arrived(self.piece(self.chip_y), 11)
        else:
            self.arrived(self.piece(self.chip_x), 10)
        self.arrived(self.piece(self.chip_xy), 12)
        if self.kept is not None:
            self.kept.wait()
        half = self.out.at[:, :, self.lanes(self.core)]
        self.go(half, half, 13, self.to_sib)

    def finish(self):
        self.arrived(self.out.at[:, :, self.lanes(1 - self.core)], 13)


def second_kernel(x_hbm, rows_ref, mask_ref, w_ref, qt_ref, kv_hbm, xn_hbm, do_in, stat_in, mixed_in, lat_in, grads_hbm, vec_in, lang_in, latsum_in, wq_ref, lat_raw, lgain_ref,
                  g_out, mixed_out, dw_out, dlat_out, small_out, glat_out, vec_out, dq_out, latn_ref,
                  x_ref, xn_ref, cols_ref, kv_ref, dkv_ref, q_ref, do_ref, stat_ref, stat_cols, dq_ref, dw_ref, dw_tmp,
                  g_half, g_chip, g_z, w_half, w_sib, w_chip, w_z, q_half, q_sib, q_chip, q_z, s_half, s_sib, s_chip, s_z,
                  small_ref, s_ref, l_sib, l_half, l_y, l_sum, l_z, l_tot, lat8_ref,
                  g_stage, w_stage, tq_ref, t_part, t_got, t_z, y_buf, c_buf, x_buf,
                  g_ss, g_rs, w_ss, w_rs, q_ss, q_rs, s_ss, s_rs, l_ss, l_rs, t_ss, t_rs, do_ss, do_rs, misc_ss, misc_rs, mix_ss, mix_rs, a_ss, a_rs, load_sem, kv_sem, stage_sem):
    items, blk, me, hi, core = places()
    shards = lax.axis_size("heads")
    seqs, width, length = x_ref.shape
    heads, rows, head_dim = q_ref.shape
    local_rows = rows // 2
    per_shard = heads // shards
    cols = per_shard * head_dim
    stat_rows = stat_in.shape[0]
    other = 1 - blk
    to_x, to_sib = mesh_at(db=other), mesh_at(di=items + 1 - 2 * core)
    to_y = mesh_at(di=(1 - hi) * 2 + core)
    z_of = [lax.rem(me + d, shards) for d in range(shards)]
    z_back = [lax.rem(me + shards - d, shards) for d in range(shards)]
    my_rows = pl.ds(pl.multiple_of(blk * local_rows, 128), local_rows)
    other_rows = pl.ds(pl.multiple_of(other * local_rows, 128), local_rows)
    pending = []
    dot_ref = w_sib.at[:, :, :, pl.ds(0, rows)]
    grads = [Reduce(None, g_half.at[pl.ds(m, 1)], None, g_chip.at[:, pl.ds(m, 1)], g_z.at[m], dlat_out.at[pl.ds(m, 1)], g_ss.at[m], g_rs.at[m], pending, m != 1,
                        g_stage.at[pl.ds(m, 1)], stage_sem.at[m])
             for m in range(3)]
    pair = [Reduce(dw_ref.at[pl.ds(m, 1)], w_half.at[pl.ds(m, 1)], w_sib.at[pl.ds(m, 1)], w_chip.at[:, pl.ds(m, 1)], w_z.at[m],
                   dw_out.at[pl.ds(m, 1)], w_ss.at[m], w_rs.at[m], pending, m == 0, w_stage.at[pl.ds(m, 1)], stage_sem.at[3 + m]) for m in range(2)]
    query = Reduce(dq_ref, q_half, q_sib, q_chip, q_z, dq_out, q_ss, q_rs, pending, False)
    small = Reduce(s_ref, s_half, s_sib, s_chip, s_z, small_out, s_ss, s_rs, pending)
    greet([to_sib, to_x, to_y] + [mesh_at(dh=z_of[d]) for d in range(1, shards)])

    def arrived(where, ss, rs):
        pltpu.make_async_remote_copy(src_ref=where, dst_ref=where, send_sem=ss, recv_sem=rs,
                                     device_id=to_sib, device_id_type=pl.DeviceIdType.MESH).wait_recv()

    pending.append(send(stat_in, stat_ref.at[pl.ds(0, stat_rows), my_rows], misc_ss.at[0], misc_rs.at[0], to_x))

    def send_do(s):
        pending.append(send(do_in.at[s], dot_ref.at[s, :, :, my_rows], do_ss.at[s], do_rs.at[s], to_x))

    near = me + 1 - 2 * lax.rem(me, 2)
    far, cross = lax.rem(me + 2, 4), lax.rem(near + 2, 4)

    def mixed_pass(block, i, there):
        pending.append(send(mixed_out.at[block], mixed_out.at[block], mix_ss.at[i], mix_rs.at[i], mesh_at(dh=there)))

    def mixed_far():
        mixed_pass(me * seqs + 1, 0, far)

    def mixed_near():
        mixed_pass(me * seqs + 1, 1, near)

    def mixed_cross_0():
        mixed_pass(far * seqs, 2, near)

    def mixed_cross_1():
        arrived(mixed_out.at[far * seqs + 1], mix_ss.at[0], mix_rs.at[0])
        mixed_pass(far * seqs + 1, 3, near)

    def latents_share():
        pending.append(send(lat_in, latn_ref.at[my_rows], misc_ss.at[1], misc_rs.at[1], to_x))

    loads = [
        pltpu.make_async_copy(xn_hbm, xn_ref, load_sem.at[0]),
        pltpu.make_async_copy(x_hbm, x_ref, load_sem.at[1]),
        pltpu.make_async_copy(grads_hbm, g_half, load_sem.at[2]),
        pltpu.make_async_copy(lat_raw.at[pl.ds(pl.multiple_of(core * 64 + hi * 32 + me * 8, 8), 8)], lat8_ref, load_sem.at[4]),
    ]
    own_sum = pltpu.make_async_copy(latsum_in.at[pl.ds(pl.multiple_of(core * (local_rows // 2), 8), local_rows // 2)], l_half, load_sem.at[13])
    own_sum.start()
    latn_ref[my_rows] = lat_in[...]
    own_do = pltpu.make_async_copy(do_in, dot_ref.at[:, :, :, my_rows], load_sem.at[5])

    def load_pair(n, start):
        s, h = n // heads, lax.rem(n, heads)
        slot = lax.rem(n, 2)
        copy = pltpu.make_async_copy(kv_hbm.at[s, :, pl.ds(pl.multiple_of(h * head_dim, 16), head_dim)], kv_ref.at[slot], kv_sem.at[slot])
        copy.start() if start else copy.wait()

    load_pair(0, True)
    for copy in loads:
        copy.start()
    own_do.start()
    stat_ref[:stat_rows, my_rows] = stat_in[...]
    stat_ref[stat_rows:] = jnp.zeros((128 - stat_rows, rows), F32)
    for h in range(heads):
        q_ref[h] = jnp.transpose(qt_ref[h % per_shard, h // per_shard])
    dq_ref[...] = jnp.zeros_like(dq_ref)
    small_ref[...] = jnp.zeros_like(small_ref)

    def stats_ready():
        arrived(stat_ref.at[pl.ds(0, stat_rows), other_rows], misc_ss.at[0], misc_rs.at[0])
        stat_cols[...] = jnp.transpose(stat_ref[...])

    scale = head_dim ** (-0.5)
    factor = LOG2E * scale
    lane = lax.broadcasted_iota(jnp.int32, (rows, 128), 1)
    cols_ref[...] = jnp.transpose(rows_ref[...])
    gain = cols_ref[:, 0:1]

    def turn_grads(s):
        arrived(dot_ref.at[s, :, :, other_rows], do_ss.at[s], do_rs.at[s])
        for h in range(heads):
            inner = h % per_shard * head_dim
            do_ref[h] = jnp.transpose(dot_ref[s, h // per_shard, inner:inner + head_dim])

    def head_steps(s, group):
        def head_step(h, _):
            n = s * heads + h
            slot = lax.rem(n, 2)
            load_pair(n, False)

            @pl.when(n + 1 < seqs * heads)
            def _():
                load_pair(n + 1, True)

            at = pl.ds(pl.multiple_of(h * head_dim, 16), head_dim)
            lse = jnp.sum(jnp.where(lane == s * 2 * heads + h, stat_cols[...], 0.0), axis=1, keepdims=True)
            delta = jnp.sum(jnp.where(lane == s * 2 * heads + heads + h, stat_cols[...], 0.0), axis=1, keepdims=True)
            keys = kv_ref[slot, 0]
            weights = jnp.exp2(dot(q_ref[h], keys) * factor + mask_ref[s] - lse)
            part = pl.ds(pl.multiple_of(lax.rem(h, per_shard) * head_dim, 16), head_dim)
            dkv_ref[s, 1, at] = dot(dot_ref[s, h // per_shard, part], weights.astype(BF16)).astype(BF16)
            grad = dot(do_ref[h], kv_ref[slot, 1]) - delta
            grad = (weights * grad).astype(BF16)
            dkv_ref[s, 0, at] = (dot(qt_ref[lax.rem(h, per_shard), h // per_shard], grad) * scale).astype(BF16)
            dq_ref[0, h // per_shard, part] += dot_nt(keys, grad) * scale
            return 0

        lax.fori_loop(2 * group, 2 * group + 2, head_step, 0)

    piece = min(256, length)

    def byte_steps(s):
        def byte_step(i, carry):
            at = pl.ds(pl.multiple_of(i * piece, piece), piece)
            grad = dot(w_ref[0], dkv_ref[s, 0, :, at]) + dot(w_ref[1], dkv_ref[s, 1, :, at])
            normed, inverse = norm_columns(x_ref[s, :, at], cols_ref[:, 2 + s:3 + s])
            small_ref[:, 0:1] += jnp.sum(grad * normed, axis=1, keepdims=True)
            small_ref[:, 1:2] += jnp.sum(grad, axis=1, keepdims=True)
            scaled = grad * gain
            first = jnp.mean(scaled, axis=0, keepdims=True)
            second = jnp.mean(scaled * normed, axis=0, keepdims=True)
            shifted = (scaled - first - normed * second) * inverse
            x_ref[s, :, at] = shifted.astype(BF16)
            return carry + jnp.sum(shifted, axis=1, keepdims=True)

        small_ref[:, 2 + s:3 + s] = lax.fori_loop(0, length // piece, byte_step, jnp.zeros((width, 1), F32))
        share = width // shards
        own = pltpu.make_async_copy(x_ref.at[s, pl.ds(pl.multiple_of(me * share, 16), share)], g_out.at[me * seqs + s], load_sem.at[6 + s])
        own.start()
        loads.append(own)

    def bytes_send(s, d):
        share = width // shards
        there = pl.ds(pl.multiple_of(z_back[d] * share, 16), share)
        pending.append(send(x_ref.at[s, there], g_out.at[me * seqs + s], a_ss.at[s, d], a_rs.at[s, d], mesh_at(dh=z_back[d])))

    half_rows, quarter = local_rows // 2, local_rows // 4
    piece_rows = quarter // shards

    def latents_send():
        theirs = latsum_in.at[pl.ds(pl.multiple_of((1 - core) * half_rows, 8), half_rows)]
        pending.append(send(theirs, l_sib, l_ss.at[0], l_rs.at[0], to_sib))

    def latents_sib():
        arrived(l_sib, l_ss.at[0], l_rs.at[0])
        own_sum.wait()
        l_half[...] += l_sib[...]
        pending.append(send(l_half.at[pl.ds(pl.multiple_of((1 - hi) * quarter, 8), quarter)], l_y, l_ss.at[1], l_rs.at[1], to_y))

    def latents_y():
        arrived(l_y, l_ss.at[1], l_rs.at[1])
        l_sum[...] = (l_half[pl.ds(pl.multiple_of(hi * quarter, 8), quarter)] + l_y[...]).reshape(l_sum.shape)
        for d in range(1, shards):
            pending.append(send(l_sum.at[z_back[d]], l_z.at[d - 1], l_ss.at[1 + d], l_rs.at[1 + d], mesh_at(dh=z_back[d])))

    def latents_z():
        total = l_sum[me]
        for d in range(1, shards):
            arrived(l_z.at[d - 1], l_ss.at[1 + d], l_rs.at[1 + d])
            total += l_z[d - 1]
        l_tot[...] = total

    def third_first():
        tq_ref[...] = jnp.transpose(dq_out[0, :, my_rows])
        rows_here = tq_ref[pl.ds(pl.multiple_of(core * half_rows + hi * quarter, 8), quarter)].astype(BF16)
        t_part[...] = dot(rows_here, wq_ref[...]).reshape(t_part.shape)
        for d in range(1, shards):
            pending.append(send(t_part.at[z_back[d]], t_got.at[d - 1], t_ss.at[0, d], t_rs.at[0, d], mesh_at(dh=z_back[d])))

    def third_z():
        grad = t_part[me]
        for d in range(1, shards):
            arrived(t_got.at[d - 1], t_ss.at[0, d], t_rs.at[0, d])
            grad += t_got[d - 1]
        loads[3].wait()
        _, normed, inverse = norm_keep(lat8_ref[...], 1.0, 0.0)
        t_z[me, :piece_rows] = l_tot[...] + norm_back(grad, normed, inverse, lgain_ref[0:1])
        t_z[me, piece_rows:] = jnp.zeros((8, lat8_ref.shape[1]), F32)
        t_z[me, piece_rows:piece_rows + 1] = jnp.sum(grad * normed, axis=0, keepdims=True)
        t_z[me, piece_rows + 1:piece_rows + 2] = jnp.sum(grad, axis=0, keepdims=True)
        for d in range(1, shards):
            pending.append(send(t_z.at[me], t_z.at[me], t_ss.at[1, d], t_rs.at[1, d], mesh_at(dh=z_back[d])))

    def third_y():
        for d in range(1, shards):
            arrived(t_z.at[z_of[d]], t_ss.at[1, d], t_rs.at[1, d])
        y_buf[hi, :quarter] = t_z[:, :piece_rows].reshape(quarter, t_z.shape[2])
        y_buf[hi, quarter:] = t_z[0, piece_rows:] + t_z[1, piece_rows:] + t_z[2, piece_rows:] + t_z[3, piece_rows:]
        pending.append(send(y_buf.at[hi], y_buf.at[hi], t_ss.at[2, 0], t_rs.at[2, 0], to_y))

    def third_core():
        arrived(y_buf.at[1 - hi], t_ss.at[2, 0], t_rs.at[2, 0])
        c_buf[core, :quarter] = y_buf[0, :quarter]
        c_buf[core, quarter:half_rows] = y_buf[1, :quarter]
        c_buf[core, half_rows:] = y_buf[0, quarter:] + y_buf[1, quarter:]
        pending.append(send(c_buf.at[core], c_buf.at[core], t_ss.at[2, 1], t_rs.at[2, 1], to_sib))

    def third_x():
        arrived(c_buf.at[1 - core], t_ss.at[2, 1], t_rs.at[2, 1])
        glat_out[:half_rows] = c_buf[0, :half_rows]
        glat_out[half_rows:] = c_buf[1, :half_rows]
        x_buf[blk] = c_buf[0, half_rows:] + c_buf[1, half_rows:]
        pending.append(send(x_buf.at[blk], x_buf.at[blk], t_ss.at[2, 2], t_rs.at[2, 2], to_x))

    def third_end():
        arrived(x_buf.at[other], t_ss.at[2, 2], t_rs.at[2, 2])
        vec_out[...] = x_buf[0] + x_buf[1]

    def small_start():
        wide_lane = lax.broadcasted_iota(jnp.int32, (width, 128), 1)
        block = jnp.where(wide_lane == 32, small_ref[:, 0:1], 0.0) + jnp.where(wide_lane == 33, small_ref[:, 1:2], 0.0)
        for s in range(seqs):
            block += small_ref[:, 2 + s:3 + s] * lang_in[s:s + 1]
        share = width // shards
        for h in range(shards):
            s_ref[0, h, :, :128] = block[h * share:(h + 1) * share]
            s_ref[0, h, :, 128:] = jnp.zeros((share, 128), F32)
            for v in range(vec_in.shape[0]):
                for b in range(vec_in.shape[1] // 128):
                    s_ref[0, h, v * 10 + b:v * 10 + b + 1, 128:] = vec_in[v:v + 1, b * 128:(b + 1) * 128]
        small.start()

    def weight_steps(part):
        def weight_step(h, _):
            at = pl.ds(pl.multiple_of(h * cols, 16), cols)
            total = dot_nt(dkv_ref[0, part, at], xn_ref[0])
            for s in range(1, seqs):
                total += dot_nt(dkv_ref[s, part, at], xn_ref[s])
            dw_tmp[...] = total.astype(BF16)
            w_half[part, h] = dw_tmp[:, pl.ds(pl.multiple_of(core * (width // 2), 128), width // 2)]
            dw_ref[part, h] = dw_tmp[:, pl.ds(pl.multiple_of((1 - core) * (width // 2), 128), width // 2)]
            return 0
        lax.fori_loop(0, shards, weight_step, 0)

    send_do(0)
    mixed_near()
    own_do.wait()
    stats_ready()
    turn_grads(0)
    send_do(1)
    mixed_far()
    head_steps(0, 0)
    latents_send()
    head_steps(0, 1)
    head_steps(0, 2)
    loads[2].wait()
    grads[2].send_chips()
    head_steps(0, 3)
    loads[1].wait()
    byte_steps(0)
    grads[1].send_chips()
    mixed_cross_0()
    bytes_send(0, 1)
    bytes_send(0, 3)
    turn_grads(1)
    head_steps(1, 0)
    head_steps(1, 1)
    bytes_send(0, 2)
    grads[0].send_chips()
    head_steps(1, 2)
    head_steps(1, 3)
    grads[2].join_first()
    query.start()
    loads[0].wait()
    weight_steps(0)
    latents_sib()
    byte_steps(1)
    query.join_sib()
    small_start()
    grads[0].join_first()
    grads[2].join_chips()
    small.join_sib()
    small.send_chips()
    query.send_chips()
    grads[1].join_first()
    pair[0].start()
    latents_y()
    weight_steps(1)
    pair[1].start()
    grads[0].join_chips()
    pair[0].join_sib()
    bytes_send(1, 3)
    query.join_first()
    pair[0].send_chips()
    grads[2].join_near()
    query.join_chips()
    latents_share()
    grads[1].join_chips()
    pair[1].join_sib()
    pair[1].send_chips()
    pair[0].join_first()
    query.join_near()
    grads[0].join_near()
    small.join_first()
    query.join_z()
    query.share_chips()
    grads[1].join_near()
    pair[1].join_first()
    small.join_chips()
    grads[2].join_z()
    bytes_send(1, 2)
    pair[0].join_chips()
    query.share_sib()
    query.finish()
    third_first()
    grads[0].join_z()
    small.join_near()
    pair[0].join_near()
    grads[0].share_chips()
    grads[2].share_chips()
    small.join_z()
    pair[1].join_chips()
    latents_z()
    grads[1].join_z()
    grads[2].share_sib()
    third_z()
    grads[0].share_sib()
    grads[1].share_chips()
    pair[0].join_z()
    pair[1].join_near()
    mixed_cross_1()
    small.share_chips()
    pair[0].share_chips()
    pair[0].share_sib()
    small.share_sib()
    grads[1].share_sib()
    third_y()
    bytes_send(1, 1)
    grads[2].finish()
    pair[1].join_z()
    grads[0].finish()
    third_core()
    pair[0].finish()
    grads[1].finish()
    pair[1].share_chips()
    pair[1].share_sib()
    third_x()
    pair[1].finish()
    small.finish()
    third_end()
    arrived(latn_ref.at[other_rows], misc_ss.at[1], misc_rs.at[1])
    arrived(mixed_out.at[near * seqs + 1], mix_ss.at[1], mix_rs.at[1])
    arrived(mixed_out.at[cross * seqs], mix_ss.at[2], mix_rs.at[2])
    arrived(mixed_out.at[cross * seqs + 1], mix_ss.at[3], mix_rs.at[3])
    for d in range(1, shards):
        for s in range(seqs):
            arrived(g_out.at[z_of[d] * seqs + s], a_ss.at[s, d], a_rs.at[s, d])
    for own in loads[4:]:
        own.wait()
    for copy in pending:
        copy.wait_send()


def second_call(x_cols, rows_in, mask, w_cols, qt, pairs, xn, grad_out, stats, mixed, lat_low, grads, vectors, lang_rows, lat_sum, w_query, lat_f32, lat_gain):
    seqs, width, length = x_cols.shape
    rows, width_lat = qt.shape[3], pairs.shape[2]
    local_rows = lat_low.shape[0]
    shards = lax.axis_size("heads")
    heads = HEADS
    head_dim = width_lat // heads
    cols = width_lat // shards
    share = cols // 4
    whole = pl.BlockSpec(memory_space=pltpu.VMEM)
    hbm = pl.BlockSpec(memory_space=pl.ANY)
    out = jax.ShapeDtypeStruct
    vmem = pltpu.VMEM
    sem = pltpu.SemaphoreType.DMA

    assert seqs == 2

    def reduce_buffers(n, lanes, kind, cols=cols):
        half, share = lanes // 2, cols // 4
        return [vmem((n, shards, cols, half), kind), vmem((n, shards, cols, half), kind), vmem((6, n, 2, share, half), kind),
                vmem((shards - 1, n, share, half), kind)]

    return pl.pallas_call(
        second_kernel,
        in_specs=[hbm, whole, whole, whole, whole, hbm, hbm, hbm, whole, hbm, whole, hbm, whole, whole, hbm, whole, hbm, whole],
        out_specs=[hbm, hbm, hbm, hbm, whole, whole, whole, whole, whole],
        input_output_aliases={9: 1},
        out_shape=[
            out((shards * seqs, width // shards, length), BF16),
            out((shards * seqs, local_rows, width_lat), BF16),
            out((2, cols, width), BF16),
            out((3, cols, width_lat), BF16),
            out((1, width // shards, 256), F32),
            out((local_rows, width_lat), F32),
            out((8, width_lat), F32),
            out((1, cols, rows), F32),
            out((rows, width_lat), BF16),
        ],
        scratch_shapes=[
            vmem((seqs, width, length), BF16),
            vmem((seqs, width, length), BF16),
            vmem((width, rows_in.shape[0]), F32),
            vmem((2, 2, head_dim, length), BF16),
            vmem((seqs, 2, width_lat, length), BF16),
            vmem((heads, rows, head_dim), BF16),
            vmem((heads, rows, head_dim), BF16),
            vmem((128, rows), F32),
            vmem((rows, 128), F32),
            vmem((1, shards, cols, rows), F32),
            vmem((2, shards, cols, width // 2), BF16),
            vmem((cols, width), BF16),
        ] + [
            vmem((3, shards, cols, width_lat // 2), BF16),
            vmem((6, 3, 2, share, width_lat // 2), BF16),
            vmem((3, 3, 1, share, width_lat // 2), BF16),
        ] + reduce_buffers(2, width, BF16)[:3] + [vmem((2, 3, 1, share, width // 2), BF16)]
        + reduce_buffers(1, rows, F32)
        + reduce_buffers(1, 256, F32, width // shards) + [
            vmem((width, 8), F32),
            vmem((1, shards, width // shards, 256), F32),
            vmem((local_rows // 2, width_lat), F32),
            vmem((local_rows // 2, width_lat), F32),
            vmem((local_rows // 4, width_lat), F32),
            vmem((shards, local_rows // 16, width_lat), F32),
            vmem((shards - 1, local_rows // 16, width_lat), F32),
            vmem((local_rows // 16, width_lat), F32),
            vmem((local_rows // 16, width_lat), F32),
            vmem((3, share, width_lat // 2), BF16),
            vmem((2, share, width // 2), BF16),
            vmem((local_rows, cols), F32),
            vmem((shards, local_rows // 16, width_lat), F32),
            vmem((shards - 1, local_rows // 16, width_lat), F32),
            vmem((shards, local_rows // 16 + 8, width_lat), F32),
            vmem((2, local_rows // 4 + 8, width_lat), F32),
            vmem((2, local_rows // 2 + 8, width_lat), F32),
            vmem((2, 8, width_lat), F32),
        ] + [sem((3, 14))] * 2 + [sem((2, 14))] * 2 + [sem((14,))] * 4 + [sem((6,))] * 2 + [sem((3, shards))] * 2 + [sem((seqs,))] * 2 + [sem((2,))] * 2 + [sem((shards,))] * 2 + [sem((seqs, shards))] * 2
        + [sem((16,)), sem((2,)), sem((5,))],
        compiler_params=pltpu.CompilerParams(vmem_limit_bytes=VMEM_LIMIT, collective_id=2, has_side_effects=True),
        name="second",
    )(x_cols, rows_in, mask, w_cols, qt, pairs, xn, grad_out, stats, mixed, lat_low, grads, vectors, lang_rows, lat_sum, w_query, lat_f32, lat_gain)


def middle_kernel(att_ref, lat_ref, cot_hbm, all_hbm, bup_tiles, vecs_ref, lse_ref,
                  mixed_all, do_ref, stat_ref, half_ref, vec_ref, sum_ref,
                  rows_ref, mid_ref, low_ref, hid_ref, norm_ref, a_ref, b_src, b_ref, bup_ref, all_ref, mixed_ref, cot_ref, slope_ref, a_ss, a_rs, b_ss, b_rs, load_sem, mix_ss, mix_rs):
    items, _, me, _, core = places()
    near = me + 1 - 2 * lax.rem(me, 2)
    far = lax.rem(me + 2, 4)
    to_sib = mesh_at(di=items + 1 - 2 * core)
    seqs, width, local_rows = att_ref.shape
    rows = seqs * local_rows
    heads = lse_ref.shape[1]
    head_dim = width // heads
    half = width // 2
    block = 256
    pending = []
    loads = [pltpu.make_async_copy(all_hbm.at[i], all_ref.at[i], load_sem.at[i]) for i in range(3)]
    cots = [pltpu.make_async_copy(cot_hbm.at[me * seqs + s], cot_ref.at[pl.ds(s * local_rows, local_rows)], load_sem.at[4 + s]) for s in range(seqs)]
    for copy in cots + loads:
        copy.start()
    greet([to_sib, mesh_at(dh=near), mesh_at(dh=far)])
    shards, cols = half_ref.shape[1:3]
    for h in range(shards):
        bup_ref[:, h * cols:(h + 1) * cols] = bup_tiles[h, 7:8, :cols]
    gain_ref, bias_ref, bdown_ref = vecs_ref.at[pl.ds(2, 1)], vecs_ref.at[pl.ds(3, 1)], vecs_ref.at[pl.ds(4, 1)]

    def block_loop(body):
        def step(i, _):
            body(pl.ds(pl.multiple_of(i * block, block), block))
            return 0
        lax.fori_loop(0, width // block, step, 0)

    def share_a(i):
        pending.append(send(a_ref.at[i, 0], a_ref.at[i, 1], a_ss.at[i], a_rs.at[i], to_sib))

    def share_b(i):
        theirs = b_src.at[i, :, pl.ds(pl.multiple_of((1 - core) * half, 128), half)]
        pending.append(send(theirs, b_ref.at[i, 1], b_ss.at[i], b_rs.at[i], to_sib))
        b_ref[i, 0] = b_src[i, :, pl.ds(pl.multiple_of(core * half, 128), half)]

    for s in range(seqs):
        at = slice(s * local_rows, (s + 1) * local_rows)
        low = att_ref[s].astype(BF16)
        a_ref[0, 0, :, at] = low
        rows_ref[at] = jnp.transpose(att_ref[s]).astype(BF16)
    share_a(0)
    for copy in cots:
        copy.wait()
    b_src[2] = cot_ref[...]
    share_b(2)

    def branch(at):
        latent = lat_ref[:, at].astype(F32)
        mid_ref[:, at] = dot(rows_ref[...], all_ref[0, :, at]) + jnp.concatenate([latent] * seqs, axis=0)
    loads[0].wait()
    block_loop(branch)
    mid_out, normed, inverse = norm_keep(mid_ref[...], gain_ref[...], bias_ref[...])
    norm_ref[...] = normed
    b_src[1] = mid_out.astype(BF16)
    share_b(1)

    def up(at):
        value = dot_nt(b_src[1], all_ref[1, at]) + bup_ref[:, at]
        square = value * value
        bend = jnp.tanh(0.7978845608028654 * (value + 0.044715 * (square * value)))
        active = 0.5 * value * (1.0 + bend)
        slope_ref[:, at] = 0.5 * (1.0 + bend) + 0.5 * value * (1.0 - bend * bend) * (0.7978845608028654 * (1.0 + 0.134145 * square))
        rows_ref[:, at] = active.astype(BF16)
        a_ref[2, 0, at] = jnp.transpose(active.astype(BF16))
    loads[1].wait()
    block_loop(up)
    share_a(2)

    def down(at):
        out = mid_ref[:, at] + dot(rows_ref[...], all_ref[2, :, at]) + bdown_ref[:, at]
        for s in range(seqs):
            mixed_ref[s, :, at] = out[s * local_rows:(s + 1) * local_rows].astype(BF16)
    loads[2].wait()
    block_loop(down)
    own_mixed = pltpu.make_async_copy(mixed_ref, mixed_all.at[pl.ds(me * seqs, seqs)], load_sem.at[3])
    own_mixed.start()
    for i, there in enumerate((far, near)):
        pending.append(send(mixed_ref.at[0], mixed_all.at[me * seqs], mix_ss.at[i], mix_rs.at[i], mesh_at(dh=there)))

    def up_back(at):
        grad = (dot_nt(cot_ref[...], all_ref[2, at]) * slope_ref[:, at]).astype(BF16)
        low_ref[:, at] = grad
        vec_ref[2:3, at] = jnp.sum(grad.astype(F32), axis=0, keepdims=True)
        a_ref[1, 0, at] = jnp.transpose(grad)
    block_loop(up_back)
    share_a(1)

    def mid_back(at):
        hid_ref[:, at] = dot(low_ref[...], all_ref[1, :, at])
    block_loop(mid_back)
    grad = hid_ref[...]
    normed = norm_ref[...]
    vec_ref[0:1] = jnp.sum(grad * normed, axis=0, keepdims=True)
    vec_ref[1:2] = jnp.sum(grad, axis=0, keepdims=True)
    vec_ref[3:4] = jnp.sum(cot_ref[...].astype(F32), axis=0, keepdims=True)
    grad = cot_ref[...].astype(F32) + norm_back(grad, normed, inverse, gain_ref[...])
    b_src[0] = grad.astype(BF16)
    share_b(0)
    total = grad[:local_rows]
    for s in range(1, seqs):
        total += grad[s * local_rows:(s + 1) * local_rows]
    sum_ref[...] = total

    def out(h, _):
        at = pl.ds(pl.multiple_of(h * head_dim, 16), head_dim)
        grad = dot_nt(all_ref[0, at], b_src[0]).astype(BF16)
        for s in range(seqs):
            part = grad[:, s * local_rows:(s + 1) * local_rows]
            do_ref[s, at] = part
            delta = jnp.sum(part.astype(F32) * att_ref[s, at], axis=0, keepdims=True)
            stat_ref[pl.ds((2 * s + 1) * heads + h, 1)] = delta
        return 0
    lax.fori_loop(0, heads, out, 0)
    for s in range(seqs):
        stat_ref[2 * s * heads:(2 * s + 1) * heads] = lse_ref[s]

    def arrived(where, ss, rs):
        pltpu.make_async_remote_copy(src_ref=where, dst_ref=where, send_sem=ss, recv_sem=rs,
                                     device_id=to_sib, device_id_type=pl.DeviceIdType.MESH).wait_recv()

    for i in (2, 1, 0):
        arrived(a_ref.at[i, 1], a_ss.at[i], a_rs.at[i])
        arrived(b_ref.at[i, 1], b_ss.at[i], b_rs.at[i])

        def weight(h, _):
            at = pl.ds(pl.multiple_of(h * cols, 16), cols)
            half_ref[i, h] = (dot(a_ref[i, 0, at], b_ref[i, 0]) + dot(a_ref[i, 1, at], b_ref[i, 1])).astype(BF16)
            return 0
        lax.fori_loop(0, shards, weight, 0)
    own_mixed.wait()
    for i, there in enumerate((far, near)):
        arrived(mixed_all.at[there * seqs], mix_ss.at[i], mix_rs.at[i])
    for copy in pending:
        copy.wait_send()


def middle_call(att, latents, cot, weights, b_up, vecs, lse):
    seqs, width, local_rows = att.shape
    rows = seqs * local_rows
    heads = lse.shape[1]
    shards = lax.axis_size("heads")
    whole = pl.BlockSpec(memory_space=pltpu.VMEM)
    out, vmem, sem = jax.ShapeDtypeStruct, pltpu.VMEM, pltpu.SemaphoreType.DMA
    return pl.pallas_call(
        middle_kernel,
        in_specs=[whole, whole, pl.BlockSpec(memory_space=pl.ANY), pl.BlockSpec(memory_space=pl.ANY), whole, whole, whole],
        out_specs=[pl.BlockSpec(memory_space=pl.ANY)] + [whole] * 5,
        out_shape=[
            out((shards * seqs, local_rows, width), BF16),
            out((seqs, width, local_rows), BF16),
            out((2 * seqs * heads, local_rows), F32),
            out((3, shards, width // shards, width // 2), BF16),
            out((4, width), F32),
            out((local_rows, width), F32),
        ],
        scratch_shapes=[
            vmem((rows, width), BF16), vmem((rows, width), F32), vmem((rows, width), BF16), vmem((rows, width), F32), vmem((rows, width), F32),
            vmem((3, 2, width, rows), BF16), vmem((3, rows, width), BF16), vmem((3, 2, rows, width // 2), BF16),
            vmem((1, width), F32), vmem((3, width, width), BF16), vmem((seqs, local_rows, width), BF16), vmem((rows, width), BF16), vmem((rows, width), F32),
            sem((3,)), sem((3,)), sem((3,)), sem((3,)), sem((4 + seqs,)), sem((2,)), sem((2,)),
        ],
        compiler_params=pltpu.CompilerParams(vmem_limit_bytes=VMEM_LIMIT, collective_id=4, has_side_effects=True),
        name="middle",
    )(att, latents, cot, weights, b_up, vecs, lse)


def finish_kernel(lat_ref, pair_ref, small_ref, vec_ref, query_ref, latn_ref,
                  table_out, igain_out, ibias_out, lgain_out, lbias_out, mgain_out, mbias_out, wq_out, wk_out, wv_out, wo_out, wu_out,
                  bup_out, wd_out, bdown_out, wq_ref, wk_ref, wv_ref, wo_ref, wu_ref, wd_ref, row_ref, sems):
    me = lax.axis_index("heads")
    copies = []

    def store(ref, out):
        copy = pltpu.make_async_copy(ref, out, sems.at[len(copies)])
        copy.start()
        copies.append(copy)

    wo_ref[...] = lat_ref[0].astype(F32)
    store(wo_ref, wo_out)
    wd_ref[...] = lat_ref[2].astype(F32)
    store(wd_ref, wd_out)
    wu_ref[...] = lat_ref[1].astype(F32)
    store(wu_ref, wu_out)
    wk_ref[...] = pair_ref[0].astype(F32)
    store(wk_ref, wk_out)
    wv_ref[...] = pair_ref[1].astype(F32)
    store(wv_ref, wv_out)
    query = query_ref[0].astype(BF16)
    for i in range(0, latn_ref.shape[1], 256):
        wq_ref[:, i:i + 256] = dot(query, latn_ref[:, i:i + 256])
    store(wq_ref, wq_out)
    turned = jnp.transpose(small_ref[0, :, :128])
    table_out[...] = turned[:table_out.shape[0]]
    igain_out[...] = turned[32]
    ibias_out[...] = turned[33]
    lgain_out[...] = vec_ref[0]
    lbias_out[...] = vec_ref[1]
    blocks = row_ref.shape[1] // 128
    for v, out in enumerate((mgain_out, mbias_out, None, bdown_out)):
        for b in range(blocks):
            row_ref[:, b * 128:(b + 1) * 128] = small_ref[0, v * blocks + b:v * blocks + b + 1, 128:]
        if out is not None:
            out[...] = row_ref[0]
        else:
            cols = bup_out.shape[0]
            total = jnp.zeros((1, cols), F32)
            for h in range(row_ref.shape[1] // cols):
                total += jnp.where(me == h, row_ref[:, h * cols:(h + 1) * cols], 0.0)
            bup_out[...] = total[0]
    for copy in copies:
        copy.wait()


def finish_call(lat_total, pair_total, small, vec, query, latn, langs):
    _, cols, width_lat = lat_total.shape
    width = pair_total.shape[2]
    share = small.shape[1]
    whole = pl.BlockSpec(memory_space=pltpu.VMEM)
    hbm = pl.BlockSpec(memory_space=pl.ANY)
    out, vmem = jax.ShapeDtypeStruct, pltpu.VMEM
    big = [(cols, width_lat), (cols, width), (cols, width), (cols, width_lat), (cols, width_lat), (cols, width_lat)]
    return pl.pallas_call(
        finish_kernel,
        in_specs=[whole] * 6,
        out_specs=[whole] * 7 + [hbm] * 5 + [whole, hbm, whole],
        out_shape=[out(shape, F32) for shape in [(langs, share), (share,), (share,)] + [(width_lat,)] * 4 + big[:5] + [(cols,)] + big[5:] + [(width_lat,)]],
        scratch_shapes=[vmem(shape, F32) for shape in big] + [vmem((1, width_lat), F32), pltpu.SemaphoreType.DMA((6,))],
        compiler_params=pltpu.CompilerParams(vmem_limit_bytes=VMEM_LIMIT),
        name="finish",
    )(lat_total, pair_total, small, vec, query, latn)


REST = ("items", "blk")
ALL = ("heads", "items", "blk")


def gather_rows(shard):
    count = lax.axis_size("items") * lax.axis_size("blk")
    me = lax.axis_index("items") * lax.axis_size("blk") + lax.axis_index("blk")
    share = shard.shape[0] // count
    part = lax.dynamic_slice_in_dim(shard, me * share, share, 0)
    return lax.all_gather(part, ALL, axis=0, tiled=True)


def scatter_rows(whole):
    part = lax.psum_scatter(whole.astype(BF16), ALL, scatter_dimension=0, tiled=True)
    return lax.all_gather(part, REST, axis=0, tiled=True)


def general_device(inputs, padding, language, lang_table, latents, in_gain, in_bias, lat_gain, lat_bias, mid_gain, mid_bias,
              w_query, w_key, w_value, w_out, w_up, b_up, w_down, b_down, cotangent):
    length, local_seqs, width = inputs.shape
    local_rows, width_lat = latents.shape
    cols = w_query.shape[1]
    head_dim = width_lat // HEADS
    per_shard = cols // head_dim
    shards = lax.axis_size("heads")
    blocks = lax.axis_size("blk")
    rows = local_rows * blocks
    seqs = local_seqs // shards
    me = lax.axis_index("heads")
    first = me * seqs

    pair_shard = jnp.concatenate([w_key.T, w_value.T], axis=0)
    pair_rows = gather_rows(pair_shard)
    latent_shard = jnp.concatenate([w_out, w_up.T, w_down], axis=0)
    lat_all = gather_rows(latent_shard).reshape(shards, 3, cols, width_lat)
    out_all, up_all, down_all = (lat_all[:, i].reshape(width_lat, width_lat) for i in range(3))

    all_latents = lax.all_gather(latents, "blk", axis=0, tiled=True).astype(F32)
    lat_out, _, _ = norm_keep(all_latents, lat_gain, lat_bias)
    lat_low = lat_out.astype(BF16)
    query_part = dot(lat_low, w_query).astype(BF16)
    queries = lax.all_gather(query_part, "heads", axis=1, tiled=True)
    q = queries.reshape(rows, HEADS, head_dim).transpose(1, 0, 2)

    own = lax.dynamic_slice_in_dim(inputs, first, seqs, 1)
    x_cols = jnp.transpose(own, (1, 2, 0))
    live = jnp.transpose(lax.dynamic_slice_in_dim(padding, first, seqs, 1))
    mask = jnp.where(live > 0, 0.0, MASKED).astype(F32)[:, None, :]
    own_lang = lax.dynamic_slice_in_dim(language, first, seqs, 0)
    onehot = (own_lang[:, None] == jnp.arange(lang_table.shape[0], dtype=jnp.int32)[None, :]).astype(F32)
    emb = jnp.dot(onehot, lang_table.astype(F32), precision=lax.Precision.HIGHEST)[:, :, None]
    gain_col, bias_col = in_gain[:, None], in_bias[:, None]

    pairs, o_cols, lse = forward_call(x_cols, emb, gain_col, bias_col, pair_rows, q, mask, per_shard)

    parts = o_cols.reshape(seqs, width_lat, blocks, local_rows).transpose(2, 0, 3, 1)
    parts = lax.all_to_all(parts, "blk", 0, 0, tiled=True).astype(F32)
    lse_parts = lse.reshape(seqs, HEADS, blocks, local_rows).transpose(2, 0, 3, 1)
    lse_parts = lax.all_to_all(lse_parts, "blk", 0, 0, tiled=True)
    top = jnp.max(lse_parts, axis=0)
    shares = jnp.exp2(lse_parts - top)
    total = jnp.sum(shares, axis=0)
    own_lse = top + jnp.log2(total)
    shares = shares / total
    attended = jnp.sum(parts.reshape(blocks, seqs, local_rows, HEADS, head_dim) * shares[..., None], axis=0)
    att_low = attended.reshape(seqs * local_rows, width_lat).astype(BF16)

    cot = lax.dynamic_slice_in_dim(cotangent, first, seqs, 0).reshape(seqs * local_rows, width_lat)
    lat_f32 = latents.astype(F32)
    middle = (lat_f32[None] + dot(att_low, out_all).reshape(seqs, local_rows, width_lat)).reshape(seqs * local_rows, width_lat)
    mid_out, mid_normed, mid_inverse = norm_keep(middle, mid_gain, mid_bias)
    mid_low = mid_out.astype(BF16)
    b_up_all = lax.all_gather(b_up, "heads", axis=0, tiled=True)
    hidden = dot_nt(mid_low, up_all) + b_up_all
    active, gelu_back = jax.vjp(jax.nn.gelu, hidden)
    active_low = active.astype(BF16)
    own_mixed = (middle + dot(active_low, down_all) + b_down).astype(BF16).reshape(seqs, local_rows, width_lat)
    mixed_latents = lax.all_gather(own_mixed, "heads", axis=0, tiled=True)

    grad_b_down = jnp.sum(cot.astype(F32), axis=0)
    grad_w_down = dot(active_low.T, cot)
    grad_active = dot_nt(cot, down_all)
    grad_hidden = gelu_back(grad_active)[0].astype(BF16)
    grad_b_up = jnp.sum(grad_hidden.astype(F32), axis=0)
    grad_w_up = dot(grad_hidden.T, mid_low)
    grad_mid_norm = dot(grad_hidden, up_all)
    grad_mid_gain = jnp.sum(grad_mid_norm * mid_normed, axis=0)
    grad_mid_bias = jnp.sum(grad_mid_norm, axis=0)
    grad_middle = cot.astype(F32) + norm_back(grad_mid_norm, mid_normed, mid_inverse, mid_gain)
    grad_branch = grad_middle.astype(BF16)
    grad_w_out = dot(att_low.T, grad_branch)
    grad_att = dot_nt(grad_branch, out_all).astype(BF16).reshape(seqs, local_rows, width_lat)
    grad_att_heads = grad_att.reshape(seqs, local_rows, HEADS, head_dim)
    delta = jnp.sum(grad_att_heads.astype(F32) * attended, axis=-1)
    lat_sum = jnp.sum(grad_middle.reshape(seqs, local_rows, width_lat), axis=0)

    all_grad_att = lax.all_gather(grad_att, "blk", axis=1, tiled=True).reshape(seqs, rows, HEADS, head_dim)
    stats = lax.all_gather(jnp.concatenate([own_lse, delta], axis=-1), "blk", axis=1, tiled=True)
    stats = jnp.transpose(stats, (0, 2, 1))[..., None]
    g_cols, dw_pair, dq, dgain, dbias, demb = backward_call(
        x_cols, emb, gain_col, bias_col, pair_rows.T, q, q.transpose(0, 2, 1),
        all_grad_att.transpose(0, 2, 1, 3), all_grad_att.transpose(0, 2, 3, 1),
        stats[:, :HEADS], stats[:, HEADS:], mask, pairs, per_shard)

    send = g_cols.reshape(seqs, shards, width // shards, length).transpose(1, 0, 2, 3)
    got = lax.all_to_all(send, "heads", 0, 0, tiled=True)
    grad_inputs = got.reshape(local_seqs, width // shards, length).transpose(2, 0, 1)

    grad_rows = jnp.stack([grad_w_out, grad_w_up, grad_w_down], axis=0).reshape(3, shards, cols, width_lat)
    lat_total = scatter_rows(grad_rows.transpose(1, 0, 2, 3).reshape(-1, width_lat)).astype(F32)
    pair_total = scatter_rows(dw_pair).astype(F32)

    dq_part = lax.psum_scatter(dq.reshape(width_lat, rows).astype(BF16), "heads", scatter_dimension=0, tiled=True)
    query_low = lax.psum(dq_part, REST)
    grad_w_query = dot(lat_low.T, query_low.T)
    lat_mine = lax.dynamic_slice_in_dim(query_low, lax.axis_index("blk") * local_rows, local_rows, 1)
    grad_lat_part = dot(lat_mine.T, w_query.T)
    grad_lat_norm = lax.psum(grad_lat_part.astype(BF16), "heads").astype(F32)
    lat_sum = lax.psum(lat_sum.astype(BF16), ("heads", "items")).astype(F32)
    _, own_normed, own_inverse = norm_keep(lat_f32, lat_gain, lat_bias)
    grad_latents = lat_sum + norm_back(grad_lat_norm, own_normed, own_inverse, lat_gain)
    lat_small = jnp.concatenate([jnp.sum(grad_lat_norm * own_normed, axis=0), jnp.sum(grad_lat_norm, axis=0)])
    lat_small = lax.psum(lat_small, "blk")

    table = jnp.dot(onehot.T, demb[:, :, 0], precision=lax.Precision.HIGHEST)
    small = jnp.concatenate([table.reshape(-1), dgain[:, 0], dbias[:, 0], grad_mid_gain, grad_mid_bias, grad_b_up, grad_b_down])
    small = lax.psum(small, ALL)
    sizes = [table.size, width, width, width_lat, width_lat, width_lat, width_lat]
    ends = [sum(sizes[:i]) for i in range(len(sizes) + 1)]
    table, dgain, dbias, dmid_gain, dmid_bias, db_up, db_down = (small[ends[i]:ends[i + 1]] for i in range(7))
    share = width // shards
    table = lax.dynamic_slice_in_dim(table.reshape(-1, width), me * share, share, 1)
    return (
        mixed_latents,
        grad_inputs,
        grad_latents,
        table,
        lax.dynamic_slice_in_dim(dgain, me * share, share, 0),
        lax.dynamic_slice_in_dim(dbias, me * share, share, 0),
        lat_small[:width_lat],
        lat_small[width_lat:],
        dmid_gain,
        dmid_bias,
        grad_w_query,
        pair_total[:cols].T,
        pair_total[cols:].T,
        lat_total[:cols],
        lat_total[cols:2 * cols].T,
        lax.dynamic_slice_in_dim(db_up, me * cols, cols, 0),
        lat_total[2 * cols:],
        db_down,
    )


def fast_device(inputs, padding, language, lang_table, latents, in_gain, in_bias, lat_gain, lat_bias, mid_gain, mid_bias,
              w_query, w_key, w_value, w_out, w_up, b_up, w_down, b_down, cotangent):
    length, local_seqs, width = inputs.shape
    local_rows, width_lat = latents.shape
    cols = w_query.shape[1]
    head_dim = width_lat // HEADS
    per_shard = cols // head_dim
    shards = lax.axis_size("heads")
    blocks = lax.axis_size("blk")
    rows = local_rows * blocks
    seqs = local_seqs // shards
    me = lax.axis_index("heads")
    first = me * seqs

    vectors = (lat_gain, lat_bias, mid_gain, mid_bias, b_down, in_gain, in_bias, b_up)
    wq_rows = w_query.T
    w_cols, lat_all, pairs, xn, att_cols, lse_cols, queries_t, lat_low, b_up_tiles, x_cols, rows_in, mask, lang_rows, lat_f32, vecs = first_call(
        inputs, padding.T, language, lang_table, vectors, latents, wq_rows,
        (w_key.T, w_value.T, w_out, w_up.T, w_down), rows, seqs)
    mixed, grad_att, stats, grads, vectors, lat_sum = middle_call(att_cols, latents, cotangent, lat_all, b_up_tiles, vecs, lse_cols)
    grad_att = grad_att.reshape(seqs, shards, cols, local_rows)
    g_cols, mixed_latents, pair_total, lat_total, small, grad_latents, lat_small, dq, lat_low_all = second_call(
        x_cols, rows_in, mask, w_cols, queries_t, pairs, xn, grad_att, stats, mixed, lat_low, grads, vectors, lang_rows, lat_sum,
        wq_rows, lat_f32, vecs)
    grad_inputs = g_cols.transpose(2, 0, 1)
    rest = finish_call(lat_total, pair_total, small, lat_small, dq, lat_low_all, lang_table.shape[0])
    rest = [x.T if i in (7, 8, 9, 11) else x for i, x in enumerate(rest)]
    return (mixed_latents, grad_inputs, grad_latents) + tuple(rest)


def solution(mesh):
    placed = (
        P("blk", "items", None), P("blk", "items"), P("items"), P(), P("blk", None), P(), P(), P(), P(), P(), P(),
        P(None, "heads"), P(None, "heads"), P(None, "heads"), P("heads", None), P(None, "heads"), P("heads"),
        P("heads", None), P(), P("items", "blk", None),
    )
    out = (
        P("items", "blk", None), P("blk", "items", "heads"), P("blk", None), P(None, "heads"), P("heads"), P("heads"),
        P(), P(), P(), P(), P(None, "heads"), P(None, "heads"), P(None, "heads"), P("heads", None), P(None, "heads"),
        P("heads"), P("heads", None), P(),
    )
    fits = mesh.shape["blk"] == 2 and mesh.shape["items"] == 4 and mesh.shape["heads"] == 4
    return jax.shard_map(fast_device if fits else general_device, mesh=mesh, in_specs=placed, out_specs=out, check_vma=False)
```

```python
import functools

import jax
import jax.numpy as jnp
from jax import lax
from jax.experimental import pallas as pl
from jax.experimental.pallas import tpu as pltpu
from jax.sharding import PartitionSpec as P

HEADS = 8
EPS = 1e-05
MASKED = -1e30
LOG2E = 1.4426950408889634
F32 = jnp.float32
BF16 = jnp.bfloat16
NT = (((1,), (1,)), ((), ()))
VMEM_LIMIT = 60 * 1024 * 1024


def dot(a, b):
    return jnp.dot(a, b, preferred_element_type=F32)


def dot_nt(a, b):
    return lax.dot_general(a, b, NT, preferred_element_type=F32)


def norm_keep(values, gain, bias):
    average = jnp.mean(values, axis=-1, keepdims=True)
    centred = values - average
    inverse = lax.rsqrt(jnp.mean(centred * centred, axis=-1, keepdims=True) + EPS)
    normed = centred * inverse
    return (normed * gain + bias, normed, inverse)


def norm_back(grad_norm, normed, inverse, gain):
    scaled = grad_norm * gain
    first = jnp.mean(scaled, axis=-1, keepdims=True)
    second = jnp.mean(scaled * normed, axis=-1, keepdims=True)
    return (scaled - first - normed * second) * inverse


def norm_columns(x, emb):
    shifted = x.astype(F32) + emb
    centred = shifted - jnp.mean(shifted, axis=0, keepdims=True)
    inverse = lax.rsqrt(jnp.mean(centred * centred, axis=0, keepdims=True) + EPS)
    return centred * inverse, inverse


def head_rows(h, per_shard, head_dim):
    key = (h // per_shard) * 2 * per_shard + lax.rem(h, per_shard)
    key_at = pl.multiple_of(key * head_dim, head_dim)
    return pl.ds(key_at, head_dim), pl.ds(pl.multiple_of(key_at + per_shard * head_dim, head_dim), head_dim)


def forward_kernel(per_shard, x_ref, emb_ref, gain_ref, bias_ref, w_ref, q_ref, mask_ref, kv_ref, o_ref, lse_ref, xn_ref, stat_ref):
    heads, rows, head_dim = q_ref.shape
    length = x_ref.shape[1]
    piece = min(256, length)

    def norm_step(i, _):
        at = pl.ds(pl.multiple_of(i * piece, piece), piece)
        normed, _unused = norm_columns(x_ref[:, at], emb_ref[...])
        xn_ref[:, at] = (normed * gain_ref[...] + bias_ref[...]).astype(BF16)
        return 0

    lax.fori_loop(0, length // piece, norm_step, 0)
    block = 512 if w_ref.shape[0] % 512 == 0 else 160

    def pair_step(i, _):
        at = pl.ds(pl.multiple_of(i * block, block), block)
        kv_ref[at] = dot(w_ref[at], xn_ref[...]).astype(BF16)
        return 0

    lax.fori_loop(0, w_ref.shape[0] // block, pair_step, 0)
    factor = LOG2E * head_dim ** (-0.5)
    lane = lax.broadcasted_iota(jnp.int32, (rows, 128), 1)
    stat_ref[...] = jnp.zeros_like(stat_ref)

    def head_step(h, _):
        at_key, at_value = head_rows(h, per_shard, head_dim)
        scores = dot(q_ref[h], kv_ref[at_key]) * factor + mask_ref[...]
        top = jnp.max(scores, axis=1, keepdims=True)
        weights = jnp.exp2(scores - top)
        total = jnp.sum(weights, axis=1, keepdims=True)
        out = dot_nt(kv_ref[at_value], weights.astype(BF16))
        stat_ref[...] = jnp.where(lane == h, top + jnp.log2(total), stat_ref[...])
        inverse = jnp.transpose(jnp.broadcast_to(1.0 / total, (rows, 128)))[:1]
        o_ref[pl.ds(pl.multiple_of(h * head_dim, head_dim), head_dim)] = (out * inverse).astype(BF16)
        return 0

    lax.fori_loop(0, heads, head_step, 0)
    lse_ref[...] = jnp.transpose(stat_ref[...])[:heads]


def forward_call(x_cols, emb, gain, bias, w_rows, q, mask, per_shard):
    seqs, width, length = x_cols.shape
    heads, rows, head_dim = q.shape
    pair_rows = w_rows.shape[0]
    whole = pl.BlockSpec(memory_space=pltpu.VMEM)

    def per_seq(*dims):
        return pl.BlockSpec((None,) + dims, lambda s: (s, 0, 0))

    return pl.pallas_call(
        functools.partial(forward_kernel, per_shard),
        grid=(seqs,),
        in_specs=[per_seq(width, length), per_seq(width, 1), whole, whole, whole, whole, per_seq(1, length)],
        out_specs=[per_seq(pair_rows, length), per_seq(heads * head_dim, rows), per_seq(heads, rows)],
        out_shape=[
            jax.ShapeDtypeStruct((seqs, pair_rows, length), BF16),
            jax.ShapeDtypeStruct((seqs, heads * head_dim, rows), BF16),
            jax.ShapeDtypeStruct((seqs, heads, rows), F32),
        ],
        scratch_shapes=[pltpu.VMEM((width, length), BF16), pltpu.VMEM((rows, 128), F32)],
        compiler_params=pltpu.CompilerParams(vmem_limit_bytes=VMEM_LIMIT),
        name="attend",
    )(x_cols, emb, gain, bias, w_rows, q, mask)


def backward_kernel(per_shard, x_ref, emb_ref, gain_ref, bias_ref, w_ref, q_ref, qt_ref, do_ref, dot_ref, lse_ref, delta_ref, mask_ref, kv_ref,
                    g_ref, dw_ref, dq_ref, dgain_ref, dbias_ref, demb_ref, xn_ref, dkv_ref):
    heads, rows, head_dim = q_ref.shape
    width, length = x_ref.shape
    piece = min(256, length)

    @pl.when(pl.program_id(0) == 0)
    def _():
        dw_ref[...] = jnp.zeros_like(dw_ref)
        dq_ref[...] = jnp.zeros_like(dq_ref)
        dgain_ref[...] = jnp.zeros_like(dgain_ref)
        dbias_ref[...] = jnp.zeros_like(dbias_ref)

    def norm_step(i, _):
        at = pl.ds(pl.multiple_of(i * piece, piece), piece)
        normed, _unused = norm_columns(x_ref[:, at], emb_ref[...])
        xn_ref[:, at] = (normed * gain_ref[...] + bias_ref[...]).astype(BF16)
        return 0

    lax.fori_loop(0, length // piece, norm_step, 0)
    scale = head_dim ** (-0.5)
    factor = LOG2E * scale

    def head_step(h, _):
        at_key, at_value = head_rows(h, per_shard, head_dim)
        keys = kv_ref[at_key]
        weights = jnp.exp2(dot(q_ref[h], keys) * factor + mask_ref[...] - lse_ref[h])
        dkv_ref[at_value] = dot(dot_ref[h], weights.astype(BF16)).astype(BF16)
        grad = dot(do_ref[h], kv_ref[at_value]) - delta_ref[h]
        grad = (weights * grad).astype(BF16)
        dkv_ref[at_key] = (dot(qt_ref[h], grad) * scale).astype(BF16)
        dq_ref[h] += dot_nt(keys, grad) * scale
        return 0

    lax.fori_loop(0, heads, head_step, 0)
    block = 512 if dw_ref.shape[0] % 512 == 0 else 160

    def weight_step(i, _):
        at = pl.ds(pl.multiple_of(i * block, block), block)
        dw_ref[at] += dot_nt(dkv_ref[at], xn_ref[...])
        return 0

    lax.fori_loop(0, dw_ref.shape[0] // block, weight_step, 0)

    def byte_step(i, carry):
        at = pl.ds(pl.multiple_of(i * piece, piece), piece)
        grad = dot(w_ref[...], dkv_ref[:, at])
        normed, inverse = norm_columns(x_ref[:, at], emb_ref[...])
        dbias_ref[...] += jnp.sum(grad, axis=1, keepdims=True)
        dgain_ref[...] += jnp.sum(grad * normed, axis=1, keepdims=True)
        scaled = grad * gain_ref[...]
        first = jnp.mean(scaled, axis=0, keepdims=True)
        second = jnp.mean(scaled * normed, axis=0, keepdims=True)
        shifted = (scaled - first - normed * second) * inverse
        g_ref[:, at] = shifted.astype(BF16)
        return carry + jnp.sum(shifted, axis=1, keepdims=True)

    demb_ref[...] = lax.fori_loop(0, length // piece, byte_step, jnp.zeros((width, 1), F32))


def backward_call(x_cols, emb, gain, bias, w, q, qt, grad_out, grad_out_t, lse, delta, mask, pairs, per_shard):
    seqs, width, length = x_cols.shape
    heads, rows, head_dim = q.shape
    pair_rows = w.shape[1]
    whole = pl.BlockSpec(memory_space=pltpu.VMEM)

    def per_seq(*dims):
        return pl.BlockSpec((None,) + dims, lambda s: (s,) + (0,) * len(dims))

    return pl.pallas_call(
        functools.partial(backward_kernel, per_shard),
        grid=(seqs,),
        in_specs=[
            per_seq(width, length), per_seq(width, 1), whole, whole, whole, whole, whole,
            per_seq(heads, rows, head_dim), per_seq(heads, head_dim, rows),
            per_seq(heads, rows, 1), per_seq(heads, rows, 1), per_seq(1, length), per_seq(pair_rows, length),
        ],
        out_specs=[per_seq(width, length), whole, whole, whole, whole, per_seq(width, 1)],
        out_shape=[
            jax.ShapeDtypeStruct((seqs, width, length), BF16),
            jax.ShapeDtypeStruct((pair_rows, width), F32),
            jax.ShapeDtypeStruct((heads, head_dim, rows), F32),
            jax.ShapeDtypeStruct((width, 1), F32),
            jax.ShapeDtypeStruct((width, 1), F32),
            jax.ShapeDtypeStruct((seqs, width, 1), F32),
        ],
        scratch_shapes=[pltpu.VMEM((width, length), BF16), pltpu.VMEM((pair_rows, length), BF16)],
        compiler_params=pltpu.CompilerParams(vmem_limit_bytes=VMEM_LIMIT),
        name="attend_back",
    )(x_cols, emb, gain, bias, w, q, qt, grad_out, grad_out_t, lse, delta, mask, pairs)


def mesh_at(di=None, db=None, dh=None, core=None):
    items, blk, heads = lax.axis_index("items"), lax.axis_index("blk"), lax.axis_index("heads")
    return (items if di is None else di, blk if db is None else db, heads if dh is None else dh)


def places():
    items, blk, heads = lax.axis_index("items"), lax.axis_index("blk"), lax.axis_index("heads")
    core = lax.rem(items, 2)
    return items, blk, heads, items // 2, core


def send(src, dst, sems, recvs, target):
    copy = pltpu.make_async_remote_copy(
        src_ref=src, dst_ref=dst, send_sem=sems, recv_sem=recvs, device_id=target, device_id_type=pl.DeviceIdType.MESH)
    copy.start()
    return copy


def greet(targets):
    barrier = pltpu.get_barrier_semaphore()
    for target in targets:
        pl.semaphore_signal(barrier, inc=1, device_id=target, device_id_type=pl.DeviceIdType.MESH)
    pl.semaphore_wait(barrier, len(targets))


def first_kernel(x_hbm, pad_ref, lang_ref, table_ref, lgain, lbias, mgain, mbias, bdown, igain, ibias, bup, lat_ref, wq_ref, wk_hbm, wv_hbm, wo_hbm, wu_hbm, wd_hbm,
                 wcols_out, all_ref, kv_out, xn_out, att_ref, lse_ref, qt_ref, latn_ref, bup_all, x_out, rows_ref, mask_ref, lang_out, latf_ref, vecs_ref,
                 wcols_ref, pair_shard, lat_shard, x_ref, xbuf, x32, xn_ref, pair_ref, kv_ref, cols_ref, q_ref, o_tmp, o_own, o_send, o_got, stat_ref, stat_send, stat_own, stat_got,
                 pair_ss, pair_rs, lat_ss, lat_rs, q_ss, q_rs, misc_ss, misc_rs, o_ss, o_rs, own_sem, xn_sem, kv_sem, x_sem, w_sem):
    items, blk, me, hi, core = places()
    shards = lax.axis_size("heads")
    seqs, width, length = x_ref.shape
    rows = qt_ref.shape[3]
    local_rows = rows // 2
    heads, _, head_dim = q_ref.shape
    cols = heads * head_dim // shards
    per_shard = heads // shards
    sibling = items + 1 - 2 * core
    other = 1 - blk
    to_sib, to_x, to_y = mesh_at(di=sibling), mesh_at(db=other), mesh_at(di=(1 - hi) * 2 + core)
    z_of = [lax.rem(me + d, shards) for d in range(shards)]
    z_back = [lax.rem(me + shards - d, shards) for d in range(shards)]
    weights = [pltpu.make_async_copy(src, dst, w_sem.at[n]) for n, (src, dst) in enumerate((
        (wk_hbm, pair_shard.at[0]), (wv_hbm, pair_shard.at[1]), (wo_hbm, lat_shard.at[0]), (wu_hbm, lat_shard.at[1]), (wd_hbm, lat_shard.at[2])))]
    for copy in weights:
        copy.start()
    greet([to_sib, to_x, to_y] + [mesh_at(dh=z_of[d]) for d in range(1, shards)])

    share = cols // 4
    chip = hi * 2 + blk
    chip_x, chip_y, chip_xy = hi * 2 + other, (1 - hi) * 2 + blk, (1 - hi) * 2 + other

    def region(ref, shard, chip_at, lanes_of):
        half = ref.shape[2] // 2
        return ref.at[:, pl.ds(pl.multiple_of(shard * cols + chip_at * share, 16), share), pl.ds(pl.multiple_of(lanes_of * half, 128), half)]

    def lane_half(ref, shard, lanes_of):
        half = ref.shape[2] // 2
        return ref.at[:, pl.ds(pl.multiple_of(shard * cols, 16), cols), pl.ds(pl.multiple_of(lanes_of * half, 128), half)]

    pending = []
    local = []
    near = me + 1 - 2 * lax.rem(me, 2)
    far, cross = lax.rem(me + 2, 4), lax.rem(near + 2, 4)
    shard_at = [me, near, far, cross]
    double = {"l1": (0, blk, to_x), "l2": (1, hi, to_y)}

    def band(ref, shard, part):
        half = ref.shape[2] // 2
        at = pl.ds(pl.multiple_of(shard * cols + part * 2 * share, 16), 2 * share)
        return ref.at[:, at, pl.ds(pl.multiple_of(core * half, 128), half)]

    kinds = {"pair": (pair_shard, pair_ref, pair_ss, pair_rs)}
    for m in range(3):
        one = pl.ds(m, 1)
        kinds[f"l{m}"] = (lat_shard.at[one], all_ref.at[one], lat_ss.at[m], lat_rs.at[m])

    def recv(kind, d, stage, where):
        _, dst, ss, rs = kinds[kind]
        pltpu.make_async_remote_copy(src_ref=where, dst_ref=where, send_sem=ss.at[d, stage], recv_sem=rs.at[d, stage],
                                     device_id=to_sib, device_id_type=pl.DeviceIdType.MESH).wait_recv()

    def out_z(kind, d):
        src, dst, ss, rs = kinds[kind]
        def own_part(ref, shard):
            return band(ref, shard, double[kind][1]) if kind in double else region(ref, shard, chip, core)

        if d == 3:
            block = own_part(dst, far)
            pending.append(send(block, block, ss.at[d, 0], rs.at[d, 0], mesh_at(dh=near)))
        else:
            pending.append(send(own_part(src, 0), own_part(dst, me), ss.at[d, 0], rs.at[d, 0], mesh_at(dh=shard_at[d])))

    def after_z(kind, d):
        _, dst, ss, rs = kinds[kind]
        if kind in double:
            mine = band(dst, shard_at[d], double[kind][1])
            recv(kind, d, 0, mine)
            pending.append(send(mine, mine, ss.at[d, 1], rs.at[d, 1], double[kind][2]))
            return
        mine = region(dst, shard_at[d], chip, core)
        recv(kind, d, 0, mine)
        pending.append(send(mine, mine, ss.at[d, 1], rs.at[d, 1], to_x))
        pending.append(send(mine, mine, ss.at[d, 2], rs.at[d, 2], to_y))

    def after_x(kind, d):
        _, dst, ss, rs = kinds[kind]
        got = region(dst, shard_at[d], chip_x, core)
        recv(kind, d, 1, got)
        pending.append(send(got, got, ss.at[d, 3], rs.at[d, 3], to_y))

    def after_y(kind, d):
        _, dst, ss, rs = kinds[kind]
        if kind in double:
            recv(kind, d, 1, band(dst, shard_at[d], 1 - double[kind][1]))
        else:
            recv(kind, d, 2, region(dst, shard_at[d], chip_y, core))
            recv(kind, d, 3, region(dst, shard_at[d], chip_xy, core))
        half = lane_half(dst, shard_at[d], core)
        pending.append(send(half, half, ss.at[d, 4], rs.at[d, 4], to_sib))

    def after_sib(kind, d):
        _, dst, ss, rs = kinds[kind]
        recv(kind, d, 4, lane_half(dst, shard_at[d], 1 - core))

    for copy in weights:
        copy.wait()
    own_pair = pltpu.make_async_copy(pair_shard, pair_ref.at[:, pl.ds(pl.multiple_of(me * cols, 16), cols)], own_sem.at[0])
    own_lat = pltpu.make_async_copy(lat_shard, all_ref.at[:, pl.ds(pl.multiple_of(me * cols, 16), cols)], own_sem.at[1])
    own_pair.start()
    own_lat.start()
    my_rows = pl.ds(pl.multiple_of(blk * local_rows, 128), local_rows)
    other_rows = pl.ds(pl.multiple_of(other * local_rows, 128), local_rows)

    vecs_ref[...] = jnp.zeros_like(vecs_ref)
    for i, vector in enumerate((lgain, lbias, mgain, mbias, bdown, igain, ibias, bup)):
        vecs_ref[i:i + 1, :vector.shape[0]] = vector[...].reshape(1, vector.shape[0])
    rows_ref[0:1] = vecs_ref[5:6, :width]
    rows_ref[1:2] = vecs_ref[6:7, :width]
    rows_ref[4:8] = jnp.zeros((4, width), F32)
    lang_out[...] = jnp.zeros_like(lang_out)
    for s in range(seqs):
        lang = lang_ref[me * seqs + s]
        picked = lax.broadcasted_iota(jnp.int32, table_ref.shape, 0) == lang
        rows_ref[2 + s:3 + s] = jnp.sum(jnp.where(picked, table_ref[...].astype(F32), 0.0), axis=0, keepdims=True)
        lang_out[s:s + 1] = jnp.where(lax.broadcasted_iota(jnp.int32, (1, 128), 1) == lang, 1.0, 0.0)
        mask_ref[s] = jnp.where(pad_ref[pl.ds(me * seqs + s, 1)] > 0, 0.0, MASKED)

    def queries_start():
        latf_ref[...] = lat_ref[...].astype(F32)
        lat_out, _, _ = norm_keep(latf_ref[...], vecs_ref[0:1], vecs_ref[1:2])
        lat_low = lat_out.astype(BF16)
        latn_ref[...] = lat_low
        at_head = pl.ds(pl.multiple_of(core * head_dim, 16), head_dim)
        qt_ref[core, me, :, my_rows] = dot_nt(wq_ref[at_head], lat_low).astype(BF16)
        bup_ref = vecs_ref.at[:, pl.ds(0, bup_all.shape[2])]
        bup_all[me] = bup_ref[...]
        for d in range(1, shards):
            my_q = qt_ref.at[core, me, :, my_rows]
            pending.append(send(my_q, my_q, q_ss.at[0, d], q_rs.at[0, d], mesh_at(dh=z_back[d])))
        for d in range(1, shards):
            pending.append(send(bup_ref, bup_all.at[me], misc_ss.at[d], misc_rs.at[d], mesh_at(dh=z_back[d])))

    cols_ref[...] = jnp.transpose(rows_ref[...])
    step_rows = xbuf.shape[1]

    def load_bytes(c):
        return pltpu.make_async_copy(x_hbm.at[pl.ds(c * step_rows, step_rows)], xbuf.at[c % 2], x_sem.at[c % 2])

    load_bytes(0).start()

    def pick_bytes(c):
        load_bytes(c).wait()
        if (c + 1) * step_rows < length:
            load_bytes(c + 1).start()
        at = slice(c * step_rows, (c + 1) * step_rows)
        for j in range(x32.shape[0]):
            lanes = slice(j * 128, (j + 1) * 128)
            x32[j] = xbuf[c % 2, :, :, lanes].astype(F32).reshape(x32.shape[1:])
            for s in range(seqs):
                x_ref[s, lanes, at] = jnp.transpose(x32[j, pl.ds(me * seqs + s, step_rows, stride=x_hbm.shape[1])]).astype(BF16)
        if (c + 1) * step_rows == length:
            copy = pltpu.make_async_copy(x_ref, x_out, x_sem.at[2])
            copy.start()
            local.append(copy)


    def queries_z():
        for d in range(1, shards):
            wait_plain(qt_ref.at[core, z_of[d], :, my_rows], q_ss.at[0, d], q_rs.at[0, d])
        part = qt_ref.at[core, :, :, my_rows]
        pending.append(send(part, part, q_ss.at[1, 0], q_rs.at[1, 0], to_x))

    def queries_x():
        wait_plain(qt_ref.at[core, :, :, other_rows], q_ss.at[1, 0], q_rs.at[1, 0])
        pending.append(send(qt_ref.at[core], qt_ref.at[core], q_ss.at[1, 1], q_rs.at[1, 1], to_sib))

    def queries_sib():
        wait_plain(qt_ref.at[1 - core], q_ss.at[1, 1], q_rs.at[1, 1])

    def wait_plain(where, ss, rs):
        pltpu.make_async_remote_copy(src_ref=where, dst_ref=where, send_sem=ss, recv_sem=rs,
                                     device_id=to_sib, device_id_type=pl.DeviceIdType.MESH).wait_recv()

    piece = min(256, length)

    def norm_bytes(s):
        def norm_step(i, _):
            at = pl.ds(pl.multiple_of(i * piece, piece), piece)
            normed, _unused = norm_columns(x_ref[s, :, at], cols_ref[:, 2 + s:3 + s])
            xn_ref[s, :, at] = (normed * cols_ref[:, 0:1] + cols_ref[:, 1:2]).astype(BF16)
            return 0
        lax.fori_loop(0, length // piece, norm_step, 0)
        copy = pltpu.make_async_copy(xn_ref.at[s], xn_out.at[s], xn_sem.at[s])
        copy.start()
        local.append(copy)

    def project(d):
        at = pl.ds(pl.multiple_of(shard_at[d] * cols, 16), cols)

        def step(i, _):
            s, part = i // 2, lax.rem(i, 2)
            kv_ref[s, part, at] = dot(pair_ref[part, at], xn_ref[s]).astype(BF16)
            return 0
        lax.fori_loop(0, 2 * seqs, step, 0)
        copy = pltpu.make_async_copy(kv_ref.at[:, :, at], kv_out.at[:, :, at], kv_sem.at[d])
        copy.start()
        local.append(copy)

    factor = LOG2E * head_dim ** (-0.5)
    lane = lax.broadcasted_iota(jnp.int32, (rows, 128), 1)
    stat_ref[...] = jnp.zeros_like(stat_ref)

    def turn_queries(d):
        for j in range(per_shard):
            h = shard_at[d] * per_shard + j
            q_ref[h] = jnp.transpose(qt_ref[j, shard_at[d]])

    def attend(d, s):
        def head_step(j, _):
            h = shard_at[d] * per_shard + j
            at = pl.ds(pl.multiple_of(h * head_dim, 16), head_dim)
            scores = dot(q_ref[h], kv_ref[s, 0, at]) * factor + mask_ref[s]
            top = jnp.max(scores, axis=1, keepdims=True)
            weights = jnp.exp2(scores - top)
            total = jnp.sum(weights, axis=1, keepdims=True)
            out = dot_nt(kv_ref[s, 1, at], weights.astype(BF16))
            stat_ref[s] = jnp.where(lane == h, top + jnp.log2(total), stat_ref[s])
            inverse = jnp.transpose(jnp.broadcast_to(1.0 / total, (rows, 128)))[:1]
            o_tmp[...] = out * inverse
            o_own[s, at] = o_tmp[:, my_rows]
            o_send[s, at] = o_tmp[:, other_rows].astype(BF16)
            return 0
        lax.fori_loop(0, per_shard, head_step, 0)
        part = pl.ds(pl.multiple_of(shard_at[d] * cols, 16), cols)
        pending.append(send(o_send.at[s, part], o_got.at[s, part], o_ss.at[d, s], o_rs.at[d, s], to_x))

    def stats_send():
        for s in range(seqs):
            at = pl.ds(s * heads, heads)
            stats = jnp.transpose(stat_ref[s])[:heads]
            stat_send[...] = stats
            stat_own[at] = stat_send[:, my_rows]
            stat_got[0, at] = stat_send[:, other_rows]
        pending.append(send(stat_got.at[0], stat_got.at[1], o_ss.at[shards, 0], o_rs.at[shards, 0], to_x))

    def turn_weights():
        block = 256
        for part in range(2):
            for i in range(pair_ref.shape[1] // block):
                wcols_ref[part, :, i * block:(i + 1) * block] = jnp.transpose(pair_ref[part, i * block:(i + 1) * block])
        copy = pltpu.make_async_copy(wcols_ref, wcols_out, w_sem.at[5])
        copy.start()
        local.append(copy)

    out_z("pair", 1)
    out_z("pair", 2)
    out_z("l0", 1)
    pick_bytes(0)
    pick_bytes(1)
    pick_bytes(2)
    pick_bytes(3)
    pick_bytes(4)
    pick_bytes(5)
    pick_bytes(6)
    after_z("l0", 1)
    out_z("l0", 2)
    pick_bytes(7)
    after_z("pair", 1)
    after_z("pair", 2)
    out_z("pair", 3)
    norm_bytes(0)
    norm_bytes(1)
    out_z("l1", 1)
    queries_start()
    after_x("l0", 1)
    own_pair.wait()
    project(0)
    after_z("pair", 3)
    after_z("l0", 2)
    out_z("l0", 3)
    out_z("l1", 2)
    after_x("pair", 1)
    after_x("pair", 2)
    queries_z()
    after_x("l0", 2)
    after_y("l0", 1)
    after_x("pair", 3)
    after_sib("l0", 1)
    after_z("l0", 3)
    out_z("l2", 1)
    queries_x()
    after_z("l1", 1)
    out_z("l2", 2)
    queries_sib()
    turn_queries(0)
    attend(0, 0)
    after_x("l0", 3)
    after_z("l1", 2)
    out_z("l1", 3)
    attend(0, 1)
    after_y("pair", 1)
    after_y("pair", 2)
    after_y("l0", 2)
    after_y("l1", 1)
    after_y("pair", 3)
    after_sib("pair", 1)
    after_sib("pair", 2)
    project(1)
    after_y("l0", 3)
    after_sib("l0", 2)
    after_z("l2", 1)
    after_sib("l1", 1)
    project(2)
    after_sib("pair", 3)
    after_y("l1", 2)
    after_z("l1", 3)
    after_z("l2", 2)
    out_z("l2", 3)
    project(3)
    after_sib("l0", 3)
    turn_queries(1)
    attend(1, 0)
    after_sib("l1", 2)
    attend(1, 1)
    after_y("l2", 1)
    turn_queries(2)
    attend(2, 0)
    after_y("l1", 3)
    after_z("l2", 3)
    attend(2, 1)
    after_y("l2", 2)
    turn_queries(3)
    attend(3, 0)
    attend(3, 1)
    after_sib("l1", 3)
    after_sib("l2", 1)
    after_sib("l2", 2)
    stats_send()
    turn_weights()
    after_y("l2", 3)
    after_sib("l2", 3)

    wait_plain(stat_got.at[1], o_ss.at[shards, 0], o_rs.at[shards, 0])
    own_lse, got_lse = stat_own[...], stat_got[1]
    top = jnp.maximum(own_lse, got_lse)
    own_share, got_share = jnp.exp2(own_lse - top), jnp.exp2(got_lse - top)
    total = own_share + got_share
    lse = top + jnp.log2(total)
    own_share, got_share = own_share / total, got_share / total
    for s in range(seqs):
        lse_ref[s] = lse[s * heads:(s + 1) * heads]
        for d in range(shards):
            part = pl.ds(pl.multiple_of(shard_at[d] * cols, 16), cols)
            wait_plain(o_got.at[s, part], o_ss.at[d, s], o_rs.at[d, s])
    for s in range(seqs):
        for h in range(heads):
            at = slice(h * head_dim, (h + 1) * head_dim)
            n = s * heads + h
            att_ref[s, at] = o_own[s, at] * own_share[n:n + 1] + o_got[s, at].astype(F32) * got_share[n:n + 1]
    for d in range(1, shards):
        wait_plain(bup_all.at[z_of[d]], misc_ss.at[d], misc_rs.at[d])
    own_lat.wait()
    for copy in local:
        copy.wait()
    for copy in pending:
        copy.wait_send()


def first_call(inputs, padding, language, table, vectors, latents, wq_rows, weights, rows, seqs):
    length, local_seqs, width = inputs.shape
    local_rows, width_lat = latents.shape
    shards = lax.axis_size("heads")
    heads = HEADS
    head_dim = width_lat // heads
    whole = pl.BlockSpec(memory_space=pltpu.VMEM)
    hbm = pl.BlockSpec(memory_space=pl.ANY)
    out = jax.ShapeDtypeStruct
    sem = pltpu.SemaphoreType.DMA
    return pl.pallas_call(
        first_kernel,
        in_specs=[hbm, whole, pl.BlockSpec(memory_space=pltpu.SMEM)] + [whole] * 11 + [hbm] * 5,
        out_specs=[hbm, hbm, hbm, hbm] + [whole] * 5 + [hbm] + [whole] * 5,
        out_shape=[
            out((2, width, width_lat), BF16),
            out((3, width_lat, width_lat), BF16),
            out((seqs, 2, width_lat, length), BF16),
            out((seqs, width, length), BF16),
            out((seqs, width_lat, local_rows), F32),
            out((seqs, heads, local_rows), F32),
            out((heads // shards, shards, head_dim, rows), BF16),
            out((local_rows, width_lat), BF16),
            out((shards, 8, 384), F32),
            out((seqs, width, length), BF16),
            out((8, width), F32),
            out((seqs, 1, length), F32),
            out((8, 128), F32),
            out((local_rows, width_lat), F32),
            out((8, width_lat), F32),
        ],
        scratch_shapes=[
            pltpu.VMEM((2, width, width_lat), BF16),
            pltpu.VMEM((2, width_lat // shards, width), BF16),
            pltpu.VMEM((3, width_lat // shards, width_lat), BF16),
            pltpu.VMEM((seqs, width, length), BF16),
            pltpu.VMEM((2, 128, local_seqs, width), BF16),
            pltpu.VMEM((width // 128, 128 * local_seqs, 128), F32),
            pltpu.VMEM((seqs, width, length), BF16),
            pltpu.VMEM((2, width_lat, width), BF16),
            pltpu.VMEM((seqs, 2, width_lat, length), BF16),
            pltpu.VMEM((width, 8), F32),
            pltpu.VMEM((heads, rows, head_dim), BF16),
            pltpu.VMEM((head_dim, rows), F32),
            pltpu.VMEM((seqs, width_lat, local_rows), F32),
            pltpu.VMEM((seqs, width_lat, local_rows), BF16),
            pltpu.VMEM((seqs, width_lat, local_rows), BF16),
            pltpu.VMEM((seqs, rows, 128), F32),
            pltpu.VMEM((heads, rows), F32),
            pltpu.VMEM((seqs * heads, local_rows), F32),
            pltpu.VMEM((2, seqs * heads, local_rows), F32),
            sem((shards, 5)), sem((shards, 5)), sem((3, shards, 5)), sem((3, shards, 5)),
            sem((2, shards)), sem((2, shards)), sem((shards,)), sem((shards,)),
            sem((shards + 1, seqs)), sem((shards + 1, seqs)), sem((2,)), sem((seqs,)), sem((shards,)), sem((3,)), sem((6,)),
        ],
        compiler_params=pltpu.CompilerParams(vmem_limit_bytes=VMEM_LIMIT, collective_id=1, has_side_effects=True),
        name="first",
    )(inputs, padding, language, table, *vectors, latents, wq_rows, *weights)


class Reduce:
    def __init__(self, src, half, got_sib, got_chip, got_z, out, ss, rs, pending, x_first=True, stage=None, stage_sem=None):
        self.src, self.half, self.got_sib, self.got_chip, self.got_z, self.out = src, half, got_sib, got_chip, got_z, out
        self.ss, self.rs, self.pending, self.x_first = ss, rs, pending, x_first
        self.stage, self.stage_sem, self.kept = stage, stage_sem, None
        self.split = src is not None and src.shape[3] == half.shape[3]
        items, blk, self.me, hi, self.core = places()
        self.shards = lax.axis_size("heads")
        other = 1 - blk
        self.chip = hi * 2 + blk
        self.chip_x, self.chip_y, self.chip_xy = hi * 2 + other, (1 - hi) * 2 + blk, (1 - hi) * 2 + other
        self.to_x, self.to_y = mesh_at(db=other), mesh_at(di=(1 - hi) * 2 + self.core)
        self.to_sib = mesh_at(di=items + 1 - 2 * self.core)
        self.n, _, self.cols, self.width = half.shape
        self.share = self.cols // 4
        self.near = self.me + 1 - 2 * lax.rem(self.me, 2)
        self.far, self.cross = lax.rem(self.me + 2, 4), lax.rem(self.near + 2, 4)

    def rows(self, chip):
        return pl.ds(pl.multiple_of(chip * self.share, 16), self.share)

    def lanes(self, core):
        return pl.ds(pl.multiple_of(core * self.width, 128), self.width)

    def go(self, src, dst, i, target):
        self.pending.append(send(src, dst, self.ss.at[i], self.rs.at[i], target))

    def arrived(self, where, i):
        pltpu.make_async_remote_copy(src_ref=where, dst_ref=where, send_sem=self.ss.at[i], recv_sem=self.rs.at[i],
                                     device_id=self.to_sib, device_id_type=pl.DeviceIdType.MESH).wait_recv()

    def start(self):
        theirs = self.src if self.split else self.src.at[:, :, :, self.lanes(1 - self.core)]
        self.go(theirs, self.got_sib, 0, self.to_sib)

    def join_sib(self):
        self.arrived(self.got_sib, 0)

        def step(i, _):
            n, h = i // self.shards, lax.rem(i, self.shards)
            own = self.half[n, h] if self.split else self.src[n, h, :, self.lanes(self.core)]
            self.half[n, h] = (own.astype(F32) + self.got_sib[n, h].astype(F32)).astype(self.half.dtype)
            return 0
        lax.fori_loop(0, self.n * self.shards, step, 0)

    def send_chips(self):
        low, high = pl.ds(0, 2), pl.ds(2, 2)
        self.go(self.half.at[:, low, self.rows(self.chip_x)], self.got_chip.at[0], 1, self.to_x)
        self.go(self.half.at[:, high, self.rows(self.chip_y)], self.got_chip.at[2], 3, self.to_y)
        self.go(self.half.at[:, low, self.rows(self.chip_xy)], self.got_chip.at[1], 2, self.to_x)
        self.go(self.half.at[:, high, self.rows(self.chip_xy)], self.got_chip.at[3], 4, self.to_y)

    def add(self, slot, first, rows):
        self.arrived(self.got_chip.at[slot], 1 + slot)
        for n in range(self.n):
            for h in range(2):
                total = self.half[n, first + h, rows].astype(F32) + self.got_chip[slot, n, h].astype(F32)
                self.half[n, first + h, rows] = total.astype(self.half.dtype)

    def join_first(self):
        self.add(1, 0, self.rows(self.chip_y))
        self.go(self.half.at[:, pl.ds(0, 2), self.rows(self.chip_y)], self.got_chip.at[4], 5, self.to_y)
        self.add(3, 2, self.rows(self.chip_x))
        self.go(self.half.at[:, pl.ds(2, 2), self.rows(self.chip_x)], self.got_chip.at[5], 6, self.to_x)
        self.add(0, 0, self.rows(self.chip))
        self.add(2, 2, self.rows(self.chip))

    def join_chips(self):
        mine = self.rows(self.chip)
        self.add(4, 0, mine)
        self.add(5, 2, mine)
        for i, shard in enumerate((self.near, self.cross)):
            self.go(self.half.at[:, shard, mine], self.got_z.at[i], 7 + i, mesh_at(dh=self.near))

    def join_near(self):
        mine = self.rows(self.chip)
        for i, shard in enumerate((self.me, self.far)):
            self.arrived(self.got_z.at[i], 7 + i)
            for n in range(self.n):
                total = self.half[n, shard, mine].astype(F32) + self.got_z[i, n].astype(F32)
                self.half[n, shard, mine] = total.astype(self.half.dtype)
        self.go(self.half.at[:, self.far, mine], self.got_z.at[2], 9, mesh_at(dh=self.far))

    def join_z(self):
        self.arrived(self.got_z.at[2], 9)
        mine = self.rows(self.chip)
        for n in range(self.n):
            total = self.half[n, self.me, mine].astype(F32) + self.got_z[2, n].astype(F32)
            if self.stage is None:
                self.out[n, mine, self.lanes(self.core)] = total.astype(self.out.dtype)
            else:
                self.stage[n] = total.astype(self.out.dtype)
        src = self.piece(self.chip)
        if self.stage is not None:
            self.kept = pltpu.make_async_copy(self.stage, src, self.stage_sem)
            self.kept.start()
            src = self.stage
        self.go(src, self.piece(self.chip), 10, self.to_x)
        self.go(src, self.piece(self.chip), 11, self.to_y)

    def piece(self, chip):
        return self.out.at[:, self.rows(chip), self.lanes(self.core)]

    def pass_on(self, chip, i, target):
        self.go(self.piece(chip), self.piece(chip), i, target)

    def share_chips(self):
        if self.x_first:
            self.arrived(self.piece(self.chip_x), 10)
            self.pass_on(self.chip_x, 12, self.to_y)
        else:
            self.arrived(self.piece(self.chip_y), 11)
            self.pass_on(self.chip_y, 12, self.to_x)

    def share_sib(self):
        if self.x_first:
            self.arrived(self.piece(self.chip_y), 11)
        else:
            self.arrived(self.piece(self.chip_x), 10)
        self.arrived(self.piece(self.chip_xy), 12)
        if self.kept is not None:
            self.kept.wait()
        half = self.out.at[:, :, self.lanes(self.core)]
        self.go(half, half, 13, self.to_sib)

    def finish(self):
        self.arrived(self.out.at[:, :, self.lanes(1 - self.core)], 13)


def second_kernel(x_hbm, rows_ref, mask_ref, w_hbm, qt_ref, kv_hbm, xn_hbm, do_in, stat_in, mixed_in, lat_in, grads_hbm, vec_in, lang_in, latsum_in, wq_ref, lat_raw, lgain_ref,
                  g_out, mixed_out, dw_out, dlat_out, small_out, glat_out, vec_out, dq_out, latn_ref,
                  w_ref, x_ref, xn_ref, cols_ref, kv_ref, dkv_ref, q_ref, do_ref, stat_ref, stat_cols, dq_ref, dw_ref, dw_tmp,
                  g_half, g_chip, g_z, w_half, w_sib, w_chip, w_z, q_half, q_sib, q_chip, q_z, s_half, s_sib, s_chip, s_z,
                  small_ref, s_ref, l_sib, l_half, l_y, l_sum, l_z, l_tot, lat8_ref,
                  g_stage, w_stage, tq_ref, t_part, t_got, t_z, y_buf, c_buf, x_buf,
                  g_ss, g_rs, w_ss, w_rs, q_ss, q_rs, s_ss, s_rs, l_ss, l_rs, t_ss, t_rs, do_ss, do_rs, misc_ss, misc_rs, mix_ss, mix_rs, a_ss, a_rs, load_sem, kv_sem, stage_sem):
    items, blk, me, hi, core = places()
    shards = lax.axis_size("heads")
    seqs, width, length = x_ref.shape
    heads, rows, head_dim = q_ref.shape
    local_rows = rows // 2
    per_shard = heads // shards
    cols = per_shard * head_dim
    stat_rows = stat_in.shape[0]
    other = 1 - blk
    to_x, to_sib = mesh_at(db=other), mesh_at(di=items + 1 - 2 * core)
    to_y = mesh_at(di=(1 - hi) * 2 + core)
    z_of = [lax.rem(me + d, shards) for d in range(shards)]
    z_back = [lax.rem(me + shards - d, shards) for d in range(shards)]
    my_rows = pl.ds(pl.multiple_of(blk * local_rows, 128), local_rows)
    other_rows = pl.ds(pl.multiple_of(other * local_rows, 128), local_rows)
    pending = []
    dot_ref = w_sib.at[:, :, :, pl.ds(0, rows)]
    grads = [Reduce(None, g_half.at[pl.ds(m, 1)], None, g_chip.at[:, pl.ds(m, 1)], g_z.at[m], dlat_out.at[pl.ds(m, 1)], g_ss.at[m], g_rs.at[m], pending, m != 1,
                        g_stage.at[pl.ds(m, 1)], stage_sem.at[m])
             for m in range(3)]
    pair = [Reduce(dw_ref.at[pl.ds(m, 1)], w_half.at[pl.ds(m, 1)], w_sib.at[pl.ds(m, 1)], w_chip.at[:, pl.ds(m, 1)], w_z.at[m],
                   dw_out.at[pl.ds(m, 1)], w_ss.at[m], w_rs.at[m], pending, m == 0, w_stage.at[pl.ds(m, 1)], stage_sem.at[3 + m]) for m in range(2)]
    query = Reduce(dq_ref, q_half, q_sib, q_chip, q_z, dq_out, q_ss, q_rs, pending, False)
    small = Reduce(s_ref, s_half, s_sib, s_chip, s_z, small_out, s_ss, s_rs, pending)
    greet([to_sib, to_x, to_y] + [mesh_at(dh=z_of[d]) for d in range(1, shards)])

    def arrived(where, ss, rs):
        pltpu.make_async_remote_copy(src_ref=where, dst_ref=where, send_sem=ss, recv_sem=rs,
                                     device_id=to_sib, device_id_type=pl.DeviceIdType.MESH).wait_recv()

    pending.append(send(stat_in, stat_ref.at[pl.ds(0, stat_rows), my_rows], misc_ss.at[0], misc_rs.at[0], to_x))

    def send_do(s):
        pending.append(send(do_in.at[s], dot_ref.at[s, :, :, my_rows], do_ss.at[s], do_rs.at[s], to_x))

    near = me + 1 - 2 * lax.rem(me, 2)
    far, cross = lax.rem(me + 2, 4), lax.rem(near + 2, 4)

    def mixed_pass(block, i, there):
        pending.append(send(mixed_out.at[block], mixed_out.at[block], mix_ss.at[i], mix_rs.at[i], mesh_at(dh=there)))

    def mixed_far():
        mixed_pass(me * seqs + 1, 0, far)

    def mixed_near():
        mixed_pass(me * seqs + 1, 1, near)

    def mixed_cross_0():
        mixed_pass(far * seqs, 2, near)

    def mixed_cross_1():
        arrived(mixed_out.at[far * seqs + 1], mix_ss.at[0], mix_rs.at[0])
        mixed_pass(far * seqs + 1, 3, near)

    def latents_share():
        pending.append(send(lat_in, latn_ref.at[my_rows], misc_ss.at[1], misc_rs.at[1], to_x))

    loads = [
        pltpu.make_async_copy(xn_hbm, xn_ref, load_sem.at[0]),
        pltpu.make_async_copy(x_hbm, x_ref, load_sem.at[1]),
        pltpu.make_async_copy(grads_hbm, g_half, load_sem.at[2]),
        pltpu.make_async_copy(lat_raw.at[pl.ds(pl.multiple_of(core * 64 + hi * 32 + me * 8, 8), 8)], lat8_ref, load_sem.at[4]),
    ]
    own_sum = pltpu.make_async_copy(latsum_in.at[pl.ds(pl.multiple_of(core * (local_rows // 2), 8), local_rows // 2)], l_half, load_sem.at[13])
    own_sum.start()
    own_do = pltpu.make_async_copy(do_in, dot_ref.at[:, :, :, my_rows], load_sem.at[5])

    def load_pair(n, start):
        s, h = n // heads, lax.rem(n, heads)
        slot = lax.rem(n, 2)
        copy = pltpu.make_async_copy(kv_hbm.at[s, :, pl.ds(pl.multiple_of(h * head_dim, 16), head_dim)], kv_ref.at[slot], kv_sem.at[slot])
        copy.start() if start else copy.wait()

    load_pair(0, True)
    own_do.start()
    own_w = pltpu.make_async_copy(w_hbm, w_ref, load_sem.at[14])
    for copy in loads + [own_w]:
        copy.start()

    def prepare():
        latn_ref[my_rows] = lat_in[...]
        cols_ref[...] = jnp.transpose(rows_ref[...])
        stat_ref[:stat_rows, my_rows] = stat_in[...]
        stat_ref[stat_rows:] = jnp.zeros((128 - stat_rows, rows), F32)
        for h in range(heads):
            q_ref[h] = jnp.transpose(qt_ref[h % per_shard, h // per_shard])
        dq_ref[...] = jnp.zeros_like(dq_ref)
        small_ref[...] = jnp.zeros_like(small_ref)

    def stats_ready():
        arrived(stat_ref.at[pl.ds(0, stat_rows), other_rows], misc_ss.at[0], misc_rs.at[0])
        stat_cols[...] = jnp.transpose(stat_ref[...])

    scale = head_dim ** (-0.5)
    factor = LOG2E * scale
    lane = lax.broadcasted_iota(jnp.int32, (rows, 128), 1)

    def turn_grads(s):
        arrived(dot_ref.at[s, :, :, other_rows], do_ss.at[s], do_rs.at[s])
        for h in range(heads):
            inner = h % per_shard * head_dim
            do_ref[h] = jnp.transpose(dot_ref[s, h // per_shard, inner:inner + head_dim])

    def head_steps(s, group):
        def head_step(h, _):
            n = s * heads + h
            slot = lax.rem(n, 2)
            load_pair(n, False)

            @pl.when(n + 1 < seqs * heads)
            def _():
                load_pair(n + 1, True)

            at = pl.ds(pl.multiple_of(h * head_dim, 16), head_dim)
            lse = jnp.sum(jnp.where(lane == s * 2 * heads + h, stat_cols[...], 0.0), axis=1, keepdims=True)
            delta = jnp.sum(jnp.where(lane == s * 2 * heads + heads + h, stat_cols[...], 0.0), axis=1, keepdims=True)
            keys = kv_ref[slot, 0]
            weights = jnp.exp2(dot(q_ref[h], keys) * factor + mask_ref[s] - lse)
            part = pl.ds(pl.multiple_of(lax.rem(h, per_shard) * head_dim, 16), head_dim)
            dkv_ref[s, 1, at] = dot(dot_ref[s, h // per_shard, part], weights.astype(BF16)).astype(BF16)
            grad = dot(do_ref[h], kv_ref[slot, 1]) - delta
            grad = (weights * grad).astype(BF16)
            dkv_ref[s, 0, at] = (dot(qt_ref[lax.rem(h, per_shard), h // per_shard], grad) * scale).astype(BF16)
            dq_ref[0, h // per_shard, part] += dot_nt(keys, grad) * scale
            return 0

        lax.fori_loop(2 * group, 2 * group + 2, head_step, 0)

    piece = min(256, length)

    def byte_steps(s):
        def byte_step(i, carry):
            at = pl.ds(pl.multiple_of(i * piece, piece), piece)
            grad = dot(w_ref[0], dkv_ref[s, 0, :, at]) + dot(w_ref[1], dkv_ref[s, 1, :, at])
            normed, inverse = norm_columns(x_ref[s, :, at], cols_ref[:, 2 + s:3 + s])
            small_ref[:, 0:1] += jnp.sum(grad * normed, axis=1, keepdims=True)
            small_ref[:, 1:2] += jnp.sum(grad, axis=1, keepdims=True)
            scaled = grad * cols_ref[:, 0:1]
            first = jnp.mean(scaled, axis=0, keepdims=True)
            second = jnp.mean(scaled * normed, axis=0, keepdims=True)
            shifted = (scaled - first - normed * second) * inverse
            x_ref[s, :, at] = shifted.astype(BF16)
            return carry + jnp.sum(shifted, axis=1, keepdims=True)

        small_ref[:, 2 + s:3 + s] = lax.fori_loop(0, length // piece, byte_step, jnp.zeros((width, 1), F32))
        share = width // shards
        own = pltpu.make_async_copy(x_ref.at[s, pl.ds(pl.multiple_of(me * share, 16), share)], g_out.at[me * seqs + s], load_sem.at[6 + s])
        own.start()
        loads.append(own)

    def bytes_send(s, d):
        share = width // shards
        there = pl.ds(pl.multiple_of(z_back[d] * share, 16), share)
        pending.append(send(x_ref.at[s, there], g_out.at[me * seqs + s], a_ss.at[s, d], a_rs.at[s, d], mesh_at(dh=z_back[d])))

    half_rows, quarter = local_rows // 2, local_rows // 4
    piece_rows = quarter // shards

    def latents_send():
        theirs = latsum_in.at[pl.ds(pl.multiple_of((1 - core) * half_rows, 8), half_rows)]
        pending.append(send(theirs, l_sib, l_ss.at[0], l_rs.at[0], to_sib))

    def latents_sib():
        arrived(l_sib, l_ss.at[0], l_rs.at[0])
        own_sum.wait()
        l_half[...] += l_sib[...]
        pending.append(send(l_half.at[pl.ds(pl.multiple_of((1 - hi) * quarter, 8), quarter)], l_y, l_ss.at[1], l_rs.at[1], to_y))

    def latents_y():
        arrived(l_y, l_ss.at[1], l_rs.at[1])
        l_sum[...] = (l_half[pl.ds(pl.multiple_of(hi * quarter, 8), quarter)] + l_y[...]).reshape(l_sum.shape)
        for d in range(1, shards):
            pending.append(send(l_sum.at[z_back[d]], l_z.at[d - 1], l_ss.at[1 + d], l_rs.at[1 + d], mesh_at(dh=z_back[d])))

    def latents_z():
        total = l_sum[me]
        for d in range(1, shards):
            arrived(l_z.at[d - 1], l_ss.at[1 + d], l_rs.at[1 + d])
            total += l_z[d - 1]
        l_tot[...] = total

    def third_first():
        tq_ref[...] = jnp.transpose(dq_out[0, :, my_rows])
        rows_here = tq_ref[pl.ds(pl.multiple_of(core * half_rows + hi * quarter, 8), quarter)].astype(BF16)
        t_part[...] = dot(rows_here, wq_ref[...]).reshape(t_part.shape)
        for d in range(1, shards):
            pending.append(send(t_part.at[z_back[d]], t_got.at[d - 1], t_ss.at[0, d], t_rs.at[0, d], mesh_at(dh=z_back[d])))

    def third_z():
        grad = t_part[me]
        for d in range(1, shards):
            arrived(t_got.at[d - 1], t_ss.at[0, d], t_rs.at[0, d])
            grad += t_got[d - 1]
        loads[3].wait()
        _, normed, inverse = norm_keep(lat8_ref[...], 1.0, 0.0)
        t_z[me, :piece_rows] = l_tot[...] + norm_back(grad, normed, inverse, lgain_ref[0:1])
        t_z[me, piece_rows:] = jnp.zeros((8, lat8_ref.shape[1]), F32)
        t_z[me, piece_rows:piece_rows + 1] = jnp.sum(grad * normed, axis=0, keepdims=True)
        t_z[me, piece_rows + 1:piece_rows + 2] = jnp.sum(grad, axis=0, keepdims=True)
        for d in range(1, shards):
            pending.append(send(t_z.at[me], t_z.at[me], t_ss.at[1, d], t_rs.at[1, d], mesh_at(dh=z_back[d])))

    def third_y():
        for d in range(1, shards):
            arrived(t_z.at[z_of[d]], t_ss.at[1, d], t_rs.at[1, d])
        y_buf[hi, :quarter] = t_z[:, :piece_rows].reshape(quarter, t_z.shape[2])
        y_buf[hi, quarter:] = t_z[0, piece_rows:] + t_z[1, piece_rows:] + t_z[2, piece_rows:] + t_z[3, piece_rows:]
        pending.append(send(y_buf.at[hi], y_buf.at[hi], t_ss.at[2, 0], t_rs.at[2, 0], to_y))

    def third_core():
        arrived(y_buf.at[1 - hi], t_ss.at[2, 0], t_rs.at[2, 0])
        c_buf[core, :quarter] = y_buf[0, :quarter]
        c_buf[core, quarter:half_rows] = y_buf[1, :quarter]
        c_buf[core, half_rows:] = y_buf[0, quarter:] + y_buf[1, quarter:]
        pending.append(send(c_buf.at[core], c_buf.at[core], t_ss.at[2, 1], t_rs.at[2, 1], to_sib))

    def third_x():
        arrived(c_buf.at[1 - core], t_ss.at[2, 1], t_rs.at[2, 1])
        glat_out[:half_rows] = c_buf[0, :half_rows]
        glat_out[half_rows:] = c_buf[1, :half_rows]
        x_buf[blk] = c_buf[0, half_rows:] + c_buf[1, half_rows:]
        pending.append(send(x_buf.at[blk], x_buf.at[blk], t_ss.at[2, 2], t_rs.at[2, 2], to_x))

    def third_end():
        arrived(x_buf.at[other], t_ss.at[2, 2], t_rs.at[2, 2])
        vec_out[...] = x_buf[0] + x_buf[1]

    def small_start():
        wide_lane = lax.broadcasted_iota(jnp.int32, (width, 128), 1)
        block = jnp.where(wide_lane == 32, small_ref[:, 0:1], 0.0) + jnp.where(wide_lane == 33, small_ref[:, 1:2], 0.0)
        for s in range(seqs):
            block += small_ref[:, 2 + s:3 + s] * lang_in[s:s + 1]
        share = width // shards
        for h in range(shards):
            s_ref[0, h, :, :128] = block[h * share:(h + 1) * share]
            s_ref[0, h, :, 128:] = jnp.zeros((share, 128), F32)
            for v in range(vec_in.shape[0]):
                for b in range(vec_in.shape[1] // 128):
                    s_ref[0, h, v * 10 + b:v * 10 + b + 1, 128:] = vec_in[v:v + 1, b * 128:(b + 1) * 128]
        small.start()

    def weight_steps(part):
        def weight_step(h, _):
            at = pl.ds(pl.multiple_of(h * cols, 16), cols)
            total = dot_nt(dkv_ref[0, part, at], xn_ref[0])
            for s in range(1, seqs):
                total += dot_nt(dkv_ref[s, part, at], xn_ref[s])
            dw_tmp[...] = total.astype(BF16)
            w_half[part, h] = dw_tmp[:, pl.ds(pl.multiple_of(core * (width // 2), 128), width // 2)]
            dw_ref[part, h] = dw_tmp[:, pl.ds(pl.multiple_of((1 - core) * (width // 2), 128), width // 2)]
            return 0
        lax.fori_loop(0, shards, weight_step, 0)

    send_do(0)
    mixed_near()
    prepare()
    own_do.wait()
    stats_ready()
    turn_grads(0)
    send_do(1)
    mixed_far()
    head_steps(0, 0)
    latents_send()
    head_steps(0, 1)
    head_steps(0, 2)
    loads[2].wait()
    grads[2].send_chips()
    head_steps(0, 3)
    loads[1].wait()
    own_w.wait()
    byte_steps(0)
    grads[1].send_chips()
    mixed_cross_0()
    bytes_send(0, 1)
    bytes_send(0, 3)
    turn_grads(1)
    head_steps(1, 0)
    head_steps(1, 1)
    bytes_send(0, 2)
    grads[0].send_chips()
    head_steps(1, 2)
    head_steps(1, 3)
    grads[2].join_first()
    query.start()
    loads[0].wait()
    weight_steps(0)
    latents_sib()
    byte_steps(1)
    query.join_sib()
    small_start()
    grads[0].join_first()
    grads[2].join_chips()
    small.join_sib()
    small.send_chips()
    query.send_chips()
    grads[1].join_first()
    pair[0].start()
    latents_y()
    weight_steps(1)
    pair[1].start()
    grads[0].join_chips()
    pair[0].join_sib()
    bytes_send(1, 3)
    query.join_first()
    pair[0].send_chips()
    grads[2].join_near()
    query.join_chips()
    latents_share()
    grads[1].join_chips()
    pair[1].join_sib()
    pair[1].send_chips()
    pair[0].join_first()
    query.join_near()
    grads[0].join_near()
    small.join_first()
    query.join_z()
    query.share_chips()
    grads[1].join_near()
    pair[1].join_first()
    small.join_chips()
    grads[2].join_z()
    bytes_send(1, 2)
    pair[0].join_chips()
    query.share_sib()
    query.finish()
    third_first()
    grads[0].join_z()
    small.join_near()
    pair[0].join_near()
    grads[0].share_chips()
    grads[2].share_chips()
    small.join_z()
    pair[1].join_chips()
    latents_z()
    grads[1].join_z()
    grads[2].share_sib()
    third_z()
    grads[0].share_sib()
    grads[1].share_chips()
    pair[0].join_z()
    pair[1].join_near()
    mixed_cross_1()
    small.share_chips()
    pair[0].share_chips()
    pair[0].share_sib()
    small.share_sib()
    grads[1].share_sib()
    third_y()
    bytes_send(1, 1)
    grads[2].finish()
    pair[1].join_z()
    grads[0].finish()
    third_core()
    pair[0].finish()
    grads[1].finish()
    pair[1].share_chips()
    pair[1].share_sib()
    third_x()
    pair[1].finish()
    small.finish()
    third_end()
    arrived(latn_ref.at[other_rows], misc_ss.at[1], misc_rs.at[1])
    arrived(mixed_out.at[near * seqs + 1], mix_ss.at[1], mix_rs.at[1])
    arrived(mixed_out.at[cross * seqs], mix_ss.at[2], mix_rs.at[2])
    arrived(mixed_out.at[cross * seqs + 1], mix_ss.at[3], mix_rs.at[3])
    for d in range(1, shards):
        for s in range(seqs):
            arrived(g_out.at[z_of[d] * seqs + s], a_ss.at[s, d], a_rs.at[s, d])
    for own in loads[4:]:
        own.wait()
    for copy in pending:
        copy.wait_send()


def second_call(x_cols, rows_in, mask, w_cols, qt, pairs, xn, grad_out, stats, mixed, lat_low, grads, vectors, lang_rows, lat_sum, w_query, lat_f32, lat_gain):
    seqs, width, length = x_cols.shape
    rows, width_lat = qt.shape[3], pairs.shape[2]
    local_rows = lat_low.shape[0]
    shards = lax.axis_size("heads")
    heads = HEADS
    head_dim = width_lat // heads
    cols = width_lat // shards
    share = cols // 4
    whole = pl.BlockSpec(memory_space=pltpu.VMEM)
    hbm = pl.BlockSpec(memory_space=pl.ANY)
    out = jax.ShapeDtypeStruct
    vmem = pltpu.VMEM
    sem = pltpu.SemaphoreType.DMA

    assert seqs == 2

    def reduce_buffers(n, lanes, kind, cols=cols):
        half, share = lanes // 2, cols // 4
        return [vmem((n, shards, cols, half), kind), vmem((n, shards, cols, half), kind), vmem((6, n, 2, share, half), kind),
                vmem((shards - 1, n, share, half), kind)]

    return pl.pallas_call(
        second_kernel,
        in_specs=[hbm, whole, whole, hbm, whole, hbm, hbm, hbm, whole, hbm, whole, hbm, whole, whole, hbm, whole, hbm, whole],
        out_specs=[hbm, hbm, hbm, hbm, whole, whole, whole, whole, whole],
        input_output_aliases={9: 1},
        out_shape=[
            out((shards * seqs, width // shards, length), BF16),
            out((shards * seqs, local_rows, width_lat), BF16),
            out((2, cols, width), BF16),
            out((3, cols, width_lat), BF16),
            out((1, width // shards, 256), F32),
            out((local_rows, width_lat), F32),
            out((8, width_lat), F32),
            out((1, cols, rows), F32),
            out((rows, width_lat), BF16),
        ],
        scratch_shapes=[
            vmem((2, width, width_lat), BF16),
            vmem((seqs, width, length), BF16),
            vmem((seqs, width, length), BF16),
            vmem((width, rows_in.shape[0]), F32),
            vmem((2, 2, head_dim, length), BF16),
            vmem((seqs, 2, width_lat, length), BF16),
            vmem((heads, rows, head_dim), BF16),
            vmem((heads, rows, head_dim), BF16),
            vmem((128, rows), F32),
            vmem((rows, 128), F32),
            vmem((1, shards, cols, rows), F32),
            vmem((2, shards, cols, width // 2), BF16),
            vmem((cols, width), BF16),
        ] + [
            vmem((3, shards, cols, width_lat // 2), BF16),
            vmem((6, 3, 2, share, width_lat // 2), BF16),
            vmem((3, 3, 1, share, width_lat // 2), BF16),
        ] + reduce_buffers(2, width, BF16)[:3] + [vmem((2, 3, 1, share, width // 2), BF16)]
        + reduce_buffers(1, rows, F32)
        + reduce_buffers(1, 256, F32, width // shards) + [
            vmem((width, 8), F32),
            vmem((1, shards, width // shards, 256), F32),
            vmem((local_rows // 2, width_lat), F32),
            vmem((local_rows // 2, width_lat), F32),
            vmem((local_rows // 4, width_lat), F32),
            vmem((shards, local_rows // 16, width_lat), F32),
            vmem((shards - 1, local_rows // 16, width_lat), F32),
            vmem((local_rows // 16, width_lat), F32),
            vmem((local_rows // 16, width_lat), F32),
            vmem((3, share, width_lat // 2), BF16),
            vmem((2, share, width // 2), BF16),
            vmem((local_rows, cols), F32),
            vmem((shards, local_rows // 16, width_lat), F32),
            vmem((shards - 1, local_rows // 16, width_lat), F32),
            vmem((shards, local_rows // 16 + 8, width_lat), F32),
            vmem((2, local_rows // 4 + 8, width_lat), F32),
            vmem((2, local_rows // 2 + 8, width_lat), F32),
            vmem((2, 8, width_lat), F32),
        ] + [sem((3, 14))] * 2 + [sem((2, 14))] * 2 + [sem((14,))] * 4 + [sem((6,))] * 2 + [sem((3, shards))] * 2 + [sem((seqs,))] * 2 + [sem((2,))] * 2 + [sem((shards,))] * 2 + [sem((seqs, shards))] * 2
        + [sem((16,)), sem((2,)), sem((5,))],
        compiler_params=pltpu.CompilerParams(vmem_limit_bytes=VMEM_LIMIT, collective_id=2, has_side_effects=True),
        name="second",
    )(x_cols, rows_in, mask, w_cols, qt, pairs, xn, grad_out, stats, mixed, lat_low, grads, vectors, lang_rows, lat_sum, w_query, lat_f32, lat_gain)


def middle_kernel(att_ref, lat_ref, cot_hbm, all_hbm, bup_tiles, vecs_ref, lse_ref,
                  mixed_all, do_ref, stat_ref, half_out, vec_ref, sum_ref,
                  rows_ref, mid_ref, low_ref, hid_ref, norm_ref, a_ref, b_src, b_ref, bup_ref, all_ref, mixed_ref, cot_ref, slope_ref, half_ref, a_ss, a_rs, b_ss, b_rs, load_sem, mix_ss, mix_rs):
    items, _, me, _, core = places()
    near = me + 1 - 2 * lax.rem(me, 2)
    far = lax.rem(me + 2, 4)
    to_sib = mesh_at(di=items + 1 - 2 * core)
    seqs, width, local_rows = att_ref.shape
    rows = seqs * local_rows
    heads = lse_ref.shape[1]
    head_dim = width // heads
    half = width // 2
    block = 256
    pending = []
    loads = [pltpu.make_async_copy(all_hbm.at[i], all_ref.at[i], load_sem.at[i]) for i in range(3)]
    cots = [pltpu.make_async_copy(cot_hbm.at[me * seqs + s], cot_ref.at[pl.ds(s * local_rows, local_rows)], load_sem.at[4 + s]) for s in range(seqs)]
    for copy in cots + loads:
        copy.start()
    greet([to_sib, mesh_at(dh=near), mesh_at(dh=far)])
    shards, cols = half_ref.shape[1:3]
    for h in range(shards):
        bup_ref[:, h * cols:(h + 1) * cols] = bup_tiles[h, 7:8, :cols]
    gain_ref, bias_ref, bdown_ref = vecs_ref.at[pl.ds(2, 1)], vecs_ref.at[pl.ds(3, 1)], vecs_ref.at[pl.ds(4, 1)]

    def block_loop(body):
        def step(i, _):
            body(pl.ds(pl.multiple_of(i * block, block), block))
            return 0
        lax.fori_loop(0, width // block, step, 0)

    def share_a(i):
        pending.append(send(a_ref.at[i, 0], a_ref.at[i, 1], a_ss.at[i], a_rs.at[i], to_sib))

    def share_b(i):
        theirs = b_src.at[i, :, pl.ds(pl.multiple_of((1 - core) * half, 128), half)]
        pending.append(send(theirs, b_ref.at[i, 1], b_ss.at[i], b_rs.at[i], to_sib))
        b_ref[i, 0] = b_src[i, :, pl.ds(pl.multiple_of(core * half, 128), half)]

    for s in range(seqs):
        at = slice(s * local_rows, (s + 1) * local_rows)
        low = att_ref[s].astype(BF16)
        a_ref[0, 0, :, at] = low
        rows_ref[at] = jnp.transpose(att_ref[s]).astype(BF16)
    share_a(0)
    for copy in cots:
        copy.wait()
    b_src[2] = cot_ref[...]
    share_b(2)

    def branch(at):
        latent = lat_ref[:, at].astype(F32)
        mid_ref[:, at] = dot(rows_ref[...], all_ref[0, :, at]) + jnp.concatenate([latent] * seqs, axis=0)
    loads[0].wait()
    block_loop(branch)
    mid_out, normed, inverse = norm_keep(mid_ref[...], gain_ref[...], bias_ref[...])
    norm_ref[...] = normed
    b_src[1] = mid_out.astype(BF16)
    share_b(1)

    def up(at):
        value = dot_nt(b_src[1], all_ref[1, at]) + bup_ref[:, at]
        square = value * value
        bend = jnp.tanh(0.7978845608028654 * (value + 0.044715 * (square * value)))
        active = 0.5 * value * (1.0 + bend)
        slope_ref[:, at] = 0.5 * (1.0 + bend) + 0.5 * value * (1.0 - bend * bend) * (0.7978845608028654 * (1.0 + 0.134145 * square))
        rows_ref[:, at] = active.astype(BF16)
        a_ref[2, 0, at] = jnp.transpose(active.astype(BF16))
    loads[1].wait()
    block_loop(up)
    share_a(2)

    def down(at):
        out = mid_ref[:, at] + dot(rows_ref[...], all_ref[2, :, at]) + bdown_ref[:, at]
        for s in range(seqs):
            mixed_ref[s, :, at] = out[s * local_rows:(s + 1) * local_rows].astype(BF16)
    loads[2].wait()
    block_loop(down)
    own_mixed = pltpu.make_async_copy(mixed_ref, mixed_all.at[pl.ds(me * seqs, seqs)], load_sem.at[3])
    own_mixed.start()
    for i, there in enumerate((far, near)):
        pending.append(send(mixed_ref.at[0], mixed_all.at[me * seqs], mix_ss.at[i], mix_rs.at[i], mesh_at(dh=there)))

    def up_back(at):
        grad = (dot_nt(cot_ref[...], all_ref[2, at]) * slope_ref[:, at]).astype(BF16)
        low_ref[:, at] = grad
        vec_ref[2:3, at] = jnp.sum(grad.astype(F32), axis=0, keepdims=True)
        a_ref[1, 0, at] = jnp.transpose(grad)
    block_loop(up_back)
    share_a(1)

    def mid_back(at):
        hid_ref[:, at] = dot(low_ref[...], all_ref[1, :, at])
    block_loop(mid_back)
    grad = hid_ref[...]
    normed = norm_ref[...]
    vec_ref[0:1] = jnp.sum(grad * normed, axis=0, keepdims=True)
    vec_ref[1:2] = jnp.sum(grad, axis=0, keepdims=True)
    vec_ref[3:4] = jnp.sum(cot_ref[...].astype(F32), axis=0, keepdims=True)
    grad = cot_ref[...].astype(F32) + norm_back(grad, normed, inverse, gain_ref[...])
    b_src[0] = grad.astype(BF16)
    share_b(0)
    total = grad[:local_rows]
    for s in range(1, seqs):
        total += grad[s * local_rows:(s + 1) * local_rows]
    sum_ref[...] = total

    def out(h, _):
        at = pl.ds(pl.multiple_of(h * head_dim, 16), head_dim)
        grad = dot_nt(all_ref[0, at], b_src[0]).astype(BF16)
        for s in range(seqs):
            part = grad[:, s * local_rows:(s + 1) * local_rows]
            do_ref[s, at] = part
            delta = jnp.sum(part.astype(F32) * att_ref[s, at], axis=0, keepdims=True)
            stat_ref[pl.ds((2 * s + 1) * heads + h, 1)] = delta
        return 0
    lax.fori_loop(0, heads, out, 0)
    for s in range(seqs):
        stat_ref[2 * s * heads:(2 * s + 1) * heads] = lse_ref[s]

    def arrived(where, ss, rs):
        pltpu.make_async_remote_copy(src_ref=where, dst_ref=where, send_sem=ss, recv_sem=rs,
                                     device_id=to_sib, device_id_type=pl.DeviceIdType.MESH).wait_recv()

    stores = []
    for i in (2, 1, 0):
        arrived(a_ref.at[i, 1], a_ss.at[i], a_rs.at[i])
        arrived(b_ref.at[i, 1], b_ss.at[i], b_rs.at[i])

        def weight(h, _):
            at = pl.ds(pl.multiple_of(h * cols, 16), cols)
            half_ref[i, h] = (dot(a_ref[i, 0, at], b_ref[i, 0]) + dot(a_ref[i, 1, at], b_ref[i, 1])).astype(BF16)
            return 0
        lax.fori_loop(0, shards, weight, 0)
        copy = pltpu.make_async_copy(half_ref.at[i], half_out.at[i], load_sem.at[4 + seqs + i])
        copy.start()
        stores.append(copy)
    own_mixed.wait()
    for copy in stores:
        copy.wait()
    for i, there in enumerate((far, near)):
        arrived(mixed_all.at[there * seqs], mix_ss.at[i], mix_rs.at[i])
    for copy in pending:
        copy.wait_send()


def middle_call(att, latents, cot, weights, b_up, vecs, lse):
    seqs, width, local_rows = att.shape
    rows = seqs * local_rows
    heads = lse.shape[1]
    shards = lax.axis_size("heads")
    whole = pl.BlockSpec(memory_space=pltpu.VMEM)
    out, vmem, sem = jax.ShapeDtypeStruct, pltpu.VMEM, pltpu.SemaphoreType.DMA
    return pl.pallas_call(
        middle_kernel,
        in_specs=[whole, whole, pl.BlockSpec(memory_space=pl.ANY), pl.BlockSpec(memory_space=pl.ANY), whole, whole, whole],
        out_specs=[pl.BlockSpec(memory_space=pl.ANY)] + [whole] * 2 + [pl.BlockSpec(memory_space=pl.ANY)] + [whole] * 2,
        out_shape=[
            out((shards * seqs, local_rows, width), BF16),
            out((seqs, width, local_rows), BF16),
            out((2 * seqs * heads, local_rows), F32),
            out((3, shards, width // shards, width // 2), BF16),
            out((4, width), F32),
            out((local_rows, width), F32),
        ],
        scratch_shapes=[
            vmem((rows, width), BF16), vmem((rows, width), F32), vmem((rows, width), BF16), vmem((rows, width), F32), vmem((rows, width), F32),
            vmem((3, 2, width, rows), BF16), vmem((3, rows, width), BF16), vmem((3, 2, rows, width // 2), BF16),
            vmem((1, width), F32), vmem((3, width, width), BF16), vmem((seqs, local_rows, width), BF16), vmem((rows, width), BF16), vmem((rows, width), F32),
            vmem((3, shards, width // shards, width // 2), BF16),
            sem((3,)), sem((3,)), sem((3,)), sem((3,)), sem((7 + seqs,)), sem((2,)), sem((2,)),
        ],
        compiler_params=pltpu.CompilerParams(vmem_limit_bytes=VMEM_LIMIT, collective_id=4, has_side_effects=True),
        name="middle",
    )(att, latents, cot, weights, b_up, vecs, lse)


def finish_kernel(lat_ref, pair_ref, small_ref, vec_ref, query_ref, latn_ref, g_hbm, mixed_hbm, glat_ref,
                  table_out, igain_out, ibias_out, lgain_out, lbias_out, mgain_out, mbias_out, wq_out, wk_out, wv_out, wo_out, wu_out,
                  bup_out, wd_out, bdown_out, g_out, mixed_out, glat_out, wq_ref, wk_ref, wv_ref, wo_ref, wu_ref, wd_ref, g_ref, mixed_ref, row_ref, sems, pass_sems):
    me = lax.axis_index("heads")
    copies = []

    def store(ref, out):
        copy = pltpu.make_async_copy(ref, out, sems.at[len(copies)])
        copy.start()
        copies.append(copy)

    loads = [pltpu.make_async_copy(g_hbm, g_ref, pass_sems.at[0]), pltpu.make_async_copy(mixed_hbm, mixed_ref, pass_sems.at[1])]
    for copy in loads:
        copy.start()
    glat_out[...] = glat_ref[...]
    wo_ref[...] = lat_ref[0].astype(F32)
    store(wo_ref, wo_out)
    wd_ref[...] = lat_ref[2].astype(F32)
    store(wd_ref, wd_out)
    wu_ref[...] = lat_ref[1].astype(F32)
    store(wu_ref, wu_out)
    wk_ref[...] = pair_ref[0].astype(F32)
    store(wk_ref, wk_out)
    wv_ref[...] = pair_ref[1].astype(F32)
    store(wv_ref, wv_out)
    loads[0].wait()
    store(g_ref, g_out)
    loads[1].wait()
    store(mixed_ref, mixed_out)
    query = query_ref[0].astype(BF16)
    for i in range(0, latn_ref.shape[1], 256):
        wq_ref[:, i:i + 256] = dot(query, latn_ref[:, i:i + 256])
    store(wq_ref, wq_out)
    turned = jnp.transpose(small_ref[0, :, :128])
    table_out[...] = turned[:table_out.shape[0]]
    igain_out[...] = turned[32]
    ibias_out[...] = turned[33]
    lgain_out[...] = vec_ref[0]
    lbias_out[...] = vec_ref[1]
    blocks = row_ref.shape[1] // 128
    for v, out in enumerate((mgain_out, mbias_out, None, bdown_out)):
        for b in range(blocks):
            row_ref[:, b * 128:(b + 1) * 128] = small_ref[0, v * blocks + b:v * blocks + b + 1, 128:]
        if out is not None:
            out[...] = row_ref[0]
        else:
            cols = bup_out.shape[0]
            total = jnp.zeros((1, cols), F32)
            for h in range(row_ref.shape[1] // cols):
                total += jnp.where(me == h, row_ref[:, h * cols:(h + 1) * cols], 0.0)
            bup_out[...] = total[0]
    for copy in copies:
        copy.wait()


def finish_call(lat_total, pair_total, small, vec, query, latn, grad, mixed, grad_lat, langs):
    _, cols, width_lat = lat_total.shape
    width = pair_total.shape[2]
    share = small.shape[1]
    whole = pl.BlockSpec(memory_space=pltpu.VMEM)
    hbm = pl.BlockSpec(memory_space=pl.ANY)
    out, vmem = jax.ShapeDtypeStruct, pltpu.VMEM
    big = [(cols, width_lat), (cols, width), (cols, width), (cols, width_lat), (cols, width_lat), (cols, width_lat)]
    return pl.pallas_call(
        finish_kernel,
        in_specs=[whole] * 6 + [hbm, hbm, whole],
        out_specs=[whole] * 7 + [hbm] * 5 + [whole, hbm, whole, hbm, hbm, whole],
        out_shape=[out(shape, F32) for shape in [(langs, share), (share,), (share,)] + [(width_lat,)] * 4 + big[:5] + [(cols,)] + big[5:] + [(width_lat,)]]
        + [out(x.shape, x.dtype) for x in (grad, mixed, grad_lat)],
        scratch_shapes=[vmem(shape, F32) for shape in big] + [vmem(x.shape, x.dtype) for x in (grad, mixed)]
        + [vmem((1, width_lat), F32), pltpu.SemaphoreType.DMA((8,)), pltpu.SemaphoreType.DMA((2,))],
        compiler_params=pltpu.CompilerParams(vmem_limit_bytes=VMEM_LIMIT),
        name="finish",
    )(lat_total, pair_total, small, vec, query, latn, grad, mixed, grad_lat)


REST = ("items", "blk")
ALL = ("heads", "items", "blk")


def gather_rows(shard):
    count = lax.axis_size("items") * lax.axis_size("blk")
    me = lax.axis_index("items") * lax.axis_size("blk") + lax.axis_index("blk")
    share = shard.shape[0] // count
    part = lax.dynamic_slice_in_dim(shard, me * share, share, 0)
    return lax.all_gather(part, ALL, axis=0, tiled=True)


def scatter_rows(whole):
    part = lax.psum_scatter(whole.astype(BF16), ALL, scatter_dimension=0, tiled=True)
    return lax.all_gather(part, REST, axis=0, tiled=True)


def general_device(inputs, padding, language, lang_table, latents, in_gain, in_bias, lat_gain, lat_bias, mid_gain, mid_bias,
              w_query, w_key, w_value, w_out, w_up, b_up, w_down, b_down, cotangent):
    length, local_seqs, width = inputs.shape
    local_rows, width_lat = latents.shape
    cols = w_query.shape[1]
    head_dim = width_lat // HEADS
    per_shard = cols // head_dim
    shards = lax.axis_size("heads")
    blocks = lax.axis_size("blk")
    rows = local_rows * blocks
    seqs = local_seqs // shards
    me = lax.axis_index("heads")
    first = me * seqs

    pair_shard = jnp.concatenate([w_key.T, w_value.T], axis=0)
    pair_rows = gather_rows(pair_shard)
    latent_shard = jnp.concatenate([w_out, w_up.T, w_down], axis=0)
    lat_all = gather_rows(latent_shard).reshape(shards, 3, cols, width_lat)
    out_all, up_all, down_all = (lat_all[:, i].reshape(width_lat, width_lat) for i in range(3))

    all_latents = lax.all_gather(latents, "blk", axis=0, tiled=True).astype(F32)
    lat_out, _, _ = norm_keep(all_latents, lat_gain, lat_bias)
    lat_low = lat_out.astype(BF16)
    query_part = dot(lat_low, w_query).astype(BF16)
    queries = lax.all_gather(query_part, "heads", axis=1, tiled=True)
    q = queries.reshape(rows, HEADS, head_dim).transpose(1, 0, 2)

    own = lax.dynamic_slice_in_dim(inputs, first, seqs, 1)
    x_cols = jnp.transpose(own, (1, 2, 0))
    live = jnp.transpose(lax.dynamic_slice_in_dim(padding, first, seqs, 1))
    mask = jnp.where(live > 0, 0.0, MASKED).astype(F32)[:, None, :]
    own_lang = lax.dynamic_slice_in_dim(language, first, seqs, 0)
    onehot = (own_lang[:, None] == jnp.arange(lang_table.shape[0], dtype=jnp.int32)[None, :]).astype(F32)
    emb = jnp.dot(onehot, lang_table.astype(F32), precision=lax.Precision.HIGHEST)[:, :, None]
    gain_col, bias_col = in_gain[:, None], in_bias[:, None]

    pairs, o_cols, lse = forward_call(x_cols, emb, gain_col, bias_col, pair_rows, q, mask, per_shard)

    parts = o_cols.reshape(seqs, width_lat, blocks, local_rows).transpose(2, 0, 3, 1)
    parts = lax.all_to_all(parts, "blk", 0, 0, tiled=True).astype(F32)
    lse_parts = lse.reshape(seqs, HEADS, blocks, local_rows).transpose(2, 0, 3, 1)
    lse_parts = lax.all_to_all(lse_parts, "blk", 0, 0, tiled=True)
    top = jnp.max(lse_parts, axis=0)
    shares = jnp.exp2(lse_parts - top)
    total = jnp.sum(shares, axis=0)
    own_lse = top + jnp.log2(total)
    shares = shares / total
    attended = jnp.sum(parts.reshape(blocks, seqs, local_rows, HEADS, head_dim) * shares[..., None], axis=0)
    att_low = attended.reshape(seqs * local_rows, width_lat).astype(BF16)

    cot = lax.dynamic_slice_in_dim(cotangent, first, seqs, 0).reshape(seqs * local_rows, width_lat)
    lat_f32 = latents.astype(F32)
    middle = (lat_f32[None] + dot(att_low, out_all).reshape(seqs, local_rows, width_lat)).reshape(seqs * local_rows, width_lat)
    mid_out, mid_normed, mid_inverse = norm_keep(middle, mid_gain, mid_bias)
    mid_low = mid_out.astype(BF16)
    b_up_all = lax.all_gather(b_up, "heads", axis=0, tiled=True)
    hidden = dot_nt(mid_low, up_all) + b_up_all
    active, gelu_back = jax.vjp(jax.nn.gelu, hidden)
    active_low = active.astype(BF16)
    own_mixed = (middle + dot(active_low, down_all) + b_down).astype(BF16).reshape(seqs, local_rows, width_lat)
    mixed_latents = lax.all_gather(own_mixed, "heads", axis=0, tiled=True)

    grad_b_down = jnp.sum(cot.astype(F32), axis=0)
    grad_w_down = dot(active_low.T, cot)
    grad_active = dot_nt(cot, down_all)
    grad_hidden = gelu_back(grad_active)[0].astype(BF16)
    grad_b_up = jnp.sum(grad_hidden.astype(F32), axis=0)
    grad_w_up = dot(grad_hidden.T, mid_low)
    grad_mid_norm = dot(grad_hidden, up_all)
    grad_mid_gain = jnp.sum(grad_mid_norm * mid_normed, axis=0)
    grad_mid_bias = jnp.sum(grad_mid_norm, axis=0)
    grad_middle = cot.astype(F32) + norm_back(grad_mid_norm, mid_normed, mid_inverse, mid_gain)
    grad_branch = grad_middle.astype(BF16)
    grad_w_out = dot(att_low.T, grad_branch)
    grad_att = dot_nt(grad_branch, out_all).astype(BF16).reshape(seqs, local_rows, width_lat)
    grad_att_heads = grad_att.reshape(seqs, local_rows, HEADS, head_dim)
    delta = jnp.sum(grad_att_heads.astype(F32) * attended, axis=-1)
    lat_sum = jnp.sum(grad_middle.reshape(seqs, local_rows, width_lat), axis=0)

    all_grad_att = lax.all_gather(grad_att, "blk", axis=1, tiled=True).reshape(seqs, rows, HEADS, head_dim)
    stats = lax.all_gather(jnp.concatenate([own_lse, delta], axis=-1), "blk", axis=1, tiled=True)
    stats = jnp.transpose(stats, (0, 2, 1))[..., None]
    g_cols, dw_pair, dq, dgain, dbias, demb = backward_call(
        x_cols, emb, gain_col, bias_col, pair_rows.T, q, q.transpose(0, 2, 1),
        all_grad_att.transpose(0, 2, 1, 3), all_grad_att.transpose(0, 2, 3, 1),
        stats[:, :HEADS], stats[:, HEADS:], mask, pairs, per_shard)

    send = g_cols.reshape(seqs, shards, width // shards, length).transpose(1, 0, 2, 3)
    got = lax.all_to_all(send, "heads", 0, 0, tiled=True)
    grad_inputs = got.reshape(local_seqs, width // shards, length).transpose(2, 0, 1)

    grad_rows = jnp.stack([grad_w_out, grad_w_up, grad_w_down], axis=0).reshape(3, shards, cols, width_lat)
    lat_total = scatter_rows(grad_rows.transpose(1, 0, 2, 3).reshape(-1, width_lat)).astype(F32)
    pair_total = scatter_rows(dw_pair).astype(F32)

    dq_part = lax.psum_scatter(dq.reshape(width_lat, rows).astype(BF16), "heads", scatter_dimension=0, tiled=True)
    query_low = lax.psum(dq_part, REST)
    grad_w_query = dot(lat_low.T, query_low.T)
    lat_mine = lax.dynamic_slice_in_dim(query_low, lax.axis_index("blk") * local_rows, local_rows, 1)
    grad_lat_part = dot(lat_mine.T, w_query.T)
    grad_lat_norm = lax.psum(grad_lat_part.astype(BF16), "heads").astype(F32)
    lat_sum = lax.psum(lat_sum.astype(BF16), ("heads", "items")).astype(F32)
    _, own_normed, own_inverse = norm_keep(lat_f32, lat_gain, lat_bias)
    grad_latents = lat_sum + norm_back(grad_lat_norm, own_normed, own_inverse, lat_gain)
    lat_small = jnp.concatenate([jnp.sum(grad_lat_norm * own_normed, axis=0), jnp.sum(grad_lat_norm, axis=0)])
    lat_small = lax.psum(lat_small, "blk")

    table = jnp.dot(onehot.T, demb[:, :, 0], precision=lax.Precision.HIGHEST)
    small = jnp.concatenate([table.reshape(-1), dgain[:, 0], dbias[:, 0], grad_mid_gain, grad_mid_bias, grad_b_up, grad_b_down])
    small = lax.psum(small, ALL)
    sizes = [table.size, width, width, width_lat, width_lat, width_lat, width_lat]
    ends = [sum(sizes[:i]) for i in range(len(sizes) + 1)]
    table, dgain, dbias, dmid_gain, dmid_bias, db_up, db_down = (small[ends[i]:ends[i + 1]] for i in range(7))
    share = width // shards
    table = lax.dynamic_slice_in_dim(table.reshape(-1, width), me * share, share, 1)
    return (
        mixed_latents,
        grad_inputs,
        grad_latents,
        table,
        lax.dynamic_slice_in_dim(dgain, me * share, share, 0),
        lax.dynamic_slice_in_dim(dbias, me * share, share, 0),
        lat_small[:width_lat],
        lat_small[width_lat:],
        dmid_gain,
        dmid_bias,
        grad_w_query,
        pair_total[:cols].T,
        pair_total[cols:].T,
        lat_total[:cols],
        lat_total[cols:2 * cols].T,
        lax.dynamic_slice_in_dim(db_up, me * cols, cols, 0),
        lat_total[2 * cols:],
        db_down,
    )


def fast_device(inputs, padding, language, lang_table, latents, in_gain, in_bias, lat_gain, lat_bias, mid_gain, mid_bias,
              w_query, w_key, w_value, w_out, w_up, b_up, w_down, b_down, cotangent):
    length, local_seqs, width = inputs.shape
    local_rows, width_lat = latents.shape
    cols = w_query.shape[1]
    head_dim = width_lat // HEADS
    per_shard = cols // head_dim
    shards = lax.axis_size("heads")
    blocks = lax.axis_size("blk")
    rows = local_rows * blocks
    seqs = local_seqs // shards
    me = lax.axis_index("heads")
    first = me * seqs

    vectors = (lat_gain, lat_bias, mid_gain, mid_bias, b_down, in_gain, in_bias, b_up)
    wq_rows = w_query.T
    w_cols, lat_all, pairs, xn, att_cols, lse_cols, queries_t, lat_low, b_up_tiles, x_cols, rows_in, mask, lang_rows, lat_f32, vecs = first_call(
        inputs, padding.T, language, lang_table, vectors, latents, wq_rows,
        (w_key.T, w_value.T, w_out, w_up.T, w_down), rows, seqs)
    mixed, grad_att, stats, grads, vectors, lat_sum = middle_call(att_cols, latents, cotangent, lat_all, b_up_tiles, vecs, lse_cols)
    grad_att = grad_att.reshape(seqs, shards, cols, local_rows)
    g_cols, mixed_latents, pair_total, lat_total, small, grad_latents, lat_small, dq, lat_low_all = second_call(
        x_cols, rows_in, mask, w_cols, queries_t, pairs, xn, grad_att, stats, mixed, lat_low, grads, vectors, lang_rows, lat_sum,
        wq_rows, lat_f32, vecs)
    rest = finish_call(
        lat_total, pair_total, small, lat_small, dq, lat_low_all, g_cols, mixed_latents, grad_latents, lang_table.shape[0])
    rest = [x.T if i in (7, 8, 9, 11) else x for i, x in enumerate(rest)]
    return (rest[-2], rest[-3].transpose(2, 0, 1), rest[-1]) + tuple(rest[:-3])


def solution(mesh):
    placed = (
        P("blk", "items", None), P("blk", "items"), P("items"), P(), P("blk", None), P(), P(), P(), P(), P(), P(),
        P(None, "heads"), P(None, "heads"), P(None, "heads"), P("heads", None), P(None, "heads"), P("heads"),
        P("heads", None), P(), P("items", "blk", None),
    )
    out = (
        P("items", "blk", None), P("blk", "items", "heads"), P("blk", None), P(None, "heads"), P("heads"), P("heads"),
        P(), P(), P(), P(), P(None, "heads"), P(None, "heads"), P(None, "heads"), P("heads", None), P(None, "heads"),
        P("heads"), P("heads", None), P(),
    )
    fits = mesh.shape["blk"] == 2 and mesh.shape["items"] == 4 and mesh.shape["heads"] == 4
    return jax.shard_map(fast_device if fits else general_device, mesh=mesh, in_specs=placed, out_specs=out, check_vma=False)
```

```python
import functools

import jax
import jax.numpy as jnp
from jax import lax
from jax.experimental import pallas as pl
from jax.experimental.pallas import tpu as pltpu
from jax.sharding import PartitionSpec as P

HEADS = 8
EPS = 1e-05
MASKED = -1e30
LOG2E = 1.4426950408889634
F32 = jnp.float32
BF16 = jnp.bfloat16
NT = (((1,), (1,)), ((), ()))
VMEM_LIMIT = 60 * 1024 * 1024


def dot(a, b):
    return jnp.dot(a, b, preferred_element_type=F32)


def dot_nt(a, b):
    return lax.dot_general(a, b, NT, preferred_element_type=F32)


def norm_keep(values, gain, bias):
    average = jnp.mean(values, axis=-1, keepdims=True)
    centred = values - average
    inverse = lax.rsqrt(jnp.mean(centred * centred, axis=-1, keepdims=True) + EPS)
    normed = centred * inverse
    return (normed * gain + bias, normed, inverse)


def norm_back(grad_norm, normed, inverse, gain):
    scaled = grad_norm * gain
    first = jnp.mean(scaled, axis=-1, keepdims=True)
    second = jnp.mean(scaled * normed, axis=-1, keepdims=True)
    return (scaled - first - normed * second) * inverse


def norm_columns(x, emb):
    shifted = x.astype(F32) + emb
    centred = shifted - jnp.mean(shifted, axis=0, keepdims=True)
    inverse = lax.rsqrt(jnp.mean(centred * centred, axis=0, keepdims=True) + EPS)
    return centred * inverse, inverse


def head_rows(h, per_shard, head_dim):
    key = (h // per_shard) * 2 * per_shard + lax.rem(h, per_shard)
    key_at = pl.multiple_of(key * head_dim, head_dim)
    return pl.ds(key_at, head_dim), pl.ds(pl.multiple_of(key_at + per_shard * head_dim, head_dim), head_dim)


def forward_kernel(per_shard, x_ref, emb_ref, gain_ref, bias_ref, w_ref, q_ref, mask_ref, kv_ref, o_ref, lse_ref, xn_ref, stat_ref):
    heads, rows, head_dim = q_ref.shape
    length = x_ref.shape[1]
    piece = min(256, length)

    def norm_step(i, _):
        at = pl.ds(pl.multiple_of(i * piece, piece), piece)
        normed, _unused = norm_columns(x_ref[:, at], emb_ref[...])
        xn_ref[:, at] = (normed * gain_ref[...] + bias_ref[...]).astype(BF16)
        return 0

    lax.fori_loop(0, length // piece, norm_step, 0)
    block = 512 if w_ref.shape[0] % 512 == 0 else 160

    def pair_step(i, _):
        at = pl.ds(pl.multiple_of(i * block, block), block)
        kv_ref[at] = dot(w_ref[at], xn_ref[...]).astype(BF16)
        return 0

    lax.fori_loop(0, w_ref.shape[0] // block, pair_step, 0)
    factor = LOG2E * head_dim ** (-0.5)
    lane = lax.broadcasted_iota(jnp.int32, (rows, 128), 1)
    stat_ref[...] = jnp.zeros_like(stat_ref)

    def head_step(h, _):
        at_key, at_value = head_rows(h, per_shard, head_dim)
        scores = dot(q_ref[h], kv_ref[at_key]) * factor + mask_ref[...]
        top = jnp.max(scores, axis=1, keepdims=True)
        weights = jnp.exp2(scores - top)
        total = jnp.sum(weights, axis=1, keepdims=True)
        out = dot_nt(kv_ref[at_value], weights.astype(BF16))
        stat_ref[...] = jnp.where(lane == h, top + jnp.log2(total), stat_ref[...])
        inverse = jnp.transpose(jnp.broadcast_to(1.0 / total, (rows, 128)))[:1]
        o_ref[pl.ds(pl.multiple_of(h * head_dim, head_dim), head_dim)] = (out * inverse).astype(BF16)
        return 0

    lax.fori_loop(0, heads, head_step, 0)
    lse_ref[...] = jnp.transpose(stat_ref[...])[:heads]


def forward_call(x_cols, emb, gain, bias, w_rows, q, mask, per_shard):
    seqs, width, length = x_cols.shape
    heads, rows, head_dim = q.shape
    pair_rows = w_rows.shape[0]
    whole = pl.BlockSpec(memory_space=pltpu.VMEM)

    def per_seq(*dims):
        return pl.BlockSpec((None,) + dims, lambda s: (s, 0, 0))

    return pl.pallas_call(
        functools.partial(forward_kernel, per_shard),
        grid=(seqs,),
        in_specs=[per_seq(width, length), per_seq(width, 1), whole, whole, whole, whole, per_seq(1, length)],
        out_specs=[per_seq(pair_rows, length), per_seq(heads * head_dim, rows), per_seq(heads, rows)],
        out_shape=[
            jax.ShapeDtypeStruct((seqs, pair_rows, length), BF16),
            jax.ShapeDtypeStruct((seqs, heads * head_dim, rows), BF16),
            jax.ShapeDtypeStruct((seqs, heads, rows), F32),
        ],
        scratch_shapes=[pltpu.VMEM((width, length), BF16), pltpu.VMEM((rows, 128), F32)],
        compiler_params=pltpu.CompilerParams(vmem_limit_bytes=VMEM_LIMIT),
        name="attend",
    )(x_cols, emb, gain, bias, w_rows, q, mask)


def backward_kernel(per_shard, x_ref, emb_ref, gain_ref, bias_ref, w_ref, q_ref, qt_ref, do_ref, dot_ref, lse_ref, delta_ref, mask_ref, kv_ref,
                    g_ref, dw_ref, dq_ref, dgain_ref, dbias_ref, demb_ref, xn_ref, dkv_ref):
    heads, rows, head_dim = q_ref.shape
    width, length = x_ref.shape
    piece = min(256, length)

    @pl.when(pl.program_id(0) == 0)
    def _():
        dw_ref[...] = jnp.zeros_like(dw_ref)
        dq_ref[...] = jnp.zeros_like(dq_ref)
        dgain_ref[...] = jnp.zeros_like(dgain_ref)
        dbias_ref[...] = jnp.zeros_like(dbias_ref)

    def norm_step(i, _):
        at = pl.ds(pl.multiple_of(i * piece, piece), piece)
        normed, _unused = norm_columns(x_ref[:, at], emb_ref[...])
        xn_ref[:, at] = (normed * gain_ref[...] + bias_ref[...]).astype(BF16)
        return 0

    lax.fori_loop(0, length // piece, norm_step, 0)
    scale = head_dim ** (-0.5)
    factor = LOG2E * scale

    def head_step(h, _):
        at_key, at_value = head_rows(h, per_shard, head_dim)
        keys = kv_ref[at_key]
        weights = jnp.exp2(dot(q_ref[h], keys) * factor + mask_ref[...] - lse_ref[h])
        dkv_ref[at_value] = dot(dot_ref[h], weights.astype(BF16)).astype(BF16)
        grad = dot(do_ref[h], kv_ref[at_value]) - delta_ref[h]
        grad = (weights * grad).astype(BF16)
        dkv_ref[at_key] = (dot(qt_ref[h], grad) * scale).astype(BF16)
        dq_ref[h] += dot_nt(keys, grad) * scale
        return 0

    lax.fori_loop(0, heads, head_step, 0)
    block = 512 if dw_ref.shape[0] % 512 == 0 else 160

    def weight_step(i, _):
        at = pl.ds(pl.multiple_of(i * block, block), block)
        dw_ref[at] += dot_nt(dkv_ref[at], xn_ref[...])
        return 0

    lax.fori_loop(0, dw_ref.shape[0] // block, weight_step, 0)

    def byte_step(i, carry):
        at = pl.ds(pl.multiple_of(i * piece, piece), piece)
        grad = dot(w_ref[...], dkv_ref[:, at])
        normed, inverse = norm_columns(x_ref[:, at], emb_ref[...])
        dbias_ref[...] += jnp.sum(grad, axis=1, keepdims=True)
        dgain_ref[...] += jnp.sum(grad * normed, axis=1, keepdims=True)
        scaled = grad * gain_ref[...]
        first = jnp.mean(scaled, axis=0, keepdims=True)
        second = jnp.mean(scaled * normed, axis=0, keepdims=True)
        shifted = (scaled - first - normed * second) * inverse
        g_ref[:, at] = shifted.astype(BF16)
        return carry + jnp.sum(shifted, axis=1, keepdims=True)

    demb_ref[...] = lax.fori_loop(0, length // piece, byte_step, jnp.zeros((width, 1), F32))


def backward_call(x_cols, emb, gain, bias, w, q, qt, grad_out, grad_out_t, lse, delta, mask, pairs, per_shard):
    seqs, width, length = x_cols.shape
    heads, rows, head_dim = q.shape
    pair_rows = w.shape[1]
    whole = pl.BlockSpec(memory_space=pltpu.VMEM)

    def per_seq(*dims):
        return pl.BlockSpec((None,) + dims, lambda s: (s,) + (0,) * len(dims))

    return pl.pallas_call(
        functools.partial(backward_kernel, per_shard),
        grid=(seqs,),
        in_specs=[
            per_seq(width, length), per_seq(width, 1), whole, whole, whole, whole, whole,
            per_seq(heads, rows, head_dim), per_seq(heads, head_dim, rows),
            per_seq(heads, rows, 1), per_seq(heads, rows, 1), per_seq(1, length), per_seq(pair_rows, length),
        ],
        out_specs=[per_seq(width, length), whole, whole, whole, whole, per_seq(width, 1)],
        out_shape=[
            jax.ShapeDtypeStruct((seqs, width, length), BF16),
            jax.ShapeDtypeStruct((pair_rows, width), F32),
            jax.ShapeDtypeStruct((heads, head_dim, rows), F32),
            jax.ShapeDtypeStruct((width, 1), F32),
            jax.ShapeDtypeStruct((width, 1), F32),
            jax.ShapeDtypeStruct((seqs, width, 1), F32),
        ],
        scratch_shapes=[pltpu.VMEM((width, length), BF16), pltpu.VMEM((pair_rows, length), BF16)],
        compiler_params=pltpu.CompilerParams(vmem_limit_bytes=VMEM_LIMIT),
        name="attend_back",
    )(x_cols, emb, gain, bias, w, q, qt, grad_out, grad_out_t, lse, delta, mask, pairs)


def mesh_at(di=None, db=None, dh=None, core=None):
    items, blk, heads = lax.axis_index("items"), lax.axis_index("blk"), lax.axis_index("heads")
    return (items if di is None else di, blk if db is None else db, heads if dh is None else dh)


def places():
    items, blk, heads = lax.axis_index("items"), lax.axis_index("blk"), lax.axis_index("heads")
    core = lax.rem(items, 2)
    return items, blk, heads, items // 2, core


def send(src, dst, sems, recvs, target):
    copy = pltpu.make_async_remote_copy(
        src_ref=src, dst_ref=dst, send_sem=sems, recv_sem=recvs, device_id=target, device_id_type=pl.DeviceIdType.MESH)
    copy.start()
    return copy


def greet(targets):
    barrier = pltpu.get_barrier_semaphore()
    for target in targets:
        pl.semaphore_signal(barrier, inc=1, device_id=target, device_id_type=pl.DeviceIdType.MESH)
    pl.semaphore_wait(barrier, len(targets))


def first_kernel(x_hbm, pad_ref, lang_ref, table_ref, lgain, lbias, mgain, mbias, bdown, igain, ibias, bup, lat_ref, wq_ref, wk_hbm, wv_hbm, wo_hbm, wu_hbm, wd_hbm,
                 wcols_out, all_ref, kv_out, xn_out, att_ref, lse_ref, qt_ref, latn_ref, bup_all, x_out, rows_ref, mask_ref, lang_out, latf_ref, vecs_ref,
                 wcols_ref, pair_shard, lat_shard, x_ref, xbuf, x32, xn_ref, pair_ref, kv_ref, cols_ref, q_ref, o_tmp, o_own, o_send, o_got, stat_ref, stat_send, stat_own, stat_got,
                 pair_ss, pair_rs, lat_ss, lat_rs, q_ss, q_rs, misc_ss, misc_rs, o_ss, o_rs, own_sem, xn_sem, kv_sem, x_sem, w_sem):
    items, blk, me, hi, core = places()
    shards = lax.axis_size("heads")
    seqs, width, length = x_ref.shape
    rows = qt_ref.shape[3]
    local_rows = rows // 2
    heads, _, head_dim = q_ref.shape
    cols = heads * head_dim // shards
    per_shard = heads // shards
    sibling = items + 1 - 2 * core
    other = 1 - blk
    to_sib, to_x, to_y = mesh_at(di=sibling), mesh_at(db=other), mesh_at(di=(1 - hi) * 2 + core)
    z_of = [lax.rem(me + d, shards) for d in range(shards)]
    z_back = [lax.rem(me + shards - d, shards) for d in range(shards)]
    weights = [pltpu.make_async_copy(src, dst, w_sem.at[n]) for n, (src, dst) in enumerate((
        (wk_hbm, pair_shard.at[0]), (wv_hbm, pair_shard.at[1]), (wo_hbm, lat_shard.at[0]), (wu_hbm, lat_shard.at[1]), (wd_hbm, lat_shard.at[2])))]
    for copy in weights:
        copy.start()
    depth, step_rows = xbuf.shape[:2]

    def load_bytes(c):
        return pltpu.make_async_copy(x_hbm.at[pl.ds(c * step_rows, step_rows)], xbuf.at[c % depth], x_sem.at[c % depth])

    for c in range(depth):
        load_bytes(c).start()
    greet([to_sib, to_x, to_y] + [mesh_at(dh=z_of[d]) for d in range(1, shards)])

    share = cols // 4
    chip = hi * 2 + blk
    chip_x, chip_y, chip_xy = hi * 2 + other, (1 - hi) * 2 + blk, (1 - hi) * 2 + other

    def region(ref, shard, chip_at, lanes_of):
        half = ref.shape[2] // 2
        return ref.at[:, pl.ds(pl.multiple_of(shard * cols + chip_at * share, 16), share), pl.ds(pl.multiple_of(lanes_of * half, 128), half)]

    def lane_half(ref, shard, lanes_of):
        half = ref.shape[2] // 2
        return ref.at[:, pl.ds(pl.multiple_of(shard * cols, 16), cols), pl.ds(pl.multiple_of(lanes_of * half, 128), half)]

    pending = []
    local = []
    near = me + 1 - 2 * lax.rem(me, 2)
    far, cross = lax.rem(me + 2, 4), lax.rem(near + 2, 4)
    shard_at = [me, near, far, cross]
    double = {"l1": (0, blk, to_x), "l2": (1, hi, to_y)}

    def band(ref, shard, part):
        half = ref.shape[2] // 2
        at = pl.ds(pl.multiple_of(shard * cols + part * 2 * share, 16), 2 * share)
        return ref.at[:, at, pl.ds(pl.multiple_of(core * half, 128), half)]

    kinds = {"pair": (pair_shard, pair_ref, pair_ss, pair_rs)}
    for m in range(3):
        one = pl.ds(m, 1)
        kinds[f"l{m}"] = (lat_shard.at[one], all_ref.at[one], lat_ss.at[m], lat_rs.at[m])

    def recv(kind, d, stage, where):
        _, dst, ss, rs = kinds[kind]
        pltpu.make_async_remote_copy(src_ref=where, dst_ref=where, send_sem=ss.at[d, stage], recv_sem=rs.at[d, stage],
                                     device_id=to_sib, device_id_type=pl.DeviceIdType.MESH).wait_recv()

    def out_z(kind, d):
        src, dst, ss, rs = kinds[kind]
        def own_part(ref, shard):
            return band(ref, shard, double[kind][1]) if kind in double else region(ref, shard, chip, core)

        if d == 3:
            block = own_part(dst, far)
            pending.append(send(block, block, ss.at[d, 0], rs.at[d, 0], mesh_at(dh=near)))
        else:
            pending.append(send(own_part(src, 0), own_part(dst, me), ss.at[d, 0], rs.at[d, 0], mesh_at(dh=shard_at[d])))

    def after_z(kind, d):
        _, dst, ss, rs = kinds[kind]
        if kind in double:
            mine = band(dst, shard_at[d], double[kind][1])
            recv(kind, d, 0, mine)
            pending.append(send(mine, mine, ss.at[d, 1], rs.at[d, 1], double[kind][2]))
            return
        mine = region(dst, shard_at[d], chip, core)
        recv(kind, d, 0, mine)
        pending.append(send(mine, mine, ss.at[d, 1], rs.at[d, 1], to_x))
        pending.append(send(mine, mine, ss.at[d, 2], rs.at[d, 2], to_y))

    def after_x(kind, d):
        _, dst, ss, rs = kinds[kind]
        got = region(dst, shard_at[d], chip_x, core)
        recv(kind, d, 1, got)
        pending.append(send(got, got, ss.at[d, 3], rs.at[d, 3], to_y))

    def after_y(kind, d):
        _, dst, ss, rs = kinds[kind]
        if kind in double:
            recv(kind, d, 1, band(dst, shard_at[d], 1 - double[kind][1]))
        else:
            recv(kind, d, 2, region(dst, shard_at[d], chip_y, core))
            recv(kind, d, 3, region(dst, shard_at[d], chip_xy, core))
        half = lane_half(dst, shard_at[d], core)
        pending.append(send(half, half, ss.at[d, 4], rs.at[d, 4], to_sib))

    def after_sib(kind, d):
        _, dst, ss, rs = kinds[kind]
        recv(kind, d, 4, lane_half(dst, shard_at[d], 1 - core))

    for copy in weights:
        copy.wait()
    own_pair = pltpu.make_async_copy(pair_shard, pair_ref.at[:, pl.ds(pl.multiple_of(me * cols, 16), cols)], own_sem.at[0])
    own_lat = pltpu.make_async_copy(lat_shard, all_ref.at[:, pl.ds(pl.multiple_of(me * cols, 16), cols)], own_sem.at[1])
    own_pair.start()
    own_lat.start()
    my_rows = pl.ds(pl.multiple_of(blk * local_rows, 128), local_rows)
    other_rows = pl.ds(pl.multiple_of(other * local_rows, 128), local_rows)

    vecs_ref[...] = jnp.zeros_like(vecs_ref)
    for i, vector in enumerate((lgain, lbias, mgain, mbias, bdown, igain, ibias, bup)):
        vecs_ref[i:i + 1, :vector.shape[0]] = vector[...].reshape(1, vector.shape[0])
    rows_ref[0:1] = vecs_ref[5:6, :width]
    rows_ref[1:2] = vecs_ref[6:7, :width]
    rows_ref[4:8] = jnp.zeros((4, width), F32)
    lang_out[...] = jnp.zeros_like(lang_out)
    for s in range(seqs):
        lang = lang_ref[me * seqs + s]
        picked = lax.broadcasted_iota(jnp.int32, table_ref.shape, 0) == lang
        rows_ref[2 + s:3 + s] = jnp.sum(jnp.where(picked, table_ref[...].astype(F32), 0.0), axis=0, keepdims=True)
        lang_out[s:s + 1] = jnp.where(lax.broadcasted_iota(jnp.int32, (1, 128), 1) == lang, 1.0, 0.0)
        mask_ref[s] = jnp.where(pad_ref[pl.ds(me * seqs + s, 1)] > 0, 0.0, MASKED)

    def queries_start():
        latf_ref[...] = lat_ref[...].astype(F32)
        lat_out, _, _ = norm_keep(latf_ref[...], vecs_ref[0:1], vecs_ref[1:2])
        lat_low = lat_out.astype(BF16)
        latn_ref[...] = lat_low
        at_head = pl.ds(pl.multiple_of(core * head_dim, 16), head_dim)
        qt_ref[core, me, :, my_rows] = dot_nt(wq_ref[at_head], lat_low).astype(BF16)
        bup_ref = vecs_ref.at[:, pl.ds(0, bup_all.shape[2])]
        bup_all[me] = bup_ref[...]
        for d in range(1, shards):
            my_q = qt_ref.at[core, me, :, my_rows]
            pending.append(send(my_q, my_q, q_ss.at[0, d], q_rs.at[0, d], mesh_at(dh=z_back[d])))
        for d in range(1, shards):
            pending.append(send(bup_ref, bup_all.at[me], misc_ss.at[d], misc_rs.at[d], mesh_at(dh=z_back[d])))

    cols_ref[...] = jnp.transpose(rows_ref[...])
    def pick_bytes(c):
        load_bytes(c).wait()
        at = slice(c * step_rows, (c + 1) * step_rows)
        for j in range(x32.shape[0]):
            lanes = slice(j * 128, (j + 1) * 128)
            x32[j] = xbuf[c % depth, :, :, lanes].astype(F32).reshape(x32.shape[1:])
            for s in range(seqs):
                x_ref[s, lanes, at] = jnp.transpose(x32[j, pl.ds(me * seqs + s, step_rows, stride=x_hbm.shape[1])]).astype(BF16)
        if (c + depth) * step_rows < length:
            load_bytes(c + depth).start()
        if (c + 1) * step_rows == length:
            copy = pltpu.make_async_copy(x_ref, x_out, x_sem.at[depth])
            copy.start()
            local.append(copy)


    def queries_z():
        for d in range(1, shards):
            wait_plain(qt_ref.at[core, z_of[d], :, my_rows], q_ss.at[0, d], q_rs.at[0, d])
        part = qt_ref.at[core, :, :, my_rows]
        pending.append(send(part, part, q_ss.at[1, 0], q_rs.at[1, 0], to_x))

    def queries_x():
        wait_plain(qt_ref.at[core, :, :, other_rows], q_ss.at[1, 0], q_rs.at[1, 0])
        pending.append(send(qt_ref.at[core], qt_ref.at[core], q_ss.at[1, 1], q_rs.at[1, 1], to_sib))

    def queries_sib():
        wait_plain(qt_ref.at[1 - core], q_ss.at[1, 1], q_rs.at[1, 1])

    def wait_plain(where, ss, rs):
        pltpu.make_async_remote_copy(src_ref=where, dst_ref=where, send_sem=ss, recv_sem=rs,
                                     device_id=to_sib, device_id_type=pl.DeviceIdType.MESH).wait_recv()

    piece = min(256, length)

    def norm_bytes(s):
        def norm_step(i, _):
            at = pl.ds(pl.multiple_of(i * piece, piece), piece)
            normed, _unused = norm_columns(x_ref[s, :, at], cols_ref[:, 2 + s:3 + s])
            xn_ref[s, :, at] = (normed * cols_ref[:, 0:1] + cols_ref[:, 1:2]).astype(BF16)
            return 0
        lax.fori_loop(0, length // piece, norm_step, 0)
        copy = pltpu.make_async_copy(xn_ref.at[s], xn_out.at[s], xn_sem.at[s])
        copy.start()
        local.append(copy)

    def project(d):
        at = pl.ds(pl.multiple_of(shard_at[d] * cols, 16), cols)

        def step(i, _):
            s, part = i // 2, lax.rem(i, 2)
            kv_ref[s, part, at] = dot(pair_ref[part, at], xn_ref[s]).astype(BF16)
            return 0
        lax.fori_loop(0, 2 * seqs, step, 0)
        copy = pltpu.make_async_copy(kv_ref.at[:, :, at], kv_out.at[:, :, at], kv_sem.at[d])
        copy.start()
        local.append(copy)

    factor = LOG2E * head_dim ** (-0.5)
    lane = lax.broadcasted_iota(jnp.int32, (rows, 128), 1)
    stat_ref[...] = jnp.zeros_like(stat_ref)

    def turn_queries(d):
        for j in range(per_shard):
            h = shard_at[d] * per_shard + j
            q_ref[h] = jnp.transpose(qt_ref[j, shard_at[d]])

    def attend(d, s):
        def head_step(j, _):
            h = shard_at[d] * per_shard + j
            at = pl.ds(pl.multiple_of(h * head_dim, 16), head_dim)
            scores = dot(q_ref[h], kv_ref[s, 0, at]) * factor + mask_ref[s]
            top = jnp.max(scores, axis=1, keepdims=True)
            weights = jnp.exp2(scores - top)
            total = jnp.sum(weights, axis=1, keepdims=True)
            out = dot_nt(kv_ref[s, 1, at], weights.astype(BF16))
            stat_ref[s] = jnp.where(lane == h, top + jnp.log2(total), stat_ref[s])
            inverse = jnp.transpose(jnp.broadcast_to(1.0 / total, (rows, 128)))[:1]
            o_tmp[...] = out * inverse
            o_own[s, at] = o_tmp[:, my_rows]
            o_send[s, at] = o_tmp[:, other_rows].astype(BF16)
            return 0
        lax.fori_loop(0, per_shard, head_step, 0)
        part = pl.ds(pl.multiple_of(shard_at[d] * cols, 16), cols)
        pending.append(send(o_send.at[s, part], o_got.at[s, part], o_ss.at[d, s], o_rs.at[d, s], to_x))

    def stats_send():
        for s in range(seqs):
            at = pl.ds(s * heads, heads)
            stats = jnp.transpose(stat_ref[s])[:heads]
            stat_send[...] = stats
            stat_own[at] = stat_send[:, my_rows]
            stat_got[0, at] = stat_send[:, other_rows]
        pending.append(send(stat_got.at[0], stat_got.at[1], o_ss.at[shards, 0], o_rs.at[shards, 0], to_x))

    def turn_weights():
        block = 256
        for part in range(2):
            for i in range(pair_ref.shape[1] // block):
                wcols_ref[part, :, i * block:(i + 1) * block] = jnp.transpose(pair_ref[part, i * block:(i + 1) * block])
        copy = pltpu.make_async_copy(wcols_ref, wcols_out, w_sem.at[5])
        copy.start()
        local.append(copy)

    out_z("pair", 1)
    out_z("pair", 2)
    out_z("l0", 1)
    pick_bytes(0)
    pick_bytes(1)
    pick_bytes(2)
    pick_bytes(3)
    pick_bytes(4)
    pick_bytes(5)
    pick_bytes(6)
    after_z("l0", 1)
    out_z("l0", 2)
    pick_bytes(7)
    after_z("pair", 1)
    after_z("pair", 2)
    out_z("pair", 3)
    norm_bytes(0)
    norm_bytes(1)
    queries_start()
    after_x("l0", 1)
    out_z("l1", 1)
    own_pair.wait()
    project(0)
    after_z("pair", 3)
    after_z("l0", 2)
    out_z("l0", 3)
    out_z("l1", 2)
    after_x("pair", 1)
    after_x("pair", 2)
    queries_z()
    after_x("l0", 2)
    after_y("l0", 1)
    after_x("pair", 3)
    after_sib("l0", 1)
    after_z("l0", 3)
    out_z("l2", 1)
    queries_x()
    queries_sib()
    turn_queries(0)
    attend(0, 0)
    after_x("l0", 3)
    after_z("l1", 1)
    after_z("l1", 2)
    out_z("l1", 3)
    attend(0, 1)
    after_y("pair", 1)
    after_y("pair", 2)
    out_z("l2", 2)
    after_z("l2", 1)
    after_y("l0", 2)
    after_y("pair", 3)
    after_sib("pair", 1)
    after_sib("pair", 2)
    project(1)
    after_y("l0", 3)
    after_sib("l0", 2)
    project(2)
    after_sib("pair", 3)
    after_z("l1", 3)
    project(3)
    after_sib("l0", 3)
    after_z("l2", 2)
    after_y("l2", 1)
    out_z("l2", 3)
    turn_queries(1)
    attend(1, 0)
    after_y("l1", 1)
    after_y("l1", 2)
    attend(1, 1)
    turn_queries(2)
    attend(2, 0)
    attend(2, 1)
    after_z("l2", 3)
    after_y("l2", 2)
    turn_queries(3)
    attend(3, 0)
    after_y("l1", 3)
    attend(3, 1)
    after_sib("l1", 1)
    after_sib("l1", 2)
    after_sib("l2", 1)
    after_sib("l2", 2)
    stats_send()
    turn_weights()
    after_y("l2", 3)
    after_sib("l1", 3)
    after_sib("l2", 3)

    wait_plain(stat_got.at[1], o_ss.at[shards, 0], o_rs.at[shards, 0])
    own_lse, got_lse = stat_own[...], stat_got[1]
    top = jnp.maximum(own_lse, got_lse)
    own_share, got_share = jnp.exp2(own_lse - top), jnp.exp2(got_lse - top)
    total = own_share + got_share
    lse = top + jnp.log2(total)
    own_share, got_share = own_share / total, got_share / total
    for s in range(seqs):
        lse_ref[s] = lse[s * heads:(s + 1) * heads]
        for d in range(shards):
            part = pl.ds(pl.multiple_of(shard_at[d] * cols, 16), cols)
            wait_plain(o_got.at[s, part], o_ss.at[d, s], o_rs.at[d, s])
    for s in range(seqs):
        for h in range(heads):
            at = slice(h * head_dim, (h + 1) * head_dim)
            n = s * heads + h
            att_ref[s, at] = o_own[s, at] * own_share[n:n + 1] + o_got[s, at].astype(F32) * got_share[n:n + 1]
    for d in range(1, shards):
        wait_plain(bup_all.at[z_of[d]], misc_ss.at[d], misc_rs.at[d])
    own_lat.wait()
    for copy in local:
        copy.wait()
    for copy in pending:
        copy.wait_send()


def first_call(inputs, padding, language, table, vectors, latents, wq_rows, weights, rows, seqs):
    length, local_seqs, width = inputs.shape
    local_rows, width_lat = latents.shape
    shards = lax.axis_size("heads")
    heads = HEADS
    head_dim = width_lat // heads
    whole = pl.BlockSpec(memory_space=pltpu.VMEM)
    hbm = pl.BlockSpec(memory_space=pl.ANY)
    out = jax.ShapeDtypeStruct
    sem = pltpu.SemaphoreType.DMA
    return pl.pallas_call(
        first_kernel,
        in_specs=[hbm, whole, pl.BlockSpec(memory_space=pltpu.SMEM)] + [whole] * 11 + [hbm] * 5,
        out_specs=[hbm, hbm, hbm, hbm] + [whole] * 5 + [hbm] + [whole] * 5,
        out_shape=[
            out((2, width, width_lat), BF16),
            out((3, width_lat, width_lat), BF16),
            out((seqs, 2, width_lat, length), BF16),
            out((seqs, width, length), BF16),
            out((seqs, width_lat, local_rows), F32),
            out((seqs, heads, local_rows), F32),
            out((heads // shards, shards, head_dim, rows), BF16),
            out((local_rows, width_lat), BF16),
            out((shards, 8, 384), F32),
            out((seqs, width, length), BF16),
            out((8, width), F32),
            out((seqs, 1, length), F32),
            out((8, 128), F32),
            out((local_rows, width_lat), F32),
            out((8, width_lat), F32),
        ],
        scratch_shapes=[
            pltpu.VMEM((2, width, width_lat), BF16),
            pltpu.VMEM((2, width_lat // shards, width), BF16),
            pltpu.VMEM((3, width_lat // shards, width_lat), BF16),
            pltpu.VMEM((seqs, width, length), BF16),
            pltpu.VMEM((4, 128, local_seqs, width), BF16),
            pltpu.VMEM((width // 128, 128 * local_seqs, 128), F32),
            pltpu.VMEM((seqs, width, length), BF16),
            pltpu.VMEM((2, width_lat, width), BF16),
            pltpu.VMEM((seqs, 2, width_lat, length), BF16),
            pltpu.VMEM((width, 8), F32),
            pltpu.VMEM((heads, rows, head_dim), BF16),
            pltpu.VMEM((head_dim, rows), F32),
            pltpu.VMEM((seqs, width_lat, local_rows), F32),
            pltpu.VMEM((seqs, width_lat, local_rows), BF16),
            pltpu.VMEM((seqs, width_lat, local_rows), BF16),
            pltpu.VMEM((seqs, rows, 128), F32),
            pltpu.VMEM((heads, rows), F32),
            pltpu.VMEM((seqs * heads, local_rows), F32),
            pltpu.VMEM((2, seqs * heads, local_rows), F32),
            sem((shards, 5)), sem((shards, 5)), sem((3, shards, 5)), sem((3, shards, 5)),
            sem((2, shards)), sem((2, shards)), sem((shards,)), sem((shards,)),
            sem((shards + 1, seqs)), sem((shards + 1, seqs)), sem((2,)), sem((seqs,)), sem((shards,)), sem((5,)), sem((6,)),
        ],
        compiler_params=pltpu.CompilerParams(vmem_limit_bytes=VMEM_LIMIT, collective_id=1, has_side_effects=True),
        name="first",
    )(inputs, padding, language, table, *vectors, latents, wq_rows, *weights)


class Reduce:
    def __init__(self, src, half, got_sib, got_chip, got_z, out, ss, rs, pending, x_first=True, stage=None, stage_sem=None):
        self.src, self.half, self.got_sib, self.got_chip, self.got_z, self.out = src, half, got_sib, got_chip, got_z, out
        self.ss, self.rs, self.pending, self.x_first = ss, rs, pending, x_first
        self.stage, self.stage_sem, self.kept = stage, stage_sem, None
        self.split = src is not None and src.shape[3] == half.shape[3]
        items, blk, self.me, hi, self.core = places()
        self.shards = lax.axis_size("heads")
        other = 1 - blk
        self.chip = hi * 2 + blk
        self.chip_x, self.chip_y, self.chip_xy = hi * 2 + other, (1 - hi) * 2 + blk, (1 - hi) * 2 + other
        self.to_x, self.to_y = mesh_at(db=other), mesh_at(di=(1 - hi) * 2 + self.core)
        self.to_sib = mesh_at(di=items + 1 - 2 * self.core)
        self.n, _, self.cols, self.width = half.shape
        self.share = self.cols // 4
        self.near = self.me + 1 - 2 * lax.rem(self.me, 2)
        self.far, self.cross = lax.rem(self.me + 2, 4), lax.rem(self.near + 2, 4)

    def rows(self, chip):
        return pl.ds(pl.multiple_of(chip * self.share, 16), self.share)

    def lanes(self, core):
        return pl.ds(pl.multiple_of(core * self.width, 128), self.width)

    def go(self, src, dst, i, target):
        self.pending.append(send(src, dst, self.ss.at[i], self.rs.at[i], target))

    def arrived(self, where, i):
        pltpu.make_async_remote_copy(src_ref=where, dst_ref=where, send_sem=self.ss.at[i], recv_sem=self.rs.at[i],
                                     device_id=self.to_sib, device_id_type=pl.DeviceIdType.MESH).wait_recv()

    def start(self):
        theirs = self.src if self.split else self.src.at[:, :, :, self.lanes(1 - self.core)]
        self.go(theirs, self.got_sib, 0, self.to_sib)

    def join_sib(self):
        self.arrived(self.got_sib, 0)

        def step(i, _):
            n, h = i // self.shards, lax.rem(i, self.shards)
            own = self.half[n, h] if self.split else self.src[n, h, :, self.lanes(self.core)]
            self.half[n, h] = (own.astype(F32) + self.got_sib[n, h].astype(F32)).astype(self.half.dtype)
            return 0
        lax.fori_loop(0, self.n * self.shards, step, 0)

    def send_chips(self):
        low, high = pl.ds(0, 2), pl.ds(2, 2)
        self.go(self.half.at[:, low, self.rows(self.chip_x)], self.got_chip.at[0], 1, self.to_x)
        self.go(self.half.at[:, high, self.rows(self.chip_y)], self.got_chip.at[2], 3, self.to_y)
        self.go(self.half.at[:, low, self.rows(self.chip_xy)], self.got_chip.at[1], 2, self.to_x)
        self.go(self.half.at[:, high, self.rows(self.chip_xy)], self.got_chip.at[3], 4, self.to_y)

    def add(self, slot, first, rows):
        self.arrived(self.got_chip.at[slot], 1 + slot)
        for n in range(self.n):
            for h in range(2):
                total = self.half[n, first + h, rows].astype(F32) + self.got_chip[slot, n, h].astype(F32)
                self.half[n, first + h, rows] = total.astype(self.half.dtype)

    def join_first(self):
        self.add(1, 0, self.rows(self.chip_y))
        self.go(self.half.at[:, pl.ds(0, 2), self.rows(self.chip_y)], self.got_chip.at[4], 5, self.to_y)
        self.add(3, 2, self.rows(self.chip_x))
        self.go(self.half.at[:, pl.ds(2, 2), self.rows(self.chip_x)], self.got_chip.at[5], 6, self.to_x)
        self.add(0, 0, self.rows(self.chip))
        self.add(2, 2, self.rows(self.chip))

    def join_chips(self):
        mine = self.rows(self.chip)
        self.add(4, 0, mine)
        self.add(5, 2, mine)
        for i, shard in enumerate((self.near, self.cross)):
            self.go(self.half.at[:, shard, mine], self.got_z.at[i], 7 + i, mesh_at(dh=self.near))

    def join_near(self):
        mine = self.rows(self.chip)
        for i, shard in enumerate((self.me, self.far)):
            self.arrived(self.got_z.at[i], 7 + i)
            for n in range(self.n):
                total = self.half[n, shard, mine].astype(F32) + self.got_z[i, n].astype(F32)
                self.half[n, shard, mine] = total.astype(self.half.dtype)
        self.go(self.half.at[:, self.far, mine], self.got_z.at[2], 9, mesh_at(dh=self.far))

    def join_z(self):
        self.arrived(self.got_z.at[2], 9)
        mine = self.rows(self.chip)
        for n in range(self.n):
            total = self.half[n, self.me, mine].astype(F32) + self.got_z[2, n].astype(F32)
            if self.stage is None:
                self.out[n, mine, self.lanes(self.core)] = total.astype(self.out.dtype)
            else:
                self.stage[n] = total.astype(self.out.dtype)
        src = self.piece(self.chip)
        if self.stage is not None:
            self.kept = pltpu.make_async_copy(self.stage, src, self.stage_sem)
            self.kept.start()
            src = self.stage
        self.go(src, self.piece(self.chip), 10, self.to_x)
        self.go(src, self.piece(self.chip), 11, self.to_y)

    def piece(self, chip):
        return self.out.at[:, self.rows(chip), self.lanes(self.core)]

    def pass_on(self, chip, i, target):
        self.go(self.piece(chip), self.piece(chip), i, target)

    def share_chips(self):
        if self.x_first:
            self.arrived(self.piece(self.chip_x), 10)
            self.pass_on(self.chip_x, 12, self.to_y)
        else:
            self.arrived(self.piece(self.chip_y), 11)
            self.pass_on(self.chip_y, 12, self.to_x)

    def share_sib(self):
        if self.x_first:
            self.arrived(self.piece(self.chip_y), 11)
        else:
            self.arrived(self.piece(self.chip_x), 10)
        self.arrived(self.piece(self.chip_xy), 12)
        if self.kept is not None:
            self.kept.wait()
        half = self.out.at[:, :, self.lanes(self.core)]
        self.go(half, half, 13, self.to_sib)

    def finish(self):
        self.arrived(self.out.at[:, :, self.lanes(1 - self.core)], 13)


def second_kernel(x_hbm, rows_ref, mask_ref, w_hbm, qt_ref, kv_hbm, xn_hbm, do_in, stat_in, mixed_in, lat_in, grads_hbm, vec_in, lang_in, latsum_in, wq_ref, lat_raw, lgain_ref,
                  g_out, mixed_out, dw_out, dlat_out, small_out, glat_out, vec_out, dq_out, latn_ref,
                  w_ref, x_ref, xn_ref, cols_ref, kv_ref, dkv_ref, q_ref, do_ref, stat_ref, stat_cols, dq_ref, dw_ref, dw_tmp,
                  g_half, g_chip, g_z, w_half, w_sib, w_chip, w_z, q_half, q_sib, q_chip, q_z, s_half, s_sib, s_chip, s_z,
                  small_ref, s_ref, l_sib, l_half, l_y, l_sum, l_z, l_tot, lat8_ref,
                  g_stage, w_stage, tq_ref, t_part, t_got, t_z, y_buf, c_buf, x_buf,
                  g_ss, g_rs, w_ss, w_rs, q_ss, q_rs, s_ss, s_rs, l_ss, l_rs, t_ss, t_rs, do_ss, do_rs, misc_ss, misc_rs, mix_ss, mix_rs, a_ss, a_rs, load_sem, kv_sem, stage_sem):
    items, blk, me, hi, core = places()
    shards = lax.axis_size("heads")
    seqs, width, length = x_ref.shape
    heads, rows, head_dim = q_ref.shape
    local_rows = rows // 2
    per_shard = heads // shards
    cols = per_shard * head_dim
    stat_rows = stat_in.shape[0]
    other = 1 - blk
    to_x, to_sib = mesh_at(db=other), mesh_at(di=items + 1 - 2 * core)
    to_y = mesh_at(di=(1 - hi) * 2 + core)
    z_of = [lax.rem(me + d, shards) for d in range(shards)]
    z_back = [lax.rem(me + shards - d, shards) for d in range(shards)]
    my_rows = pl.ds(pl.multiple_of(blk * local_rows, 128), local_rows)
    other_rows = pl.ds(pl.multiple_of(other * local_rows, 128), local_rows)
    pending = []
    dot_ref = w_sib.at[:, :, :, pl.ds(0, rows)]
    grads = [Reduce(None, g_half.at[pl.ds(m, 1)], None, g_chip.at[:, pl.ds(m, 1)], g_z.at[m], dlat_out.at[pl.ds(m, 1)], g_ss.at[m], g_rs.at[m], pending, m != 1,
                        g_stage.at[pl.ds(m, 1)], stage_sem.at[m])
             for m in range(3)]
    pair = [Reduce(dw_ref.at[pl.ds(m, 1)], w_half.at[pl.ds(m, 1)], w_sib.at[pl.ds(m, 1)], w_chip.at[:, pl.ds(m, 1)], w_z.at[m],
                   dw_out.at[pl.ds(m, 1)], w_ss.at[m], w_rs.at[m], pending, m == 0, w_stage.at[pl.ds(m, 1)], stage_sem.at[3 + m]) for m in range(2)]
    query = Reduce(dq_ref, q_half, q_sib, q_chip, q_z, dq_out, q_ss, q_rs, pending, False)
    small = Reduce(s_ref, s_half, s_sib, s_chip, s_z, small_out, s_ss, s_rs, pending)
    greet([to_sib, to_x, to_y] + [mesh_at(dh=z_of[d]) for d in range(1, shards)])

    def arrived(where, ss, rs):
        pltpu.make_async_remote_copy(src_ref=where, dst_ref=where, send_sem=ss, recv_sem=rs,
                                     device_id=to_sib, device_id_type=pl.DeviceIdType.MESH).wait_recv()

    pending.append(send(stat_in, stat_ref.at[pl.ds(0, stat_rows), my_rows], misc_ss.at[0], misc_rs.at[0], to_x))

    def send_do(s):
        pending.append(send(do_in.at[s], dot_ref.at[s, :, :, my_rows], do_ss.at[s], do_rs.at[s], to_x))

    near = me + 1 - 2 * lax.rem(me, 2)
    far, cross = lax.rem(me + 2, 4), lax.rem(near + 2, 4)

    def mixed_pass(block, i, there):
        pending.append(send(mixed_out.at[block], mixed_out.at[block], mix_ss.at[i], mix_rs.at[i], mesh_at(dh=there)))

    def mixed_far():
        mixed_pass(me * seqs + 1, 0, far)

    def mixed_near():
        mixed_pass(me * seqs + 1, 1, near)

    def mixed_cross_0():
        mixed_pass(far * seqs, 2, near)

    def mixed_cross_1():
        arrived(mixed_out.at[far * seqs + 1], mix_ss.at[0], mix_rs.at[0])
        mixed_pass(far * seqs + 1, 3, near)

    def latents_share():
        pending.append(send(lat_in, latn_ref.at[my_rows], misc_ss.at[1], misc_rs.at[1], to_x))

    loads = [
        pltpu.make_async_copy(xn_hbm, xn_ref, load_sem.at[0]),
        pltpu.make_async_copy(x_hbm, x_ref, load_sem.at[1]),
        pltpu.make_async_copy(grads_hbm, g_half, load_sem.at[2]),
        pltpu.make_async_copy(lat_raw.at[pl.ds(pl.multiple_of(core * 64 + hi * 32 + me * 8, 8), 8)], lat8_ref, load_sem.at[4]),
    ]
    own_sum = pltpu.make_async_copy(latsum_in.at[pl.ds(pl.multiple_of(core * (local_rows // 2), 8), local_rows // 2)], l_half, load_sem.at[13])
    own_sum.start()
    own_do = pltpu.make_async_copy(do_in, dot_ref.at[:, :, :, my_rows], load_sem.at[5])

    def load_pair(n, start):
        s, h = n // heads, lax.rem(n, heads)
        slot = lax.rem(n, 2)
        copy = pltpu.make_async_copy(kv_hbm.at[s, :, pl.ds(pl.multiple_of(h * head_dim, 16), head_dim)], kv_ref.at[slot], kv_sem.at[slot])
        copy.start() if start else copy.wait()

    load_pair(0, True)
    own_do.start()
    own_w = pltpu.make_async_copy(w_hbm, w_ref, load_sem.at[14])
    for copy in loads + [own_w]:
        copy.start()

    def prepare():
        latn_ref[my_rows] = lat_in[...]
        cols_ref[...] = jnp.transpose(rows_ref[...])
        stat_ref[:stat_rows, my_rows] = stat_in[...]
        stat_ref[stat_rows:] = jnp.zeros((128 - stat_rows, rows), F32)
        for h in range(heads):
            q_ref[h] = jnp.transpose(qt_ref[h % per_shard, h // per_shard])
        dq_ref[...] = jnp.zeros_like(dq_ref)
        small_ref[...] = jnp.zeros_like(small_ref)

    def stats_ready():
        arrived(stat_ref.at[pl.ds(0, stat_rows), other_rows], misc_ss.at[0], misc_rs.at[0])
        stat_cols[...] = jnp.transpose(stat_ref[...])

    scale = head_dim ** (-0.5)
    factor = LOG2E * scale
    lane = lax.broadcasted_iota(jnp.int32, (rows, 128), 1)

    def turn_grads(s):
        arrived(dot_ref.at[s, :, :, other_rows], do_ss.at[s], do_rs.at[s])
        for h in range(heads):
            inner = h % per_shard * head_dim
            do_ref[h] = jnp.transpose(dot_ref[s, h // per_shard, inner:inner + head_dim])

    def head_steps(s, group):
        def head_step(h, _):
            n = s * heads + h
            slot = lax.rem(n, 2)
            load_pair(n, False)

            @pl.when(n + 1 < seqs * heads)
            def _():
                load_pair(n + 1, True)

            at = pl.ds(pl.multiple_of(h * head_dim, 16), head_dim)
            lse = jnp.sum(jnp.where(lane == s * 2 * heads + h, stat_cols[...], 0.0), axis=1, keepdims=True)
            delta = jnp.sum(jnp.where(lane == s * 2 * heads + heads + h, stat_cols[...], 0.0), axis=1, keepdims=True)
            keys = kv_ref[slot, 0]
            weights = jnp.exp2(dot(q_ref[h], keys) * factor + mask_ref[s] - lse)
            part = pl.ds(pl.multiple_of(lax.rem(h, per_shard) * head_dim, 16), head_dim)
            dkv_ref[s, 1, at] = dot(dot_ref[s, h // per_shard, part], weights.astype(BF16)).astype(BF16)
            grad = dot(do_ref[h], kv_ref[slot, 1]) - delta
            grad = (weights * grad).astype(BF16)
            dkv_ref[s, 0, at] = (dot(qt_ref[lax.rem(h, per_shard), h // per_shard], grad) * scale).astype(BF16)
            dq_ref[0, h // per_shard, part] += dot_nt(keys, grad) * scale
            return 0

        lax.fori_loop(2 * group, 2 * group + 2, head_step, 0)

    piece = min(256, length)

    def byte_steps(s):
        def byte_step(i, carry):
            at = pl.ds(pl.multiple_of(i * piece, piece), piece)
            grad = dot(w_ref[0], dkv_ref[s, 0, :, at]) + dot(w_ref[1], dkv_ref[s, 1, :, at])
            normed, inverse = norm_columns(x_ref[s, :, at], cols_ref[:, 2 + s:3 + s])
            small_ref[:, 0:1] += jnp.sum(grad * normed, axis=1, keepdims=True)
            small_ref[:, 1:2] += jnp.sum(grad, axis=1, keepdims=True)
            scaled = grad * cols_ref[:, 0:1]
            first = jnp.mean(scaled, axis=0, keepdims=True)
            second = jnp.mean(scaled * normed, axis=0, keepdims=True)
            shifted = (scaled - first - normed * second) * inverse
            x_ref[s, :, at] = shifted.astype(BF16)
            return carry + jnp.sum(shifted, axis=1, keepdims=True)

        small_ref[:, 2 + s:3 + s] = lax.fori_loop(0, length // piece, byte_step, jnp.zeros((width, 1), F32))
        share = width // shards
        own = pltpu.make_async_copy(x_ref.at[s, pl.ds(pl.multiple_of(me * share, 16), share)], g_out.at[me * seqs + s], load_sem.at[6 + s])
        own.start()
        loads.append(own)

    def bytes_send(s, d):
        share = width // shards
        there = pl.ds(pl.multiple_of(z_back[d] * share, 16), share)
        pending.append(send(x_ref.at[s, there], g_out.at[me * seqs + s], a_ss.at[s, d], a_rs.at[s, d], mesh_at(dh=z_back[d])))

    half_rows, quarter = local_rows // 2, local_rows // 4
    piece_rows = quarter // shards

    def latents_send():
        theirs = latsum_in.at[pl.ds(pl.multiple_of((1 - core) * half_rows, 8), half_rows)]
        pending.append(send(theirs, l_sib, l_ss.at[0], l_rs.at[0], to_sib))

    def latents_sib():
        arrived(l_sib, l_ss.at[0], l_rs.at[0])
        own_sum.wait()
        l_half[...] += l_sib[...]
        pending.append(send(l_half.at[pl.ds(pl.multiple_of((1 - hi) * quarter, 8), quarter)], l_y, l_ss.at[1], l_rs.at[1], to_y))

    def latents_y():
        arrived(l_y, l_ss.at[1], l_rs.at[1])
        l_sum[...] = (l_half[pl.ds(pl.multiple_of(hi * quarter, 8), quarter)] + l_y[...]).reshape(l_sum.shape)
        for d in range(1, shards):
            pending.append(send(l_sum.at[z_back[d]], l_z.at[d - 1], l_ss.at[1 + d], l_rs.at[1 + d], mesh_at(dh=z_back[d])))

    def latents_z():
        total = l_sum[me]
        for d in range(1, shards):
            arrived(l_z.at[d - 1], l_ss.at[1 + d], l_rs.at[1 + d])
            total += l_z[d - 1]
        l_tot[...] = total

    def third_first():
        tq_ref[...] = jnp.transpose(dq_out[0, :, my_rows])
        rows_here = tq_ref[pl.ds(pl.multiple_of(core * half_rows + hi * quarter, 8), quarter)].astype(BF16)
        t_part[...] = dot(rows_here, wq_ref[...]).reshape(t_part.shape)
        for d in range(1, shards):
            pending.append(send(t_part.at[z_back[d]], t_got.at[d - 1], t_ss.at[0, d], t_rs.at[0, d], mesh_at(dh=z_back[d])))

    def third_z():
        grad = t_part[me]
        for d in range(1, shards):
            arrived(t_got.at[d - 1], t_ss.at[0, d], t_rs.at[0, d])
            grad += t_got[d - 1]
        loads[3].wait()
        _, normed, inverse = norm_keep(lat8_ref[...], 1.0, 0.0)
        t_z[me, :piece_rows] = l_tot[...] + norm_back(grad, normed, inverse, lgain_ref[0:1])
        t_z[me, piece_rows:] = jnp.zeros((8, lat8_ref.shape[1]), F32)
        t_z[me, piece_rows:piece_rows + 1] = jnp.sum(grad * normed, axis=0, keepdims=True)
        t_z[me, piece_rows + 1:piece_rows + 2] = jnp.sum(grad, axis=0, keepdims=True)
        for d in range(1, shards):
            pending.append(send(t_z.at[me], t_z.at[me], t_ss.at[1, d], t_rs.at[1, d], mesh_at(dh=z_back[d])))

    def third_y():
        for d in range(1, shards):
            arrived(t_z.at[z_of[d]], t_ss.at[1, d], t_rs.at[1, d])
        y_buf[hi, :quarter] = t_z[:, :piece_rows].reshape(quarter, t_z.shape[2])
        y_buf[hi, quarter:] = t_z[0, piece_rows:] + t_z[1, piece_rows:] + t_z[2, piece_rows:] + t_z[3, piece_rows:]
        pending.append(send(y_buf.at[hi], y_buf.at[hi], t_ss.at[2, 0], t_rs.at[2, 0], to_y))

    def third_core():
        arrived(y_buf.at[1 - hi], t_ss.at[2, 0], t_rs.at[2, 0])
        c_buf[core, :quarter] = y_buf[0, :quarter]
        c_buf[core, quarter:half_rows] = y_buf[1, :quarter]
        c_buf[core, half_rows:] = y_buf[0, quarter:] + y_buf[1, quarter:]
        pending.append(send(c_buf.at[core], c_buf.at[core], t_ss.at[2, 1], t_rs.at[2, 1], to_sib))

    def third_x():
        arrived(c_buf.at[1 - core], t_ss.at[2, 1], t_rs.at[2, 1])
        glat_out[:half_rows] = c_buf[0, :half_rows]
        glat_out[half_rows:] = c_buf[1, :half_rows]
        x_buf[blk] = c_buf[0, half_rows:] + c_buf[1, half_rows:]
        pending.append(send(x_buf.at[blk], x_buf.at[blk], t_ss.at[2, 2], t_rs.at[2, 2], to_x))

    def third_end():
        arrived(x_buf.at[other], t_ss.at[2, 2], t_rs.at[2, 2])
        vec_out[...] = x_buf[0] + x_buf[1]

    def small_start():
        wide_lane = lax.broadcasted_iota(jnp.int32, (width, 128), 1)
        block = jnp.where(wide_lane == 32, small_ref[:, 0:1], 0.0) + jnp.where(wide_lane == 33, small_ref[:, 1:2], 0.0)
        for s in range(seqs):
            block += small_ref[:, 2 + s:3 + s] * lang_in[s:s + 1]
        share = width // shards
        for h in range(shards):
            s_ref[0, h, :, :128] = block[h * share:(h + 1) * share]
            s_ref[0, h, :, 128:] = jnp.zeros((share, 128), F32)
            for v in range(vec_in.shape[0]):
                for b in range(vec_in.shape[1] // 128):
                    s_ref[0, h, v * 10 + b:v * 10 + b + 1, 128:] = vec_in[v:v + 1, b * 128:(b + 1) * 128]
        small.start()

    def weight_steps(part):
        def weight_step(h, _):
            at = pl.ds(pl.multiple_of(h * cols, 16), cols)
            total = dot_nt(dkv_ref[0, part, at], xn_ref[0])
            for s in range(1, seqs):
                total += dot_nt(dkv_ref[s, part, at], xn_ref[s])
            dw_tmp[...] = total.astype(BF16)
            w_half[part, h] = dw_tmp[:, pl.ds(pl.multiple_of(core * (width // 2), 128), width // 2)]
            dw_ref[part, h] = dw_tmp[:, pl.ds(pl.multiple_of((1 - core) * (width // 2), 128), width // 2)]
            return 0
        lax.fori_loop(0, shards, weight_step, 0)

    send_do(0)
    mixed_near()
    prepare()
    own_do.wait()
    stats_ready()
    turn_grads(0)
    send_do(1)
    mixed_far()
    head_steps(0, 0)
    latents_send()
    head_steps(0, 1)
    head_steps(0, 2)
    loads[2].wait()
    grads[2].send_chips()
    head_steps(0, 3)
    loads[1].wait()
    own_w.wait()
    byte_steps(0)
    grads[1].send_chips()
    mixed_cross_0()
    bytes_send(0, 1)
    bytes_send(0, 3)
    turn_grads(1)
    head_steps(1, 0)
    head_steps(1, 1)
    bytes_send(0, 2)
    grads[0].send_chips()
    head_steps(1, 2)
    head_steps(1, 3)
    grads[2].join_first()
    query.start()
    loads[0].wait()
    weight_steps(0)
    latents_sib()
    byte_steps(1)
    query.join_sib()
    small_start()
    grads[0].join_first()
    grads[2].join_chips()
    small.join_sib()
    small.send_chips()
    query.send_chips()
    grads[1].join_first()
    pair[0].start()
    latents_y()
    weight_steps(1)
    pair[1].start()
    grads[0].join_chips()
    pair[0].join_sib()
    bytes_send(1, 3)
    query.join_first()
    pair[0].send_chips()
    grads[2].join_near()
    query.join_chips()
    latents_share()
    grads[1].join_chips()
    pair[1].join_sib()
    pair[1].send_chips()
    pair[0].join_first()
    query.join_near()
    grads[0].join_near()
    small.join_first()
    query.join_z()
    query.share_chips()
    grads[1].join_near()
    pair[1].join_first()
    small.join_chips()
    grads[2].join_z()
    bytes_send(1, 2)
    pair[0].join_chips()
    query.share_sib()
    query.finish()
    third_first()
    grads[0].join_z()
    small.join_near()
    pair[0].join_near()
    grads[0].share_chips()
    grads[2].share_chips()
    small.join_z()
    pair[1].join_chips()
    latents_z()
    grads[1].join_z()
    grads[2].share_sib()
    third_z()
    grads[0].share_sib()
    grads[1].share_chips()
    pair[0].join_z()
    pair[1].join_near()
    mixed_cross_1()
    small.share_chips()
    pair[0].share_chips()
    pair[0].share_sib()
    small.share_sib()
    grads[1].share_sib()
    third_y()
    bytes_send(1, 1)
    grads[2].finish()
    pair[1].join_z()
    grads[0].finish()
    third_core()
    pair[0].finish()
    grads[1].finish()
    pair[1].share_chips()
    pair[1].share_sib()
    third_x()
    pair[1].finish()
    small.finish()
    third_end()
    arrived(latn_ref.at[other_rows], misc_ss.at[1], misc_rs.at[1])
    arrived(mixed_out.at[near * seqs + 1], mix_ss.at[1], mix_rs.at[1])
    arrived(mixed_out.at[cross * seqs], mix_ss.at[2], mix_rs.at[2])
    arrived(mixed_out.at[cross * seqs + 1], mix_ss.at[3], mix_rs.at[3])
    for d in range(1, shards):
        for s in range(seqs):
            arrived(g_out.at[z_of[d] * seqs + s], a_ss.at[s, d], a_rs.at[s, d])
    for own in loads[4:]:
        own.wait()
    for copy in pending:
        copy.wait_send()


def second_call(x_cols, rows_in, mask, w_cols, qt, pairs, xn, grad_out, stats, mixed, lat_low, grads, vectors, lang_rows, lat_sum, w_query, lat_f32, lat_gain):
    seqs, width, length = x_cols.shape
    rows, width_lat = qt.shape[3], pairs.shape[2]
    local_rows = lat_low.shape[0]
    shards = lax.axis_size("heads")
    heads = HEADS
    head_dim = width_lat // heads
    cols = width_lat // shards
    share = cols // 4
    whole = pl.BlockSpec(memory_space=pltpu.VMEM)
    hbm = pl.BlockSpec(memory_space=pl.ANY)
    out = jax.ShapeDtypeStruct
    vmem = pltpu.VMEM
    sem = pltpu.SemaphoreType.DMA

    assert seqs == 2

    def reduce_buffers(n, lanes, kind, cols=cols):
        half, share = lanes // 2, cols // 4
        return [vmem((n, shards, cols, half), kind), vmem((n, shards, cols, half), kind), vmem((6, n, 2, share, half), kind),
                vmem((shards - 1, n, share, half), kind)]

    return pl.pallas_call(
        second_kernel,
        in_specs=[hbm, whole, whole, hbm, whole, hbm, hbm, hbm, whole, hbm, whole, hbm, whole, whole, hbm, whole, hbm, whole],
        out_specs=[hbm, hbm, hbm, hbm, whole, whole, whole, whole, whole],
        input_output_aliases={9: 1},
        out_shape=[
            out((shards * seqs, width // shards, length), BF16),
            out((shards * seqs, local_rows, width_lat), BF16),
            out((2, cols, width), BF16),
            out((3, cols, width_lat), BF16),
            out((1, width // shards, 256), F32),
            out((local_rows, width_lat), F32),
            out((8, width_lat), F32),
            out((1, cols, rows), F32),
            out((rows, width_lat), BF16),
        ],
        scratch_shapes=[
            vmem((2, width, width_lat), BF16),
            vmem((seqs, width, length), BF16),
            vmem((seqs, width, length), BF16),
            vmem((width, rows_in.shape[0]), F32),
            vmem((2, 2, head_dim, length), BF16),
            vmem((seqs, 2, width_lat, length), BF16),
            vmem((heads, rows, head_dim), BF16),
            vmem((heads, rows, head_dim), BF16),
            vmem((128, rows), F32),
            vmem((rows, 128), F32),
            vmem((1, shards, cols, rows), F32),
            vmem((2, shards, cols, width // 2), BF16),
            vmem((cols, width), BF16),
        ] + [
            vmem((3, shards, cols, width_lat // 2), BF16),
            vmem((6, 3, 2, share, width_lat // 2), BF16),
            vmem((3, 3, 1, share, width_lat // 2), BF16),
        ] + reduce_buffers(2, width, BF16)[:3] + [vmem((2, 3, 1, share, width // 2), BF16)]
        + reduce_buffers(1, rows, F32)
        + reduce_buffers(1, 256, F32, width // shards) + [
            vmem((width, 8), F32),
            vmem((1, shards, width // shards, 256), F32),
            vmem((local_rows // 2, width_lat), F32),
            vmem((local_rows // 2, width_lat), F32),
            vmem((local_rows // 4, width_lat), F32),
            vmem((shards, local_rows // 16, width_lat), F32),
            vmem((shards - 1, local_rows // 16, width_lat), F32),
            vmem((local_rows // 16, width_lat), F32),
            vmem((local_rows // 16, width_lat), F32),
            vmem((3, share, width_lat // 2), BF16),
            vmem((2, share, width // 2), BF16),
            vmem((local_rows, cols), F32),
            vmem((shards, local_rows // 16, width_lat), F32),
            vmem((shards - 1, local_rows // 16, width_lat), F32),
            vmem((shards, local_rows // 16 + 8, width_lat), F32),
            vmem((2, local_rows // 4 + 8, width_lat), F32),
            vmem((2, local_rows // 2 + 8, width_lat), F32),
            vmem((2, 8, width_lat), F32),
        ] + [sem((3, 14))] * 2 + [sem((2, 14))] * 2 + [sem((14,))] * 4 + [sem((6,))] * 2 + [sem((3, shards))] * 2 + [sem((seqs,))] * 2 + [sem((2,))] * 2 + [sem((shards,))] * 2 + [sem((seqs, shards))] * 2
        + [sem((16,)), sem((2,)), sem((5,))],
        compiler_params=pltpu.CompilerParams(vmem_limit_bytes=VMEM_LIMIT, collective_id=2, has_side_effects=True),
        name="second",
    )(x_cols, rows_in, mask, w_cols, qt, pairs, xn, grad_out, stats, mixed, lat_low, grads, vectors, lang_rows, lat_sum, w_query, lat_f32, lat_gain)


def middle_kernel(att_ref, lat_ref, cot_hbm, all_hbm, bup_tiles, vecs_ref, lse_ref,
                  mixed_all, do_ref, stat_ref, half_out, vec_ref, sum_ref,
                  rows_ref, mid_ref, low_ref, hid_ref, norm_ref, a_ref, b_src, b_ref, bup_ref, all_ref, mixed_ref, cot_ref, slope_ref, half_ref, a_ss, a_rs, b_ss, b_rs, load_sem, mix_ss, mix_rs):
    items, _, me, _, core = places()
    near = me + 1 - 2 * lax.rem(me, 2)
    far = lax.rem(me + 2, 4)
    to_sib = mesh_at(di=items + 1 - 2 * core)
    seqs, width, local_rows = att_ref.shape
    rows = seqs * local_rows
    heads = lse_ref.shape[1]
    head_dim = width // heads
    half = width // 2
    block = 256
    pending = []
    loads = [pltpu.make_async_copy(all_hbm.at[i], all_ref.at[i], load_sem.at[i]) for i in range(3)]
    cots = [pltpu.make_async_copy(cot_hbm.at[me * seqs + s], cot_ref.at[pl.ds(s * local_rows, local_rows)], load_sem.at[4 + s]) for s in range(seqs)]
    for copy in cots + loads:
        copy.start()
    greet([to_sib, mesh_at(dh=near), mesh_at(dh=far)])
    shards, cols = half_ref.shape[1:3]
    for h in range(shards):
        bup_ref[:, h * cols:(h + 1) * cols] = bup_tiles[h, 7:8, :cols]
    gain_ref, bias_ref, bdown_ref = vecs_ref.at[pl.ds(2, 1)], vecs_ref.at[pl.ds(3, 1)], vecs_ref.at[pl.ds(4, 1)]

    def block_loop(body):
        def step(i, _):
            body(pl.ds(pl.multiple_of(i * block, block), block))
            return 0
        lax.fori_loop(0, width // block, step, 0)

    def share_a(i):
        pending.append(send(a_ref.at[i, 0], a_ref.at[i, 1], a_ss.at[i], a_rs.at[i], to_sib))

    def share_b(i):
        theirs = b_src.at[i, :, pl.ds(pl.multiple_of((1 - core) * half, 128), half)]
        pending.append(send(theirs, b_ref.at[i, 1], b_ss.at[i], b_rs.at[i], to_sib))
        b_ref[i, 0] = b_src[i, :, pl.ds(pl.multiple_of(core * half, 128), half)]

    for s in range(seqs):
        at = slice(s * local_rows, (s + 1) * local_rows)
        low = att_ref[s].astype(BF16)
        a_ref[0, 0, :, at] = low
        rows_ref[at] = jnp.transpose(att_ref[s]).astype(BF16)
    share_a(0)
    for copy in cots:
        copy.wait()
    b_src[2] = cot_ref[...]
    share_b(2)

    def branch(at):
        latent = lat_ref[:, at].astype(F32)
        mid_ref[:, at] = dot(rows_ref[...], all_ref[0, :, at]) + jnp.concatenate([latent] * seqs, axis=0)
    loads[0].wait()
    block_loop(branch)
    mid_out, normed, inverse = norm_keep(mid_ref[...], gain_ref[...], bias_ref[...])
    norm_ref[...] = normed
    b_src[1] = mid_out.astype(BF16)
    share_b(1)

    def up(at):
        value = dot_nt(b_src[1], all_ref[1, at]) + bup_ref[:, at]
        square = value * value
        bend = jnp.tanh(0.7978845608028654 * (value + 0.044715 * (square * value)))
        active = 0.5 * value * (1.0 + bend)
        slope_ref[:, at] = 0.5 * (1.0 + bend) + 0.5 * value * (1.0 - bend * bend) * (0.7978845608028654 * (1.0 + 0.134145 * square))
        rows_ref[:, at] = active.astype(BF16)
        a_ref[2, 0, at] = jnp.transpose(active.astype(BF16))
    loads[1].wait()
    block_loop(up)
    share_a(2)

    def down(at):
        out = mid_ref[:, at] + dot(rows_ref[...], all_ref[2, :, at]) + bdown_ref[:, at]
        for s in range(seqs):
            mixed_ref[s, :, at] = out[s * local_rows:(s + 1) * local_rows].astype(BF16)
    loads[2].wait()
    block_loop(down)
    own_mixed = pltpu.make_async_copy(mixed_ref, mixed_all.at[pl.ds(me * seqs, seqs)], load_sem.at[3])
    own_mixed.start()
    for i, there in enumerate((far, near)):
        pending.append(send(mixed_ref.at[0], mixed_all.at[me * seqs], mix_ss.at[i], mix_rs.at[i], mesh_at(dh=there)))

    def up_back(at):
        grad = (dot_nt(cot_ref[...], all_ref[2, at]) * slope_ref[:, at]).astype(BF16)
        low_ref[:, at] = grad
        vec_ref[2:3, at] = jnp.sum(grad.astype(F32), axis=0, keepdims=True)
        a_ref[1, 0, at] = jnp.transpose(grad)
    block_loop(up_back)
    share_a(1)

    def mid_back(at):
        hid_ref[:, at] = dot(low_ref[...], all_ref[1, :, at])
    block_loop(mid_back)
    grad = hid_ref[...]
    normed = norm_ref[...]
    vec_ref[0:1] = jnp.sum(grad * normed, axis=0, keepdims=True)
    vec_ref[1:2] = jnp.sum(grad, axis=0, keepdims=True)
    vec_ref[3:4] = jnp.sum(cot_ref[...].astype(F32), axis=0, keepdims=True)
    grad = cot_ref[...].astype(F32) + norm_back(grad, normed, inverse, gain_ref[...])
    b_src[0] = grad.astype(BF16)
    share_b(0)
    total = grad[:local_rows]
    for s in range(1, seqs):
        total += grad[s * local_rows:(s + 1) * local_rows]
    sum_ref[...] = total

    def out(h, _):
        at = pl.ds(pl.multiple_of(h * head_dim, 16), head_dim)
        grad = dot_nt(all_ref[0, at], b_src[0]).astype(BF16)
        for s in range(seqs):
            part = grad[:, s * local_rows:(s + 1) * local_rows]
            do_ref[s, at] = part
            delta = jnp.sum(part.astype(F32) * att_ref[s, at], axis=0, keepdims=True)
            stat_ref[pl.ds((2 * s + 1) * heads + h, 1)] = delta
        return 0
    lax.fori_loop(0, heads, out, 0)
    for s in range(seqs):
        stat_ref[2 * s * heads:(2 * s + 1) * heads] = lse_ref[s]

    def arrived(where, ss, rs):
        pltpu.make_async_remote_copy(src_ref=where, dst_ref=where, send_sem=ss, recv_sem=rs,
                                     device_id=to_sib, device_id_type=pl.DeviceIdType.MESH).wait_recv()

    stores = []
    for i in (2, 1, 0):
        arrived(a_ref.at[i, 1], a_ss.at[i], a_rs.at[i])
        arrived(b_ref.at[i, 1], b_ss.at[i], b_rs.at[i])

        def weight(h, _):
            at = pl.ds(pl.multiple_of(h * cols, 16), cols)
            half_ref[i, h] = (dot(a_ref[i, 0, at], b_ref[i, 0]) + dot(a_ref[i, 1, at], b_ref[i, 1])).astype(BF16)
            return 0
        lax.fori_loop(0, shards, weight, 0)
        copy = pltpu.make_async_copy(half_ref.at[i], half_out.at[i], load_sem.at[4 + seqs + i])
        copy.start()
        stores.append(copy)
    own_mixed.wait()
    for copy in stores:
        copy.wait()
    for i, there in enumerate((far, near)):
        arrived(mixed_all.at[there * seqs], mix_ss.at[i], mix_rs.at[i])
    for copy in pending:
        copy.wait_send()


def middle_call(att, latents, cot, weights, b_up, vecs, lse):
    seqs, width, local_rows = att.shape
    rows = seqs * local_rows
    heads = lse.shape[1]
    shards = lax.axis_size("heads")
    whole = pl.BlockSpec(memory_space=pltpu.VMEM)
    out, vmem, sem = jax.ShapeDtypeStruct, pltpu.VMEM, pltpu.SemaphoreType.DMA
    return pl.pallas_call(
        middle_kernel,
        in_specs=[whole, whole, pl.BlockSpec(memory_space=pl.ANY), pl.BlockSpec(memory_space=pl.ANY), whole, whole, whole],
        out_specs=[pl.BlockSpec(memory_space=pl.ANY)] + [whole] * 2 + [pl.BlockSpec(memory_space=pl.ANY)] + [whole] * 2,
        out_shape=[
            out((shards * seqs, local_rows, width), BF16),
            out((seqs, width, local_rows), BF16),
            out((2 * seqs * heads, local_rows), F32),
            out((3, shards, width // shards, width // 2), BF16),
            out((4, width), F32),
            out((local_rows, width), F32),
        ],
        scratch_shapes=[
            vmem((rows, width), BF16), vmem((rows, width), F32), vmem((rows, width), BF16), vmem((rows, width), F32), vmem((rows, width), F32),
            vmem((3, 2, width, rows), BF16), vmem((3, rows, width), BF16), vmem((3, 2, rows, width // 2), BF16),
            vmem((1, width), F32), vmem((3, width, width), BF16), vmem((seqs, local_rows, width), BF16), vmem((rows, width), BF16), vmem((rows, width), F32),
            vmem((3, shards, width // shards, width // 2), BF16),
            sem((3,)), sem((3,)), sem((3,)), sem((3,)), sem((7 + seqs,)), sem((2,)), sem((2,)),
        ],
        compiler_params=pltpu.CompilerParams(vmem_limit_bytes=VMEM_LIMIT, collective_id=4, has_side_effects=True),
        name="middle",
    )(att, latents, cot, weights, b_up, vecs, lse)


def finish_kernel(lat_hbm, pair_hbm, small_ref, vec_ref, query_ref, latn_hbm, g_hbm, mixed_hbm, glat_hbm,
                  table_out, igain_out, ibias_out, lgain_out, lbias_out, mgain_out, mbias_out, wq_out, wk_out, wv_out, wo_out, wu_out,
                  bup_out, wd_out, bdown_out, g_out, mixed_out, glat_out, wq_ref, wk_ref, wv_ref, wo_ref, wu_ref, wd_ref, g_ref, mixed_ref, lat_ref, pair_ref, latn_ref, glat_ref, row_ref, sems, pass_sems):
    me = lax.axis_index("heads")
    copies = []

    def store(ref, out):
        copy = pltpu.make_async_copy(ref, out, sems.at[len(copies)])
        copy.start()
        copies.append(copy)

    sources = ((g_hbm, g_ref), (mixed_hbm, mixed_ref), (lat_hbm, lat_ref), (pair_hbm, pair_ref), (latn_hbm, latn_ref), (glat_hbm, glat_ref))
    loads = [pltpu.make_async_copy(src, dst, pass_sems.at[i]) for i, (src, dst) in enumerate(sources)]
    for copy in loads:
        copy.start()
    loads[2].wait()
    wo_ref[...] = lat_ref[0].astype(F32)
    store(wo_ref, wo_out)
    wd_ref[...] = lat_ref[2].astype(F32)
    store(wd_ref, wd_out)
    wu_ref[...] = lat_ref[1].astype(F32)
    store(wu_ref, wu_out)
    loads[0].wait()
    store(g_ref, g_out)
    loads[1].wait()
    store(mixed_ref, mixed_out)
    loads[3].wait()
    wk_ref[...] = pair_ref[0].astype(F32)
    store(wk_ref, wk_out)
    wv_ref[...] = pair_ref[1].astype(F32)
    store(wv_ref, wv_out)
    loads[5].wait()
    store(glat_ref, glat_out)
    loads[4].wait()
    query = query_ref[0].astype(BF16)
    for i in range(0, latn_ref.shape[1], 256):
        wq_ref[:, i:i + 256] = dot(query, latn_ref[:, i:i + 256])
    store(wq_ref, wq_out)
    turned = jnp.transpose(small_ref[0, :, :128])
    table_out[...] = turned[:table_out.shape[0]]
    igain_out[...] = turned[32]
    ibias_out[...] = turned[33]
    lgain_out[...] = vec_ref[0]
    lbias_out[...] = vec_ref[1]
    blocks = row_ref.shape[1] // 128
    for v, out in enumerate((mgain_out, mbias_out, None, bdown_out)):
        for b in range(blocks):
            row_ref[:, b * 128:(b + 1) * 128] = small_ref[0, v * blocks + b:v * blocks + b + 1, 128:]
        if out is not None:
            out[...] = row_ref[0]
        else:
            cols = bup_out.shape[0]
            total = jnp.zeros((1, cols), F32)
            for h in range(row_ref.shape[1] // cols):
                total += jnp.where(me == h, row_ref[:, h * cols:(h + 1) * cols], 0.0)
            bup_out[...] = total[0]
    for copy in copies:
        copy.wait()


def finish_call(lat_total, pair_total, small, vec, query, latn, grad, mixed, grad_lat, langs):
    _, cols, width_lat = lat_total.shape
    width = pair_total.shape[2]
    share = small.shape[1]
    whole = pl.BlockSpec(memory_space=pltpu.VMEM)
    hbm = pl.BlockSpec(memory_space=pl.ANY)
    out, vmem = jax.ShapeDtypeStruct, pltpu.VMEM
    big = [(cols, width_lat), (cols, width), (cols, width), (cols, width_lat), (cols, width_lat), (cols, width_lat)]
    return pl.pallas_call(
        finish_kernel,
        in_specs=[hbm, hbm, whole, whole, whole, hbm, hbm, hbm, hbm],
        out_specs=[whole] * 7 + [hbm] * 5 + [whole, hbm, whole, hbm, hbm, hbm],
        out_shape=[out(shape, F32) for shape in [(langs, share), (share,), (share,)] + [(width_lat,)] * 4 + big[:5] + [(cols,)] + big[5:] + [(width_lat,)]]
        + [out(x.shape, x.dtype) for x in (grad, mixed, grad_lat)],
        scratch_shapes=[vmem(shape, F32) for shape in big] + [vmem(x.shape, x.dtype) for x in (grad, mixed, lat_total, pair_total, latn, grad_lat)]
        + [vmem((1, width_lat), F32), pltpu.SemaphoreType.DMA((9,)), pltpu.SemaphoreType.DMA((6,))],
        compiler_params=pltpu.CompilerParams(vmem_limit_bytes=VMEM_LIMIT),
        name="finish",
    )(lat_total, pair_total, small, vec, query, latn, grad, mixed, grad_lat)


REST = ("items", "blk")
ALL = ("heads", "items", "blk")


def gather_rows(shard):
    count = lax.axis_size("items") * lax.axis_size("blk")
    me = lax.axis_index("items") * lax.axis_size("blk") + lax.axis_index("blk")
    share = shard.shape[0] // count
    part = lax.dynamic_slice_in_dim(shard, me * share, share, 0)
    return lax.all_gather(part, ALL, axis=0, tiled=True)


def scatter_rows(whole):
    part = lax.psum_scatter(whole.astype(BF16), ALL, scatter_dimension=0, tiled=True)
    return lax.all_gather(part, REST, axis=0, tiled=True)


def general_device(inputs, padding, language, lang_table, latents, in_gain, in_bias, lat_gain, lat_bias, mid_gain, mid_bias,
              w_query, w_key, w_value, w_out, w_up, b_up, w_down, b_down, cotangent):
    length, local_seqs, width = inputs.shape
    local_rows, width_lat = latents.shape
    cols = w_query.shape[1]
    head_dim = width_lat // HEADS
    per_shard = cols // head_dim
    shards = lax.axis_size("heads")
    blocks = lax.axis_size("blk")
    rows = local_rows * blocks
    seqs = local_seqs // shards
    me = lax.axis_index("heads")
    first = me * seqs

    pair_shard = jnp.concatenate([w_key.T, w_value.T], axis=0)
    pair_rows = gather_rows(pair_shard)
    latent_shard = jnp.concatenate([w_out, w_up.T, w_down], axis=0)
    lat_all = gather_rows(latent_shard).reshape(shards, 3, cols, width_lat)
    out_all, up_all, down_all = (lat_all[:, i].reshape(width_lat, width_lat) for i in range(3))

    all_latents = lax.all_gather(latents, "blk", axis=0, tiled=True).astype(F32)
    lat_out, _, _ = norm_keep(all_latents, lat_gain, lat_bias)
    lat_low = lat_out.astype(BF16)
    query_part = dot(lat_low, w_query).astype(BF16)
    queries = lax.all_gather(query_part, "heads", axis=1, tiled=True)
    q = queries.reshape(rows, HEADS, head_dim).transpose(1, 0, 2)

    own = lax.dynamic_slice_in_dim(inputs, first, seqs, 1)
    x_cols = jnp.transpose(own, (1, 2, 0))
    live = jnp.transpose(lax.dynamic_slice_in_dim(padding, first, seqs, 1))
    mask = jnp.where(live > 0, 0.0, MASKED).astype(F32)[:, None, :]
    own_lang = lax.dynamic_slice_in_dim(language, first, seqs, 0)
    onehot = (own_lang[:, None] == jnp.arange(lang_table.shape[0], dtype=jnp.int32)[None, :]).astype(F32)
    emb = jnp.dot(onehot, lang_table.astype(F32), precision=lax.Precision.HIGHEST)[:, :, None]
    gain_col, bias_col = in_gain[:, None], in_bias[:, None]

    pairs, o_cols, lse = forward_call(x_cols, emb, gain_col, bias_col, pair_rows, q, mask, per_shard)

    parts = o_cols.reshape(seqs, width_lat, blocks, local_rows).transpose(2, 0, 3, 1)
    parts = lax.all_to_all(parts, "blk", 0, 0, tiled=True).astype(F32)
    lse_parts = lse.reshape(seqs, HEADS, blocks, local_rows).transpose(2, 0, 3, 1)
    lse_parts = lax.all_to_all(lse_parts, "blk", 0, 0, tiled=True)
    top = jnp.max(lse_parts, axis=0)
    shares = jnp.exp2(lse_parts - top)
    total = jnp.sum(shares, axis=0)
    own_lse = top + jnp.log2(total)
    shares = shares / total
    attended = jnp.sum(parts.reshape(blocks, seqs, local_rows, HEADS, head_dim) * shares[..., None], axis=0)
    att_low = attended.reshape(seqs * local_rows, width_lat).astype(BF16)

    cot = lax.dynamic_slice_in_dim(cotangent, first, seqs, 0).reshape(seqs * local_rows, width_lat)
    lat_f32 = latents.astype(F32)
    middle = (lat_f32[None] + dot(att_low, out_all).reshape(seqs, local_rows, width_lat)).reshape(seqs * local_rows, width_lat)
    mid_out, mid_normed, mid_inverse = norm_keep(middle, mid_gain, mid_bias)
    mid_low = mid_out.astype(BF16)
    b_up_all = lax.all_gather(b_up, "heads", axis=0, tiled=True)
    hidden = dot_nt(mid_low, up_all) + b_up_all
    active, gelu_back = jax.vjp(jax.nn.gelu, hidden)
    active_low = active.astype(BF16)
    own_mixed = (middle + dot(active_low, down_all) + b_down).astype(BF16).reshape(seqs, local_rows, width_lat)
    mixed_latents = lax.all_gather(own_mixed, "heads", axis=0, tiled=True)

    grad_b_down = jnp.sum(cot.astype(F32), axis=0)
    grad_w_down = dot(active_low.T, cot)
    grad_active = dot_nt(cot, down_all)
    grad_hidden = gelu_back(grad_active)[0].astype(BF16)
    grad_b_up = jnp.sum(grad_hidden.astype(F32), axis=0)
    grad_w_up = dot(grad_hidden.T, mid_low)
    grad_mid_norm = dot(grad_hidden, up_all)
    grad_mid_gain = jnp.sum(grad_mid_norm * mid_normed, axis=0)
    grad_mid_bias = jnp.sum(grad_mid_norm, axis=0)
    grad_middle = cot.astype(F32) + norm_back(grad_mid_norm, mid_normed, mid_inverse, mid_gain)
    grad_branch = grad_middle.astype(BF16)
    grad_w_out = dot(att_low.T, grad_branch)
    grad_att = dot_nt(grad_branch, out_all).astype(BF16).reshape(seqs, local_rows, width_lat)
    grad_att_heads = grad_att.reshape(seqs, local_rows, HEADS, head_dim)
    delta = jnp.sum(grad_att_heads.astype(F32) * attended, axis=-1)
    lat_sum = jnp.sum(grad_middle.reshape(seqs, local_rows, width_lat), axis=0)

    all_grad_att = lax.all_gather(grad_att, "blk", axis=1, tiled=True).reshape(seqs, rows, HEADS, head_dim)
    stats = lax.all_gather(jnp.concatenate([own_lse, delta], axis=-1), "blk", axis=1, tiled=True)
    stats = jnp.transpose(stats, (0, 2, 1))[..., None]
    g_cols, dw_pair, dq, dgain, dbias, demb = backward_call(
        x_cols, emb, gain_col, bias_col, pair_rows.T, q, q.transpose(0, 2, 1),
        all_grad_att.transpose(0, 2, 1, 3), all_grad_att.transpose(0, 2, 3, 1),
        stats[:, :HEADS], stats[:, HEADS:], mask, pairs, per_shard)

    send = g_cols.reshape(seqs, shards, width // shards, length).transpose(1, 0, 2, 3)
    got = lax.all_to_all(send, "heads", 0, 0, tiled=True)
    grad_inputs = got.reshape(local_seqs, width // shards, length).transpose(2, 0, 1)

    grad_rows = jnp.stack([grad_w_out, grad_w_up, grad_w_down], axis=0).reshape(3, shards, cols, width_lat)
    lat_total = scatter_rows(grad_rows.transpose(1, 0, 2, 3).reshape(-1, width_lat)).astype(F32)
    pair_total = scatter_rows(dw_pair).astype(F32)

    dq_part = lax.psum_scatter(dq.reshape(width_lat, rows).astype(BF16), "heads", scatter_dimension=0, tiled=True)
    query_low = lax.psum(dq_part, REST)
    grad_w_query = dot(lat_low.T, query_low.T)
    lat_mine = lax.dynamic_slice_in_dim(query_low, lax.axis_index("blk") * local_rows, local_rows, 1)
    grad_lat_part = dot(lat_mine.T, w_query.T)
    grad_lat_norm = lax.psum(grad_lat_part.astype(BF16), "heads").astype(F32)
    lat_sum = lax.psum(lat_sum.astype(BF16), ("heads", "items")).astype(F32)
    _, own_normed, own_inverse = norm_keep(lat_f32, lat_gain, lat_bias)
    grad_latents = lat_sum + norm_back(grad_lat_norm, own_normed, own_inverse, lat_gain)
    lat_small = jnp.concatenate([jnp.sum(grad_lat_norm * own_normed, axis=0), jnp.sum(grad_lat_norm, axis=0)])
    lat_small = lax.psum(lat_small, "blk")

    table = jnp.dot(onehot.T, demb[:, :, 0], precision=lax.Precision.HIGHEST)
    small = jnp.concatenate([table.reshape(-1), dgain[:, 0], dbias[:, 0], grad_mid_gain, grad_mid_bias, grad_b_up, grad_b_down])
    small = lax.psum(small, ALL)
    sizes = [table.size, width, width, width_lat, width_lat, width_lat, width_lat]
    ends = [sum(sizes[:i]) for i in range(len(sizes) + 1)]
    table, dgain, dbias, dmid_gain, dmid_bias, db_up, db_down = (small[ends[i]:ends[i + 1]] for i in range(7))
    share = width // shards
    table = lax.dynamic_slice_in_dim(table.reshape(-1, width), me * share, share, 1)
    return (
        mixed_latents,
        grad_inputs,
        grad_latents,
        table,
        lax.dynamic_slice_in_dim(dgain, me * share, share, 0),
        lax.dynamic_slice_in_dim(dbias, me * share, share, 0),
        lat_small[:width_lat],
        lat_small[width_lat:],
        dmid_gain,
        dmid_bias,
        grad_w_query,
        pair_total[:cols].T,
        pair_total[cols:].T,
        lat_total[:cols],
        lat_total[cols:2 * cols].T,
        lax.dynamic_slice_in_dim(db_up, me * cols, cols, 0),
        lat_total[2 * cols:],
        db_down,
    )


def fast_device(inputs, padding, language, lang_table, latents, in_gain, in_bias, lat_gain, lat_bias, mid_gain, mid_bias,
              w_query, w_key, w_value, w_out, w_up, b_up, w_down, b_down, cotangent):
    length, local_seqs, width = inputs.shape
    local_rows, width_lat = latents.shape
    cols = w_query.shape[1]
    head_dim = width_lat // HEADS
    per_shard = cols // head_dim
    shards = lax.axis_size("heads")
    blocks = lax.axis_size("blk")
    rows = local_rows * blocks
    seqs = local_seqs // shards
    me = lax.axis_index("heads")
    first = me * seqs

    vectors = (lat_gain, lat_bias, mid_gain, mid_bias, b_down, in_gain, in_bias, b_up)
    wq_rows = w_query.T
    w_cols, lat_all, pairs, xn, att_cols, lse_cols, queries_t, lat_low, b_up_tiles, x_cols, rows_in, mask, lang_rows, lat_f32, vecs = first_call(
        inputs, padding.T, language, lang_table, vectors, latents, wq_rows,
        (w_key.T, w_value.T, w_out, w_up.T, w_down), rows, seqs)
    mixed, grad_att, stats, grads, vectors, lat_sum = middle_call(att_cols, latents, cotangent, lat_all, b_up_tiles, vecs, lse_cols)
    grad_att = grad_att.reshape(seqs, shards, cols, local_rows)
    g_cols, mixed_latents, pair_total, lat_total, small, grad_latents, lat_small, dq, lat_low_all = second_call(
        x_cols, rows_in, mask, w_cols, queries_t, pairs, xn, grad_att, stats, mixed, lat_low, grads, vectors, lang_rows, lat_sum,
        wq_rows, lat_f32, vecs)
    rest = finish_call(
        lat_total, pair_total, small, lat_small, dq, lat_low_all, g_cols, mixed_latents, grad_latents, lang_table.shape[0])
    rest = [x.T if i in (7, 8, 9, 11) else x for i, x in enumerate(rest)]
    return (rest[-2], rest[-3].transpose(2, 0, 1), rest[-1]) + tuple(rest[:-3])


def solution(mesh):
    placed = (
        P("blk", "items", None), P("blk", "items"), P("items"), P(), P("blk", None), P(), P(), P(), P(), P(), P(),
        P(None, "heads"), P(None, "heads"), P(None, "heads"), P("heads", None), P(None, "heads"), P("heads"),
        P("heads", None), P(), P("items", "blk", None),
    )
    out = (
        P("items", "blk", None), P("blk", "items", "heads"), P("blk", None), P(None, "heads"), P("heads"), P("heads"),
        P(), P(), P(), P(), P(None, "heads"), P(None, "heads"), P(None, "heads"), P("heads", None), P(None, "heads"),
        P("heads"), P("heads", None), P(),
    )
    fits = mesh.shape["blk"] == 2 and mesh.shape["items"] == 4 and mesh.shape["heads"] == 4
    return jax.shard_map(fast_device if fits else general_device, mesh=mesh, in_specs=placed, out_specs=out, check_vma=False)
```

```python
import functools

import jax
import jax.numpy as jnp
from jax import lax
from jax.experimental import pallas as pl
from jax.experimental.pallas import tpu as pltpu
from jax.sharding import PartitionSpec as P

HEADS = 8
EPS = 1e-05
MASKED = -1e30
LOG2E = 1.4426950408889634
F32 = jnp.float32
BF16 = jnp.bfloat16
NT = (((1,), (1,)), ((), ()))
VMEM_LIMIT = 60 * 1024 * 1024


def dot(a, b):
    return jnp.dot(a, b, preferred_element_type=F32)


def dot_nt(a, b):
    return lax.dot_general(a, b, NT, preferred_element_type=F32)


def norm_keep(values, gain, bias):
    average = jnp.mean(values, axis=-1, keepdims=True)
    centred = values - average
    inverse = lax.rsqrt(jnp.mean(centred * centred, axis=-1, keepdims=True) + EPS)
    normed = centred * inverse
    return (normed * gain + bias, normed, inverse)


def norm_back(grad_norm, normed, inverse, gain):
    scaled = grad_norm * gain
    first = jnp.mean(scaled, axis=-1, keepdims=True)
    second = jnp.mean(scaled * normed, axis=-1, keepdims=True)
    return (scaled - first - normed * second) * inverse


def norm_columns(x, emb):
    shifted = x.astype(F32) + emb
    centred = shifted - jnp.mean(shifted, axis=0, keepdims=True)
    inverse = lax.rsqrt(jnp.mean(centred * centred, axis=0, keepdims=True) + EPS)
    return centred * inverse, inverse


def head_rows(h, per_shard, head_dim):
    key = (h // per_shard) * 2 * per_shard + lax.rem(h, per_shard)
    key_at = pl.multiple_of(key * head_dim, head_dim)
    return pl.ds(key_at, head_dim), pl.ds(pl.multiple_of(key_at + per_shard * head_dim, head_dim), head_dim)


def forward_kernel(per_shard, x_ref, emb_ref, gain_ref, bias_ref, w_ref, q_ref, mask_ref, kv_ref, o_ref, lse_ref, xn_ref, stat_ref):
    heads, rows, head_dim = q_ref.shape
    length = x_ref.shape[1]
    piece = min(256, length)

    def norm_step(i, _):
        at = pl.ds(pl.multiple_of(i * piece, piece), piece)
        normed, _unused = norm_columns(x_ref[:, at], emb_ref[...])
        xn_ref[:, at] = (normed * gain_ref[...] + bias_ref[...]).astype(BF16)
        return 0

    lax.fori_loop(0, length // piece, norm_step, 0)
    block = 512 if w_ref.shape[0] % 512 == 0 else 160

    def pair_step(i, _):
        at = pl.ds(pl.multiple_of(i * block, block), block)
        kv_ref[at] = dot(w_ref[at], xn_ref[...]).astype(BF16)
        return 0

    lax.fori_loop(0, w_ref.shape[0] // block, pair_step, 0)
    factor = LOG2E * head_dim ** (-0.5)
    lane = lax.broadcasted_iota(jnp.int32, (rows, 128), 1)
    stat_ref[...] = jnp.zeros_like(stat_ref)

    def head_step(h, _):
        at_key, at_value = head_rows(h, per_shard, head_dim)
        scores = dot(q_ref[h], kv_ref[at_key]) * factor + mask_ref[...]
        top = jnp.max(scores, axis=1, keepdims=True)
        weights = jnp.exp2(scores - top)
        total = jnp.sum(weights, axis=1, keepdims=True)
        out = dot_nt(kv_ref[at_value], weights.astype(BF16))
        stat_ref[...] = jnp.where(lane == h, top + jnp.log2(total), stat_ref[...])
        inverse = jnp.transpose(jnp.broadcast_to(1.0 / total, (rows, 128)))[:1]
        o_ref[pl.ds(pl.multiple_of(h * head_dim, head_dim), head_dim)] = (out * inverse).astype(BF16)
        return 0

    lax.fori_loop(0, heads, head_step, 0)
    lse_ref[...] = jnp.transpose(stat_ref[...])[:heads]


def forward_call(x_cols, emb, gain, bias, w_rows, q, mask, per_shard):
    seqs, width, length = x_cols.shape
    heads, rows, head_dim = q.shape
    pair_rows = w_rows.shape[0]
    whole = pl.BlockSpec(memory_space=pltpu.VMEM)

    def per_seq(*dims):
        return pl.BlockSpec((None,) + dims, lambda s: (s, 0, 0))

    return pl.pallas_call(
        functools.partial(forward_kernel, per_shard),
        grid=(seqs,),
        in_specs=[per_seq(width, length), per_seq(width, 1), whole, whole, whole, whole, per_seq(1, length)],
        out_specs=[per_seq(pair_rows, length), per_seq(heads * head_dim, rows), per_seq(heads, rows)],
        out_shape=[
            jax.ShapeDtypeStruct((seqs, pair_rows, length), BF16),
            jax.ShapeDtypeStruct((seqs, heads * head_dim, rows), BF16),
            jax.ShapeDtypeStruct((seqs, heads, rows), F32),
        ],
        scratch_shapes=[pltpu.VMEM((width, length), BF16), pltpu.VMEM((rows, 128), F32)],
        compiler_params=pltpu.CompilerParams(vmem_limit_bytes=VMEM_LIMIT),
        name="attend",
    )(x_cols, emb, gain, bias, w_rows, q, mask)


def backward_kernel(per_shard, x_ref, emb_ref, gain_ref, bias_ref, w_ref, q_ref, qt_ref, do_ref, dot_ref, lse_ref, delta_ref, mask_ref, kv_ref,
                    g_ref, dw_ref, dq_ref, dgain_ref, dbias_ref, demb_ref, xn_ref, dkv_ref):
    heads, rows, head_dim = q_ref.shape
    width, length = x_ref.shape
    piece = min(256, length)

    @pl.when(pl.program_id(0) == 0)
    def _():
        dw_ref[...] = jnp.zeros_like(dw_ref)
        dq_ref[...] = jnp.zeros_like(dq_ref)
        dgain_ref[...] = jnp.zeros_like(dgain_ref)
        dbias_ref[...] = jnp.zeros_like(dbias_ref)

    def norm_step(i, _):
        at = pl.ds(pl.multiple_of(i * piece, piece), piece)
        normed, _unused = norm_columns(x_ref[:, at], emb_ref[...])
        xn_ref[:, at] = (normed * gain_ref[...] + bias_ref[...]).astype(BF16)
        return 0

    lax.fori_loop(0, length // piece, norm_step, 0)
    scale = head_dim ** (-0.5)
    factor = LOG2E * scale

    def head_step(h, _):
        at_key, at_value = head_rows(h, per_shard, head_dim)
        keys = kv_ref[at_key]
        weights = jnp.exp2(dot(q_ref[h], keys) * factor + mask_ref[...] - lse_ref[h])
        dkv_ref[at_value] = dot(dot_ref[h], weights.astype(BF16)).astype(BF16)
        grad = dot(do_ref[h], kv_ref[at_value]) - delta_ref[h]
        grad = (weights * grad).astype(BF16)
        dkv_ref[at_key] = (dot(qt_ref[h], grad) * scale).astype(BF16)
        dq_ref[h] += dot_nt(keys, grad) * scale
        return 0

    lax.fori_loop(0, heads, head_step, 0)
    block = 512 if dw_ref.shape[0] % 512 == 0 else 160

    def weight_step(i, _):
        at = pl.ds(pl.multiple_of(i * block, block), block)
        dw_ref[at] += dot_nt(dkv_ref[at], xn_ref[...])
        return 0

    lax.fori_loop(0, dw_ref.shape[0] // block, weight_step, 0)

    def byte_step(i, carry):
        at = pl.ds(pl.multiple_of(i * piece, piece), piece)
        grad = dot(w_ref[...], dkv_ref[:, at])
        normed, inverse = norm_columns(x_ref[:, at], emb_ref[...])
        dbias_ref[...] += jnp.sum(grad, axis=1, keepdims=True)
        dgain_ref[...] += jnp.sum(grad * normed, axis=1, keepdims=True)
        scaled = grad * gain_ref[...]
        first = jnp.mean(scaled, axis=0, keepdims=True)
        second = jnp.mean(scaled * normed, axis=0, keepdims=True)
        shifted = (scaled - first - normed * second) * inverse
        g_ref[:, at] = shifted.astype(BF16)
        return carry + jnp.sum(shifted, axis=1, keepdims=True)

    demb_ref[...] = lax.fori_loop(0, length // piece, byte_step, jnp.zeros((width, 1), F32))


def backward_call(x_cols, emb, gain, bias, w, q, qt, grad_out, grad_out_t, lse, delta, mask, pairs, per_shard):
    seqs, width, length = x_cols.shape
    heads, rows, head_dim = q.shape
    pair_rows = w.shape[1]
    whole = pl.BlockSpec(memory_space=pltpu.VMEM)

    def per_seq(*dims):
        return pl.BlockSpec((None,) + dims, lambda s: (s,) + (0,) * len(dims))

    return pl.pallas_call(
        functools.partial(backward_kernel, per_shard),
        grid=(seqs,),
        in_specs=[
            per_seq(width, length), per_seq(width, 1), whole, whole, whole, whole, whole,
            per_seq(heads, rows, head_dim), per_seq(heads, head_dim, rows),
            per_seq(heads, rows, 1), per_seq(heads, rows, 1), per_seq(1, length), per_seq(pair_rows, length),
        ],
        out_specs=[per_seq(width, length), whole, whole, whole, whole, per_seq(width, 1)],
        out_shape=[
            jax.ShapeDtypeStruct((seqs, width, length), BF16),
            jax.ShapeDtypeStruct((pair_rows, width), F32),
            jax.ShapeDtypeStruct((heads, head_dim, rows), F32),
            jax.ShapeDtypeStruct((width, 1), F32),
            jax.ShapeDtypeStruct((width, 1), F32),
            jax.ShapeDtypeStruct((seqs, width, 1), F32),
        ],
        scratch_shapes=[pltpu.VMEM((width, length), BF16), pltpu.VMEM((pair_rows, length), BF16)],
        compiler_params=pltpu.CompilerParams(vmem_limit_bytes=VMEM_LIMIT),
        name="attend_back",
    )(x_cols, emb, gain, bias, w, q, qt, grad_out, grad_out_t, lse, delta, mask, pairs)


def mesh_at(di=None, db=None, dh=None, core=None):
    items, blk, heads = lax.axis_index("items"), lax.axis_index("blk"), lax.axis_index("heads")
    return (items if di is None else di, blk if db is None else db, heads if dh is None else dh)


def places():
    items, blk, heads = lax.axis_index("items"), lax.axis_index("blk"), lax.axis_index("heads")
    core = lax.rem(items, 2)
    return items, blk, heads, items // 2, core


def send(src, dst, sems, recvs, target):
    copy = pltpu.make_async_remote_copy(
        src_ref=src, dst_ref=dst, send_sem=sems, recv_sem=recvs, device_id=target, device_id_type=pl.DeviceIdType.MESH)
    copy.start()
    return copy


def greet(targets):
    barrier = pltpu.get_barrier_semaphore()
    for target in targets:
        pl.semaphore_signal(barrier, inc=1, device_id=target, device_id_type=pl.DeviceIdType.MESH)
    pl.semaphore_wait(barrier, len(targets))


def first_kernel(x_hbm, pad_ref, lang_ref, table_ref, lgain, lbias, mgain, mbias, bdown, igain, ibias, bup, lat_ref, wq_ref, wk_hbm, wv_hbm, wo_hbm, wu_hbm, wd_hbm,
                 wcols_out, all_ref, kv_out, xn_out, att_ref, lse_ref, qt_ref, latn_ref, bup_all, x_out, rows_ref, mask_ref, lang_out, latf_ref, vecs_ref,
                 wcols_ref, pair_shard, lat_shard, x_ref, xbuf, x32, xn_ref, pair_ref, kv_ref, cols_ref, q_ref, o_tmp, o_own, o_send, o_got, stat_ref, stat_send, stat_own, stat_got,
                 pair_ss, pair_rs, lat_ss, lat_rs, q_ss, q_rs, misc_ss, misc_rs, o_ss, o_rs, own_sem, xn_sem, kv_sem, x_sem, w_sem):
    items, blk, me, hi, core = places()
    shards = lax.axis_size("heads")
    seqs, width, length = x_ref.shape
    rows = qt_ref.shape[3]
    local_rows = rows // 2
    heads, _, head_dim = q_ref.shape
    cols = heads * head_dim // shards
    per_shard = heads // shards
    sibling = items + 1 - 2 * core
    other = 1 - blk
    to_sib, to_x, to_y = mesh_at(di=sibling), mesh_at(db=other), mesh_at(di=(1 - hi) * 2 + core)
    z_of = [lax.rem(me + d, shards) for d in range(shards)]
    z_back = [lax.rem(me + shards - d, shards) for d in range(shards)]
    weights = [pltpu.make_async_copy(src, dst, w_sem.at[n]) for n, (src, dst) in enumerate((
        (wk_hbm, pair_shard.at[0]), (wv_hbm, pair_shard.at[1]), (wo_hbm, lat_shard.at[0]), (wu_hbm, lat_shard.at[1]), (wd_hbm, lat_shard.at[2])))]
    for copy in weights:
        copy.start()
    depth, step_rows = xbuf.shape[:2]

    def load_bytes(c):
        return pltpu.make_async_copy(x_hbm.at[pl.ds(c * step_rows, step_rows)], xbuf.at[c % depth], x_sem.at[c % depth])

    for c in range(depth):
        load_bytes(c).start()
    greet([to_sib, to_x, to_y] + [mesh_at(dh=z_of[d]) for d in range(1, shards)])

    share = cols // 4
    chip = hi * 2 + blk
    chip_x, chip_y, chip_xy = hi * 2 + other, (1 - hi) * 2 + blk, (1 - hi) * 2 + other

    def region(ref, shard, chip_at, lanes_of):
        half = ref.shape[2] // 2
        return ref.at[:, pl.ds(pl.multiple_of(shard * cols + chip_at * share, 16), share), pl.ds(pl.multiple_of(lanes_of * half, 128), half)]

    def lane_half(ref, shard, lanes_of):
        half = ref.shape[2] // 2
        return ref.at[:, pl.ds(pl.multiple_of(shard * cols, 16), cols), pl.ds(pl.multiple_of(lanes_of * half, 128), half)]

    pending = []
    local = []
    near = me + 1 - 2 * lax.rem(me, 2)
    far, cross = lax.rem(me + 2, 4), lax.rem(near + 2, 4)
    shard_at = [me, near, far, cross]
    double = {"l1": (0, blk, to_x), "l2": (1, hi, to_y)}

    def band(ref, shard, part):
        half = ref.shape[2] // 2
        at = pl.ds(pl.multiple_of(shard * cols + part * 2 * share, 16), 2 * share)
        return ref.at[:, at, pl.ds(pl.multiple_of(core * half, 128), half)]

    kinds = {"pair": (pair_shard, pair_ref, pair_ss, pair_rs)}
    for m in range(3):
        one = pl.ds(m, 1)
        kinds[f"l{m}"] = (lat_shard.at[one], all_ref.at[one], lat_ss.at[m], lat_rs.at[m])

    def recv(kind, d, stage, where):
        _, dst, ss, rs = kinds[kind]
        pltpu.make_async_remote_copy(src_ref=where, dst_ref=where, send_sem=ss.at[d, stage], recv_sem=rs.at[d, stage],
                                     device_id=to_sib, device_id_type=pl.DeviceIdType.MESH).wait_recv()

    def out_z(kind, d):
        src, dst, ss, rs = kinds[kind]
        def own_part(ref, shard):
            return band(ref, shard, double[kind][1]) if kind in double else region(ref, shard, chip, core)

        if d == 3:
            block = own_part(dst, far)
            pending.append(send(block, block, ss.at[d, 0], rs.at[d, 0], mesh_at(dh=near)))
        else:
            pending.append(send(own_part(src, 0), own_part(dst, me), ss.at[d, 0], rs.at[d, 0], mesh_at(dh=shard_at[d])))

    def after_z(kind, d):
        _, dst, ss, rs = kinds[kind]
        if kind in double:
            mine = band(dst, shard_at[d], double[kind][1])
            recv(kind, d, 0, mine)
            pending.append(send(mine, mine, ss.at[d, 1], rs.at[d, 1], double[kind][2]))
            return
        mine = region(dst, shard_at[d], chip, core)
        recv(kind, d, 0, mine)
        pending.append(send(mine, mine, ss.at[d, 1], rs.at[d, 1], to_x))
        pending.append(send(mine, mine, ss.at[d, 2], rs.at[d, 2], to_y))

    def after_x(kind, d):
        _, dst, ss, rs = kinds[kind]
        got = region(dst, shard_at[d], chip_x, core)
        recv(kind, d, 1, got)
        pending.append(send(got, got, ss.at[d, 3], rs.at[d, 3], to_y))

    def after_y(kind, d):
        _, dst, ss, rs = kinds[kind]
        if kind in double:
            recv(kind, d, 1, band(dst, shard_at[d], 1 - double[kind][1]))
        else:
            recv(kind, d, 2, region(dst, shard_at[d], chip_y, core))
            recv(kind, d, 3, region(dst, shard_at[d], chip_xy, core))
        half = lane_half(dst, shard_at[d], core)
        pending.append(send(half, half, ss.at[d, 4], rs.at[d, 4], to_sib))

    def after_sib(kind, d):
        _, dst, ss, rs = kinds[kind]
        recv(kind, d, 4, lane_half(dst, shard_at[d], 1 - core))

    for copy in weights:
        copy.wait()
    own_pair = pltpu.make_async_copy(pair_shard, pair_ref.at[:, pl.ds(pl.multiple_of(me * cols, 16), cols)], own_sem.at[0])
    own_lat = pltpu.make_async_copy(lat_shard, all_ref.at[:, pl.ds(pl.multiple_of(me * cols, 16), cols)], own_sem.at[1])
    own_pair.start()
    own_lat.start()
    my_rows = pl.ds(pl.multiple_of(blk * local_rows, 128), local_rows)
    other_rows = pl.ds(pl.multiple_of(other * local_rows, 128), local_rows)

    vecs_ref[...] = jnp.zeros_like(vecs_ref)
    for i, vector in enumerate((lgain, lbias, mgain, mbias, bdown, igain, ibias, bup)):
        vecs_ref[i:i + 1, :vector.shape[0]] = vector[...].reshape(1, vector.shape[0])
    rows_ref[0:1] = vecs_ref[5:6, :width]
    rows_ref[1:2] = vecs_ref[6:7, :width]
    rows_ref[4:8] = jnp.zeros((4, width), F32)
    lang_out[...] = jnp.zeros_like(lang_out)
    for s in range(seqs):
        lang = lang_ref[me * seqs + s]
        picked = lax.broadcasted_iota(jnp.int32, table_ref.shape, 0) == lang
        rows_ref[2 + s:3 + s] = jnp.sum(jnp.where(picked, table_ref[...].astype(F32), 0.0), axis=0, keepdims=True)
        lang_out[s:s + 1] = jnp.where(lax.broadcasted_iota(jnp.int32, (1, 128), 1) == lang, 1.0, 0.0)
        mask_ref[s] = jnp.where(pad_ref[pl.ds(me * seqs + s, 1)] > 0, 0.0, MASKED)

    def queries_start():
        latf_ref[...] = lat_ref[...].astype(F32)
        lat_out, _, _ = norm_keep(latf_ref[...], vecs_ref[0:1], vecs_ref[1:2])
        lat_low = lat_out.astype(BF16)
        latn_ref[...] = lat_low
        at_head = pl.ds(pl.multiple_of(core * head_dim, 16), head_dim)
        qt_ref[core, me, :, my_rows] = dot_nt(wq_ref[at_head], lat_low).astype(BF16)
        bup_ref = vecs_ref.at[:, pl.ds(0, bup_all.shape[2])]
        bup_all[me] = bup_ref[...]
        for d in range(1, shards):
            my_q = qt_ref.at[core, me, :, my_rows]
            pending.append(send(my_q, my_q, q_ss.at[0, d], q_rs.at[0, d], mesh_at(dh=z_back[d])))
        for d in range(1, shards):
            pending.append(send(bup_ref, bup_all.at[me], misc_ss.at[d], misc_rs.at[d], mesh_at(dh=z_back[d])))

    cols_ref[...] = jnp.transpose(rows_ref[...])
    def pick_bytes(c):
        load_bytes(c).wait()
        at = slice(c * step_rows, (c + 1) * step_rows)
        for j in range(x32.shape[0]):
            lanes = slice(j * 128, (j + 1) * 128)
            x32[j] = xbuf[c % depth, :, :, lanes].astype(F32).reshape(x32.shape[1:])
            for s in range(seqs):
                x_ref[s, lanes, at] = jnp.transpose(x32[j, pl.ds(me * seqs + s, step_rows, stride=x_hbm.shape[1])]).astype(BF16)
        if (c + depth) * step_rows < length:
            load_bytes(c + depth).start()
        if (c + 1) * step_rows == length:
            copy = pltpu.make_async_copy(x_ref, x_out, x_sem.at[depth])
            copy.start()
            local.append(copy)


    def queries_z():
        for d in range(1, shards):
            wait_plain(qt_ref.at[core, z_of[d], :, my_rows], q_ss.at[0, d], q_rs.at[0, d])
        part = qt_ref.at[core, :, :, my_rows]
        pending.append(send(part, part, q_ss.at[1, 0], q_rs.at[1, 0], to_x))

    def queries_x():
        wait_plain(qt_ref.at[core, :, :, other_rows], q_ss.at[1, 0], q_rs.at[1, 0])
        pending.append(send(qt_ref.at[core], qt_ref.at[core], q_ss.at[1, 1], q_rs.at[1, 1], to_sib))

    def queries_sib():
        wait_plain(qt_ref.at[1 - core], q_ss.at[1, 1], q_rs.at[1, 1])

    def wait_plain(where, ss, rs):
        pltpu.make_async_remote_copy(src_ref=where, dst_ref=where, send_sem=ss, recv_sem=rs,
                                     device_id=to_sib, device_id_type=pl.DeviceIdType.MESH).wait_recv()

    piece = min(256, length)

    def norm_bytes(s):
        def norm_step(i, _):
            at = pl.ds(pl.multiple_of(i * piece, piece), piece)
            normed, _unused = norm_columns(x_ref[s, :, at], cols_ref[:, 2 + s:3 + s])
            xn_ref[s, :, at] = (normed * cols_ref[:, 0:1] + cols_ref[:, 1:2]).astype(BF16)
            return 0
        lax.fori_loop(0, length // piece, norm_step, 0)
        copy = pltpu.make_async_copy(xn_ref.at[s], xn_out.at[s], xn_sem.at[s])
        copy.start()
        local.append(copy)

    def project(d):
        at = pl.ds(pl.multiple_of(shard_at[d] * cols, 16), cols)

        def step(i, _):
            s, part = i // 2, lax.rem(i, 2)
            kv_ref[s, part, at] = dot(pair_ref[part, at], xn_ref[s]).astype(BF16)
            return 0
        lax.fori_loop(0, 2 * seqs, step, 0)
        copy = pltpu.make_async_copy(kv_ref.at[:, :, at], kv_out.at[:, :, at], kv_sem.at[d])
        copy.start()
        local.append(copy)

    factor = LOG2E * head_dim ** (-0.5)
    lane = lax.broadcasted_iota(jnp.int32, (rows, 128), 1)
    stat_ref[...] = jnp.zeros_like(stat_ref)

    def turn_queries(d):
        for j in range(per_shard):
            h = shard_at[d] * per_shard + j
            q_ref[h] = jnp.transpose(qt_ref[j, shard_at[d]])

    def attend(d, s):
        def head_step(j, _):
            h = shard_at[d] * per_shard + j
            at = pl.ds(pl.multiple_of(h * head_dim, 16), head_dim)
            scores = dot(q_ref[h], kv_ref[s, 0, at]) * factor + mask_ref[s]
            top = jnp.max(scores, axis=1, keepdims=True)
            weights = jnp.exp2(scores - top)
            total = jnp.sum(weights, axis=1, keepdims=True)
            out = dot_nt(kv_ref[s, 1, at], weights.astype(BF16))
            stat_ref[s] = jnp.where(lane == h, top + jnp.log2(total), stat_ref[s])
            inverse = jnp.transpose(jnp.broadcast_to(1.0 / total, (rows, 128)))[:1]
            o_tmp[...] = out * inverse
            o_own[s, at] = o_tmp[:, my_rows]
            o_send[s, at] = o_tmp[:, other_rows].astype(BF16)
            return 0
        lax.fori_loop(0, per_shard, head_step, 0)
        part = pl.ds(pl.multiple_of(shard_at[d] * cols, 16), cols)
        pending.append(send(o_send.at[s, part], o_got.at[s, part], o_ss.at[d, s], o_rs.at[d, s], to_x))

    def stats_send():
        for s in range(seqs):
            at = pl.ds(s * heads, heads)
            stats = jnp.transpose(stat_ref[s])[:heads]
            stat_send[...] = stats
            stat_own[at] = stat_send[:, my_rows]
            stat_got[0, at] = stat_send[:, other_rows]
        pending.append(send(stat_got.at[0], stat_got.at[1], o_ss.at[shards, 0], o_rs.at[shards, 0], to_x))

    def turn_weights():
        block = 256
        for part in range(2):
            for i in range(pair_ref.shape[1] // block):
                wcols_ref[part, :, i * block:(i + 1) * block] = jnp.transpose(pair_ref[part, i * block:(i + 1) * block])
        copy = pltpu.make_async_copy(wcols_ref, wcols_out, w_sem.at[5])
        copy.start()
        local.append(copy)

    out_z("pair", 1)
    out_z("pair", 2)
    out_z("l0", 1)
    pick_bytes(0)
    pick_bytes(1)
    pick_bytes(2)
    pick_bytes(3)
    pick_bytes(4)
    pick_bytes(5)
    pick_bytes(6)
    after_z("l0", 1)
    out_z("l0", 2)
    pick_bytes(7)
    after_z("pair", 1)
    after_z("pair", 2)
    out_z("pair", 3)
    norm_bytes(0)
    norm_bytes(1)
    queries_start()
    after_x("l0", 1)
    out_z("l1", 1)
    own_pair.wait()
    project(0)
    after_z("pair", 3)
    after_z("l0", 2)
    out_z("l0", 3)
    out_z("l1", 2)
    after_x("pair", 1)
    after_x("pair", 2)
    queries_z()
    after_x("l0", 2)
    after_y("l0", 1)
    after_x("pair", 3)
    after_sib("l0", 1)
    after_z("l0", 3)
    out_z("l2", 1)
    queries_x()
    queries_sib()
    turn_queries(0)
    attend(0, 0)
    after_x("l0", 3)
    after_z("l1", 1)
    after_z("l1", 2)
    out_z("l1", 3)
    attend(0, 1)
    after_y("pair", 1)
    after_y("pair", 2)
    out_z("l2", 2)
    after_z("l2", 1)
    after_y("l0", 2)
    after_y("pair", 3)
    after_sib("pair", 1)
    after_sib("pair", 2)
    project(1)
    after_y("l0", 3)
    after_sib("l0", 2)
    project(2)
    after_sib("pair", 3)
    after_z("l1", 3)
    project(3)
    after_sib("l0", 3)
    after_z("l2", 2)
    after_y("l2", 1)
    out_z("l2", 3)
    turn_queries(1)
    attend(1, 0)
    after_y("l1", 1)
    after_y("l1", 2)
    attend(1, 1)
    turn_queries(2)
    attend(2, 0)
    attend(2, 1)
    after_z("l2", 3)
    after_y("l2", 2)
    turn_queries(3)
    attend(3, 0)
    after_y("l1", 3)
    attend(3, 1)
    after_sib("l1", 1)
    after_sib("l1", 2)
    after_sib("l2", 1)
    after_sib("l2", 2)
    stats_send()
    turn_weights()
    after_y("l2", 3)
    after_sib("l1", 3)
    after_sib("l2", 3)

    wait_plain(stat_got.at[1], o_ss.at[shards, 0], o_rs.at[shards, 0])
    own_lse, got_lse = stat_own[...], stat_got[1]
    top = jnp.maximum(own_lse, got_lse)
    own_share, got_share = jnp.exp2(own_lse - top), jnp.exp2(got_lse - top)
    total = own_share + got_share
    lse = top + jnp.log2(total)
    own_share, got_share = own_share / total, got_share / total
    for s in range(seqs):
        lse_ref[s] = lse[s * heads:(s + 1) * heads]
        for d in range(shards):
            part = pl.ds(pl.multiple_of(shard_at[d] * cols, 16), cols)
            wait_plain(o_got.at[s, part], o_ss.at[d, s], o_rs.at[d, s])
    for s in range(seqs):
        for h in range(heads):
            at = slice(h * head_dim, (h + 1) * head_dim)
            n = s * heads + h
            att_ref[s, at] = o_own[s, at] * own_share[n:n + 1] + o_got[s, at].astype(F32) * got_share[n:n + 1]
    for d in range(1, shards):
        wait_plain(bup_all.at[z_of[d]], misc_ss.at[d], misc_rs.at[d])
    own_lat.wait()
    for copy in local:
        copy.wait()
    for copy in pending:
        copy.wait_send()


def first_call(inputs, padding, language, table, vectors, latents, wq_rows, weights, rows, seqs):
    length, local_seqs, width = inputs.shape
    local_rows, width_lat = latents.shape
    shards = lax.axis_size("heads")
    heads = HEADS
    head_dim = width_lat // heads
    whole = pl.BlockSpec(memory_space=pltpu.VMEM)
    hbm = pl.BlockSpec(memory_space=pl.ANY)
    out = jax.ShapeDtypeStruct
    sem = pltpu.SemaphoreType.DMA
    return pl.pallas_call(
        first_kernel,
        in_specs=[hbm, whole, pl.BlockSpec(memory_space=pltpu.SMEM)] + [whole] * 11 + [hbm] * 5,
        out_specs=[hbm, hbm, hbm, hbm] + [whole] * 5 + [hbm] + [whole] * 5,
        out_shape=[
            out((2, width, width_lat), BF16),
            out((3, width_lat, width_lat), BF16),
            out((seqs, 2, width_lat, length), BF16),
            out((seqs, width, length), BF16),
            out((seqs, width_lat, local_rows), F32),
            out((seqs, heads, local_rows), F32),
            out((heads // shards, shards, head_dim, rows), BF16),
            out((local_rows, width_lat), BF16),
            out((shards, 8, 384), F32),
            out((seqs, width, length), BF16),
            out((8, width), F32),
            out((seqs, 1, length), F32),
            out((8, 128), F32),
            out((local_rows, width_lat), F32),
            out((8, width_lat), F32),
        ],
        scratch_shapes=[
            pltpu.VMEM((2, width, width_lat), BF16),
            pltpu.VMEM((2, width_lat // shards, width), BF16),
            pltpu.VMEM((3, width_lat // shards, width_lat), BF16),
            pltpu.VMEM((seqs, width, length), BF16),
            pltpu.VMEM((4, 128, local_seqs, width), BF16),
            pltpu.VMEM((width // 128, 128 * local_seqs, 128), F32),
            pltpu.VMEM((seqs, width, length), BF16),
            pltpu.VMEM((2, width_lat, width), BF16),
            pltpu.VMEM((seqs, 2, width_lat, length), BF16),
            pltpu.VMEM((width, 8), F32),
            pltpu.VMEM((heads, rows, head_dim), BF16),
            pltpu.VMEM((head_dim, rows), F32),
            pltpu.VMEM((seqs, width_lat, local_rows), F32),
            pltpu.VMEM((seqs, width_lat, local_rows), BF16),
            pltpu.VMEM((seqs, width_lat, local_rows), BF16),
            pltpu.VMEM((seqs, rows, 128), F32),
            pltpu.VMEM((heads, rows), F32),
            pltpu.VMEM((seqs * heads, local_rows), F32),
            pltpu.VMEM((2, seqs * heads, local_rows), F32),
            sem((shards, 5)), sem((shards, 5)), sem((3, shards, 5)), sem((3, shards, 5)),
            sem((2, shards)), sem((2, shards)), sem((shards,)), sem((shards,)),
            sem((shards + 1, seqs)), sem((shards + 1, seqs)), sem((2,)), sem((seqs,)), sem((shards,)), sem((5,)), sem((6,)),
        ],
        compiler_params=pltpu.CompilerParams(vmem_limit_bytes=VMEM_LIMIT, collective_id=1, has_side_effects=True),
        name="first",
    )(inputs, padding, language, table, *vectors, latents, wq_rows, *weights)


class Reduce:
    def __init__(self, src, half, got_sib, got_chip, got_z, out, ss, rs, pending, x_first=True, stage=None, stage_sem=None):
        self.src, self.half, self.got_sib, self.got_chip, self.got_z, self.out = src, half, got_sib, got_chip, got_z, out
        self.ss, self.rs, self.pending, self.x_first = ss, rs, pending, x_first
        self.stage, self.stage_sem, self.kept = stage, stage_sem, None
        self.split = src is not None and src.shape[3] == half.shape[3]
        items, blk, self.me, hi, self.core = places()
        self.shards = lax.axis_size("heads")
        other = 1 - blk
        self.chip = hi * 2 + blk
        self.chip_x, self.chip_y, self.chip_xy = hi * 2 + other, (1 - hi) * 2 + blk, (1 - hi) * 2 + other
        self.to_x, self.to_y = mesh_at(db=other), mesh_at(di=(1 - hi) * 2 + self.core)
        self.to_sib = mesh_at(di=items + 1 - 2 * self.core)
        self.n, _, self.cols, self.width = half.shape
        self.share = self.cols // 4
        self.near = self.me + 1 - 2 * lax.rem(self.me, 2)
        self.far, self.cross = lax.rem(self.me + 2, 4), lax.rem(self.near + 2, 4)

    def rows(self, chip):
        return pl.ds(pl.multiple_of(chip * self.share, 16), self.share)

    def lanes(self, core):
        return pl.ds(pl.multiple_of(core * self.width, 128), self.width)

    def go(self, src, dst, i, target):
        self.pending.append(send(src, dst, self.ss.at[i], self.rs.at[i], target))

    def arrived(self, where, i):
        pltpu.make_async_remote_copy(src_ref=where, dst_ref=where, send_sem=self.ss.at[i], recv_sem=self.rs.at[i],
                                     device_id=self.to_sib, device_id_type=pl.DeviceIdType.MESH).wait_recv()

    def start(self):
        theirs = self.src if self.split else self.src.at[:, :, :, self.lanes(1 - self.core)]
        self.go(theirs, self.got_sib, 0, self.to_sib)

    def join_sib(self):
        self.arrived(self.got_sib, 0)

        def step(i, _):
            n, h = i // self.shards, lax.rem(i, self.shards)
            own = self.half[n, h] if self.split else self.src[n, h, :, self.lanes(self.core)]
            self.half[n, h] = (own.astype(F32) + self.got_sib[n, h].astype(F32)).astype(self.half.dtype)
            return 0
        lax.fori_loop(0, self.n * self.shards, step, 0)

    def send_chips(self):
        low, high = pl.ds(0, 2), pl.ds(2, 2)
        self.go(self.half.at[:, low, self.rows(self.chip_x)], self.got_chip.at[0], 1, self.to_x)
        self.go(self.half.at[:, high, self.rows(self.chip_y)], self.got_chip.at[2], 3, self.to_y)
        self.go(self.half.at[:, low, self.rows(self.chip_xy)], self.got_chip.at[1], 2, self.to_x)
        self.go(self.half.at[:, high, self.rows(self.chip_xy)], self.got_chip.at[3], 4, self.to_y)

    def add(self, slot, first, rows):
        self.arrived(self.got_chip.at[slot], 1 + slot)
        for n in range(self.n):
            for h in range(2):
                total = self.half[n, first + h, rows].astype(F32) + self.got_chip[slot, n, h].astype(F32)
                self.half[n, first + h, rows] = total.astype(self.half.dtype)

    def join_first(self):
        self.add(1, 0, self.rows(self.chip_y))
        self.go(self.half.at[:, pl.ds(0, 2), self.rows(self.chip_y)], self.got_chip.at[4], 5, self.to_y)
        self.add(3, 2, self.rows(self.chip_x))
        self.go(self.half.at[:, pl.ds(2, 2), self.rows(self.chip_x)], self.got_chip.at[5], 6, self.to_x)
        self.add(0, 0, self.rows(self.chip))
        self.add(2, 2, self.rows(self.chip))

    def join_chips(self):
        mine = self.rows(self.chip)
        self.add(4, 0, mine)
        self.add(5, 2, mine)
        for i, shard in enumerate((self.near, self.cross)):
            self.go(self.half.at[:, shard, mine], self.got_z.at[i], 7 + i, mesh_at(dh=self.near))

    def join_near(self):
        mine = self.rows(self.chip)
        for i, shard in enumerate((self.me, self.far)):
            self.arrived(self.got_z.at[i], 7 + i)
            for n in range(self.n):
                total = self.half[n, shard, mine].astype(F32) + self.got_z[i, n].astype(F32)
                self.half[n, shard, mine] = total.astype(self.half.dtype)
        self.go(self.half.at[:, self.far, mine], self.got_z.at[2], 9, mesh_at(dh=self.far))

    def join_z(self):
        self.arrived(self.got_z.at[2], 9)
        mine = self.rows(self.chip)
        for n in range(self.n):
            total = self.half[n, self.me, mine].astype(F32) + self.got_z[2, n].astype(F32)
            if self.stage is None:
                self.out[n, mine, self.lanes(self.core)] = total.astype(self.out.dtype)
            else:
                self.stage[n] = total.astype(self.out.dtype)
        src = self.piece(self.chip)
        if self.stage is not None:
            self.kept = pltpu.make_async_copy(self.stage, src, self.stage_sem)
            self.kept.start()
            src = self.stage
        self.go(src, self.piece(self.chip), 10, self.to_x)
        self.go(src, self.piece(self.chip), 11, self.to_y)

    def piece(self, chip):
        return self.out.at[:, self.rows(chip), self.lanes(self.core)]

    def pass_on(self, chip, i, target):
        self.go(self.piece(chip), self.piece(chip), i, target)

    def share_chips(self):
        if self.x_first:
            self.arrived(self.piece(self.chip_x), 10)
            self.pass_on(self.chip_x, 12, self.to_y)
        else:
            self.arrived(self.piece(self.chip_y), 11)
            self.pass_on(self.chip_y, 12, self.to_x)

    def share_sib(self):
        if self.x_first:
            self.arrived(self.piece(self.chip_y), 11)
        else:
            self.arrived(self.piece(self.chip_x), 10)
        self.arrived(self.piece(self.chip_xy), 12)
        if self.kept is not None:
            self.kept.wait()
        half = self.out.at[:, :, self.lanes(self.core)]
        self.go(half, half, 13, self.to_sib)

    def finish(self):
        self.arrived(self.out.at[:, :, self.lanes(1 - self.core)], 13)


def second_kernel(x_hbm, rows_ref, mask_ref, w_hbm, qt_ref, kv_hbm, xn_hbm, do_in, stat_in, mixed_in, lat_in, grads_hbm, vec_in, lang_in, latsum_in, wq_ref, lat_raw, lgain_ref,
                  g_out, mixed_out, dw_out, dlat_out, small_out, glat_out, vec_out, dq_out, latn_ref,
                  w_ref, x_ref, xn_ref, cols_ref, kv_ref, dkv_ref, q_ref, do_ref, stat_ref, stat_cols, dq_ref, dw_ref, dw_tmp,
                  g_half, g_chip, g_z, w_half, w_sib, w_chip, w_z, q_half, q_sib, q_chip, q_z, s_half, s_sib, s_chip, s_z,
                  small_ref, s_ref, l_sib, l_half, l_y, l_sum, l_z, l_tot, lat8_ref,
                  g_stage, w_stage, tq_ref, t_part, t_got, t_z, y_buf, c_buf, x_buf,
                  g_ss, g_rs, w_ss, w_rs, q_ss, q_rs, s_ss, s_rs, l_ss, l_rs, t_ss, t_rs, do_ss, do_rs, misc_ss, misc_rs, mix_ss, mix_rs, a_ss, a_rs, load_sem, kv_sem, stage_sem):
    items, blk, me, hi, core = places()
    shards = lax.axis_size("heads")
    seqs, width, length = x_ref.shape
    heads, rows, head_dim = q_ref.shape
    local_rows = rows // 2
    per_shard = heads // shards
    cols = per_shard * head_dim
    stat_rows = stat_in.shape[0]
    other = 1 - blk
    to_x, to_sib = mesh_at(db=other), mesh_at(di=items + 1 - 2 * core)
    to_y = mesh_at(di=(1 - hi) * 2 + core)
    z_of = [lax.rem(me + d, shards) for d in range(shards)]
    z_back = [lax.rem(me + shards - d, shards) for d in range(shards)]
    my_rows = pl.ds(pl.multiple_of(blk * local_rows, 128), local_rows)
    other_rows = pl.ds(pl.multiple_of(other * local_rows, 128), local_rows)
    pending = []
    dot_ref = w_sib.at[:, :, :, pl.ds(0, rows)]
    grads = [Reduce(None, g_half.at[pl.ds(m, 1)], None, g_chip.at[:, pl.ds(m, 1)], g_z.at[m], dlat_out.at[pl.ds(m, 1)], g_ss.at[m], g_rs.at[m], pending, m != 1,
                        g_stage.at[pl.ds(m, 1)], stage_sem.at[m])
             for m in range(3)]
    pair = [Reduce(dw_ref.at[pl.ds(m, 1)], w_half.at[pl.ds(m, 1)], w_sib.at[pl.ds(m, 1)], w_chip.at[:, pl.ds(m, 1)], w_z.at[m],
                   dw_out.at[pl.ds(m, 1)], w_ss.at[m], w_rs.at[m], pending, m == 0, w_stage.at[pl.ds(m, 1)], stage_sem.at[3 + m]) for m in range(2)]
    query = Reduce(dq_ref, q_half, q_sib, q_chip, q_z, dq_out, q_ss, q_rs, pending, False)
    small = Reduce(s_ref, s_half, s_sib, s_chip, s_z, small_out, s_ss, s_rs, pending)
    greet([to_sib, to_x, to_y] + [mesh_at(dh=z_of[d]) for d in range(1, shards)])

    def arrived(where, ss, rs):
        pltpu.make_async_remote_copy(src_ref=where, dst_ref=where, send_sem=ss, recv_sem=rs,
                                     device_id=to_sib, device_id_type=pl.DeviceIdType.MESH).wait_recv()

    pending.append(send(stat_in, stat_ref.at[pl.ds(0, stat_rows), my_rows], misc_ss.at[0], misc_rs.at[0], to_x))

    def send_do(s):
        pending.append(send(do_in.at[s], dot_ref.at[s, :, :, my_rows], do_ss.at[s], do_rs.at[s], to_x))

    near = me + 1 - 2 * lax.rem(me, 2)
    far, cross = lax.rem(me + 2, 4), lax.rem(near + 2, 4)

    def mixed_pass(block, i, there):
        pending.append(send(mixed_out.at[block], mixed_out.at[block], mix_ss.at[i], mix_rs.at[i], mesh_at(dh=there)))

    def mixed_far():
        mixed_pass(me * seqs + 1, 0, far)

    def mixed_near():
        mixed_pass(me * seqs + 1, 1, near)
        mixed_pass(me * seqs, 4, near)

    def mixed_cross_0():
        mixed_pass(far * seqs, 2, near)

    def mixed_cross_1():
        arrived(mixed_out.at[far * seqs + 1], mix_ss.at[0], mix_rs.at[0])
        mixed_pass(far * seqs + 1, 3, near)

    def latents_share():
        pending.append(send(lat_in, latn_ref.at[my_rows], misc_ss.at[1], misc_rs.at[1], to_x))

    loads = [
        pltpu.make_async_copy(xn_hbm, xn_ref, load_sem.at[0]),
        pltpu.make_async_copy(x_hbm, x_ref, load_sem.at[1]),
        pltpu.make_async_copy(grads_hbm, g_half, load_sem.at[2]),
        pltpu.make_async_copy(lat_raw.at[pl.ds(pl.multiple_of(core * 64 + hi * 32 + me * 8, 8), 8)], lat8_ref, load_sem.at[4]),
    ]
    own_sum = pltpu.make_async_copy(latsum_in.at[pl.ds(pl.multiple_of(core * (local_rows // 2), 8), local_rows // 2)], l_half, load_sem.at[13])
    own_sum.start()
    own_do = pltpu.make_async_copy(do_in, dot_ref.at[:, :, :, my_rows], load_sem.at[5])

    def load_pair(n, start):
        s, h = n // heads, lax.rem(n, heads)
        slot = lax.rem(n, 2)
        copy = pltpu.make_async_copy(kv_hbm.at[s, :, pl.ds(pl.multiple_of(h * head_dim, 16), head_dim)], kv_ref.at[slot], kv_sem.at[slot])
        copy.start() if start else copy.wait()

    load_pair(0, True)
    own_do.start()
    own_w = pltpu.make_async_copy(w_hbm, w_ref, load_sem.at[14])
    for copy in loads + [own_w]:
        copy.start()

    def prepare():
        latn_ref[my_rows] = lat_in[...]
        cols_ref[...] = jnp.transpose(rows_ref[...])
        stat_ref[:stat_rows, my_rows] = stat_in[...]
        stat_ref[stat_rows:] = jnp.zeros((128 - stat_rows, rows), F32)
        for h in range(heads):
            q_ref[h] = jnp.transpose(qt_ref[h % per_shard, h // per_shard])
        dq_ref[...] = jnp.zeros_like(dq_ref)
        small_ref[...] = jnp.zeros_like(small_ref)

    def stats_ready():
        arrived(stat_ref.at[pl.ds(0, stat_rows), other_rows], misc_ss.at[0], misc_rs.at[0])
        stat_cols[...] = jnp.transpose(stat_ref[...])

    scale = head_dim ** (-0.5)
    factor = LOG2E * scale
    lane = lax.broadcasted_iota(jnp.int32, (rows, 128), 1)

    def turn_grads(s):
        arrived(dot_ref.at[s, :, :, other_rows], do_ss.at[s], do_rs.at[s])
        for h in range(heads):
            inner = h % per_shard * head_dim
            do_ref[h] = jnp.transpose(dot_ref[s, h // per_shard, inner:inner + head_dim])

    def head_steps(s, group):
        def head_step(h, _):
            n = s * heads + h
            slot = lax.rem(n, 2)
            load_pair(n, False)

            @pl.when(n + 1 < seqs * heads)
            def _():
                load_pair(n + 1, True)

            at = pl.ds(pl.multiple_of(h * head_dim, 16), head_dim)
            lse = jnp.sum(jnp.where(lane == s * 2 * heads + h, stat_cols[...], 0.0), axis=1, keepdims=True)
            delta = jnp.sum(jnp.where(lane == s * 2 * heads + heads + h, stat_cols[...], 0.0), axis=1, keepdims=True)
            keys = kv_ref[slot, 0]
            weights = jnp.exp2(dot(q_ref[h], keys) * factor + mask_ref[s] - lse)
            part = pl.ds(pl.multiple_of(lax.rem(h, per_shard) * head_dim, 16), head_dim)
            dkv_ref[s, 1, at] = dot(dot_ref[s, h // per_shard, part], weights.astype(BF16)).astype(BF16)
            grad = dot(do_ref[h], kv_ref[slot, 1]) - delta
            grad = (weights * grad).astype(BF16)
            dkv_ref[s, 0, at] = (dot(qt_ref[lax.rem(h, per_shard), h // per_shard], grad) * scale).astype(BF16)
            dq_ref[0, h // per_shard, part] += dot_nt(keys, grad) * scale
            return 0

        lax.fori_loop(2 * group, 2 * group + 2, head_step, 0)

    piece = min(256, length)

    def byte_steps(s):
        def byte_step(i, carry):
            at = pl.ds(pl.multiple_of(i * piece, piece), piece)
            grad = dot(w_ref[0], dkv_ref[s, 0, :, at]) + dot(w_ref[1], dkv_ref[s, 1, :, at])
            normed, inverse = norm_columns(x_ref[s, :, at], cols_ref[:, 2 + s:3 + s])
            small_ref[:, 0:1] += jnp.sum(grad * normed, axis=1, keepdims=True)
            small_ref[:, 1:2] += jnp.sum(grad, axis=1, keepdims=True)
            scaled = grad * cols_ref[:, 0:1]
            first = jnp.mean(scaled, axis=0, keepdims=True)
            second = jnp.mean(scaled * normed, axis=0, keepdims=True)
            shifted = (scaled - first - normed * second) * inverse
            x_ref[s, :, at] = shifted.astype(BF16)
            return carry + jnp.sum(shifted, axis=1, keepdims=True)

        small_ref[:, 2 + s:3 + s] = lax.fori_loop(0, length // piece, byte_step, jnp.zeros((width, 1), F32))
        share = width // shards
        own = pltpu.make_async_copy(x_ref.at[s, pl.ds(pl.multiple_of(me * share, 16), share)], g_out.at[me * seqs + s], load_sem.at[6 + s])
        own.start()
        loads.append(own)

    def bytes_send(s, d):
        share = width // shards
        there = pl.ds(pl.multiple_of(z_back[d] * share, 16), share)
        pending.append(send(x_ref.at[s, there], g_out.at[me * seqs + s], a_ss.at[s, d], a_rs.at[s, d], mesh_at(dh=z_back[d])))

    half_rows, quarter = local_rows // 2, local_rows // 4
    piece_rows = quarter // shards

    def latents_send():
        theirs = latsum_in.at[pl.ds(pl.multiple_of((1 - core) * half_rows, 8), half_rows)]
        pending.append(send(theirs, l_sib, l_ss.at[0], l_rs.at[0], to_sib))

    def latents_sib():
        arrived(l_sib, l_ss.at[0], l_rs.at[0])
        own_sum.wait()
        l_half[...] += l_sib[...]
        pending.append(send(l_half.at[pl.ds(pl.multiple_of((1 - hi) * quarter, 8), quarter)], l_y, l_ss.at[1], l_rs.at[1], to_y))

    def latents_y():
        arrived(l_y, l_ss.at[1], l_rs.at[1])
        l_sum[...] = (l_half[pl.ds(pl.multiple_of(hi * quarter, 8), quarter)] + l_y[...]).reshape(l_sum.shape)
        for d in range(1, shards):
            pending.append(send(l_sum.at[z_back[d]], l_z.at[d - 1], l_ss.at[1 + d], l_rs.at[1 + d], mesh_at(dh=z_back[d])))

    def latents_z():
        total = l_sum[me]
        for d in range(1, shards):
            arrived(l_z.at[d - 1], l_ss.at[1 + d], l_rs.at[1 + d])
            total += l_z[d - 1]
        l_tot[...] = total

    def third_first():
        tq_ref[...] = jnp.transpose(dq_out[0, :, my_rows])
        rows_here = tq_ref[pl.ds(pl.multiple_of(core * half_rows + hi * quarter, 8), quarter)].astype(BF16)
        t_part[...] = dot(rows_here, wq_ref[...]).reshape(t_part.shape)
        for d in range(1, shards):
            pending.append(send(t_part.at[z_back[d]], t_got.at[d - 1], t_ss.at[0, d], t_rs.at[0, d], mesh_at(dh=z_back[d])))

    def third_z():
        grad = t_part[me]
        for d in range(1, shards):
            arrived(t_got.at[d - 1], t_ss.at[0, d], t_rs.at[0, d])
            grad += t_got[d - 1]
        loads[3].wait()
        _, normed, inverse = norm_keep(lat8_ref[...], 1.0, 0.0)
        t_z[me, :piece_rows] = l_tot[...] + norm_back(grad, normed, inverse, lgain_ref[0:1])
        t_z[me, piece_rows:] = jnp.zeros((8, lat8_ref.shape[1]), F32)
        t_z[me, piece_rows:piece_rows + 1] = jnp.sum(grad * normed, axis=0, keepdims=True)
        t_z[me, piece_rows + 1:piece_rows + 2] = jnp.sum(grad, axis=0, keepdims=True)
        for d in range(1, shards):
            pending.append(send(t_z.at[me], t_z.at[me], t_ss.at[1, d], t_rs.at[1, d], mesh_at(dh=z_back[d])))

    def third_y():
        for d in range(1, shards):
            arrived(t_z.at[z_of[d]], t_ss.at[1, d], t_rs.at[1, d])
        y_buf[hi, :quarter] = t_z[:, :piece_rows].reshape(quarter, t_z.shape[2])
        y_buf[hi, quarter:] = t_z[0, piece_rows:] + t_z[1, piece_rows:] + t_z[2, piece_rows:] + t_z[3, piece_rows:]
        pending.append(send(y_buf.at[hi], y_buf.at[hi], t_ss.at[2, 0], t_rs.at[2, 0], to_y))

    def third_core():
        arrived(y_buf.at[1 - hi], t_ss.at[2, 0], t_rs.at[2, 0])
        c_buf[core, :quarter] = y_buf[0, :quarter]
        c_buf[core, quarter:half_rows] = y_buf[1, :quarter]
        c_buf[core, half_rows:] = y_buf[0, quarter:] + y_buf[1, quarter:]
        pending.append(send(c_buf.at[core], c_buf.at[core], t_ss.at[2, 1], t_rs.at[2, 1], to_sib))

    def third_x():
        arrived(c_buf.at[1 - core], t_ss.at[2, 1], t_rs.at[2, 1])
        glat_out[:half_rows] = c_buf[0, :half_rows]
        glat_out[half_rows:] = c_buf[1, :half_rows]
        x_buf[blk] = c_buf[0, half_rows:] + c_buf[1, half_rows:]
        pending.append(send(x_buf.at[blk], x_buf.at[blk], t_ss.at[2, 2], t_rs.at[2, 2], to_x))

    def third_end():
        arrived(x_buf.at[other], t_ss.at[2, 2], t_rs.at[2, 2])
        vec_out[...] = x_buf[0] + x_buf[1]

    def small_start():
        wide_lane = lax.broadcasted_iota(jnp.int32, (width, 128), 1)
        block = jnp.where(wide_lane == 32, small_ref[:, 0:1], 0.0) + jnp.where(wide_lane == 33, small_ref[:, 1:2], 0.0)
        for s in range(seqs):
            block += small_ref[:, 2 + s:3 + s] * lang_in[s:s + 1]
        share = width // shards
        for h in range(shards):
            s_ref[0, h, :, :128] = block[h * share:(h + 1) * share]
            s_ref[0, h, :, 128:] = jnp.zeros((share, 128), F32)
            for v in range(vec_in.shape[0]):
                for b in range(vec_in.shape[1] // 128):
                    s_ref[0, h, v * 10 + b:v * 10 + b + 1, 128:] = vec_in[v:v + 1, b * 128:(b + 1) * 128]
        small.start()

    def weight_steps(part):
        def weight_step(h, _):
            at = pl.ds(pl.multiple_of(h * cols, 16), cols)
            total = dot_nt(dkv_ref[0, part, at], xn_ref[0])
            for s in range(1, seqs):
                total += dot_nt(dkv_ref[s, part, at], xn_ref[s])
            dw_tmp[...] = total.astype(BF16)
            w_half[part, h] = dw_tmp[:, pl.ds(pl.multiple_of(core * (width // 2), 128), width // 2)]
            dw_ref[part, h] = dw_tmp[:, pl.ds(pl.multiple_of((1 - core) * (width // 2), 128), width // 2)]
            return 0
        lax.fori_loop(0, shards, weight_step, 0)

    send_do(0)
    mixed_near()
    prepare()
    own_do.wait()
    stats_ready()
    turn_grads(0)
    send_do(1)
    mixed_far()
    head_steps(0, 0)
    latents_send()
    head_steps(0, 1)
    head_steps(0, 2)
    loads[2].wait()
    grads[2].send_chips()
    head_steps(0, 3)
    loads[1].wait()
    own_w.wait()
    byte_steps(0)
    grads[1].send_chips()
    mixed_cross_0()
    bytes_send(0, 1)
    bytes_send(0, 3)
    turn_grads(1)
    head_steps(1, 0)
    head_steps(1, 1)
    bytes_send(0, 2)
    grads[0].send_chips()
    head_steps(1, 2)
    head_steps(1, 3)
    grads[2].join_first()
    query.start()
    loads[0].wait()
    weight_steps(0)
    latents_sib()
    byte_steps(1)
    query.join_sib()
    small_start()
    grads[0].join_first()
    grads[2].join_chips()
    small.join_sib()
    small.send_chips()
    query.send_chips()
    grads[1].join_first()
    pair[0].start()
    latents_y()
    weight_steps(1)
    pair[1].start()
    grads[0].join_chips()
    pair[0].join_sib()
    bytes_send(1, 3)
    query.join_first()
    pair[0].send_chips()
    grads[2].join_near()
    query.join_chips()
    latents_share()
    grads[1].join_chips()
    pair[1].join_sib()
    pair[1].send_chips()
    pair[0].join_first()
    query.join_near()
    grads[0].join_near()
    small.join_first()
    query.join_z()
    query.share_chips()
    grads[1].join_near()
    pair[1].join_first()
    small.join_chips()
    grads[2].join_z()
    bytes_send(1, 2)
    pair[0].join_chips()
    query.share_sib()
    query.finish()
    third_first()
    grads[0].join_z()
    small.join_near()
    pair[0].join_near()
    grads[0].share_chips()
    grads[2].share_chips()
    small.join_z()
    pair[1].join_chips()
    latents_z()
    grads[1].join_z()
    grads[2].share_sib()
    third_z()
    grads[0].share_sib()
    grads[1].share_chips()
    pair[0].join_z()
    pair[1].join_near()
    mixed_cross_1()
    small.share_chips()
    pair[0].share_chips()
    pair[0].share_sib()
    small.share_sib()
    grads[1].share_sib()
    third_y()
    bytes_send(1, 1)
    grads[2].finish()
    pair[1].join_z()
    grads[0].finish()
    third_core()
    pair[0].finish()
    grads[1].finish()
    pair[1].share_chips()
    pair[1].share_sib()
    third_x()
    pair[1].finish()
    small.finish()
    third_end()
    arrived(latn_ref.at[other_rows], misc_ss.at[1], misc_rs.at[1])
    arrived(mixed_out.at[near * seqs + 1], mix_ss.at[1], mix_rs.at[1])
    arrived(mixed_out.at[near * seqs], mix_ss.at[4], mix_rs.at[4])
    arrived(mixed_out.at[cross * seqs], mix_ss.at[2], mix_rs.at[2])
    arrived(mixed_out.at[cross * seqs + 1], mix_ss.at[3], mix_rs.at[3])
    for d in range(1, shards):
        for s in range(seqs):
            arrived(g_out.at[z_of[d] * seqs + s], a_ss.at[s, d], a_rs.at[s, d])
    for own in loads[4:]:
        own.wait()
    for copy in pending:
        copy.wait_send()


def second_call(x_cols, rows_in, mask, w_cols, qt, pairs, xn, grad_out, stats, mixed, lat_low, grads, vectors, lang_rows, lat_sum, w_query, lat_f32, lat_gain):
    seqs, width, length = x_cols.shape
    rows, width_lat = qt.shape[3], pairs.shape[2]
    local_rows = lat_low.shape[0]
    shards = lax.axis_size("heads")
    heads = HEADS
    head_dim = width_lat // heads
    cols = width_lat // shards
    share = cols // 4
    whole = pl.BlockSpec(memory_space=pltpu.VMEM)
    hbm = pl.BlockSpec(memory_space=pl.ANY)
    out = jax.ShapeDtypeStruct
    vmem = pltpu.VMEM
    sem = pltpu.SemaphoreType.DMA

    assert seqs == 2

    def reduce_buffers(n, lanes, kind, cols=cols):
        half, share = lanes // 2, cols // 4
        return [vmem((n, shards, cols, half), kind), vmem((n, shards, cols, half), kind), vmem((6, n, 2, share, half), kind),
                vmem((shards - 1, n, share, half), kind)]

    return pl.pallas_call(
        second_kernel,
        in_specs=[hbm, whole, whole, hbm, whole, hbm, hbm, hbm, whole, hbm, whole, hbm, whole, whole, hbm, whole, hbm, whole],
        out_specs=[hbm, hbm, hbm, hbm, whole, whole, whole, whole, whole],
        input_output_aliases={9: 1},
        out_shape=[
            out((shards * seqs, width // shards, length), BF16),
            out((shards * seqs, local_rows, width_lat), BF16),
            out((2, cols, width), BF16),
            out((3, cols, width_lat), BF16),
            out((1, width // shards, 256), F32),
            out((local_rows, width_lat), F32),
            out((8, width_lat), F32),
            out((1, cols, rows), F32),
            out((rows, width_lat), BF16),
        ],
        scratch_shapes=[
            vmem((2, width, width_lat), BF16),
            vmem((seqs, width, length), BF16),
            vmem((seqs, width, length), BF16),
            vmem((width, rows_in.shape[0]), F32),
            vmem((2, 2, head_dim, length), BF16),
            vmem((seqs, 2, width_lat, length), BF16),
            vmem((heads, rows, head_dim), BF16),
            vmem((heads, rows, head_dim), BF16),
            vmem((128, rows), F32),
            vmem((rows, 128), F32),
            vmem((1, shards, cols, rows), F32),
            vmem((2, shards, cols, width // 2), BF16),
            vmem((cols, width), BF16),
        ] + [
            vmem((3, shards, cols, width_lat // 2), BF16),
            vmem((6, 3, 2, share, width_lat // 2), BF16),
            vmem((3, 3, 1, share, width_lat // 2), BF16),
        ] + reduce_buffers(2, width, BF16)[:3] + [vmem((2, 3, 1, share, width // 2), BF16)]
        + reduce_buffers(1, rows, F32)
        + reduce_buffers(1, 256, F32, width // shards) + [
            vmem((width, 8), F32),
            vmem((1, shards, width // shards, 256), F32),
            vmem((local_rows // 2, width_lat), F32),
            vmem((local_rows // 2, width_lat), F32),
            vmem((local_rows // 4, width_lat), F32),
            vmem((shards, local_rows // 16, width_lat), F32),
            vmem((shards - 1, local_rows // 16, width_lat), F32),
            vmem((local_rows // 16, width_lat), F32),
            vmem((local_rows // 16, width_lat), F32),
            vmem((3, share, width_lat // 2), BF16),
            vmem((2, share, width // 2), BF16),
            vmem((local_rows, cols), F32),
            vmem((shards, local_rows // 16, width_lat), F32),
            vmem((shards - 1, local_rows // 16, width_lat), F32),
            vmem((shards, local_rows // 16 + 8, width_lat), F32),
            vmem((2, local_rows // 4 + 8, width_lat), F32),
            vmem((2, local_rows // 2 + 8, width_lat), F32),
            vmem((2, 8, width_lat), F32),
        ] + [sem((3, 14))] * 2 + [sem((2, 14))] * 2 + [sem((14,))] * 4 + [sem((6,))] * 2 + [sem((3, shards))] * 2 + [sem((seqs,))] * 2 + [sem((2,))] * 2 + [sem((shards + 1,))] * 2 + [sem((seqs, shards))] * 2
        + [sem((16,)), sem((2,)), sem((5,))],
        compiler_params=pltpu.CompilerParams(vmem_limit_bytes=VMEM_LIMIT, collective_id=2, has_side_effects=True),
        name="second",
    )(x_cols, rows_in, mask, w_cols, qt, pairs, xn, grad_out, stats, mixed, lat_low, grads, vectors, lang_rows, lat_sum, w_query, lat_f32, lat_gain)


def middle_kernel(att_ref, lat_ref, cot_hbm, all_hbm, bup_tiles, vecs_ref, lse_ref,
                  mixed_all, do_ref, stat_ref, half_out, vec_ref, sum_ref,
                  rows_ref, mid_ref, low_ref, hid_ref, norm_ref, a_ref, b_src, b_ref, bup_ref, all_ref, mixed_ref, cot_ref, slope_ref, half_ref, a_ss, a_rs, b_ss, b_rs, load_sem, mix_ss, mix_rs):
    items, _, me, _, core = places()
    far = lax.rem(me + 2, 4)
    to_sib = mesh_at(di=items + 1 - 2 * core)
    seqs, width, local_rows = att_ref.shape
    rows = seqs * local_rows
    heads = lse_ref.shape[1]
    head_dim = width // heads
    half = width // 2
    block = 256
    pending = []
    loads = [pltpu.make_async_copy(all_hbm.at[i], all_ref.at[i], load_sem.at[i]) for i in range(3)]
    cots = [pltpu.make_async_copy(cot_hbm.at[me * seqs + s], cot_ref.at[pl.ds(s * local_rows, local_rows)], load_sem.at[4 + s]) for s in range(seqs)]
    for copy in cots + loads:
        copy.start()
    greet([to_sib, mesh_at(dh=far)])
    shards, cols = half_ref.shape[1:3]
    for h in range(shards):
        bup_ref[:, h * cols:(h + 1) * cols] = bup_tiles[h, 7:8, :cols]
    gain_ref, bias_ref, bdown_ref = vecs_ref.at[pl.ds(2, 1)], vecs_ref.at[pl.ds(3, 1)], vecs_ref.at[pl.ds(4, 1)]

    def block_loop(body):
        def step(i, _):
            body(pl.ds(pl.multiple_of(i * block, block), block))
            return 0
        lax.fori_loop(0, width // block, step, 0)

    def share_a(i):
        pending.append(send(a_ref.at[i, 0], a_ref.at[i, 1], a_ss.at[i], a_rs.at[i], to_sib))

    def share_b(i):
        theirs = b_src.at[i, :, pl.ds(pl.multiple_of((1 - core) * half, 128), half)]
        pending.append(send(theirs, b_ref.at[i, 1], b_ss.at[i], b_rs.at[i], to_sib))
        b_ref[i, 0] = b_src[i, :, pl.ds(pl.multiple_of(core * half, 128), half)]

    for s in range(seqs):
        at = slice(s * local_rows, (s + 1) * local_rows)
        low = att_ref[s].astype(BF16)
        a_ref[0, 0, :, at] = low
        rows_ref[at] = jnp.transpose(att_ref[s]).astype(BF16)
    share_a(0)
    for copy in cots:
        copy.wait()
    b_src[2] = cot_ref[...]
    share_b(2)

    def branch(at):
        latent = lat_ref[:, at].astype(F32)
        mid_ref[:, at] = dot(rows_ref[...], all_ref[0, :, at]) + jnp.concatenate([latent] * seqs, axis=0)
    loads[0].wait()
    block_loop(branch)
    mid_out, normed, inverse = norm_keep(mid_ref[...], gain_ref[...], bias_ref[...])
    norm_ref[...] = normed
    b_src[1] = mid_out.astype(BF16)
    share_b(1)

    def up(at):
        value = dot_nt(b_src[1], all_ref[1, at]) + bup_ref[:, at]
        square = value * value
        bend = jnp.tanh(0.7978845608028654 * (value + 0.044715 * (square * value)))
        active = 0.5 * value * (1.0 + bend)
        slope_ref[:, at] = 0.5 * (1.0 + bend) + 0.5 * value * (1.0 - bend * bend) * (0.7978845608028654 * (1.0 + 0.134145 * square))
        rows_ref[:, at] = active.astype(BF16)
        a_ref[2, 0, at] = jnp.transpose(active.astype(BF16))
    loads[1].wait()
    block_loop(up)
    share_a(2)

    def down(at):
        out = mid_ref[:, at] + dot(rows_ref[...], all_ref[2, :, at]) + bdown_ref[:, at]
        for s in range(seqs):
            mixed_ref[s, :, at] = out[s * local_rows:(s + 1) * local_rows].astype(BF16)
    loads[2].wait()
    block_loop(down)
    own_mixed = pltpu.make_async_copy(mixed_ref, mixed_all.at[pl.ds(me * seqs, seqs)], load_sem.at[3])
    own_mixed.start()
    for i, there in enumerate((far,)):
        pending.append(send(mixed_ref.at[0], mixed_all.at[me * seqs], mix_ss.at[i], mix_rs.at[i], mesh_at(dh=there)))

    def up_back(at):
        grad = (dot_nt(cot_ref[...], all_ref[2, at]) * slope_ref[:, at]).astype(BF16)
        low_ref[:, at] = grad
        vec_ref[2:3, at] = jnp.sum(grad.astype(F32), axis=0, keepdims=True)
        a_ref[1, 0, at] = jnp.transpose(grad)
    block_loop(up_back)
    share_a(1)

    def mid_back(at):
        hid_ref[:, at] = dot(low_ref[...], all_ref[1, :, at])
    block_loop(mid_back)
    grad = hid_ref[...]
    normed = norm_ref[...]
    vec_ref[0:1] = jnp.sum(grad * normed, axis=0, keepdims=True)
    vec_ref[1:2] = jnp.sum(grad, axis=0, keepdims=True)
    vec_ref[3:4] = jnp.sum(cot_ref[...].astype(F32), axis=0, keepdims=True)
    grad = cot_ref[...].astype(F32) + norm_back(grad, normed, inverse, gain_ref[...])
    b_src[0] = grad.astype(BF16)
    share_b(0)
    total = grad[:local_rows]
    for s in range(1, seqs):
        total += grad[s * local_rows:(s + 1) * local_rows]
    sum_ref[...] = total

    def out(h, _):
        at = pl.ds(pl.multiple_of(h * head_dim, 16), head_dim)
        grad = dot_nt(all_ref[0, at], b_src[0]).astype(BF16)
        for s in range(seqs):
            part = grad[:, s * local_rows:(s + 1) * local_rows]
            do_ref[s, at] = part
            delta = jnp.sum(part.astype(F32) * att_ref[s, at], axis=0, keepdims=True)
            stat_ref[pl.ds((2 * s + 1) * heads + h, 1)] = delta
        return 0
    lax.fori_loop(0, heads, out, 0)
    for s in range(seqs):
        stat_ref[2 * s * heads:(2 * s + 1) * heads] = lse_ref[s]

    def arrived(where, ss, rs):
        pltpu.make_async_remote_copy(src_ref=where, dst_ref=where, send_sem=ss, recv_sem=rs,
                                     device_id=to_sib, device_id_type=pl.DeviceIdType.MESH).wait_recv()

    stores = []
    for i in (2, 1, 0):
        arrived(a_ref.at[i, 1], a_ss.at[i], a_rs.at[i])
        arrived(b_ref.at[i, 1], b_ss.at[i], b_rs.at[i])

        def weight(h, _):
            at = pl.ds(pl.multiple_of(h * cols, 16), cols)
            half_ref[i, h] = (dot(a_ref[i, 0, at], b_ref[i, 0]) + dot(a_ref[i, 1, at], b_ref[i, 1])).astype(BF16)
            return 0
        lax.fori_loop(0, shards, weight, 0)
        copy = pltpu.make_async_copy(half_ref.at[i], half_out.at[i], load_sem.at[4 + seqs + i])
        copy.start()
        stores.append(copy)
    own_mixed.wait()
    for copy in stores:
        copy.wait()
    for i, there in enumerate((far,)):
        arrived(mixed_all.at[there * seqs], mix_ss.at[i], mix_rs.at[i])
    for copy in pending:
        copy.wait_send()


def middle_call(att, latents, cot, weights, b_up, vecs, lse):
    seqs, width, local_rows = att.shape
    rows = seqs * local_rows
    heads = lse.shape[1]
    shards = lax.axis_size("heads")
    whole = pl.BlockSpec(memory_space=pltpu.VMEM)
    out, vmem, sem = jax.ShapeDtypeStruct, pltpu.VMEM, pltpu.SemaphoreType.DMA
    return pl.pallas_call(
        middle_kernel,
        in_specs=[whole, whole, pl.BlockSpec(memory_space=pl.ANY), pl.BlockSpec(memory_space=pl.ANY), whole, whole, whole],
        out_specs=[pl.BlockSpec(memory_space=pl.ANY)] + [whole] * 2 + [pl.BlockSpec(memory_space=pl.ANY)] + [whole] * 2,
        out_shape=[
            out((shards * seqs, local_rows, width), BF16),
            out((seqs, width, local_rows), BF16),
            out((2 * seqs * heads, local_rows), F32),
            out((3, shards, width // shards, width // 2), BF16),
            out((4, width), F32),
            out((local_rows, width), F32),
        ],
        scratch_shapes=[
            vmem((rows, width), BF16), vmem((rows, width), F32), vmem((rows, width), BF16), vmem((rows, width), F32), vmem((rows, width), F32),
            vmem((3, 2, width, rows), BF16), vmem((3, rows, width), BF16), vmem((3, 2, rows, width // 2), BF16),
            vmem((1, width), F32), vmem((3, width, width), BF16), vmem((seqs, local_rows, width), BF16), vmem((rows, width), BF16), vmem((rows, width), F32),
            vmem((3, shards, width // shards, width // 2), BF16),
            sem((3,)), sem((3,)), sem((3,)), sem((3,)), sem((7 + seqs,)), sem((1,)), sem((1,)),
        ],
        compiler_params=pltpu.CompilerParams(vmem_limit_bytes=VMEM_LIMIT, collective_id=4, has_side_effects=True),
        name="middle",
    )(att, latents, cot, weights, b_up, vecs, lse)


def finish_kernel(lat_hbm, pair_hbm, small_ref, vec_ref, query_ref, latn_hbm, g_hbm, mixed_hbm, glat_hbm,
                  table_out, igain_out, ibias_out, lgain_out, lbias_out, mgain_out, mbias_out, wq_out, wk_out, wv_out, wo_out, wu_out,
                  bup_out, wd_out, bdown_out, g_out, mixed_out, glat_out, wq_ref, wk_ref, wv_ref, wo_ref, wu_ref, wd_ref, g_ref, mixed_ref, lat_ref, pair_ref, latn_ref, glat_ref, row_ref, sems, pass_sems):
    me = lax.axis_index("heads")
    copies = []

    def store(ref, out):
        copy = pltpu.make_async_copy(ref, out, sems.at[len(copies)])
        copy.start()
        copies.append(copy)

    sources = ((g_hbm, g_ref), (mixed_hbm, mixed_ref), (lat_hbm, lat_ref), (pair_hbm, pair_ref), (latn_hbm, latn_ref), (glat_hbm, glat_ref))
    loads = [pltpu.make_async_copy(src, dst, pass_sems.at[i]) for i, (src, dst) in enumerate(sources)]
    for copy in loads:
        copy.start()
    loads[2].wait()
    wo_ref[...] = lat_ref[0].astype(F32)
    store(wo_ref, wo_out)
    wd_ref[...] = lat_ref[2].astype(F32)
    store(wd_ref, wd_out)
    wu_ref[...] = lat_ref[1].astype(F32)
    store(wu_ref, wu_out)
    loads[0].wait()
    store(g_ref, g_out)
    loads[1].wait()
    store(mixed_ref, mixed_out)
    loads[3].wait()
    wk_ref[...] = pair_ref[0].astype(F32)
    store(wk_ref, wk_out)
    wv_ref[...] = pair_ref[1].astype(F32)
    store(wv_ref, wv_out)
    loads[5].wait()
    store(glat_ref, glat_out)
    loads[4].wait()
    query = query_ref[0].astype(BF16)
    for i in range(0, latn_ref.shape[1], 256):
        wq_ref[:, i:i + 256] = dot(query, latn_ref[:, i:i + 256])
    store(wq_ref, wq_out)
    turned = jnp.transpose(small_ref[0, :, :128])
    table_out[...] = turned[:table_out.shape[0]]
    igain_out[...] = turned[32]
    ibias_out[...] = turned[33]
    lgain_out[...] = vec_ref[0]
    lbias_out[...] = vec_ref[1]
    blocks = row_ref.shape[1] // 128
    for v, out in enumerate((mgain_out, mbias_out, None, bdown_out)):
        for b in range(blocks):
            row_ref[:, b * 128:(b + 1) * 128] = small_ref[0, v * blocks + b:v * blocks + b + 1, 128:]
        if out is not None:
            out[...] = row_ref[0]
        else:
            cols = bup_out.shape[0]
            total = jnp.zeros((1, cols), F32)
            for h in range(row_ref.shape[1] // cols):
                total += jnp.where(me == h, row_ref[:, h * cols:(h + 1) * cols], 0.0)
            bup_out[...] = total[0]
    for copy in copies:
        copy.wait()


def finish_call(lat_total, pair_total, small, vec, query, latn, grad, mixed, grad_lat, langs):
    _, cols, width_lat = lat_total.shape
    width = pair_total.shape[2]
    share = small.shape[1]
    whole = pl.BlockSpec(memory_space=pltpu.VMEM)
    hbm = pl.BlockSpec(memory_space=pl.ANY)
    out, vmem = jax.ShapeDtypeStruct, pltpu.VMEM
    big = [(cols, width_lat), (cols, width), (cols, width), (cols, width_lat), (cols, width_lat), (cols, width_lat)]
    return pl.pallas_call(
        finish_kernel,
        in_specs=[hbm, hbm, whole, whole, whole, hbm, hbm, hbm, hbm],
        out_specs=[whole] * 7 + [hbm] * 5 + [whole, hbm, whole, hbm, hbm, hbm],
        out_shape=[out(shape, F32) for shape in [(langs, share), (share,), (share,)] + [(width_lat,)] * 4 + big[:5] + [(cols,)] + big[5:] + [(width_lat,)]]
        + [out(x.shape, x.dtype) for x in (grad, mixed, grad_lat)],
        scratch_shapes=[vmem(shape, F32) for shape in big] + [vmem(x.shape, x.dtype) for x in (grad, mixed, lat_total, pair_total, latn, grad_lat)]
        + [vmem((1, width_lat), F32), pltpu.SemaphoreType.DMA((9,)), pltpu.SemaphoreType.DMA((6,))],
        compiler_params=pltpu.CompilerParams(vmem_limit_bytes=VMEM_LIMIT),
        name="finish",
    )(lat_total, pair_total, small, vec, query, latn, grad, mixed, grad_lat)


REST = ("items", "blk")
ALL = ("heads", "items", "blk")


def gather_rows(shard):
    count = lax.axis_size("items") * lax.axis_size("blk")
    me = lax.axis_index("items") * lax.axis_size("blk") + lax.axis_index("blk")
    share = shard.shape[0] // count
    part = lax.dynamic_slice_in_dim(shard, me * share, share, 0)
    return lax.all_gather(part, ALL, axis=0, tiled=True)


def scatter_rows(whole):
    part = lax.psum_scatter(whole.astype(BF16), ALL, scatter_dimension=0, tiled=True)
    return lax.all_gather(part, REST, axis=0, tiled=True)


def general_device(inputs, padding, language, lang_table, latents, in_gain, in_bias, lat_gain, lat_bias, mid_gain, mid_bias,
              w_query, w_key, w_value, w_out, w_up, b_up, w_down, b_down, cotangent):
    length, local_seqs, width = inputs.shape
    local_rows, width_lat = latents.shape
    cols = w_query.shape[1]
    head_dim = width_lat // HEADS
    per_shard = cols // head_dim
    shards = lax.axis_size("heads")
    blocks = lax.axis_size("blk")
    rows = local_rows * blocks
    seqs = local_seqs // shards
    me = lax.axis_index("heads")
    first = me * seqs

    pair_shard = jnp.concatenate([w_key.T, w_value.T], axis=0)
    pair_rows = gather_rows(pair_shard)
    latent_shard = jnp.concatenate([w_out, w_up.T, w_down], axis=0)
    lat_all = gather_rows(latent_shard).reshape(shards, 3, cols, width_lat)
    out_all, up_all, down_all = (lat_all[:, i].reshape(width_lat, width_lat) for i in range(3))

    all_latents = lax.all_gather(latents, "blk", axis=0, tiled=True).astype(F32)
    lat_out, _, _ = norm_keep(all_latents, lat_gain, lat_bias)
    lat_low = lat_out.astype(BF16)
    query_part = dot(lat_low, w_query).astype(BF16)
    queries = lax.all_gather(query_part, "heads", axis=1, tiled=True)
    q = queries.reshape(rows, HEADS, head_dim).transpose(1, 0, 2)

    own = lax.dynamic_slice_in_dim(inputs, first, seqs, 1)
    x_cols = jnp.transpose(own, (1, 2, 0))
    live = jnp.transpose(lax.dynamic_slice_in_dim(padding, first, seqs, 1))
    mask = jnp.where(live > 0, 0.0, MASKED).astype(F32)[:, None, :]
    own_lang = lax.dynamic_slice_in_dim(language, first, seqs, 0)
    onehot = (own_lang[:, None] == jnp.arange(lang_table.shape[0], dtype=jnp.int32)[None, :]).astype(F32)
    emb = jnp.dot(onehot, lang_table.astype(F32), precision=lax.Precision.HIGHEST)[:, :, None]
    gain_col, bias_col = in_gain[:, None], in_bias[:, None]

    pairs, o_cols, lse = forward_call(x_cols, emb, gain_col, bias_col, pair_rows, q, mask, per_shard)

    parts = o_cols.reshape(seqs, width_lat, blocks, local_rows).transpose(2, 0, 3, 1)
    parts = lax.all_to_all(parts, "blk", 0, 0, tiled=True).astype(F32)
    lse_parts = lse.reshape(seqs, HEADS, blocks, local_rows).transpose(2, 0, 3, 1)
    lse_parts = lax.all_to_all(lse_parts, "blk", 0, 0, tiled=True)
    top = jnp.max(lse_parts, axis=0)
    shares = jnp.exp2(lse_parts - top)
    total = jnp.sum(shares, axis=0)
    own_lse = top + jnp.log2(total)
    shares = shares / total
    attended = jnp.sum(parts.reshape(blocks, seqs, local_rows, HEADS, head_dim) * shares[..., None], axis=0)
    att_low = attended.reshape(seqs * local_rows, width_lat).astype(BF16)

    cot = lax.dynamic_slice_in_dim(cotangent, first, seqs, 0).reshape(seqs * local_rows, width_lat)
    lat_f32 = latents.astype(F32)
    middle = (lat_f32[None] + dot(att_low, out_all).reshape(seqs, local_rows, width_lat)).reshape(seqs * local_rows, width_lat)
    mid_out, mid_normed, mid_inverse = norm_keep(middle, mid_gain, mid_bias)
    mid_low = mid_out.astype(BF16)
    b_up_all = lax.all_gather(b_up, "heads", axis=0, tiled=True)
    hidden = dot_nt(mid_low, up_all) + b_up_all
    active, gelu_back = jax.vjp(jax.nn.gelu, hidden)
    active_low = active.astype(BF16)
    own_mixed = (middle + dot(active_low, down_all) + b_down).astype(BF16).reshape(seqs, local_rows, width_lat)
    mixed_latents = lax.all_gather(own_mixed, "heads", axis=0, tiled=True)

    grad_b_down = jnp.sum(cot.astype(F32), axis=0)
    grad_w_down = dot(active_low.T, cot)
    grad_active = dot_nt(cot, down_all)
    grad_hidden = gelu_back(grad_active)[0].astype(BF16)
    grad_b_up = jnp.sum(grad_hidden.astype(F32), axis=0)
    grad_w_up = dot(grad_hidden.T, mid_low)
    grad_mid_norm = dot(grad_hidden, up_all)
    grad_mid_gain = jnp.sum(grad_mid_norm * mid_normed, axis=0)
    grad_mid_bias = jnp.sum(grad_mid_norm, axis=0)
    grad_middle = cot.astype(F32) + norm_back(grad_mid_norm, mid_normed, mid_inverse, mid_gain)
    grad_branch = grad_middle.astype(BF16)
    grad_w_out = dot(att_low.T, grad_branch)
    grad_att = dot_nt(grad_branch, out_all).astype(BF16).reshape(seqs, local_rows, width_lat)
    grad_att_heads = grad_att.reshape(seqs, local_rows, HEADS, head_dim)
    delta = jnp.sum(grad_att_heads.astype(F32) * attended, axis=-1)
    lat_sum = jnp.sum(grad_middle.reshape(seqs, local_rows, width_lat), axis=0)

    all_grad_att = lax.all_gather(grad_att, "blk", axis=1, tiled=True).reshape(seqs, rows, HEADS, head_dim)
    stats = lax.all_gather(jnp.concatenate([own_lse, delta], axis=-1), "blk", axis=1, tiled=True)
    stats = jnp.transpose(stats, (0, 2, 1))[..., None]
    g_cols, dw_pair, dq, dgain, dbias, demb = backward_call(
        x_cols, emb, gain_col, bias_col, pair_rows.T, q, q.transpose(0, 2, 1),
        all_grad_att.transpose(0, 2, 1, 3), all_grad_att.transpose(0, 2, 3, 1),
        stats[:, :HEADS], stats[:, HEADS:], mask, pairs, per_shard)

    send = g_cols.reshape(seqs, shards, width // shards, length).transpose(1, 0, 2, 3)
    got = lax.all_to_all(send, "heads", 0, 0, tiled=True)
    grad_inputs = got.reshape(local_seqs, width // shards, length).transpose(2, 0, 1)

    grad_rows = jnp.stack([grad_w_out, grad_w_up, grad_w_down], axis=0).reshape(3, shards, cols, width_lat)
    lat_total = scatter_rows(grad_rows.transpose(1, 0, 2, 3).reshape(-1, width_lat)).astype(F32)
    pair_total = scatter_rows(dw_pair).astype(F32)

    dq_part = lax.psum_scatter(dq.reshape(width_lat, rows).astype(BF16), "heads", scatter_dimension=0, tiled=True)
    query_low = lax.psum(dq_part, REST)
    grad_w_query = dot(lat_low.T, query_low.T)
    lat_mine = lax.dynamic_slice_in_dim(query_low, lax.axis_index("blk") * local_rows, local_rows, 1)
    grad_lat_part = dot(lat_mine.T, w_query.T)
    grad_lat_norm = lax.psum(grad_lat_part.astype(BF16), "heads").astype(F32)
    lat_sum = lax.psum(lat_sum.astype(BF16), ("heads", "items")).astype(F32)
    _, own_normed, own_inverse = norm_keep(lat_f32, lat_gain, lat_bias)
    grad_latents = lat_sum + norm_back(grad_lat_norm, own_normed, own_inverse, lat_gain)
    lat_small = jnp.concatenate([jnp.sum(grad_lat_norm * own_normed, axis=0), jnp.sum(grad_lat_norm, axis=0)])
    lat_small = lax.psum(lat_small, "blk")

    table = jnp.dot(onehot.T, demb[:, :, 0], precision=lax.Precision.HIGHEST)
    small = jnp.concatenate([table.reshape(-1), dgain[:, 0], dbias[:, 0], grad_mid_gain, grad_mid_bias, grad_b_up, grad_b_down])
    small = lax.psum(small, ALL)
    sizes = [table.size, width, width, width_lat, width_lat, width_lat, width_lat]
    ends = [sum(sizes[:i]) for i in range(len(sizes) + 1)]
    table, dgain, dbias, dmid_gain, dmid_bias, db_up, db_down = (small[ends[i]:ends[i + 1]] for i in range(7))
    share = width // shards
    table = lax.dynamic_slice_in_dim(table.reshape(-1, width), me * share, share, 1)
    return (
        mixed_latents,
        grad_inputs,
        grad_latents,
        table,
        lax.dynamic_slice_in_dim(dgain, me * share, share, 0),
        lax.dynamic_slice_in_dim(dbias, me * share, share, 0),
        lat_small[:width_lat],
        lat_small[width_lat:],
        dmid_gain,
        dmid_bias,
        grad_w_query,
        pair_total[:cols].T,
        pair_total[cols:].T,
        lat_total[:cols],
        lat_total[cols:2 * cols].T,
        lax.dynamic_slice_in_dim(db_up, me * cols, cols, 0),
        lat_total[2 * cols:],
        db_down,
    )


def fast_device(inputs, padding, language, lang_table, latents, in_gain, in_bias, lat_gain, lat_bias, mid_gain, mid_bias,
              w_query, w_key, w_value, w_out, w_up, b_up, w_down, b_down, cotangent):
    length, local_seqs, width = inputs.shape
    local_rows, width_lat = latents.shape
    cols = w_query.shape[1]
    head_dim = width_lat // HEADS
    per_shard = cols // head_dim
    shards = lax.axis_size("heads")
    blocks = lax.axis_size("blk")
    rows = local_rows * blocks
    seqs = local_seqs // shards
    me = lax.axis_index("heads")
    first = me * seqs

    vectors = (lat_gain, lat_bias, mid_gain, mid_bias, b_down, in_gain, in_bias, b_up)
    wq_rows = w_query.T
    w_cols, lat_all, pairs, xn, att_cols, lse_cols, queries_t, lat_low, b_up_tiles, x_cols, rows_in, mask, lang_rows, lat_f32, vecs = first_call(
        inputs, padding.T, language, lang_table, vectors, latents, wq_rows,
        (w_key.T, w_value.T, w_out, w_up.T, w_down), rows, seqs)
    mixed, grad_att, stats, grads, vectors, lat_sum = middle_call(att_cols, latents, cotangent, lat_all, b_up_tiles, vecs, lse_cols)
    grad_att = grad_att.reshape(seqs, shards, cols, local_rows)
    g_cols, mixed_latents, pair_total, lat_total, small, grad_latents, lat_small, dq, lat_low_all = second_call(
        x_cols, rows_in, mask, w_cols, queries_t, pairs, xn, grad_att, stats, mixed, lat_low, grads, vectors, lang_rows, lat_sum,
        wq_rows, lat_f32, vecs)
    rest = finish_call(
        lat_total, pair_total, small, lat_small, dq, lat_low_all, g_cols, mixed_latents, grad_latents, lang_table.shape[0])
    rest = [x.T if i in (7, 8, 9, 11) else x for i, x in enumerate(rest)]
    return (rest[-2], rest[-3].transpose(2, 0, 1), rest[-1]) + tuple(rest[:-3])


def solution(mesh):
    placed = (
        P("blk", "items", None), P("blk", "items"), P("items"), P(), P("blk", None), P(), P(), P(), P(), P(), P(),
        P(None, "heads"), P(None, "heads"), P(None, "heads"), P("heads", None), P(None, "heads"), P("heads"),
        P("heads", None), P(), P("items", "blk", None),
    )
    out = (
        P("items", "blk", None), P("blk", "items", "heads"), P("blk", None), P(None, "heads"), P("heads"), P("heads"),
        P(), P(), P(), P(), P(None, "heads"), P(None, "heads"), P(None, "heads"), P("heads", None), P(None, "heads"),
        P("heads"), P("heads", None), P(),
    )
    fits = mesh.shape["blk"] == 2 and mesh.shape["items"] == 4 and mesh.shape["heads"] == 4
    return jax.shard_map(fast_device if fits else general_device, mesh=mesh, in_specs=placed, out_specs=out, check_vma=False)
```
